32 devices in a mesh: rows: 8 (over y, x, core), cols: 4 (over z).
Axes of the slice: x: 2, y: 2, z: 4, core: 2. Of those that a mesh axis runs over, the one named last changes fastest.
Arguments:
- affinity: bfloat16 [4, 64, 4, 8, 4096], P(None, 'rows', 'cols'), may hold values from -6 to 6
- block_columns: int32 [4, 64, 4, 8], P(None, 'rows', 'cols'), may hold values from 0 to 63
- block_counts: int32 [4, 64, 4], P(None, 'rows', 'cols'), may hold values from 0 to 8
- inv_degree: float32 [4, 64, 64], P('cols', 'rows'), may hold values from 0.4 to 6.1
- panel: float32 [4, 64, 4096], P('cols', 'rows'), may hold values from -6 to 6
Outputs:
- panel_out: float32 [4, 64, 4096], P('cols', 'rows')
The draws below stay inside these ranges and needn't reach their ends.
Inputs may be any that keep to these rules, and one draw needn't show every extreme that they name: `block_columns`: slots at or past a block row's count are ignored; listed block columns may repeat, and their blocks then add.
All inputs are finite; a program needn't handle non-finite values.
Results may differ from the reference program's by a relative error of at most 0.019.
Values may be sent and summed in bfloat16 or wider, within the bound.
No kernel may reach another device: no remote copies, remote signals or barrier semaphores. Data moves between devices by JAX's collectives and lax.ppermute only.
A program may use at most 128 MiB of HBM per device.

```python
import jax
import jax.numpy as jnp
from jax import lax

B = 64
K = 64
MAXB = 8
ITERS = 2
NBR = 256
N = 16384
N_COLS = 4


def draw_block_counts(key, part):
    shape = (N_COLS, NBR // N_COLS, N_COLS)
    first, second, third = jax.random.split(jax.random.fold_in(key, 7), 3)
    base = jax.random.randint(first, shape, 0, MAXB // 2 + 1)
    heavy = jax.random.randint(second, shape, 0, 4) == 0
    upper = MAXB - jax.random.randint(third, shape, 0, 2)
    counts = jnp.where(heavy, upper, base).astype(jnp.int32)
    counts = counts.at[0, 0, 0].set(MAXB)
    counts = counts.at[0, 0, N_COLS - 1].set(0)
    return counts


def draw_inv_degree(key, part):
    shape = (N_COLS, NBR // N_COLS, B)
    order = lax.broadcasted_iota(jnp.float32, shape, 0) * float(NBR // N_COLS) + lax.broadcasted_iota(jnp.float32, shape, 1)
    trend = 1.0 + 2.0 * order / float(NBR)
    inner = jax.random.fold_in(key, 11)
    rough = jnp.exp(jax.random.uniform(inner, shape, jnp.float32, -0.7, 0.7))
    return rough * trend


def with_ends(result, key, low, top_value):
    extent = result.shape
    index_at = [jax.random.randint(jax.random.fold_in(key, axis), (), 0, extent[axis]) for axis in range(len(extent))]
    result = result.at[tuple(index_at)].set(low)
    longest = extent.index(max(extent))
    index_at[longest] = (index_at[longest] + 1) % extent[longest]
    return result.at[tuple(index_at)].set(top_value)


def levels(stream_key, extent, cuts, least, largest):
    def one(position, blocks):
        heights = jax.random.uniform(jax.random.fold_in(jax.random.fold_in(stream_key, 6), position), (blocks,), jnp.float32, least / len(cuts), largest / len(cuts))
        return jnp.repeat(jnp.exp(heights), extent[position] // blocks).reshape((-1,) + (1,) * (len(extent) - position - 1))

    gain = one(*cuts[0])
    for cut in cuts[1:]:
        gain = gain * one(*cut)
    return gain


def bell_draw(rng, shape, spread, bound, cuts=(), kind=jnp.bfloat16):
    entries = spread * jax.random.normal(rng, shape, jnp.float32)
    if cuts:
        entries = entries * levels(rng, shape, cuts, -0.22, 0.18)
    return jnp.clip(entries, -bound, bound).astype(kind)


def setup_inputs(seed: int = 0) -> dict:
    key_of = jax.random.split(jax.random.key(seed), 6)
    return {
        "affinity": bell_draw(key_of[0], (N_COLS, NBR // N_COLS, N_COLS, MAXB, B * B), 1.0, 6.0, ((1, 8), (2, 4))),
        "block_columns": with_ends(jax.random.randint(key_of[1], (N_COLS, NBR // N_COLS, N_COLS, MAXB), 0, NBR // N_COLS), jax.random.fold_in(key_of[1], 1), 0, (NBR // N_COLS) - 1).astype(jnp.int32),
        "block_counts": draw_block_counts(jax.random.fold_in(key_of[5], 71), 0),
        "inv_degree": draw_inv_degree(jax.random.fold_in(key_of[5], 71), 0),
        "panel": bell_draw(key_of[4], (N_COLS, NBR // N_COLS, B * K), 1.0, 6.0, ((0, 4), (1, 8)), jnp.float32),
    }


def block_terms(values_slice, columns_slice, counts_slice, panel_blocks):
    groups = values_slice.shape[0]
    block_rows = values_slice.shape[1]
    accum = jnp.zeros((groups, block_rows, B, K), jnp.float32)
    for slot_index in range(MAXB):
        picked = jnp.take(panel_blocks, columns_slice[:, :, slot_index].astype(jnp.int32), axis=0)
        live = (counts_slice > slot_index)[:, :, None, None]
        picked = jnp.where(live, picked, jnp.zeros_like(picked))
        matrix = values_slice[:, :, slot_index].reshape(groups, block_rows, B, B)
        accum = accum + jnp.einsum('giab,gibk->giak', matrix.astype(jnp.float32), picked.astype(jnp.float32))
    return accum

def reference(affinity, block_columns, block_counts, inv_degree, panel):
    per_range = NBR // N_COLS
    current = panel
    identity = jnp.eye(K, dtype=jnp.float32)
    for iteration in range(ITERS):
        scaled = (current.reshape(N_COLS, per_range, B, K) * inv_degree[..., None]).astype(jnp.bfloat16)

        def one_range(range_index, accum):
            values_slice = lax.dynamic_index_in_dim(affinity, range_index, 2, keepdims=False)
            columns_slice = lax.dynamic_index_in_dim(block_columns, range_index, 2, keepdims=False)
            counts_slice = lax.dynamic_index_in_dim(block_counts, range_index, 2, keepdims=False)
            panel_blocks = lax.dynamic_index_in_dim(scaled, range_index, 0, keepdims=False)
            term = block_terms(values_slice, columns_slice, counts_slice, panel_blocks)
            rounded = lax.optimization_barrier(term.astype(jnp.bfloat16))
            return accum + rounded.astype(jnp.float32)
        summed = lax.fori_loop(0, N_COLS, one_range, jnp.zeros((N_COLS, per_range, B, K), jnp.float32))
        rows_out = (summed * inv_degree[..., None]).reshape(-1, K)
        gram_matrix = jnp.dot(rows_out.T, rows_out, precision=lax.Precision.HIGHEST) / float(N)
        lower_factor = jnp.linalg.cholesky(gram_matrix)
        inverse = lax.linalg.triangular_solve(lower_factor, identity, left_side=True, lower=True)
        current = jnp.dot(rows_out, inverse.T, precision=lax.Precision.HIGHEST).reshape(N_COLS, per_range, B * K)
    return current
```

```python
import functools

import jax
import jax.numpy as jnp
from jax import lax
from jax.experimental import pallas as pl
from jax.experimental.pallas import tpu as pltpu
from jax.sharding import PartitionSpec as P

ITERS = 2
BF16 = jnp.bfloat16
F32 = jnp.float32
HIGHEST = lax.Precision.HIGHEST
VMEM_LIMIT = 48 * 1024 * 1024


def params():
    return pltpu.CompilerParams(vmem_limit_bytes=VMEM_LIMIT)


def vmem():
    return pl.BlockSpec(memory_space=pltpu.VMEM)


def smem():
    return pl.BlockSpec(memory_space=pltpu.SMEM)


def iota(shape, dim):
    return lax.broadcasted_iota(jnp.int32, shape, dim)


def start_kernel(panel_ref, inv_ref, scaled_ref, degree_ref, scratch):
    block_rows, block_size = inv_ref.shape[1], inv_ref.shape[2]
    half = block_size // 2
    for t in range(half):
        scratch[t * block_rows : (t + 1) * block_rows, :] = panel_ref[0, :, t * 128 : (t + 1) * 128]
    pair = iota((half, block_size), 1) // 2 == iota((half, block_size), 0)
    spread = (iota((block_size, 128), 0) % 2 == iota((block_size, 128), 1) // 64).astype(F32)
    rows = [
        jnp.where(pair, jnp.broadcast_to(inv_ref[0, i : i + 1, :], (half, block_size)), 0.0)
        for i in range(block_rows)
    ]
    degree = jnp.dot(
        jnp.concatenate(rows, axis=0), spread, precision=HIGHEST, preferred_element_type=F32
    )
    for i in range(block_rows):
        part = degree[i * half : (i + 1) * half]
        degree_ref[i] = part
        scaled_ref[i] = (scratch[pl.ds(i, half, stride=block_rows), :] * part).astype(BF16)


def start(panel, inv_degree):
    block_rows, block_size = inv_degree.shape[1:]
    shape = (block_rows, block_size // 2, 128)
    return pl.pallas_call(
        start_kernel,
        out_shape=(jax.ShapeDtypeStruct(shape, BF16), jax.ShapeDtypeStruct(shape, F32)),
        in_specs=[vmem(), vmem()],
        out_specs=(vmem(), vmem()),
        scratch_shapes=[pltpu.VMEM((block_rows * block_size // 2, 128), F32)],
        compiler_params=params(),
        name="start",
    )(panel, inv_degree)


def prep_kernel(place_ref, counts_ref, affinity_ref, out_ref, scratch):
    block_rows, slots = affinity_ref.shape[1], affinity_ref.shape[3]
    half = affinity_ref.shape[4] // 128
    group = pl.program_id(0) ^ place_ref[1]
    source, target = iota((256, 256), 0), iota((256, 256), 1)
    moved = (source // 64 % 2) * 128 + (source // 128) * 64 + (source % 2) * 32 + source % 64 // 2
    permute = (moved == target).astype(BF16)
    for i in range(block_rows):
        count = counts_ref[group, i, 0]
        block = affinity_ref[0, i, 0].astype(F32)
        live = iota(block.shape, 0) < count
        block = jnp.where(live, block, 0.0)
        for t in range(half):
            scratch[i % 2, t * slots : (t + 1) * slots, :] = block[:, t * 128 : (t + 1) * 128]
        parts = [
            scratch[i % 2, pl.ds(s, half, stride=slots), :].astype(BF16) for s in range(slots)
        ]
        pairs = [
            jnp.concatenate(parts[s : s + 2], axis=1) for s in range(0, slots, 2)
        ]
        moved_pairs = jnp.dot(
            jnp.concatenate(pairs, axis=0), permute, preferred_element_type=F32
        ).astype(BF16)
        for s in range(slots // 2):
            piece = moved_pairs[s * half : (s + 1) * half]
            out_ref[0, i, :half, s * 128 : (s + 1) * 128] = piece[:, :128]
            out_ref[0, i, half:, s * 128 : (s + 1) * 128] = piece[:, 128:]


def prep(place, block_counts, affinity):
    groups, block_rows, _, slots, flat = affinity.shape
    return pl.pallas_call(
        prep_kernel,
        grid_spec=pltpu.PrefetchScalarGridSpec(
            num_scalar_prefetch=2,
            grid=(groups,),
            in_specs=[
                pl.BlockSpec(
                    (1, block_rows, 1, slots, flat),
                    lambda m, place, counts: (m ^ place[1], 0, 0, 0, 0),
                )
            ],
            out_specs=pl.BlockSpec(
                (1, block_rows, 64, slots * 64), lambda m, place, counts: (m, 0, 0, 0)
            ),
            scratch_shapes=[pltpu.VMEM((2, flat // 128 * slots, 128), F32)],
        ),
        out_shape=jax.ShapeDtypeStruct((groups, block_rows, 64, slots * 64), BF16),
        compiler_params=params(),
        name="prep",
    )(place, block_counts, affinity)


def product_kernel(offsets, place_ref, columns_ref, matrix_ref, *refs):
    pieces, outs, table = refs[:2], refs[2:-1], refs[-1]
    groups, block_rows, block_size, _ = matrix_ref.shape
    slots = columns_ref.shape[3]
    half = block_size // 2
    blocks = table.shape[0]
    low = iota((half, 128), 1) < 64
    for index, offset in enumerate(offsets):
        per_piece = len(offsets) // 2
        source = pieces[index // per_piece]
        base = (place_ref[0] ^ offset) * block_rows
        for i in range(block_rows):
            block = source[index % per_piece, i]
            turned = jnp.concatenate([block[:, 64:], block[:, :64]], axis=1)
            table[base + i, :half] = jnp.where(low, block, turned)
            table[base + i, half:] = jnp.where(low, turned, block)
    for m in range(groups):
        group = m ^ place_ref[1]

        def one(i, carry):
            picked = [
                table[columns_ref[group, i, 0, s] & (blocks - 1)] for s in range(slots)
            ]
            result = jnp.dot(
                matrix_ref[m, i], jnp.concatenate(picked, axis=0), preferred_element_type=F32
            )
            outs[m][i] = jnp.where(low, result[:half], result[half:]).astype(BF16)
            return carry

        lax.fori_loop(0, block_rows, one, 0, unroll=True)


def product(offsets, place, block_columns, matrix, near, far):
    groups, block_rows, block_size, _ = matrix.shape
    blocks = 2 * near.shape[0] * block_rows
    shape = jax.ShapeDtypeStruct((block_rows, block_size // 2, 128), BF16)
    return pl.pallas_call(
        functools.partial(product_kernel, offsets),
        out_shape=(shape,) * groups,
        in_specs=[smem(), smem(), vmem(), vmem(), vmem()],
        out_specs=(vmem(),) * groups,
        scratch_shapes=[pltpu.VMEM((blocks, block_size, 128), BF16)],
        compiler_params=params(),
        name="product",
    )(place, block_columns, matrix, near, far)


def collect_kernel(degree_ref, *refs):
    terms, rows_ref, gram_ref = refs[:-2], refs[-2], refs[-1]
    summed = terms[0][...].astype(F32)
    for term in terms[1:]:
        summed = summed + term[...].astype(F32)
    rows = summed * degree_ref[...]
    rows_ref[...] = rows
    flat = rows.reshape(-1, 128)
    both = lax.dot_general(
        flat, flat, (((0,), (0,)), ((), ())), precision=HIGHEST, preferred_element_type=F32
    )
    gram = both[:64, :64] + both[64:, 64:]
    gram_ref[...] = jnp.concatenate([gram[:32], gram[32:]], axis=1)


def collect(degree, terms):
    return pl.pallas_call(
        collect_kernel,
        out_shape=(
            jax.ShapeDtypeStruct(degree.shape, F32),
            jax.ShapeDtypeStruct((32, 128), F32),
        ),
        in_specs=[vmem()] * (1 + len(terms)),
        out_specs=(vmem(), vmem()),
        compiler_params=params(),
        name="collect",
    )(degree, *terms)


def inverse_factor(gram):
    size = gram.shape[0]
    row_at = iota((size, 128), 0)
    unit = (iota((size, 64), 0) == iota((size, 64), 1)).astype(F32)
    work = jnp.concatenate([gram, unit], axis=1)
    for j in range(size):
        column = jnp.broadcast_to(work[:, j : j + 1], (size, 128))
        scale = lax.rsqrt(column[j : j + 1])
        row = work[j : j + 1] * scale
        column = jnp.where(row_at > j, column * scale, 0.0)
        work = jnp.where(row_at == j, row, work) - column * row
    return work[:, 64:]


def unpack_gram(parts, total):
    packed = parts[0][...]
    for part in parts[1:]:
        packed = packed + part[...]
    return jnp.concatenate([packed[:, :64], packed[:, 64:]], axis=0) / total


def apply_factor(rows, inverse):
    zero = jnp.zeros_like(inverse)
    both = jnp.concatenate(
        [jnp.concatenate([inverse, zero], axis=1), jnp.concatenate([zero, inverse], axis=1)], axis=0
    )
    return lax.dot_general(
        rows, both, (((1,), (1,)), ((), ())), precision=HIGHEST, preferred_element_type=F32
    )


def middle_kernel(total, degree_ref, rows_ref, *refs):
    inverse = inverse_factor(unpack_gram(refs[:-1], total))
    current = apply_factor(rows_ref[...].reshape(-1, 128), inverse)
    refs[-1][...] = (current.reshape(degree_ref.shape) * degree_ref[...]).astype(BF16)


def middle(total, degree, rows, grams):
    return pl.pallas_call(
        functools.partial(middle_kernel, total),
        out_shape=jax.ShapeDtypeStruct(degree.shape, BF16),
        in_specs=[vmem()] * (2 + len(grams)),
        out_specs=vmem(),
        compiler_params=params(),
        name="middle",
    )(degree, rows, *grams)


def finish_kernel(total, rows_ref, *refs):
    out_ref, scratch = refs[-2:]
    block_rows, half, _ = rows_ref.shape
    inverse = inverse_factor(unpack_gram(refs[:-2], total))
    current = apply_factor(rows_ref[...].reshape(-1, 128), inverse)
    for i in range(block_rows):
        scratch[pl.ds(i, half, stride=block_rows), :] = current[i * half : (i + 1) * half]
    for t in range(half):
        out_ref[0, :, t * 128 : (t + 1) * 128] = scratch[t * block_rows : (t + 1) * block_rows, :]


def finish(total, rows, grams):
    block_rows, half, _ = rows.shape
    return pl.pallas_call(
        functools.partial(finish_kernel, total),
        out_shape=jax.ShapeDtypeStruct((1, block_rows, half * 128), F32),
        in_specs=[vmem()] * (1 + len(grams)),
        out_specs=vmem(),
        scratch_shapes=[pltpu.VMEM((block_rows * half, 128), F32)],
        compiler_params=params(),
        name="finish",
    )(rows, *grams)


def swap(value, axis, mask):
    size = lax.axis_size(axis)
    return lax.ppermute(value, axis, [(index, index ^ mask) for index in range(size)])


def stages(size):
    if size == 8:
        return [[2, 4, 6], [1]]
    bits, bit = [], 1
    while bit < size:
        bits.append([bit])
        bit *= 2
    return bits


def gather_rows(scaled):
    plan = stages(lax.axis_size("rows"))
    held, offsets = scaled[None], [0]
    for masks in plan[:-1]:
        held = jnp.concatenate([held] + [swap(held, "rows", mask) for mask in masks], axis=0)
        offsets = offsets + [mask ^ offset for mask in masks for offset in offsets]
    (last,) = plan[-1]
    offsets = offsets + [last ^ offset for offset in offsets]
    return held, swap(held, "rows", last), offsets


def add_grams(gram):
    for masks in reversed(stages(lax.axis_size("rows"))):
        gram = sum([swap(gram, "rows", mask) for mask in masks], gram)
    return [gram] + [swap(gram, "cols", mask) for mask in range(1, lax.axis_size("cols"))]


def body(affinity, block_columns, block_counts, inv_degree, panel):
    block_rows, block_size = inv_degree.shape[1:]
    groups = affinity.shape[0]
    total = float(groups * lax.axis_size("rows") * block_rows * block_size)
    place = jnp.stack([lax.axis_index("rows"), lax.axis_index("cols")]).astype(jnp.int32)
    scaled, degree = start(panel, inv_degree)
    matrix = prep(place, block_counts, affinity)
    for iteration in range(ITERS):
        near, far, offsets = gather_rows(scaled)
        terms = product(offsets, place, block_columns, matrix, near, far)
        terms = [terms[0]] + [swap(terms[m], "cols", m) for m in range(1, groups)]
        rows, gram = collect(degree, terms)
        grams = add_grams(gram)
        if iteration < ITERS - 1:
            scaled = middle(total, degree, rows, grams)
    return finish(total, rows, grams)


def solution(mesh):
    return jax.shard_map(
        body,
        mesh=mesh,
        in_specs=(
            P(None, "rows", "cols", None, None),
            P(None, "rows", "cols", None),
            P(None, "rows", "cols"),
            P("cols", "rows", None),
            P("cols", "rows", None),
        ),
        out_specs=P("cols", "rows", None),
        check_vma=False,
    )
```

```python
import functools

import jax
import jax.numpy as jnp
from jax import lax
from jax.experimental import pallas as pl
from jax.experimental.pallas import tpu as pltpu
from jax.sharding import PartitionSpec as P

BF16 = jnp.bfloat16
F32 = jnp.float32
HIGHEST = lax.Precision.HIGHEST
VMEM_LIMIT = 48 * 1024 * 1024


def params():
    return pltpu.CompilerParams(vmem_limit_bytes=VMEM_LIMIT)


def vmem():
    return pl.BlockSpec(memory_space=pltpu.VMEM)


def smem():
    return pl.BlockSpec(memory_space=pltpu.SMEM)


def iota(shape, dim):
    return lax.broadcasted_iota(jnp.int32, shape, dim)


def start_kernel(panel_hbm, inv_hbm, scaled_ref, degree_ref, panel_ref, inv_ref, scratch, sems):
    block_rows, block_size = inv_ref.shape[1], inv_ref.shape[2]
    half = block_size // 2
    copies = [
        pltpu.make_async_copy(inv_hbm, inv_ref, sems.at[0]),
        pltpu.make_async_copy(panel_hbm, panel_ref, sems.at[1]),
    ]
    for copy in copies:
        copy.start()
    for copy in copies:
        copy.wait()
    for t in range(half):
        scratch[t * block_rows : (t + 1) * block_rows, :] = panel_ref[0, :, t * 128 : (t + 1) * 128]
    pair = iota((half, block_size), 1) // 2 == iota((half, block_size), 0)
    spread = (iota((block_size, 128), 0) % 2 == iota((block_size, 128), 1) // 64).astype(F32)
    rows = [
        jnp.where(pair, jnp.broadcast_to(inv_ref[0, i : i + 1, :], (half, block_size)), 0.0)
        for i in range(block_rows)
    ]
    degree = jnp.dot(
        jnp.concatenate(rows, axis=0), spread, precision=HIGHEST, preferred_element_type=F32
    )
    for i in range(block_rows):
        part = degree[i * half : (i + 1) * half]
        degree_ref[i] = part
        scaled_ref[i] = (scratch[pl.ds(i, half, stride=block_rows), :] * part).astype(BF16)


def start(panel, inv_degree):
    block_rows, block_size = inv_degree.shape[1:]
    shape = (block_rows, block_size // 2, 128)
    return pl.pallas_call(
        start_kernel,
        out_shape=(jax.ShapeDtypeStruct(shape, BF16), jax.ShapeDtypeStruct(shape, F32)),
        in_specs=[pl.BlockSpec(memory_space=pl.ANY)] * 2,
        out_specs=(vmem(), vmem()),
        scratch_shapes=[
            pltpu.VMEM(panel.shape, F32),
            pltpu.VMEM(inv_degree.shape, F32),
            pltpu.VMEM((block_rows * block_size // 2, 128), F32),
            pltpu.SemaphoreType.DMA((2,)),
        ],
        compiler_params=params(),
        name="start",
    )(panel, inv_degree)


def prep_kernel(place_ref, counts_ref, affinity_ref, out_ref, done_ref, scratch):
    done_ref[...] = jnp.zeros_like(done_ref)
    block_rows, slots = affinity_ref.shape[1], affinity_ref.shape[3]
    half = affinity_ref.shape[4] // 128
    group = pl.program_id(0) ^ place_ref[1]
    source, target = iota((256, 256), 0), iota((256, 256), 1)
    moved = (source // 64 % 2) * 128 + (source // 128) * 64 + (source % 2) * 32 + source % 64 // 2
    permute = (moved == target).astype(BF16)
    for i in range(block_rows):
        count = counts_ref[group, i, 0]
        block = affinity_ref[0, i, 0].astype(F32)
        live = iota(block.shape, 0) < count
        block = jnp.where(live, block, 0.0)
        for t in range(half):
            scratch[i % 2, t * slots : (t + 1) * slots, :] = block[:, t * 128 : (t + 1) * 128]
        parts = [
            scratch[i % 2, pl.ds(s, half, stride=slots), :].astype(BF16) for s in range(slots)
        ]
        pairs = [
            jnp.concatenate(parts[s : s + 2], axis=1) for s in range(0, slots, 2)
        ]
        moved_pairs = jnp.dot(
            jnp.concatenate(pairs, axis=0), permute, preferred_element_type=F32
        ).astype(BF16)
        for s in range(slots // 2):
            piece = moved_pairs[s * half : (s + 1) * half]
            out_ref[0, i, :half, s * 128 : (s + 1) * 128] = piece[:, :128]
            out_ref[0, i, half:, s * 128 : (s + 1) * 128] = piece[:, 128:]


def prep(place, block_counts, affinity):
    groups, block_rows, _, slots, flat = affinity.shape
    return pl.pallas_call(
        prep_kernel,
        grid_spec=pltpu.PrefetchScalarGridSpec(
            num_scalar_prefetch=2,
            grid=(groups,),
            in_specs=[
                pl.BlockSpec(
                    (1, block_rows, 1, slots, flat),
                    lambda m, place, counts: (m ^ place[1], 0, 0, 0, 0),
                )
            ],
            out_specs=[
                pl.BlockSpec(
                    (1, block_rows, 64, slots * 64), lambda m, place, counts: (m, 0, 0, 0)
                ),
                pl.BlockSpec((8, 128), lambda m, place, counts: (0, 0)),
            ],
            scratch_shapes=[pltpu.VMEM((2, flat // 128 * slots, 128), F32)],
        ),
        out_shape=[
            jax.ShapeDtypeStruct((groups, block_rows, 64, slots * 64), BF16),
            jax.ShapeDtypeStruct((8, 128), F32),
        ],
        compiler_params=params(),
        name="prep",
    )(place, block_counts, affinity)


def stack_kernel(count, *refs):
    for index in range(count):
        refs[-1][index] = refs[index][...]


def stack(pieces, after):
    shape = pieces[0].shape
    return pl.pallas_call(
        functools.partial(stack_kernel, len(pieces)),
        out_shape=jax.ShapeDtypeStruct((len(pieces),) + shape, BF16),
        in_specs=[vmem()] * (len(pieces) + len(after)),
        out_specs=vmem(),
        compiler_params=params(),
        name="stack",
    )(*pieces, *after)


def split(value):
    high = value.astype(BF16)
    rest = value - high.astype(F32)
    middle = rest.astype(BF16)
    return high, middle, (rest - middle.astype(F32)).astype(BF16)


def joined(ref, where, first):
    high, middle, low = (ref[(*where, first + part)].astype(F32) for part in range(3))
    return high + (middle + low)


def product_kernel(offsets, with_gram, place_ref, columns_ref, matrix_ref, *refs):
    pieces, outs, table = refs[:2], refs[2:-1], refs[-1]
    groups, block_rows, block_size, _ = matrix_ref.shape
    slots = columns_ref.shape[3]
    half = block_size // 2
    blocks = table.shape[0]
    per_piece = len(offsets) // 2
    low = iota((half, 128), 1) < 64
    if with_gram:
        gram = joined(pieces[0], (0,), block_rows)
        for index in range(1, len(offsets)):
            gram = gram + joined(pieces[index // per_piece], (index % per_piece,), block_rows)
        outs[-1][...] = gram
        for part, value in enumerate(split(gram)):
            for m in range(1, groups):
                outs[m][block_rows + part] = value
    for index, offset in enumerate(offsets):
        source = pieces[index // per_piece]
        base = (place_ref[0] ^ offset) * block_rows
        for i in range(block_rows):
            block = source[index % per_piece, i]
            turned = jnp.concatenate([block[:, 64:], block[:, :64]], axis=1)
            table[base + i, :half] = jnp.where(low, block, turned)
            table[base + i, half:] = jnp.where(low, turned, block)
    for m in range(groups):
        group = m ^ place_ref[1]

        def one(i, carry):
            picked = [
                table[columns_ref[group, i, 0, s] & (blocks - 1)] for s in range(slots)
            ]
            result = jnp.dot(
                matrix_ref[m, i], jnp.concatenate(picked, axis=0), preferred_element_type=F32
            )
            outs[m][i] = jnp.where(low, result[:half], result[half:]).astype(BF16)
            return carry

        lax.fori_loop(0, block_rows, one, 0, unroll=True)


def product(offsets, place, block_columns, matrix, near, far):
    groups, block_rows, block_size, _ = matrix.shape
    with_gram = near.shape[1] > block_rows
    half = block_size // 2
    blocks = 2 * near.shape[0] * block_rows
    shapes = [jax.ShapeDtypeStruct((block_rows, half, 128), BF16)]
    shapes += [jax.ShapeDtypeStruct(near.shape[1:], BF16)] * (groups - 1)
    if with_gram:
        shapes.append(jax.ShapeDtypeStruct((32, 128), F32))
    return pl.pallas_call(
        functools.partial(product_kernel, offsets, with_gram),
        out_shape=shapes,
        in_specs=[smem(), smem(), vmem(), vmem(), vmem()],
        out_specs=[vmem()] * len(shapes),
        scratch_shapes=[pltpu.VMEM((blocks, block_size, 128), BF16)],
        compiler_params=params(),
        name="product",
    )(place, block_columns, matrix, near, far)


def add_terms(terms, block_rows):
    summed = terms[0][...].astype(F32)
    for term in terms[1:]:
        summed = summed + term[:block_rows].astype(F32)
    return summed


def local_gram(rows):
    flat = rows.reshape(-1, 128)
    both = lax.dot_general(
        flat, flat, (((0,), (0,)), ((), ())), precision=HIGHEST, preferred_element_type=F32
    )
    gram = both[:64, :64] + both[64:, 64:]
    return jnp.concatenate([gram[:32], gram[32:]], axis=1)


def middle_kernel(degree_ref, *refs):
    terms, out_ref = refs[:-1], refs[-1]
    block_rows = degree_ref.shape[0]
    degree = degree_ref[...]
    rows = add_terms(terms, block_rows) * degree
    out_ref[:block_rows] = (rows * degree).astype(BF16)
    for part, value in enumerate(split(local_gram(rows))):
        out_ref[block_rows + part] = value


def middle(degree, terms):
    block_rows, half, width = degree.shape
    return pl.pallas_call(
        middle_kernel,
        out_shape=jax.ShapeDtypeStruct((block_rows + 3, half, width), BF16),
        in_specs=[vmem()] * (1 + len(terms)),
        out_specs=vmem(),
        compiler_params=params(),
        name="middle",
    )(degree, *terms)


def collect_kernel(total, degree_ref, first_ref, *refs):
    terms, (rows_ref, gram_ref, first_out_ref) = refs[:-3], refs[-3:]
    block_rows = degree_ref.shape[0]
    first = first_ref[...]
    for term in terms[1:]:
        first = first + joined(term, (), block_rows)
    first = first / total
    row, lane = iota(first.shape, 0), iota(first.shape, 1)
    diagonal = lane % 64 == row + lane // 64 * 32
    trace = jnp.sum(jnp.where(diagonal, first, 0.0), axis=(0, 1), keepdims=True)
    scale = lax.rsqrt(trace / 64.0)
    first_out_ref[...] = first * (scale * scale)
    rows = add_terms(terms, block_rows) * degree_ref[...] * scale[None]
    rows_ref[...] = rows
    gram_ref[...] = local_gram(rows)


def collect(total, degree, first, terms):
    small = jax.ShapeDtypeStruct((32, 128), F32)
    return pl.pallas_call(
        functools.partial(collect_kernel, total),
        out_shape=(jax.ShapeDtypeStruct(degree.shape, F32), small, small),
        in_specs=[vmem()] * (2 + len(terms)),
        out_specs=(vmem(),) * 3,
        compiler_params=params(),
        name="collect",
    )(degree, first, *terms)


def factor_and_solve(gram, right):
    size = gram.shape[0]
    row_at = iota((size, 128), 0)
    work = jnp.concatenate([gram, right], axis=1)
    for j in range(size):
        column = jnp.broadcast_to(work[:, j : j + 1], (size, 128))
        scale = lax.rsqrt(column[j : j + 1])
        row = work[j : j + 1] * scale
        column = jnp.where(row_at > j, column * scale, 0.0)
        work = jnp.where(row_at == j, row, work) - column * row
    return work[:, 64:]


def unpacked(packed):
    return jnp.concatenate([packed[:, :64], packed[:, 64:]], axis=0)


def first_factor_kernel(gram_ref, out_ref):
    unit = (iota((64, 64), 0) == iota((64, 64), 1)).astype(F32)
    out_ref[...] = factor_and_solve(unpacked(gram_ref[...]), unit)


def first_factor(gram):
    return pl.pallas_call(
        first_factor_kernel,
        out_shape=jax.ShapeDtypeStruct((64, 64), F32),
        in_specs=[vmem()],
        out_specs=vmem(),
        compiler_params=params(),
        name="first_factor",
    )(gram)


def dot_turned(left, right):
    return lax.dot_general(
        left, right, (((1,), (1,)), ((), ())), precision=HIGHEST, preferred_element_type=F32
    )


def finish_kernel(total, rows_ref, inverse_ref, *refs):
    out_ref, scratch = refs[-2:]
    block_rows, half, _ = rows_ref.shape
    packed = refs[0][...]
    for part in refs[1:-2]:
        packed = packed + part[...]
    first = inverse_ref[...]
    gram = dot_turned(
        jnp.dot(first, unpacked(packed), precision=HIGHEST, preferred_element_type=F32), first
    )
    inverse = factor_and_solve(gram / total, first)
    zero = jnp.zeros_like(inverse)
    both = jnp.concatenate(
        [jnp.concatenate([inverse, zero], axis=1), jnp.concatenate([zero, inverse], axis=1)], axis=0
    )
    current = dot_turned(rows_ref[...].reshape(-1, 128), both)
    for i in range(block_rows):
        scratch[pl.ds(i, half, stride=block_rows), :] = current[i * half : (i + 1) * half]
    for t in range(half):
        out_ref[0, :, t * 128 : (t + 1) * 128] = scratch[t * block_rows : (t + 1) * block_rows, :]


def finish(total, rows, inverse, grams):
    block_rows, half, _ = rows.shape
    return pl.pallas_call(
        functools.partial(finish_kernel, total),
        out_shape=jax.ShapeDtypeStruct((1, block_rows, half * 128), F32),
        in_specs=[vmem()] * (2 + len(grams)),
        out_specs=vmem(),
        scratch_shapes=[pltpu.VMEM((block_rows * half, 128), F32)],
        compiler_params=params(),
        name="finish",
    )(rows, inverse, *grams)


def swap(value, axis, mask):
    size = lax.axis_size(axis)
    return lax.ppermute(value, axis, [(index, index ^ mask) for index in range(size)])


def stages(size):
    if size == 8:
        return [[2, 4, 6], [1]]
    bits, bit = [], 1
    while bit < size:
        bits.append([bit])
        bit *= 2
    return bits


def gather_rows(message, after):
    plan = stages(lax.axis_size("rows"))
    held, offsets = [message], [0]
    for masks in plan[:-1]:
        held = held + [swap(piece, "rows", mask) for mask in masks for piece in held]
        offsets = offsets + [mask ^ offset for mask in masks for offset in offsets]
    near = stack(held, after)
    (last,) = plan[-1]
    offsets = offsets + [last ^ offset for offset in offsets]
    return near, swap(near, "rows", last), offsets


def add_grams(gram):
    for masks in reversed(stages(lax.axis_size("rows"))):
        gram = sum([swap(gram, "rows", mask) for mask in masks], gram)
    return [gram] + [swap(gram, "cols", mask) for mask in range(1, lax.axis_size("cols"))]


def body(affinity, block_columns, block_counts, inv_degree, panel):
    block_rows, block_size = inv_degree.shape[1:]
    groups = affinity.shape[0]
    total = float(groups * lax.axis_size("rows") * block_rows * block_size)
    place = jnp.stack([lax.axis_index("rows"), lax.axis_index("cols")]).astype(jnp.int32)
    scaled, degree = start(panel, inv_degree)
    matrix, done = prep(place, block_counts, affinity)
    near, far, offsets = gather_rows(scaled, [done])
    terms = product(offsets, place, block_columns, matrix, near, far)
    terms = [terms[0]] + [swap(terms[m], "cols", m) for m in range(1, groups)]
    message = middle(degree, terms)
    near, far, offsets = gather_rows(message, [])
    *terms, first = product(offsets, place, block_columns, matrix, near, far)
    terms = [terms[0]] + [swap(terms[m], "cols", m) for m in range(1, groups)]
    rows, gram, first = collect(total, degree, first, terms)
    inverse = first_factor(first)
    return finish(total, rows, inverse, add_grams(gram))


def solution(mesh):
    return jax.shard_map(
        body,
        mesh=mesh,
        in_specs=(
            P(None, "rows", "cols", None, None),
            P(None, "rows", "cols", None),
            P(None, "rows", "cols"),
            P("cols", "rows", None),
            P("cols", "rows", None),
        ),
        out_specs=P("cols", "rows", None),
        check_vma=False,
    )
```

```python
import functools

import jax
import jax.numpy as jnp
from jax import lax
from jax.experimental import pallas as pl
from jax.experimental.pallas import tpu as pltpu
from jax.sharding import PartitionSpec as P

BF16 = jnp.bfloat16
F32 = jnp.float32
HIGHEST = lax.Precision.HIGHEST
MIB = 1024 * 1024


def params(limit=48 * MIB):
    return pltpu.CompilerParams(vmem_limit_bytes=limit)


def vmem():
    return pl.BlockSpec(memory_space=pltpu.VMEM)


def hbm():
    return pl.BlockSpec(memory_space=pltpu.HBM)


def smem():
    return pl.BlockSpec(memory_space=pltpu.SMEM)


def shaped(shape, dtype):
    return jax.ShapeDtypeStruct(shape, dtype)


def iota(shape, dim):
    return lax.broadcasted_iota(jnp.int32, shape, dim)


def call(kernel, name, ins, outs, operands, scratch=(), limit=48 * MIB, **kwargs):
    return pl.pallas_call(
        kernel,
        out_shape=outs,
        in_specs=ins,
        out_specs=jax.tree.map(lambda _: vmem(), outs),
        scratch_shapes=list(scratch),
        compiler_params=params(limit),
        name=name,
        **kwargs,
    )(*operands)


def start_kernel(panel_hbm, inv_hbm, scaled_ref, degree_ref, panel_ref, inv_ref, scratch, sems):
    block_rows, block_size = inv_ref.shape[1], inv_ref.shape[2]
    half = block_size // 2
    copies = [
        pltpu.make_async_copy(inv_hbm, inv_ref, sems.at[0]),
        pltpu.make_async_copy(panel_hbm, panel_ref, sems.at[1]),
    ]
    for copy in copies:
        copy.start()
    copies[0].wait()
    pair = iota((half, block_size), 1) // 2 == iota((half, block_size), 0)
    spread = (iota((block_size, 128), 0) % 2 == iota((block_size, 128), 1) // 64).astype(F32)
    rows = [
        jnp.where(pair, jnp.broadcast_to(inv_ref[0, i : i + 1, :], (half, block_size)), 0.0)
        for i in range(block_rows)
    ]
    degree_ref[...] = jnp.dot(
        jnp.concatenate(rows, axis=0), spread, precision=HIGHEST, preferred_element_type=F32
    )
    copies[1].wait()
    for t in range(half):
        scratch[t * block_rows : (t + 1) * block_rows, :] = panel_ref[0, :, t * 128 : (t + 1) * 128]
    for i in range(block_rows):
        where = slice(i * half, (i + 1) * half)
        part = scratch[pl.ds(i, half, stride=block_rows), :] * degree_ref[where, :]
        scaled_ref[where, :] = part.astype(BF16)


def start(panel, inv_degree):
    block_rows, block_size = inv_degree.shape[1:]
    shape = (block_rows * block_size // 2, 128)
    return call(
        start_kernel,
        "start",
        [hbm(), hbm()],
        (shaped(shape, BF16), shaped(shape, F32)),
        (panel, inv_degree),
        [
            pltpu.VMEM(panel.shape, F32),
            pltpu.VMEM(inv_degree.shape, F32),
            pltpu.VMEM(shape, F32),
            pltpu.SemaphoreType.DMA((2,)),
        ],
    )


def prep_kernel(place_ref, affinity_hbm, out_ref, done_ref, affinity_ref, scratch, sems):
    done_ref[...] = jnp.zeros_like(done_ref)
    groups, block_rows, _, slots, flat = affinity_ref.shape
    half = flat // 128
    copies = [
        pltpu.make_async_copy(affinity_hbm.at[m ^ place_ref[1]], affinity_ref.at[m], sems.at[m])
        for m in range(groups)
    ]
    for copy in copies:
        copy.start()
    source, target = iota((256, 256), 0), iota((256, 256), 1)
    moved = (source // 64 % 2) * 128 + (source // 128) * 64 + (source % 2) * 32 + source % 64 // 2
    permute = (moved == target).astype(BF16)
    for m in range(groups):
        copies[m].wait()
        for i in range(block_rows):
            block = affinity_ref[m, i, 0].astype(F32)
            for t in range(half):
                scratch[i % 2, t * slots : (t + 1) * slots, :] = block[:, t * 128 : (t + 1) * 128]
            parts = [
                scratch[i % 2, pl.ds(s, half, stride=slots), :].astype(BF16) for s in range(slots)
            ]
            pairs = [jnp.concatenate(parts[s : s + 2], axis=1) for s in range(0, slots, 2)]
            moved_pairs = jnp.dot(
                jnp.concatenate(pairs, axis=0), permute, preferred_element_type=F32
            ).astype(BF16)
            for s in range(slots // 2):
                piece = moved_pairs[s * half : (s + 1) * half]
                out_ref[m, i, :half, s * 128 : (s + 1) * 128] = piece[:, :128]
                out_ref[m, i, half:, s * 128 : (s + 1) * 128] = piece[:, 128:]


def prep(place, affinity):
    groups, block_rows, _, slots, flat = affinity.shape
    return call(
        prep_kernel,
        "prep",
        [smem(), hbm()],
        (shaped((groups, block_rows, 64, slots * 64), BF16), shaped((8, 128), F32)),
        (place, affinity),
        [
            pltpu.VMEM(affinity.shape, BF16),
            pltpu.VMEM((2, flat // 128 * slots, 128), F32),
            pltpu.SemaphoreType.DMA((groups,)),
        ],
    )


def split(value):
    high = value.astype(BF16)
    rest = value - high.astype(F32)
    middle = rest.astype(BF16)
    return high, middle, (rest - middle.astype(F32)).astype(BF16)


def joined(ref, index, first):
    high, middle, low = (
        ref[index, first + 32 * part : first + 32 * (part + 1)].astype(F32) for part in range(3)
    )
    return high + (middle + low)


def stack_kernel(count, *refs):
    for index in range(count):
        refs[-1][index] = refs[index][...]


def stack(pieces, after):
    return call(
        functools.partial(stack_kernel, len(pieces)),
        "stack",
        [vmem()] * (len(pieces) + len(after)),
        shaped((len(pieces),) + pieces[0].shape, BF16),
        (*pieces, *after),
    )


def fill_table(place_ref, pieces_ref, offsets, table):
    block_rows = (table.shape[0] - 1) // (2 * len(offsets))
    low = iota((32, 128), 1) < 64
    for index, offset in enumerate(offsets):
        base = (place_ref[0] ^ offset) * block_rows
        for i in range(block_rows):
            block = pieces_ref[index, i * 32 : (i + 1) * 32, :]
            turned = jnp.concatenate([block[:, 64:], block[:, :64]], axis=1)
            table[base + i, :32] = jnp.where(low, block, turned)
            table[base + i, 32:] = jnp.where(low, turned, block)


def near_kernel(offsets, place_ref, near_ref, table):
    table[table.shape[0] - 1] = jnp.zeros(table.shape[1:], BF16)
    fill_table(place_ref, near_ref, offsets, table)


def far_kernel(offsets, place_ref, far_ref, near_ref, old_table, table, *grams):
    del old_table
    fill_table(place_ref, far_ref, offsets, table)
    if grams:
        gram_ref, trace_ref = grams
        first = (table.shape[0] - 1) // (2 * len(offsets)) * 32
        gram = joined(near_ref, 0, first) + joined(far_ref, 0, first)
        for index in range(1, len(offsets)):
            gram = gram + joined(near_ref, index, first) + joined(far_ref, index, first)
        gram_ref[...] = gram
        row, lane = iota(gram.shape, 0), iota(gram.shape, 1)
        diagonal = lane % 64 == row + lane // 64 * 32
        trace = jnp.sum(jnp.where(diagonal, gram, 0.0), axis=(0, 1), keepdims=True)
        trace_ref[...] = jnp.broadcast_to(trace, trace_ref.shape).astype(BF16)


def tables(offsets, place, near, far, block_rows):
    count = near.shape[0]
    table_shape = shaped((2 * count * block_rows + 1, 64, 128), BF16)
    table = call(
        functools.partial(near_kernel, offsets[:count]),
        "near",
        [smem(), vmem()],
        table_shape,
        (place, near),
    )
    outs = [table_shape]
    if near.shape[1] > block_rows * 32:
        outs += [shaped((32, 128), F32), shaped((16, 128), BF16)]
    return call(
        functools.partial(far_kernel, offsets[count:]),
        "far",
        [smem(), vmem(), vmem(), vmem()],
        outs,
        (place, far, near, table),
        input_output_aliases={3: 0},
    )


def product_kernel(m, place_ref, columns_ref, matrix_ref, table, *refs):
    out_ref = refs[-1]
    block_rows, slots = columns_ref.shape[1], columns_ref.shape[3]
    group = m ^ place_ref[1]
    low = iota((32, 128), 1) < 64
    for i in range(block_rows):
        picked = [table[columns_ref[group, i, 0, s]] for s in range(slots)]
        result = jnp.dot(
            matrix_ref[m, i], jnp.concatenate(picked, axis=0), preferred_element_type=F32
        )
        out_ref[i * 32 : (i + 1) * 32, :] = jnp.where(low, result[:32], result[32:]).astype(BF16)
    if len(refs) > 1:
        out_ref[block_rows * 32 :, :] = refs[0][...]


def product(m, place, columns, matrix, table, trace):
    rows = matrix.shape[1] * 32 + sum(extra.shape[0] for extra in trace)
    return call(
        functools.partial(product_kernel, m),
        "product",
        [smem(), smem()] + [vmem()] * (2 + len(trace)),
        shaped((rows, 128), BF16),
        (place, columns, matrix, table, *trace),
    )


def products(place, columns, matrix, table, trace):
    groups = matrix.shape[0]
    terms = []
    for m in range(groups - 1, 0, -1):
        terms.append(swap(product(m, place, columns, matrix, table, trace), "cols", m))
    return [product(0, place, columns, matrix, table, trace)] + terms


def add_terms(terms, rows):
    summed = terms[0][:rows].astype(F32)
    for term in terms[1:]:
        summed = summed + term[:rows].astype(F32)
    return summed


def local_gram(rows):
    both = lax.dot_general(
        rows, rows, (((0,), (0,)), ((), ())), precision=HIGHEST, preferred_element_type=F32
    )
    gram = both[:64, :64] + both[64:, 64:]
    return jnp.concatenate([gram[:32], gram[32:]], axis=1)


def middle_kernel(degree_ref, *refs):
    terms, out_ref = refs[:-1], refs[-1]
    count = degree_ref.shape[0]
    degree = degree_ref[...]
    rows = add_terms(terms, count) * degree
    out_ref[:count] = (rows * degree).astype(BF16)
    for part, value in enumerate(split(local_gram(rows))):
        out_ref[count + part * 32 : count + (part + 1) * 32] = value


def middle(degree, terms):
    return call(
        middle_kernel,
        "middle",
        [vmem()] * (1 + len(terms)),
        shaped((degree.shape[0] + 96, 128), BF16),
        (degree, *terms),
    )


def collect_kernel(total, degree_ref, first_ref, *refs):
    terms, (rows_ref, grams_ref) = refs[:-2], refs[-2:]
    count = degree_ref.shape[0]
    largest = terms[0][count:].astype(F32)
    for term in terms[1:]:
        largest = jnp.maximum(largest, term[count:].astype(F32))
    scale = lax.rsqrt(largest[:1] / total)
    rows = add_terms(terms, count) * degree_ref[...] * scale
    rows_ref[...] = rows
    grams_ref[32:] = first_ref[...] * (scale * scale)
    grams_ref[:32] = local_gram(rows)


def collect(total, degree, first, terms):
    return call(
        functools.partial(collect_kernel, total),
        "collect",
        [vmem()] * (2 + len(terms)),
        (shaped(degree.shape, F32), shaped((64, 128), F32)),
        (degree, first, *terms),
    )


def lower_solve(gram, right):
    work = jnp.concatenate([gram, right], axis=1)
    blocks = gram.shape[0] // 8
    rows = [work[8 * i : 8 * i + 8] for i in range(blocks)]
    at = iota((8, 128), 0)

    def columns(first, column):
        return [
            jnp.broadcast_to(rows[i][:, column : column + 1], (8, 128))
            for i in range(first, blocks)
        ]

    def spread(block, row):
        return jnp.broadcast_to(block[row : row + 1], (8, 128))

    current = [columns(0, q) for q in range(8)]
    for b in range(blocks):
        count = blocks - b
        later = []
        if count > 1:
            later = [columns(b + 1, 8 * (b + 1) + q) for q in range(8)]
        for q in range(8):
            root = lax.rsqrt(spread(current[q][0], q))
            inverse = root * root
            raw = spread(rows[b], q)
            scaled = raw * inverse
            for p in range(q + 1, 8):
                weight = spread(current[q][0], p) * inverse
                current[p] = [x - y * weight for x, y in zip(current[p], current[q])]
            below = rows[b] - current[q][0] * scaled
            rows[b] = jnp.where(at == q, raw * root, jnp.where(at > q, below, rows[b]))
            for i in range(1, count):
                rows[b + i] = rows[b + i] - current[q][i] * scaled
            for p in range(len(later)):
                weight = spread(current[q][1], p) * inverse
                later[p] = [x - y * weight for x, y in zip(later[p], current[q][1:])]
        current = later
    return jnp.concatenate(rows, axis=0)[:, 64:]


def unpacked(packed):
    return jnp.concatenate([packed[:, :64], packed[:, 64:]], axis=0)


def add_columns_kernel(total, *refs):
    parts, (gram_ref, first_ref) = refs[:-2], refs[-2:]
    summed = parts[0][...]
    for part in parts[1:]:
        summed = summed + part[...]
    gram_ref[...] = summed[:32]
    first_ref[...] = summed[32:] / total


def add_columns(total, parts):
    return call(
        functools.partial(add_columns_kernel, total),
        "add_columns",
        [vmem()] * len(parts),
        (shaped((32, 128), F32), shaped((32, 128), F32)),
        parts,
    )


def first_factor_kernel(gram_ref, out_ref):
    unit = (iota((64, 64), 0) == iota((64, 64), 1)).astype(F32)
    out_ref[...] = lower_solve(unpacked(gram_ref[...]), unit)


def first_factor(gram):
    return call(first_factor_kernel, "first_factor", [vmem()], shaped((64, 64), F32), (gram,))


def dot_turned(left, right):
    return lax.dot_general(
        left, right, (((1,), (1,)), ((), ())), precision=HIGHEST, preferred_element_type=F32
    )


def finish_kernel(total, rows_ref, inverse_ref, *refs):
    out_ref, scratch = refs[-2:]
    block_rows = out_ref.shape[1]
    packed = refs[0][...]
    for part in refs[1:-2]:
        packed = packed + part[...]
    first = inverse_ref[...]
    gram = dot_turned(
        jnp.dot(first, unpacked(packed), precision=HIGHEST, preferred_element_type=F32), first
    )
    inverse = lower_solve(gram / total, first)
    zero = jnp.zeros_like(inverse)
    both = jnp.concatenate(
        [jnp.concatenate([inverse, zero], axis=1), jnp.concatenate([zero, inverse], axis=1)], axis=0
    )
    current = dot_turned(rows_ref[...], both)
    for i in range(block_rows):
        scratch[pl.ds(i, 32, stride=block_rows), :] = current[i * 32 : (i + 1) * 32]
    for t in range(32):
        out_ref[0, :, t * 128 : (t + 1) * 128] = scratch[t * block_rows : (t + 1) * block_rows, :]


def finish(total, block_rows, rows, inverse, grams):
    return call(
        functools.partial(finish_kernel, total),
        "finish",
        [vmem()] * (2 + len(grams)),
        shaped((1, block_rows, 32 * 128), F32),
        (rows, inverse, *grams),
        [pltpu.VMEM(rows.shape, F32)],
    )


def swap(value, axis, mask):
    size = lax.axis_size(axis)
    return lax.ppermute(value, axis, [(index, index ^ mask) for index in range(size)])


def stages(size):
    if size == 8:
        return [[6, 4, 2], [1]]
    bits, bit = [], 1
    while bit < size:
        bits.append([bit])
        bit *= 2
    return bits


def gather_rows(message, after):
    plan = stages(lax.axis_size("rows"))
    held, offsets = [message], [0]
    for masks in plan[:-1]:
        held = held + [swap(piece, "rows", mask) for mask in masks for piece in held]
        offsets = offsets + [mask ^ offset for mask in masks for offset in offsets]
    near = stack(held, after)
    (last,) = plan[-1]
    offsets = offsets + [last ^ offset for offset in offsets]
    return near, swap(near, "rows", last), offsets


def add_rows(gram):
    *plan, (last,) = stages(lax.axis_size("rows"))
    for masks in plan:
        gram = sum([swap(gram, "rows", mask) for mask in masks], gram)
    return [gram, swap(gram, "rows", last)]


def body(affinity, block_columns, block_counts, inv_degree, panel):
    block_rows, block_size = inv_degree.shape[1:]
    groups, _, _, slots, _ = affinity.shape
    ranks = lax.axis_size("rows")
    total = float(groups * ranks * block_rows * block_size)
    blocks = ranks * block_rows
    place = jnp.stack([lax.axis_index("rows"), lax.axis_index("cols")]).astype(jnp.int32)
    live = iota(block_columns.shape, 3) < block_counts[..., None]
    columns = jnp.where(live, jnp.clip(block_columns, 0, blocks - 1), blocks)

    panel, inv_degree, affinity = (
        pltpu.with_memory_space_constraint(value, pltpu.HBM) for value in (panel, inv_degree, affinity)
    )
    scaled, degree = start(panel, inv_degree)
    matrix, done = prep(place, affinity)
    near, far, offsets = gather_rows(scaled, [done])
    (table,) = tables(offsets, place, near, far, block_rows)
    terms = products(place, columns, matrix, table, [])
    near, far, offsets = gather_rows(middle(degree, terms), [])
    table, first, trace = tables(offsets, place, near, far, block_rows)
    terms = products(place, columns, matrix, table, [trace])
    rows, grams = collect(total, degree, first, terms)
    parts = [grams] + [swap(grams, "cols", m) for m in range(groups - 1, 0, -1)]
    gram, first = add_columns(total, parts)
    return finish(total, block_rows, rows, first_factor(first), add_rows(gram))


def solution(mesh):
    return jax.shard_map(
        body,
        mesh=mesh,
        in_specs=(
            P(None, "rows", "cols", None, None),
            P(None, "rows", "cols", None),
            P(None, "rows", "cols"),
            P("cols", "rows", None),
            P("cols", "rows", None),
        ),
        out_specs=P("cols", "rows", None),
        check_vma=False,
    )
```

```python
import functools

import jax
import jax.numpy as jnp
from jax import lax
from jax.experimental import pallas as pl
from jax.experimental.pallas import tpu as pltpu
from jax.sharding import PartitionSpec as P

BF16 = jnp.bfloat16
F32 = jnp.float32
HIGHEST = lax.Precision.HIGHEST
MIB = 1024 * 1024


def params(limit=48 * MIB):
    return pltpu.CompilerParams(vmem_limit_bytes=limit)


def vmem():
    return pl.BlockSpec(memory_space=pltpu.VMEM)


def hbm():
    return pl.BlockSpec(memory_space=pltpu.HBM)


def smem():
    return pl.BlockSpec(memory_space=pltpu.SMEM)


def shaped(shape, dtype):
    return jax.ShapeDtypeStruct(shape, dtype)


def iota(shape, dim):
    return lax.broadcasted_iota(jnp.int32, shape, dim)


def call(kernel, name, ins, outs, operands, scratch=(), limit=48 * MIB, **kwargs):
    return pl.pallas_call(
        kernel,
        out_shape=outs,
        in_specs=ins,
        out_specs=jax.tree.map(lambda _: vmem(), outs),
        scratch_shapes=list(scratch),
        compiler_params=params(limit),
        name=name,
        **kwargs,
    )(*operands)


def start_kernel(panel_hbm, inv_hbm, scaled_ref, degree_ref, panel_ref, inv_ref, scratch, sems):
    block_rows, block_size = inv_ref.shape[1], inv_ref.shape[2]
    half = block_size // 2
    copies = [
        pltpu.make_async_copy(inv_hbm, inv_ref, sems.at[0]),
        pltpu.make_async_copy(panel_hbm, panel_ref, sems.at[1]),
    ]
    for copy in copies:
        copy.start()
    copies[0].wait()
    pair = iota((half, block_size), 1) // 2 == iota((half, block_size), 0)
    spread = (iota((block_size, 128), 0) % 2 == iota((block_size, 128), 1) // 64).astype(F32)
    rows = [
        jnp.where(pair, jnp.broadcast_to(inv_ref[0, i : i + 1, :], (half, block_size)), 0.0)
        for i in range(block_rows)
    ]
    degree_ref[...] = jnp.dot(
        jnp.concatenate(rows, axis=0), spread, precision=HIGHEST, preferred_element_type=F32
    )
    copies[1].wait()
    for t in range(half):
        scratch[t * block_rows : (t + 1) * block_rows, :] = panel_ref[0, :, t * 128 : (t + 1) * 128]
    for i in range(block_rows):
        where = slice(i * half, (i + 1) * half)
        part = scratch[pl.ds(i, half, stride=block_rows), :] * degree_ref[where, :]
        scaled_ref[where, :] = part.astype(BF16)


def start(panel, inv_degree):
    block_rows, block_size = inv_degree.shape[1:]
    shape = (block_rows * block_size // 2, 128)
    return call(
        start_kernel,
        "start",
        [hbm(), hbm()],
        (shaped(shape, BF16), shaped(shape, F32)),
        (panel, inv_degree),
        [
            pltpu.VMEM(panel.shape, F32),
            pltpu.VMEM(inv_degree.shape, F32),
            pltpu.VMEM(shape, F32),
            pltpu.SemaphoreType.DMA((2,)),
        ],
    )


def prep_kernel(ranges, affinity_hbm, out_ref, done_ref, affinity_ref, scratch, sems):
    done_ref[...] = jnp.zeros_like(done_ref)
    count, block_rows, _, slots, flat = affinity_ref.shape
    half = flat // 128
    own = lax.axis_index("cols")
    copies = [
        pltpu.make_async_copy(affinity_hbm.at[m ^ own], affinity_ref.at[place], sems.at[place])
        for place, m in enumerate(ranges)
    ]
    for copy in copies:
        copy.start()
    source, target = iota((256, 256), 0), iota((256, 256), 1)
    moved = (source // 64 % 2) * 128 + (source // 128) * 64 + (source % 2) * 32 + source % 64 // 2
    permute = (moved == target).astype(BF16)
    for m in range(count):
        copies[m].wait()
        for i in range(block_rows):
            block = affinity_ref[m, i, 0].astype(F32)
            for t in range(half):
                scratch[i % 2, t * slots : (t + 1) * slots, :] = block[:, t * 128 : (t + 1) * 128]
            parts = [
                scratch[i % 2, pl.ds(s, half, stride=slots), :].astype(BF16) for s in range(slots)
            ]
            pairs = [jnp.concatenate(parts[s : s + 2], axis=1) for s in range(0, slots, 2)]
            moved_pairs = jnp.dot(
                jnp.concatenate(pairs, axis=0), permute, preferred_element_type=F32
            ).astype(BF16)
            for s in range(slots // 2):
                piece = moved_pairs[s * half : (s + 1) * half]
                out_ref[m, i, :half, s * 128 : (s + 1) * 128] = piece[:, :128]
                out_ref[m, i, half:, s * 128 : (s + 1) * 128] = piece[:, 128:]


def prep(ranges, affinity):
    _, block_rows, _, slots, flat = affinity.shape
    count = len(ranges)
    return call(
        functools.partial(prep_kernel, ranges),
        "prep",
        [hbm()],
        (shaped((count, block_rows, 64, slots * 64), BF16), shaped((8, 128), F32)),
        (affinity,),
        [
            pltpu.VMEM((count,) + affinity.shape[1:], BF16),
            pltpu.VMEM((2, flat // 128 * slots, 128), F32),
            pltpu.SemaphoreType.DMA((count,)),
        ],
    )


def split(value):
    high = value.astype(BF16)
    rest = value - high.astype(F32)
    middle = rest.astype(BF16)
    return high, middle, (rest - middle.astype(F32)).astype(BF16)


def joined(ref, index, first):
    high, middle, low = (
        ref[index, first + 32 * part : first + 32 * (part + 1)].astype(F32) for part in range(3)
    )
    return high + (middle + low)


def stack_kernel(count, *refs):
    for index in range(count):
        refs[-1][index] = refs[index][...]


def stack(pieces, after):
    return call(
        functools.partial(stack_kernel, len(pieces)),
        "stack",
        [vmem()] * (len(pieces) + len(after)),
        shaped((len(pieces),) + pieces[0].shape, BF16),
        (*pieces, *after),
    )


def fill_table(pieces_ref, offsets, table):
    block_rows = (table.shape[0] - 1) // (2 * len(offsets))
    low = iota((32, 128), 1) < 64
    for index, offset in enumerate(offsets):
        base = (lax.axis_index("rows") ^ offset) * block_rows
        for i in range(block_rows):
            block = pieces_ref[index, i * 32 : (i + 1) * 32, :]
            turned = jnp.concatenate([block[:, 64:], block[:, :64]], axis=1)
            table[base + i, :32] = jnp.where(low, block, turned)
            table[base + i, 32:] = jnp.where(low, turned, block)


def near_kernel(offsets, near_ref, table):
    table[table.shape[0] - 1] = jnp.zeros(table.shape[1:], BF16)
    fill_table(near_ref, offsets, table)


def near_table(offsets, near, block_rows):
    count = near.shape[0]
    return call(
        functools.partial(near_kernel, offsets[:count]),
        "near",
        [vmem()],
        shaped((2 * count * block_rows + 1, 64, 128), BF16),
        (near,),
    )


def one_product(group, columns, matrix, table, out_ref):
    block_rows, slots = columns.shape[1], columns.shape[3]
    low = iota((32, 128), 1) < 64
    for i in range(block_rows):
        picked = [table[columns[group, i, 0, s]] for s in range(slots)]
        result = jnp.dot(matrix[i], jnp.concatenate(picked, axis=0), preferred_element_type=F32)
        out_ref[i * 32 : (i + 1) * 32, :] = jnp.where(low, result[:32], result[32:]).astype(BF16)


def others_kernel(offsets, ranges, columns_any, matrix_ref, far_ref, near_ref, old_table, table, *refs):
    del old_table
    *outs, columns, sem = refs
    copy = pltpu.make_async_copy(columns_any, columns, sem)
    copy.start()
    fill_table(far_ref, offsets, table)
    terms, grams = outs[: len(ranges)], outs[len(ranges) :]
    first = matrix_ref.shape[1] * 32
    if grams:
        gram_ref, trace_ref = grams
        gram = joined(near_ref, 0, first) + joined(far_ref, 0, first)
        for index in range(1, len(offsets)):
            gram = gram + joined(near_ref, index, first) + joined(far_ref, index, first)
        gram_ref[...] = gram
        row, lane = iota(gram.shape, 0), iota(gram.shape, 1)
        diagonal = lane % 64 == row + lane // 64 * 32
        trace = jnp.sum(jnp.where(diagonal, gram, 0.0), axis=(0, 1), keepdims=True)
        trace = jnp.broadcast_to(trace, trace_ref.shape).astype(BF16)
        trace_ref[...] = trace
        for term in terms:
            term[first:, :] = trace
    copy.wait()
    for place, m in enumerate(ranges):
        group = m ^ lax.axis_index("cols")
        one_product(group, columns, matrix_ref.at[place], table, terms[place])


def own_kernel(columns, matrix_ref, table, out_ref):
    one_product(lax.axis_index("cols"), columns, matrix_ref.at[0], table, out_ref)


def products(offsets, ranges, columns, matrix, own_matrix, near, far, table):
    block_rows, count = matrix.shape[1], near.shape[0]
    extra = near.shape[1] > block_rows * 32
    rows = block_rows * 32
    outs = [shaped(table.shape, BF16)] + [shaped((rows + 16 * extra, 128), BF16)] * len(ranges)
    if extra:
        outs += [shaped((32, 128), F32), shaped((16, 128), BF16)]
    table, *outs = call(
        functools.partial(others_kernel, offsets[count:], ranges),
        "others",
        [pl.BlockSpec(memory_space=pl.ANY)] + [vmem()] * 4,
        outs,
        (columns, matrix, far, near, table),
        [pltpu.SMEM(columns.shape, jnp.int32), pltpu.SemaphoreType.DMA],
        input_output_aliases={4: 0},
    )
    terms = [swap(term, "cols", m) for m, term in zip(ranges, outs)]
    own = call(
        own_kernel,
        "own",
        [smem(), vmem(), vmem()],
        shaped((rows, 128), BF16),
        (columns, own_matrix, table),
    )
    return [own] + terms, outs[len(ranges) :]


def add_terms(terms, rows):
    summed = terms[0][:rows].astype(F32)
    for term in terms[1:]:
        summed = summed + term[:rows].astype(F32)
    return summed


def local_gram(rows):
    both = lax.dot_general(
        rows, rows, (((0,), (0,)), ((), ())), precision=HIGHEST, preferred_element_type=F32
    )
    gram = both[:64, :64] + both[64:, 64:]
    return jnp.concatenate([gram[:32], gram[32:]], axis=1)


def middle_kernel(degree_ref, *refs):
    terms, out_ref = refs[:-1], refs[-1]
    count = degree_ref.shape[0]
    degree = degree_ref[...]
    rows = add_terms(terms, count) * degree
    out_ref[:count] = (rows * degree).astype(BF16)
    for part, value in enumerate(split(local_gram(rows))):
        out_ref[count + part * 32 : count + (part + 1) * 32] = value


def middle(degree, terms):
    return call(
        middle_kernel,
        "middle",
        [vmem()] * (1 + len(terms)),
        shaped((degree.shape[0] + 96, 128), BF16),
        (degree, *terms),
    )


def collect_kernel(total, degree_ref, first_ref, trace_ref, *refs):
    terms, (rows_ref, grams_ref) = refs[:-2], refs[-2:]
    count = degree_ref.shape[0]
    largest = trace_ref[...].astype(F32)
    for term in terms[1:]:
        largest = jnp.maximum(largest, term[count:].astype(F32))
    scale = lax.rsqrt(largest[:1] / total)
    rows = add_terms(terms, count) * degree_ref[...] * scale
    rows_ref[...] = rows
    grams_ref[32:] = first_ref[...] * (scale * scale)
    grams_ref[:32] = local_gram(rows)


def collect(total, degree, first, trace, terms):
    return call(
        functools.partial(collect_kernel, total),
        "collect",
        [vmem()] * (3 + len(terms)),
        (shaped(degree.shape, F32), shaped((64, 128), F32)),
        (degree, first, trace, *terms),
    )


def lower_solve(gram, right):
    work = jnp.concatenate([gram, right], axis=1)
    blocks = gram.shape[0] // 8
    rows = [work[8 * i : 8 * i + 8] for i in range(blocks)]
    at = iota((8, 128), 0)

    def columns(first, column):
        return [
            jnp.broadcast_to(rows[i][:, column : column + 1], (8, 128))
            for i in range(first, blocks)
        ]

    def spread(block, row):
        return jnp.broadcast_to(block[row : row + 1], (8, 128))

    current = [columns(0, q) for q in range(8)]
    for b in range(blocks):
        count = blocks - b
        later = []
        if count > 1:
            later = [columns(b + 1, 8 * (b + 1) + q) for q in range(8)]
        for q in range(8):
            root = lax.rsqrt(spread(current[q][0], q))
            inverse = root * root
            raw = spread(rows[b], q)
            scaled = raw * inverse
            for p in range(q + 1, 8):
                weight = spread(current[q][0], p) * inverse
                current[p] = [x - y * weight for x, y in zip(current[p], current[q])]
            below = rows[b] - current[q][0] * scaled
            rows[b] = jnp.where(at == q, raw * root, jnp.where(at > q, below, rows[b]))
            for i in range(1, count):
                rows[b + i] = rows[b + i] - current[q][i] * scaled
            for p in range(len(later)):
                weight = spread(current[q][1], p) * inverse
                later[p] = [x - y * weight for x, y in zip(later[p], current[q][1:])]
        current = later
    return jnp.concatenate(rows, axis=0)[:, 64:]


def unpacked(packed):
    return jnp.concatenate([packed[:, :64], packed[:, 64:]], axis=0)


def add_columns_kernel(total, *refs):
    parts, (gram_ref, first_ref) = refs[:-2], refs[-2:]
    summed = parts[0][...]
    for part in parts[1:]:
        summed = summed + part[...]
    gram_ref[...] = summed[:32]
    first_ref[...] = summed[32:] / total


def add_columns(total, parts):
    return call(
        functools.partial(add_columns_kernel, total),
        "add_columns",
        [vmem()] * len(parts),
        (shaped((32, 128), F32), shaped((32, 128), F32)),
        parts,
    )


def add_parts_kernel(count, *refs):
    summed = refs[0][...]
    for part in refs[1:count]:
        summed = summed + part[...]
    refs[-1][...] = summed


def add_parts(parts, after):
    return call(
        functools.partial(add_parts_kernel, len(parts)),
        "add_parts",
        [vmem()] * (len(parts) + len(after)),
        shaped(parts[0].shape, F32),
        (*parts, *after),
    )


def first_factor_kernel(gram_ref, out_ref):
    unit = (iota((64, 64), 0) == iota((64, 64), 1)).astype(F32)
    out_ref[...] = lower_solve(unpacked(gram_ref[...]), unit)


def first_factor(gram):
    return call(first_factor_kernel, "first_factor", [vmem()], shaped((64, 64), F32), (gram,))


def dot_turned(left, right):
    return lax.dot_general(
        left, right, (((1,), (1,)), ((), ())), precision=HIGHEST, preferred_element_type=F32
    )


def finish_kernel(total, rows_ref, inverse_ref, *refs):
    out_ref, scratch = refs[-2:]
    block_rows = out_ref.shape[1]
    packed = refs[0][...]
    for part in refs[1:-2]:
        packed = packed + part[...]
    first = inverse_ref[...]
    gram = dot_turned(
        jnp.dot(first, unpacked(packed), precision=HIGHEST, preferred_element_type=F32), first
    )
    inverse = lower_solve(gram / total, first)
    zero = jnp.zeros_like(inverse)
    both = jnp.concatenate(
        [jnp.concatenate([inverse, zero], axis=1), jnp.concatenate([zero, inverse], axis=1)], axis=0
    )
    current = dot_turned(rows_ref[...], both)
    for i in range(block_rows):
        scratch[pl.ds(i, 32, stride=block_rows), :] = current[i * 32 : (i + 1) * 32]
    for t in range(32):
        out_ref[0, :, t * 128 : (t + 1) * 128] = scratch[t * block_rows : (t + 1) * block_rows, :]


def finish(total, block_rows, rows, inverse, grams):
    return call(
        functools.partial(finish_kernel, total),
        "finish",
        [vmem()] * (2 + len(grams)),
        shaped((1, block_rows, 32 * 128), F32),
        (rows, inverse, *grams),
        [pltpu.VMEM(rows.shape, F32)],
    )


def swap(value, axis, mask):
    size = lax.axis_size(axis)
    return lax.ppermute(value, axis, [(index, index ^ mask) for index in range(size)])


def stages(size):
    if size == 8:
        return [[6, 4, 2], [1]]
    bits, bit = [], 1
    while bit < size:
        bits.append([bit])
        bit *= 2
    return bits


def gather_rows(message, after):
    plan = stages(lax.axis_size("rows"))
    held, offsets = [message], [0]
    for masks in plan[:-1]:
        held = held + [swap(piece, "rows", mask) for mask in masks for piece in held]
        offsets = offsets + [mask ^ offset for mask in masks for offset in offsets]
    near = stack(held, after)
    (last,) = plan[-1]
    offsets = offsets + [last ^ offset for offset in offsets]
    return near, swap(near, "rows", last), offsets


def add_rows(gram, after):
    *plan, (last,) = stages(lax.axis_size("rows"))
    for masks in plan:
        gram = add_parts([gram] + [swap(gram, "rows", mask) for mask in masks], after)
    return [gram, swap(gram, "rows", last)]


def body(affinity, block_columns, block_counts, inv_degree, panel):
    block_rows, block_size = inv_degree.shape[1:]
    groups, _, _, slots, _ = affinity.shape
    ranks = lax.axis_size("rows")
    total = float(groups * ranks * block_rows * block_size)
    blocks = ranks * block_rows
    live = iota(block_columns.shape, 3) < block_counts[..., None]
    columns = jnp.where(live, jnp.clip(block_columns, 0, blocks - 1), blocks)
    panel, inv_degree, affinity = (
        pltpu.with_memory_space_constraint(value, pltpu.HBM) for value in (panel, inv_degree, affinity)
    )
    ranges = list(range(groups - 1, 0, -1))

    scaled, degree = start(panel, inv_degree)
    matrix, done = prep(ranges, affinity)
    own_matrix, _ = prep([0], affinity)
    near, far, offsets = gather_rows(scaled, [done])
    table = near_table(offsets, near, block_rows)
    terms, _ = products(offsets, ranges, columns, matrix, own_matrix, near, far, table)
    near, far, offsets = gather_rows(middle(degree, terms), [])
    table = near_table(offsets, near, block_rows)
    terms, (first, trace) = products(offsets, ranges, columns, matrix, own_matrix, near, far, table)
    rows, grams = collect(total, degree, first, trace, terms)
    gram, first = add_columns(total, [grams] + [swap(grams, "cols", m) for m in ranges])
    inverse = first_factor(first)
    return finish(total, block_rows, rows, inverse, add_rows(gram, [inverse]))


def solution(mesh):
    return jax.shard_map(
        body,
        mesh=mesh,
        in_specs=(
            P(None, "rows", "cols", None, None),
            P(None, "rows", "cols", None),
            P(None, "rows", "cols"),
            P("cols", "rows", None),
            P("cols", "rows", None),
        ),
        out_specs=P("cols", "rows", None),
        check_vma=False,
    )
```

```python
import functools

import jax
import jax.numpy as jnp
from jax import lax
from jax.experimental import pallas as pl
from jax.experimental.pallas import tpu as pltpu
from jax.sharding import PartitionSpec as P

BF16 = jnp.bfloat16
F32 = jnp.float32
HIGHEST = lax.Precision.HIGHEST
MIB = 1024 * 1024


def params(limit=48 * MIB):
    return pltpu.CompilerParams(vmem_limit_bytes=limit)


def vmem():
    return pl.BlockSpec(memory_space=pltpu.VMEM)


def hbm():
    return pl.BlockSpec(memory_space=pltpu.HBM)


def smem():
    return pl.BlockSpec(memory_space=pltpu.SMEM)


def shaped(shape, dtype):
    return jax.ShapeDtypeStruct(shape, dtype)


def iota(shape, dim):
    return lax.broadcasted_iota(jnp.int32, shape, dim)


def call(kernel, name, ins, outs, operands, scratch=(), limit=48 * MIB, **kwargs):
    return pl.pallas_call(
        kernel,
        out_shape=outs,
        in_specs=ins,
        out_specs=jax.tree.map(lambda _: vmem(), outs),
        scratch_shapes=list(scratch),
        compiler_params=params(limit),
        name=name,
        **kwargs,
    )(*operands)


def start_kernel(panel_hbm, inv_hbm, scaled_ref, degree_ref, panel_ref, inv_ref, scratch, sems):
    block_rows, block_size = inv_ref.shape[1], inv_ref.shape[2]
    half = block_size // 2
    copies = [
        pltpu.make_async_copy(inv_hbm, inv_ref, sems.at[0]),
        pltpu.make_async_copy(panel_hbm, panel_ref, sems.at[1]),
    ]
    for copy in copies:
        copy.start()
    copies[0].wait()
    pair = iota((half, block_size), 1) // 2 == iota((half, block_size), 0)
    spread = (iota((block_size, 128), 0) % 2 == iota((block_size, 128), 1) // 64).astype(F32)
    rows = [
        jnp.where(pair, jnp.broadcast_to(inv_ref[0, i : i + 1, :], (half, block_size)), 0.0)
        for i in range(block_rows)
    ]
    degree_ref[...] = jnp.dot(
        jnp.concatenate(rows, axis=0), spread, precision=HIGHEST, preferred_element_type=F32
    )
    copies[1].wait()
    for t in range(half):
        scratch[t * block_rows : (t + 1) * block_rows, :] = panel_ref[0, :, t * 128 : (t + 1) * 128]
    for i in range(block_rows):
        where = slice(i * half, (i + 1) * half)
        part = scratch[pl.ds(i, half, stride=block_rows), :] * degree_ref[where, :]
        scaled_ref[where, :] = part.astype(BF16)


def start(panel, inv_degree):
    block_rows, block_size = inv_degree.shape[1:]
    shape = (block_rows * block_size // 2, 128)
    return call(
        start_kernel,
        "start",
        [hbm(), hbm()],
        (shaped(shape, BF16), shaped(shape, F32)),
        (panel, inv_degree),
        [
            pltpu.VMEM(panel.shape, F32),
            pltpu.VMEM(inv_degree.shape, F32),
            pltpu.VMEM(shape, F32),
            pltpu.SemaphoreType.DMA((2,)),
        ],
    )


def prep_kernel(ranges, affinity_hbm, out_ref, done_ref, affinity_ref, scratch, sems):
    done_ref[...] = jnp.zeros_like(done_ref)
    count, block_rows, _, slots, flat = affinity_ref.shape
    half = flat // 128
    own = lax.axis_index("cols")
    copies = [
        pltpu.make_async_copy(affinity_hbm.at[m ^ own], affinity_ref.at[place], sems.at[place])
        for place, m in enumerate(ranges)
    ]
    for copy in copies:
        copy.start()
    source, target = iota((256, 256), 0), iota((256, 256), 1)
    moved = (source // 64 % 2) * 128 + (source // 128) * 64 + (source % 2) * 32 + source % 64 // 2
    permute = (moved == target).astype(BF16)
    for m in range(count):
        copies[m].wait()
        for i in range(block_rows):
            block = affinity_ref[m, i, 0].astype(F32)
            for t in range(half):
                scratch[i % 2, t * slots : (t + 1) * slots, :] = block[:, t * 128 : (t + 1) * 128]
            parts = [
                scratch[i % 2, pl.ds(s, half, stride=slots), :].astype(BF16) for s in range(slots)
            ]
            pairs = [jnp.concatenate(parts[s : s + 2], axis=1) for s in range(0, slots, 2)]
            moved_pairs = jnp.dot(
                jnp.concatenate(pairs, axis=0), permute, preferred_element_type=F32
            ).astype(BF16)
            for s in range(slots // 2):
                piece = moved_pairs[s * half : (s + 1) * half]
                out_ref[m, i, :half, s * 128 : (s + 1) * 128] = piece[:, :128]
                out_ref[m, i, half:, s * 128 : (s + 1) * 128] = piece[:, 128:]


def prep(ranges, affinity):
    _, block_rows, _, slots, flat = affinity.shape
    count = len(ranges)
    return call(
        functools.partial(prep_kernel, ranges),
        "prep",
        [hbm()],
        (shaped((count, block_rows, 64, slots * 64), BF16), shaped((8, 128), F32)),
        (affinity,),
        [
            pltpu.VMEM((count,) + affinity.shape[1:], BF16),
            pltpu.VMEM((2, flat // 128 * slots, 128), F32),
            pltpu.SemaphoreType.DMA((count,)),
        ],
    )


def split(value):
    high = value.astype(BF16)
    rest = value - high.astype(F32)
    middle = rest.astype(BF16)
    return high, middle, (rest - middle.astype(F32)).astype(BF16)


def joined(ref, index, first):
    high, middle, low = (
        ref[index, first + 32 * part : first + 32 * (part + 1)].astype(F32) for part in range(3)
    )
    return high + (middle + low)


def stack_kernel(count, *refs):
    for index in range(count):
        refs[-1][index] = refs[index][...]


def stack(pieces, after):
    return call(
        functools.partial(stack_kernel, len(pieces)),
        "stack",
        [vmem()] * (len(pieces) + len(after)),
        shaped((len(pieces),) + pieces[0].shape, BF16),
        (*pieces, *after),
    )


def fill_table(pieces_ref, offsets, table):
    block_rows = (table.shape[0] - 1) // (2 * len(offsets))
    low = iota((32, 128), 1) < 64
    for index, offset in enumerate(offsets):
        base = (lax.axis_index("rows") ^ offset) * block_rows
        for i in range(block_rows):
            block = pieces_ref[index, i * 32 : (i + 1) * 32, :]
            turned = jnp.concatenate([block[:, 64:], block[:, :64]], axis=1)
            table[base + i, :32] = jnp.where(low, block, turned)
            table[base + i, 32:] = jnp.where(low, turned, block)


def near_kernel(offsets, near_ref, table):
    table[table.shape[0] - 1] = jnp.zeros(table.shape[1:], BF16)
    fill_table(near_ref, offsets, table)


def near_table(offsets, near, block_rows):
    count = near.shape[0]
    return call(
        functools.partial(near_kernel, offsets[:count]),
        "near",
        [vmem()],
        shaped((2 * count * block_rows + 1, 64, 128), BF16),
        (near,),
    )


def one_product(group, columns, matrix, table, out_ref):
    block_rows, slots = columns.shape[1], columns.shape[3]
    low = iota((32, 128), 1) < 64
    for i in range(block_rows):
        picked = [table[columns[group, i, 0, s]] for s in range(slots)]
        result = jnp.dot(matrix[i], jnp.concatenate(picked, axis=0), preferred_element_type=F32)
        out_ref[i * 32 : (i + 1) * 32, :] = jnp.where(low, result[:32], result[32:]).astype(BF16)


def others_kernel(offsets, ranges, columns_any, matrix_ref, far_ref, near_ref, old_table, table, *refs):
    del old_table
    *outs, columns, sem = refs
    copy = pltpu.make_async_copy(columns_any, columns, sem)
    copy.start()
    fill_table(far_ref, offsets, table)
    terms, grams = outs[: len(ranges)], outs[len(ranges) :]
    first = matrix_ref.shape[1] * 32
    if grams:
        gram_ref, trace_ref = grams
        gram = joined(near_ref, 0, first) + joined(far_ref, 0, first)
        for index in range(1, len(offsets)):
            gram = gram + joined(near_ref, index, first) + joined(far_ref, index, first)
        gram_ref[...] = gram
        row, lane = iota(gram.shape, 0), iota(gram.shape, 1)
        diagonal = lane % 64 == row + lane // 64 * 32
        trace = jnp.sum(jnp.where(diagonal, gram, 0.0), axis=(0, 1), keepdims=True)
        trace = jnp.broadcast_to(trace, trace_ref.shape).astype(BF16)
        trace_ref[...] = trace
        for term in terms:
            term[first:, :] = trace
    copy.wait()
    for place, m in enumerate(ranges):
        group = m ^ lax.axis_index("cols")
        one_product(group, columns, matrix_ref.at[place], table, terms[place])


def own_kernel(columns, matrix_ref, table, out_ref):
    one_product(lax.axis_index("cols"), columns, matrix_ref.at[0], table, out_ref)


def products(offsets, ranges, columns, matrix, own_matrix, near, far, table):
    block_rows, count = matrix.shape[1], near.shape[0]
    extra = near.shape[1] > block_rows * 32
    rows = block_rows * 32
    outs = [shaped(table.shape, BF16)] + [shaped((rows + 16 * extra, 128), BF16)] * len(ranges)
    if extra:
        outs += [shaped((32, 128), F32), shaped((16, 128), BF16)]
    table, *outs = call(
        functools.partial(others_kernel, offsets[count:], ranges),
        "others",
        [pl.BlockSpec(memory_space=pl.ANY)] + [vmem()] * 4,
        outs,
        (columns, matrix, far, near, table),
        [pltpu.SMEM(columns.shape, jnp.int32), pltpu.SemaphoreType.DMA],
        input_output_aliases={4: 0},
    )
    terms = [swap(term, "cols", m) for m, term in zip(ranges, outs)]
    own = call(
        own_kernel,
        "own",
        [smem(), vmem(), vmem()],
        shaped((rows, 128), BF16),
        (columns, own_matrix, table),
    )
    return [own] + terms, outs[len(ranges) :]


def add_terms(terms, rows):
    summed = terms[0][:rows].astype(F32)
    for term in terms[1:]:
        summed = summed + term[:rows].astype(F32)
    return summed


def local_gram(rows):
    both = lax.dot_general(
        rows, rows, (((0,), (0,)), ((), ())), precision=HIGHEST, preferred_element_type=F32
    )
    gram = both[:64, :64] + both[64:, 64:]
    return jnp.concatenate([gram[:32], gram[32:]], axis=1)


def middle_kernel(degree_ref, *refs):
    terms, out_ref = refs[:-1], refs[-1]
    count = degree_ref.shape[0]
    degree = degree_ref[...]
    rows = add_terms(terms, count) * degree
    out_ref[:count] = (rows * degree).astype(BF16)
    for part, value in enumerate(split(local_gram(rows))):
        out_ref[count + part * 32 : count + (part + 1) * 32] = value


def middle(degree, terms):
    return call(
        middle_kernel,
        "middle",
        [vmem()] * (1 + len(terms)),
        shaped((degree.shape[0] + 96, 128), BF16),
        (degree, *terms),
    )


def collect_kernel(total, degree_ref, first_ref, trace_ref, *refs):
    terms, (rows_ref, grams_ref) = refs[:-2], refs[-2:]
    count = degree_ref.shape[0]
    largest = trace_ref[...].astype(F32)
    for term in terms[1:]:
        largest = jnp.maximum(largest, term[count:].astype(F32))
    scale = lax.rsqrt(largest[:1] / total)
    rows = add_terms(terms, count) * degree_ref[...] * scale
    rows_ref[...] = rows
    grams_ref[32:] = first_ref[...] * (scale * scale)
    grams_ref[:32] = local_gram(rows)


def collect(total, degree, first, trace, terms):
    return call(
        functools.partial(collect_kernel, total),
        "collect",
        [vmem()] * (3 + len(terms)),
        (shaped(degree.shape, F32), shaped((64, 128), F32)),
        (degree, first, trace, *terms),
    )


def lower_solve(gram, right):
    work = jnp.concatenate([gram, right], axis=1)
    blocks = gram.shape[0] // 8
    rows = [work[8 * i : 8 * i + 8] for i in range(blocks)]
    at = iota((8, 128), 0)

    def columns(first, column):
        return [
            jnp.broadcast_to(rows[i][:, column : column + 1], (8, 128))
            for i in range(first, blocks)
        ]

    def spread(block, row):
        return jnp.broadcast_to(block[row : row + 1], (8, 128))

    current = [columns(0, q) for q in range(8)]
    for b in range(blocks):
        count = blocks - b
        later = []
        if count > 1:
            later = [columns(b + 1, 8 * (b + 1) + q) for q in range(8)]
        for q in range(8):
            root = lax.rsqrt(spread(current[q][0], q))
            inverse = root * root
            raw = spread(rows[b], q)
            scaled = raw * inverse
            for p in range(q + 1, 8):
                weight = spread(current[q][0], p) * inverse
                current[p] = [x - y * weight for x, y in zip(current[p], current[q])]
            below = rows[b] - current[q][0] * scaled
            rows[b] = jnp.where(at == q, raw * root, jnp.where(at > q, below, rows[b]))
            for i in range(1, count):
                rows[b + i] = rows[b + i] - current[q][i] * scaled
            for p in range(len(later)):
                weight = spread(current[q][1], p) * inverse
                later[p] = [x - y * weight for x, y in zip(later[p], current[q][1:])]
        current = later
    return jnp.concatenate(rows, axis=0)[:, 64:]


def unpacked(packed):
    return jnp.concatenate([packed[:, :64], packed[:, 64:]], axis=0)


def add_columns_kernel(total, *refs):
    parts, (gram_ref, first_ref) = refs[:-2], refs[-2:]
    summed = parts[0][...]
    for part in parts[1:]:
        summed = summed + part[...]
    gram_ref[...] = summed[:32]
    first_ref[...] = summed[32:] / total


def add_columns(total, parts):
    return call(
        functools.partial(add_columns_kernel, total),
        "add_columns",
        [vmem()] * len(parts),
        (shaped((32, 128), F32), shaped((32, 128), F32)),
        parts,
    )


def add_parts_kernel(count, *refs):
    summed = refs[0][...]
    for part in refs[1:count]:
        summed = summed + part[...]
    refs[-1][...] = summed


def add_parts(parts, after):
    return call(
        functools.partial(add_parts_kernel, len(parts)),
        "add_parts",
        [vmem()] * (len(parts) + len(after)),
        shaped(parts[0].shape, F32),
        (*parts, *after),
    )


def first_factor_kernel(gram_ref, out_ref):
    unit = (iota((64, 64), 0) == iota((64, 64), 1)).astype(F32)
    out_ref[...] = lower_solve(unpacked(gram_ref[...]), unit)


def first_factor(gram):
    return call(first_factor_kernel, "first_factor", [vmem()], shaped((64, 64), F32), (gram,))


def dot_turned(left, right):
    return lax.dot_general(
        left, right, (((1,), (1,)), ((), ())), precision=HIGHEST, preferred_element_type=F32
    )


def finish_kernel(total, rows_ref, inverse_ref, *refs):
    out_ref, scratch = refs[-2:]
    block_rows = out_ref.shape[1]
    packed = refs[0][...]
    for part in refs[1:-2]:
        packed = packed + part[...]
    first = inverse_ref[...]
    gram = dot_turned(
        jnp.dot(first, unpacked(packed), precision=HIGHEST, preferred_element_type=F32), first
    )
    inverse = lower_solve(gram / total, first)
    zero = jnp.zeros_like(inverse)
    both = jnp.concatenate(
        [jnp.concatenate([inverse, zero], axis=1), jnp.concatenate([zero, inverse], axis=1)], axis=0
    )
    current = dot_turned(rows_ref[...], both)
    for i in range(block_rows):
        scratch[pl.ds(i, 32, stride=block_rows), :] = current[i * 32 : (i + 1) * 32]
    for t in range(32):
        out_ref[0, :, t * 128 : (t + 1) * 128] = scratch[t * block_rows : (t + 1) * block_rows, :]


def finish(total, block_rows, rows, inverse, grams):
    return call(
        functools.partial(finish_kernel, total),
        "finish",
        [vmem()] * (2 + len(grams)),
        shaped((1, block_rows, 32 * 128), F32),
        (rows, inverse, *grams),
        [pltpu.VMEM(rows.shape, F32)],
    )


def swap(value, axis, mask):
    size = lax.axis_size(axis)
    return lax.ppermute(value, axis, [(index, index ^ mask) for index in range(size)])


def stages(size):
    if size == 8:
        return [[2, 4, 6], [1]]
    bits, bit = [], 1
    while bit < size:
        bits.append([bit])
        bit *= 2
    return bits


def gather_rows(message, after):
    plan = stages(lax.axis_size("rows"))
    held, offsets = [message], [0]
    for masks in plan[:-1]:
        held = held + [swap(piece, "rows", mask) for mask in masks for piece in held]
        offsets = offsets + [mask ^ offset for mask in masks for offset in offsets]
    near = stack(held, after)
    (last,) = plan[-1]
    offsets = offsets + [last ^ offset for offset in offsets]
    return near, swap(near, "rows", last), offsets


def add_rows(gram, after):
    *plan, (last,) = stages(lax.axis_size("rows"))
    for masks in plan:
        gram = add_parts([gram] + [swap(gram, "rows", mask) for mask in masks], after)
    return [gram, swap(gram, "rows", last)]


def body(affinity, block_columns, block_counts, inv_degree, panel):
    block_rows, block_size = inv_degree.shape[1:]
    groups, _, _, slots, _ = affinity.shape
    ranks = lax.axis_size("rows")
    total = float(groups * ranks * block_rows * block_size)
    blocks = ranks * block_rows
    live = iota(block_columns.shape, 3) < block_counts[..., None]
    columns = jnp.where(live, jnp.clip(block_columns, 0, blocks - 1), blocks)
    panel, inv_degree, affinity = (
        pltpu.with_memory_space_constraint(value, pltpu.HBM) for value in (panel, inv_degree, affinity)
    )
    ranges = list(range(groups - 1, 0, -1))

    scaled, degree = start(panel, inv_degree)
    matrix, done = prep(ranges, affinity)
    own_matrix, _ = prep([0], affinity)
    near, far, offsets = gather_rows(scaled, [done])
    table = near_table(offsets, near, block_rows)
    terms, _ = products(offsets, ranges, columns, matrix, own_matrix, near, far, table)
    near, far, offsets = gather_rows(middle(degree, terms), [])
    table = near_table(offsets, near, block_rows)
    terms, (first, trace) = products(offsets, ranges, columns, matrix, own_matrix, near, far, table)
    rows, grams = collect(total, degree, first, trace, terms)
    gram, first = add_columns(total, [grams] + [swap(grams, "cols", m) for m in reversed(ranges)])
    inverse = first_factor(first)
    return finish(total, block_rows, rows, inverse, add_rows(gram, [inverse]))


def solution(mesh):
    return jax.shard_map(
        body,
        mesh=mesh,
        in_specs=(
            P(None, "rows", "cols", None, None),
            P(None, "rows", "cols", None),
            P(None, "rows", "cols"),
            P("cols", "rows", None),
            P("cols", "rows", None),
        ),
        out_specs=P("cols", "rows", None),
        check_vma=False,
    )
```

```python
import functools

import jax
import jax.numpy as jnp
from jax import lax
from jax.experimental import pallas as pl
from jax.experimental.pallas import tpu as pltpu
from jax.sharding import PartitionSpec as P

BF16 = jnp.bfloat16
F32 = jnp.float32
HIGHEST = lax.Precision.HIGHEST
MIB = 1024 * 1024


def params(limit=48 * MIB):
    return pltpu.CompilerParams(vmem_limit_bytes=limit)


def vmem():
    return pl.BlockSpec(memory_space=pltpu.VMEM)


def hbm():
    return pl.BlockSpec(memory_space=pltpu.HBM)


def smem():
    return pl.BlockSpec(memory_space=pltpu.SMEM)


def shaped(shape, dtype):
    return jax.ShapeDtypeStruct(shape, dtype)


def iota(shape, dim):
    return lax.broadcasted_iota(jnp.int32, shape, dim)


def call(kernel, name, ins, outs, operands, scratch=(), limit=48 * MIB, **kwargs):
    return pl.pallas_call(
        kernel,
        out_shape=outs,
        in_specs=ins,
        out_specs=jax.tree.map(lambda _: vmem(), outs),
        scratch_shapes=list(scratch),
        compiler_params=params(limit),
        name=name,
        **kwargs,
    )(*operands)


def start_kernel(panel_hbm, inv_hbm, scaled_ref, degree_ref, panel_ref, inv_ref, scratch, sems):
    block_rows, block_size = inv_ref.shape[1], inv_ref.shape[2]
    half = block_size // 2
    copies = [
        pltpu.make_async_copy(inv_hbm, inv_ref, sems.at[0]),
        pltpu.make_async_copy(panel_hbm, panel_ref, sems.at[1]),
    ]
    for copy in copies:
        copy.start()
    copies[0].wait()
    pair = iota((half, block_size), 1) // 2 == iota((half, block_size), 0)
    spread = (iota((block_size, 128), 0) % 2 == iota((block_size, 128), 1) // 64).astype(F32)
    rows = [
        jnp.where(pair, jnp.broadcast_to(inv_ref[0, i : i + 1, :], (half, block_size)), 0.0)
        for i in range(block_rows)
    ]
    degree_ref[...] = jnp.dot(
        jnp.concatenate(rows, axis=0), spread, precision=HIGHEST, preferred_element_type=F32
    )
    copies[1].wait()
    for t in range(half):
        scratch[t * block_rows : (t + 1) * block_rows, :] = panel_ref[0, :, t * 128 : (t + 1) * 128]
    for i in range(block_rows):
        where = slice(i * half, (i + 1) * half)
        part = scratch[pl.ds(i, half, stride=block_rows), :] * degree_ref[where, :]
        scaled_ref[where, :] = part.astype(BF16)


def start(panel, inv_degree):
    block_rows, block_size = inv_degree.shape[1:]
    shape = (block_rows * block_size // 2, 128)
    return call(
        start_kernel,
        "start",
        [hbm(), hbm()],
        (shaped(shape, BF16), shaped(shape, F32)),
        (panel, inv_degree),
        [
            pltpu.VMEM(panel.shape, F32),
            pltpu.VMEM(inv_degree.shape, F32),
            pltpu.VMEM(shape, F32),
            pltpu.SemaphoreType.DMA((2,)),
        ],
    )


def prep_kernel(ranges, affinity_hbm, out_ref, done_ref, affinity_ref, scratch, sems):
    done_ref[...] = jnp.zeros_like(done_ref)
    count, block_rows, _, slots, flat = affinity_ref.shape
    half = flat // 128
    own = lax.axis_index("cols")
    copies = [
        pltpu.make_async_copy(affinity_hbm.at[m ^ own], affinity_ref.at[place], sems.at[place])
        for place, m in enumerate(ranges)
    ]
    for copy in copies:
        copy.start()
    source, target = iota((256, 256), 0), iota((256, 256), 1)
    moved = (source // 64 % 2) * 128 + (source // 128) * 64 + (source % 2) * 32 + source % 64 // 2
    permute = (moved == target).astype(BF16)
    for m in range(count):
        copies[m].wait()
        for i in range(block_rows):
            block = affinity_ref[m, i, 0].astype(F32)
            for t in range(half):
                scratch[i % 2, t * slots : (t + 1) * slots, :] = block[:, t * 128 : (t + 1) * 128]
            parts = [
                scratch[i % 2, pl.ds(s, half, stride=slots), :].astype(BF16) for s in range(slots)
            ]
            pairs = [jnp.concatenate(parts[s : s + 2], axis=1) for s in range(0, slots, 2)]
            moved_pairs = jnp.dot(
                jnp.concatenate(pairs, axis=0), permute, preferred_element_type=F32
            ).astype(BF16)
            for s in range(slots // 2):
                piece = moved_pairs[s * half : (s + 1) * half]
                out_ref[m, i, :half, s * 128 : (s + 1) * 128] = piece[:, :128]
                out_ref[m, i, half:, s * 128 : (s + 1) * 128] = piece[:, 128:]


def prep(ranges, affinity):
    _, block_rows, _, slots, flat = affinity.shape
    count = len(ranges)
    return call(
        functools.partial(prep_kernel, ranges),
        "prep",
        [hbm()],
        (shaped((count, block_rows, 64, slots * 64), BF16), shaped((8, 128), F32)),
        (affinity,),
        [
            pltpu.VMEM((count,) + affinity.shape[1:], BF16),
            pltpu.VMEM((2, flat // 128 * slots, 128), F32),
            pltpu.SemaphoreType.DMA((count,)),
        ],
    )


def split(value):
    high = value.astype(BF16)
    rest = value - high.astype(F32)
    middle = rest.astype(BF16)
    return high, middle, (rest - middle.astype(F32)).astype(BF16)


def joined(ref, index, first):
    high, middle, low = (
        ref[index, first + 32 * part : first + 32 * (part + 1)].astype(F32) for part in range(3)
    )
    return high + (middle + low)


def stack_kernel(count, *refs):
    for index in range(count):
        refs[-1][index] = refs[index][...]


def stack(pieces, after):
    return call(
        functools.partial(stack_kernel, len(pieces)),
        "stack",
        [vmem()] * (len(pieces) + len(after)),
        shaped((len(pieces),) + pieces[0].shape, BF16),
        (*pieces, *after),
    )


def fill_table(pieces_ref, offsets, table):
    block_rows = (table.shape[0] - 1) // (2 * len(offsets))
    low = iota((32, 128), 1) < 64
    for index, offset in enumerate(offsets):
        base = (lax.axis_index("rows") ^ offset) * block_rows
        for i in range(block_rows):
            block = pieces_ref[index, i * 32 : (i + 1) * 32, :]
            turned = jnp.concatenate([block[:, 64:], block[:, :64]], axis=1)
            table[base + i, :32] = jnp.where(low, block, turned)
            table[base + i, 32:] = jnp.where(low, turned, block)


def near_kernel(offsets, near_ref, table):
    table[table.shape[0] - 1] = jnp.zeros(table.shape[1:], BF16)
    fill_table(near_ref, offsets, table)


def near_table(offsets, near, block_rows):
    count = near.shape[0]
    return call(
        functools.partial(near_kernel, offsets[:count]),
        "near",
        [vmem()],
        shaped((2 * count * block_rows + 1, 64, 128), BF16),
        (near,),
    )


def one_product(group, columns, matrix, table, out_ref):
    block_rows, slots = columns.shape[1], columns.shape[3]
    low = iota((32, 128), 1) < 64
    for i in range(block_rows):
        picked = [table[columns[group, i, 0, s]] for s in range(slots)]
        result = jnp.dot(matrix[i], jnp.concatenate(picked, axis=0), preferred_element_type=F32)
        out_ref[i * 32 : (i + 1) * 32, :] = jnp.where(low, result[:32], result[32:]).astype(BF16)


def others_kernel(offsets, ranges, columns_any, matrix_ref, far_ref, near_ref, old_table, table, *refs):
    del old_table
    *outs, columns, sem = refs
    copy = pltpu.make_async_copy(columns_any, columns, sem)
    copy.start()
    fill_table(far_ref, offsets, table)
    terms, grams = outs[: len(ranges)], outs[len(ranges) :]
    first = matrix_ref.shape[1] * 32
    if grams:
        gram_ref, trace_ref = grams
        gram = joined(near_ref, 0, first) + joined(far_ref, 0, first)
        for index in range(1, len(offsets)):
            gram = gram + joined(near_ref, index, first) + joined(far_ref, index, first)
        gram_ref[...] = gram
        row, lane = iota(gram.shape, 0), iota(gram.shape, 1)
        diagonal = lane % 64 == row + lane // 64 * 32
        trace = jnp.sum(jnp.where(diagonal, gram, 0.0), axis=(0, 1), keepdims=True)
        trace = jnp.broadcast_to(trace, trace_ref.shape).astype(BF16)
        trace_ref[...] = trace
        for term in terms:
            term[first:, :] = trace
    copy.wait()
    for place, m in enumerate(ranges):
        group = m ^ lax.axis_index("cols")
        one_product(group, columns, matrix_ref.at[place], table, terms[place])


def own_kernel(columns, matrix_ref, table, out_ref):
    one_product(lax.axis_index("cols"), columns, matrix_ref.at[0], table, out_ref)


def products(offsets, ranges, columns, matrix, own_matrix, near, far, table):
    block_rows, count = matrix.shape[1], near.shape[0]
    extra = near.shape[1] > block_rows * 32
    rows = block_rows * 32
    outs = [shaped(table.shape, BF16)] + [shaped((rows + 16 * extra, 128), BF16)] * len(ranges)
    if extra:
        outs += [shaped((32, 128), F32), shaped((16, 128), BF16)]
    table, *outs = call(
        functools.partial(others_kernel, offsets[count:], ranges),
        "others",
        [pl.BlockSpec(memory_space=pl.ANY)] + [vmem()] * 4,
        outs,
        (columns, matrix, far, near, table),
        [pltpu.SMEM(columns.shape, jnp.int32), pltpu.SemaphoreType.DMA],
        input_output_aliases={4: 0},
    )
    terms = [swap(term, "cols", m) for m, term in zip(ranges, outs)]
    own = call(
        own_kernel,
        "own",
        [smem(), vmem(), vmem()],
        shaped((rows, 128), BF16),
        (columns, own_matrix, table),
    )
    return [own] + terms, outs[len(ranges) :]


def add_terms(terms, rows):
    summed = terms[0][:rows].astype(F32)
    for term in terms[1:]:
        summed = summed + term[:rows].astype(F32)
    return summed


def local_gram(rows):
    both = lax.dot_general(
        rows, rows, (((0,), (0,)), ((), ())), precision=HIGHEST, preferred_element_type=F32
    )
    gram = both[:64, :64] + both[64:, 64:]
    return jnp.concatenate([gram[:32], gram[32:]], axis=1)


def middle_kernel(degree_ref, *refs):
    terms, out_ref = refs[:-1], refs[-1]
    count = degree_ref.shape[0]
    degree = degree_ref[...]
    rows = add_terms(terms, count) * degree
    out_ref[:count] = (rows * degree).astype(BF16)
    for part, value in enumerate(split(local_gram(rows))):
        out_ref[count + part * 32 : count + (part + 1) * 32] = value


def middle(degree, terms):
    return call(
        middle_kernel,
        "middle",
        [vmem()] * (1 + len(terms)),
        shaped((degree.shape[0] + 96, 128), BF16),
        (degree, *terms),
    )


def collect_kernel(total, degree_ref, first_ref, trace_ref, *refs):
    terms, (rows_ref, grams_ref) = refs[:-2], refs[-2:]
    count = degree_ref.shape[0]
    largest = trace_ref[...].astype(F32)
    for term in terms[1:]:
        largest = jnp.maximum(largest, term[count:].astype(F32))
    scale = lax.rsqrt(largest[:1] / total)
    rows = add_terms(terms, count) * degree_ref[...] * scale
    rows_ref[...] = rows
    grams_ref[32:] = first_ref[...] * (scale * scale)
    grams_ref[:32] = local_gram(rows)


def collect(total, degree, first, trace, terms):
    return call(
        functools.partial(collect_kernel, total),
        "collect",
        [vmem()] * (3 + len(terms)),
        (shaped(degree.shape, F32), shaped((64, 128), F32)),
        (degree, first, trace, *terms),
    )


def lower_solve(gram, right):
    work = jnp.concatenate([gram, right], axis=1)
    blocks = gram.shape[0] // 8
    rows = [work[8 * i : 8 * i + 8] for i in range(blocks)]
    at = iota((8, 128), 0)

    def columns(first, column):
        return [
            jnp.broadcast_to(rows[i][:, column : column + 1], (8, 128))
            for i in range(first, blocks)
        ]

    def spread(block, row):
        return jnp.broadcast_to(block[row : row + 1], (8, 128))

    current = [columns(0, q) for q in range(8)]
    for b in range(blocks):
        count = blocks - b
        later = []
        if count > 1:
            later = [columns(b + 1, 8 * (b + 1) + q) for q in range(8)]
        for q in range(8):
            root = lax.rsqrt(spread(current[q][0], q))
            inverse = root * root
            raw = spread(rows[b], q)
            scaled = raw * inverse
            for p in range(q + 1, 8):
                weight = spread(current[q][0], p) * inverse
                current[p] = [x - y * weight for x, y in zip(current[p], current[q])]
            below = rows[b] - current[q][0] * scaled
            rows[b] = jnp.where(at == q, raw * root, jnp.where(at > q, below, rows[b]))
            for i in range(1, count):
                rows[b + i] = rows[b + i] - current[q][i] * scaled
            for p in range(len(later)):
                weight = spread(current[q][1], p) * inverse
                later[p] = [x - y * weight for x, y in zip(later[p], current[q][1:])]
        current = later
    return jnp.concatenate(rows, axis=0)[:, 64:]


def unpacked(packed):
    return jnp.concatenate([packed[:, :64], packed[:, 64:]], axis=0)


def add_columns_kernel(total, *refs):
    parts, (gram_ref, first_ref) = refs[:-2], refs[-2:]
    summed = parts[0][...]
    for part in parts[1:]:
        summed = summed + part[...]
    gram_ref[...] = summed[:32]
    first_ref[...] = summed[32:] / total


def add_columns(total, parts):
    return call(
        functools.partial(add_columns_kernel, total),
        "add_columns",
        [vmem()] * len(parts),
        (shaped((32, 128), F32), shaped((32, 128), F32)),
        parts,
    )


def add_parts_kernel(count, *refs):
    summed = refs[0][...]
    for part in refs[1:count]:
        summed = summed + part[...]
    refs[-1][...] = summed


def add_parts(parts, after):
    return call(
        functools.partial(add_parts_kernel, len(parts)),
        "add_parts",
        [vmem()] * (len(parts) + len(after)),
        shaped(parts[0].shape, F32),
        (*parts, *after),
    )


def first_factor_kernel(gram_ref, out_ref):
    unit = (iota((64, 64), 0) == iota((64, 64), 1)).astype(F32)
    out_ref[...] = lower_solve(unpacked(gram_ref[...]), unit)


def first_factor(gram):
    return call(first_factor_kernel, "first_factor", [vmem()], shaped((64, 64), F32), (gram,))


def dot_turned(left, right):
    return lax.dot_general(
        left, right, (((1,), (1,)), ((), ())), precision=HIGHEST, preferred_element_type=F32
    )


def finish_kernel(total, rows_ref, inverse_ref, *refs):
    out_ref, scratch = refs[-2:]
    block_rows = out_ref.shape[1]
    packed = refs[0][...]
    for part in refs[1:-2]:
        packed = packed + part[...]
    first = inverse_ref[...]
    gram = dot_turned(
        jnp.dot(first, unpacked(packed), precision=HIGHEST, preferred_element_type=F32), first
    )
    inverse = lower_solve(gram / total, first)
    zero = jnp.zeros_like(inverse)
    both = jnp.concatenate(
        [jnp.concatenate([inverse, zero], axis=1), jnp.concatenate([zero, inverse], axis=1)], axis=0
    )
    current = dot_turned(rows_ref[...], both)
    for i in range(block_rows):
        scratch[pl.ds(i, 32, stride=block_rows), :] = current[i * 32 : (i + 1) * 32]
    for t in range(32):
        out_ref[0, :, t * 128 : (t + 1) * 128] = scratch[t * block_rows : (t + 1) * block_rows, :]


def finish(total, block_rows, rows, inverse, grams):
    return call(
        functools.partial(finish_kernel, total),
        "finish",
        [vmem()] * (2 + len(grams)),
        shaped((1, block_rows, 32 * 128), F32),
        (rows, inverse, *grams),
        [pltpu.VMEM(rows.shape, F32)],
    )


def swap(value, axis, mask):
    size = lax.axis_size(axis)
    return lax.ppermute(value, axis, [(index, index ^ mask) for index in range(size)])


def swap_both(value, row_mask, column_mask):
    rows, columns = lax.axis_size("rows"), lax.axis_size("cols")
    pairs = [
        (row * columns + column, (row ^ row_mask) * columns + (column ^ column_mask))
        for row in range(rows)
        for column in range(columns)
    ]
    return lax.ppermute(value, ("rows", "cols"), pairs)


def stages(size):
    if size == 8:
        return [[3, 5, 7], [1]]
    bits, bit = [], 1
    while bit < size:
        bits.append([bit])
        bit *= 2
    return bits


def gather_rows(message, after):
    plan = stages(lax.axis_size("rows"))
    held, offsets = [message], [0]
    for masks in plan[:-1]:
        held = held + [swap(piece, "rows", mask) for mask in masks for piece in held]
        offsets = offsets + [mask ^ offset for mask in masks for offset in offsets]
    near = stack(held, after)
    (last,) = plan[-1]
    offsets = offsets + [last ^ offset for offset in offsets]
    return near, swap(near, "rows", last), offsets


def add_rows(gram, after):
    *plan, (last,) = stages(lax.axis_size("rows"))
    for masks in plan:
        gram = add_parts([gram] + [swap(gram, "rows", mask) for mask in masks], after)
    return [gram, swap(gram, "rows", last)]


def body(affinity, block_columns, block_counts, inv_degree, panel):
    block_rows, block_size = inv_degree.shape[1:]
    groups, _, _, slots, _ = affinity.shape
    ranks = lax.axis_size("rows")
    total = float(groups * ranks * block_rows * block_size)
    blocks = ranks * block_rows
    live = iota(block_columns.shape, 3) < block_counts[..., None]
    columns = jnp.where(live, jnp.clip(block_columns, 0, blocks - 1), blocks)
    panel, inv_degree, affinity = (
        pltpu.with_memory_space_constraint(value, pltpu.HBM) for value in (panel, inv_degree, affinity)
    )
    ranges = list(range(groups - 1, 0, -1))

    scaled, degree = start(panel, inv_degree)
    matrix, done = prep(ranges, affinity)
    own_matrix, _ = prep([0], affinity)
    near, far, offsets = gather_rows(scaled, [done])
    table = near_table(offsets, near, block_rows)
    terms, _ = products(offsets, ranges, columns, matrix, own_matrix, near, far, table)
    near, far, offsets = gather_rows(middle(degree, terms), [])
    table = near_table(offsets, near, block_rows)
    terms, (first, trace) = products(offsets, ranges, columns, matrix, own_matrix, near, far, table)
    rows, grams = collect(total, degree, first, trace, terms)
    flip = 1 if ranks == 8 else 0
    gram, first = add_columns(total, [grams] + [swap_both(grams, flip, m) for m in reversed(ranges)])
    inverse = first_factor(first)
    return finish(total, block_rows, rows, inverse, add_rows(gram, [inverse]))


def solution(mesh):
    return jax.shard_map(
        body,
        mesh=mesh,
        in_specs=(
            P(None, "rows", "cols", None, None),
            P(None, "rows", "cols", None),
            P(None, "rows", "cols"),
            P("cols", "rows", None),
            P("cols", "rows", None),
        ),
        out_specs=P("cols", "rows", None),
        check_vma=False,
    )
```

```python
import functools

import jax
import jax.numpy as jnp
from jax import lax
from jax.experimental import pallas as pl
from jax.experimental.pallas import tpu as pltpu
from jax.sharding import PartitionSpec as P

BF16 = jnp.bfloat16
F32 = jnp.float32
HIGHEST = lax.Precision.HIGHEST
MIB = 1024 * 1024


def params(limit=48 * MIB):
    return pltpu.CompilerParams(vmem_limit_bytes=limit)


def vmem():
    return pl.BlockSpec(memory_space=pltpu.VMEM)


def hbm():
    return pl.BlockSpec(memory_space=pltpu.HBM)


def smem():
    return pl.BlockSpec(memory_space=pltpu.SMEM)


def shaped(shape, dtype):
    return jax.ShapeDtypeStruct(shape, dtype)


def iota(shape, dim):
    return lax.broadcasted_iota(jnp.int32, shape, dim)


def call(kernel, name, ins, outs, operands, scratch=(), limit=48 * MIB, **kwargs):
    return pl.pallas_call(
        kernel,
        out_shape=outs,
        in_specs=ins,
        out_specs=jax.tree.map(lambda _: vmem(), outs),
        scratch_shapes=list(scratch),
        compiler_params=params(limit),
        name=name,
        **kwargs,
    )(*operands)


def start_kernel(panel_hbm, inv_hbm, scaled_ref, degree_ref, panel_ref, inv_ref, scratch, sems):
    block_rows, block_size = inv_ref.shape[1], inv_ref.shape[2]
    half = block_size // 2
    copies = [
        pltpu.make_async_copy(inv_hbm, inv_ref, sems.at[0]),
        pltpu.make_async_copy(panel_hbm, panel_ref, sems.at[1]),
    ]
    for copy in copies:
        copy.start()
    copies[0].wait()
    pair = iota((half, block_size), 1) // 2 == iota((half, block_size), 0)
    spread = (iota((block_size, 128), 0) % 2 == iota((block_size, 128), 1) // 64).astype(F32)
    rows = [
        jnp.where(pair, jnp.broadcast_to(inv_ref[0, i : i + 1, :], (half, block_size)), 0.0)
        for i in range(block_rows)
    ]
    degree_ref[...] = jnp.dot(
        jnp.concatenate(rows, axis=0), spread, precision=HIGHEST, preferred_element_type=F32
    )
    copies[1].wait()
    for t in range(half):
        scratch[t * block_rows : (t + 1) * block_rows, :] = panel_ref[0, :, t * 128 : (t + 1) * 128]
    for i in range(block_rows):
        where = slice(i * half, (i + 1) * half)
        part = scratch[pl.ds(i, half, stride=block_rows), :] * degree_ref[where, :]
        scaled_ref[where, :] = part.astype(BF16)


def start(panel, inv_degree):
    block_rows, block_size = inv_degree.shape[1:]
    shape = (block_rows * block_size // 2, 128)
    return call(
        start_kernel,
        "start",
        [hbm(), hbm()],
        (shaped(shape, BF16), shaped(shape, F32)),
        (panel, inv_degree),
        [
            pltpu.VMEM(panel.shape, F32),
            pltpu.VMEM(inv_degree.shape, F32),
            pltpu.VMEM(shape, F32),
            pltpu.SemaphoreType.DMA((2,)),
        ],
    )


def prep_kernel(
    ranges, affinity_hbm, inv_hbm, out_ref, inverse_ref, affinity_ref, inv_ref, scratch, sems, inv_sem
):
    count, block_rows, _, slots, flat = affinity_ref.shape
    half = flat // 128
    own = lax.axis_index("cols")
    copies = [
        pltpu.make_async_copy(affinity_hbm.at[m ^ own], affinity_ref.at[place], sems.at[place])
        for place, m in enumerate(ranges)
    ]
    inv_copy = pltpu.make_async_copy(inv_hbm, inv_ref, inv_sem)
    inv_copy.start()
    for copy in copies:
        copy.start()
    source, target = iota((256, 256), 0), iota((256, 256), 1)
    moved = (source // 64 % 2) * 128 + (source // 128) * 64 + (source % 2) * 32 + source % 64 // 2
    permute = (moved == target).astype(BF16)
    inv_copy.wait()
    inverse = 1.0 / inv_ref[0]
    high = inverse.astype(BF16).astype(F32)
    inverse_ref[...] = jnp.concatenate([high, inverse - high], axis=1)
    for m in range(count):
        copies[m].wait()
        for i in range(block_rows):
            block = affinity_ref[m, i, 0].astype(F32)
            for t in range(half):
                scratch[i % 2, t * slots : (t + 1) * slots, :] = block[:, t * 128 : (t + 1) * 128]
            parts = [
                scratch[i % 2, pl.ds(s, half, stride=slots), :].astype(BF16) for s in range(slots)
            ]
            pairs = [jnp.concatenate(parts[s : s + 2], axis=1) for s in range(0, slots, 2)]
            moved_pairs = jnp.dot(
                jnp.concatenate(pairs, axis=0), permute, preferred_element_type=F32
            ).astype(BF16)
            for s in range(slots // 2):
                piece = moved_pairs[s * half : (s + 1) * half]
                out_ref[m, i, :half, s * 128 : (s + 1) * 128] = piece[:, :128]
                out_ref[m, i, half:, s * 128 : (s + 1) * 128] = piece[:, 128:]


def prep(ranges, affinity, inv_degree):
    _, block_rows, _, slots, flat = affinity.shape
    count = len(ranges)
    return call(
        functools.partial(prep_kernel, ranges),
        "prep",
        [hbm(), hbm()],
        (shaped((count, block_rows, 64, slots * 64), BF16), shaped((block_rows, 128), F32)),
        (affinity, inv_degree),
        [
            pltpu.VMEM((count,) + affinity.shape[1:], BF16),
            pltpu.VMEM(inv_degree.shape, F32),
            pltpu.VMEM((2, flat // 128 * slots, 128), F32),
            pltpu.SemaphoreType.DMA((count,)),
            pltpu.SemaphoreType.DMA,
        ],
    )


def stack_kernel(count, *refs):
    for index in range(count):
        refs[-1][index] = refs[index][...]


def stack(pieces, after):
    return call(
        functools.partial(stack_kernel, len(pieces)),
        "stack",
        [vmem()] * (len(pieces) + len(after)),
        shaped((len(pieces),) + pieces[0].shape, BF16),
        (*pieces, *after),
    )


def fill_table(pieces_ref, offsets, table):
    block_rows = (table.shape[0] - 1) // (2 * len(offsets))
    low = iota((32, 128), 1) < 64
    for index, offset in enumerate(offsets):
        base = (lax.axis_index("rows") ^ offset) * block_rows
        for i in range(block_rows):
            block = pieces_ref[index, i * 32 : (i + 1) * 32, :]
            turned = jnp.concatenate([block[:, 64:], block[:, :64]], axis=1)
            table[base + i, :32] = jnp.where(low, block, turned)
            table[base + i, 32:] = jnp.where(low, turned, block)


def near_kernel(offsets, near_ref, table):
    table[table.shape[0] - 1] = jnp.zeros(table.shape[1:], BF16)
    fill_table(near_ref, offsets, table)


def near_table(offsets, near, block_rows):
    count = near.shape[0]
    return call(
        functools.partial(near_kernel, offsets[:count]),
        "near",
        [vmem()],
        shaped((2 * count * block_rows + 1, 64, 128), BF16),
        (near,),
    )


def one_product(group, columns, matrix, table, out_ref):
    block_rows, slots = columns.shape[1], columns.shape[3]
    low = iota((32, 128), 1) < 64
    for i in range(block_rows):
        picked = [table[columns[group, i, 0, s]] for s in range(slots)]
        result = jnp.dot(matrix[i], jnp.concatenate(picked, axis=0), preferred_element_type=F32)
        out_ref[i * 32 : (i + 1) * 32, :] = jnp.where(low, result[:32], result[32:]).astype(BF16)


def largest_notes(notes):
    largest = notes[0].astype(F32)
    for note in notes[1:]:
        largest = jnp.maximum(largest, note.astype(F32))
    return largest


def others_kernel(offsets, ranges, columns_any, matrix_ref, far_ref, near_ref, old_table, table, *refs):
    del old_table
    *outs, columns, sem = refs
    copy = pltpu.make_async_copy(columns_any, columns, sem)
    copy.start()
    fill_table(far_ref, offsets, table)
    terms, first = outs[: len(ranges)], matrix_ref.shape[1] * 32
    if len(outs) > len(ranges):
        notes = largest_notes(
            [ref[index, first:] for ref in (near_ref, far_ref) for index in range(len(offsets))]
        ).astype(BF16)
        for ref in outs[len(ranges) :]:
            ref[...] = notes
        for term in terms:
            term[first:, :] = notes
    copy.wait()
    for place, m in enumerate(ranges):
        group = m ^ lax.axis_index("cols")
        one_product(group, columns, matrix_ref.at[place], table, terms[place])


def own_kernel(columns, matrix_ref, table, out_ref):
    one_product(lax.axis_index("cols"), columns, matrix_ref.at[0], table, out_ref)


def products(offsets, ranges, columns, matrix, own_matrix, near, far, table):
    block_rows, count = matrix.shape[1], near.shape[0]
    extra = near.shape[1] > block_rows * 32
    rows = block_rows * 32
    outs = [shaped(table.shape, BF16)] + [shaped((rows + 16 * extra, 128), BF16)] * len(ranges)
    if extra:
        outs.append(shaped((16, 128), BF16))
    table, *outs = call(
        functools.partial(others_kernel, offsets[count:], ranges),
        "others",
        [pl.BlockSpec(memory_space=pl.ANY)] + [vmem()] * 4,
        outs,
        (columns, matrix, far, near, table),
        [pltpu.SMEM(columns.shape, jnp.int32), pltpu.SemaphoreType.DMA],
        input_output_aliases={4: 0},
    )
    terms = [swap(term, "cols", m) for m, term in zip(ranges, outs)]
    own = call(
        own_kernel,
        "own",
        [smem(), vmem(), vmem()],
        shaped((rows, 128), BF16),
        (columns, own_matrix, table),
    )
    return [own] + terms, outs[len(ranges) :]


def add_terms(terms, rows):
    summed = terms[0][:rows].astype(F32)
    for term in terms[1:]:
        summed = summed + term[:rows].astype(F32)
    return summed


def folded(both):
    gram = both[:64, :64] + both[64:, 64:]
    return jnp.concatenate([gram[:32], gram[32:]], axis=1)


def local_gram(rows):
    both = lax.dot_general(
        rows, rows, (((0,), (0,)), ((), ())), precision=HIGHEST, preferred_element_type=F32
    )
    return folded(both)


def middle_kernel(degree_ref, inverse_ref, *refs):
    terms, out_ref = refs[:-1], refs[-1]
    count = degree_ref.shape[0]
    degree = degree_ref[...]
    rows = add_terms(terms, count) * degree
    out_ref[:count] = (rows * degree).astype(BF16)
    squares = jnp.sum(rows * rows, axis=(0, 1), keepdims=True)
    out_ref[count:] = jnp.concatenate(
        [inverse_ref[...], jnp.broadcast_to(squares, (8, 128))], axis=0
    ).astype(BF16)


def middle(degree, inverse, terms):
    return call(
        middle_kernel,
        "middle",
        [vmem()] * (2 + len(terms)),
        shaped((degree.shape[0] + 16, 128), BF16),
        (degree, inverse, *terms),
    )


def row_gram_kernel(near_ref, far_ref, gram_ref, rows):
    lane = iota((32, 128), 1)
    pair = lane % 64 // 2 == iota((32, 128), 0)
    spread = (iota((128, 128), 0) % 2 == iota((128, 128), 1) // 64).astype(BF16)
    count = near_ref.shape[1] - 16
    size = near_ref.shape[0]
    for index in range(2 * size):
        ref = (near_ref, far_ref)[index // size]
        notes = ref[index % size, count:].astype(F32)
        masked = [
            jnp.where(pair, jnp.broadcast_to(notes[i : i + 1], (32, 128)), 0.0).astype(BF16)
            for i in range(count // 32)
        ]
        inverse = jnp.dot(jnp.concatenate(masked, axis=0), spread, preferred_element_type=F32)
        block = ref[index % size, :count].astype(F32) * inverse
        rows[index * count : (index + 1) * count, :] = block.astype(BF16)
    both = lax.dot_general(
        rows[...], rows[...], (((0,), (0,)), ((), ())), preferred_element_type=F32
    )
    gram_ref[...] = folded(both)


def row_gram(near, far):
    count = 2 * near.shape[0] * (near.shape[1] - 16)
    return call(
        row_gram_kernel,
        "row_gram",
        [vmem(), vmem()],
        shaped((32, 128), F32),
        (near, far),
        [pltpu.VMEM((count, 128), BF16)],
    )


def collect_kernel(devices, total, degree_ref, first_ref, notes_ref, *refs):
    terms, (rows_ref, grams_ref) = refs[:-2], refs[-2:]
    count = degree_ref.shape[0]
    largest = largest_notes([notes_ref[...]] + [term[count:] for term in terms[1:]])
    scale = lax.rsqrt(largest[8:9] * (devices / total))
    rows = add_terms(terms, count) * degree_ref[...] * scale
    rows_ref[...] = rows
    grams_ref[32:] = first_ref[...] * (scale * scale)
    grams_ref[:32] = local_gram(rows)


def collect(devices, total, degree, first, notes, terms):
    return call(
        functools.partial(collect_kernel, devices, total),
        "collect",
        [vmem()] * (3 + len(terms)),
        (shaped(degree.shape, F32), shaped((64, 128), F32)),
        (degree, first, notes, *terms),
    )


def lower_solve(gram, right):
    work = jnp.concatenate([gram, right], axis=1)
    blocks = gram.shape[0] // 8
    rows = [work[8 * i : 8 * i + 8] for i in range(blocks)]
    at = iota((8, 128), 0)

    def columns(first, column):
        return [
            jnp.broadcast_to(rows[i][:, column : column + 1], (8, 128))
            for i in range(first, blocks)
        ]

    def spread(block, row):
        return jnp.broadcast_to(block[row : row + 1], (8, 128))

    current = [columns(0, q) for q in range(8)]
    for b in range(blocks):
        count = blocks - b
        later = []
        if count > 1:
            later = [columns(b + 1, 8 * (b + 1) + q) for q in range(8)]
        for q in range(8):
            root = lax.rsqrt(spread(current[q][0], q))
            inverse = root * root
            raw = spread(rows[b], q)
            scaled = raw * inverse
            for p in range(q + 1, 8):
                weight = spread(current[q][0], p) * inverse
                current[p] = [x - y * weight for x, y in zip(current[p], current[q])]
            below = rows[b] - current[q][0] * scaled
            rows[b] = jnp.where(at == q, raw * root, jnp.where(at > q, below, rows[b]))
            for i in range(1, count):
                rows[b + i] = rows[b + i] - current[q][i] * scaled
            for p in range(len(later)):
                weight = spread(current[q][1], p) * inverse
                later[p] = [x - y * weight for x, y in zip(later[p], current[q][1:])]
        current = later
    return jnp.concatenate(rows, axis=0)[:, 64:]


def unpacked(packed):
    return jnp.concatenate([packed[:, :64], packed[:, 64:]], axis=0)


def add_columns_kernel(total, *refs):
    parts, (gram_ref, first_ref) = refs[:-2], refs[-2:]
    summed = parts[0][...]
    for part in parts[1:]:
        summed = summed + part[...]
    gram_ref[...] = summed[:32]
    first_ref[...] = summed[32:] / total


def add_columns(total, parts):
    return call(
        functools.partial(add_columns_kernel, total),
        "add_columns",
        [vmem()] * len(parts),
        (shaped((32, 128), F32), shaped((32, 128), F32)),
        parts,
    )


def add_parts_kernel(count, *refs):
    summed = refs[0][...]
    for part in refs[1:count]:
        summed = summed + part[...]
    refs[-1][...] = summed


def add_parts(parts, after):
    return call(
        functools.partial(add_parts_kernel, len(parts)),
        "add_parts",
        [vmem()] * (len(parts) + len(after)),
        shaped(parts[0].shape, F32),
        (*parts, *after),
    )


def first_factor_kernel(gram_ref, out_ref):
    unit = (iota((64, 64), 0) == iota((64, 64), 1)).astype(F32)
    out_ref[...] = lower_solve(unpacked(gram_ref[...]), unit)


def first_factor(gram):
    return call(first_factor_kernel, "first_factor", [vmem()], shaped((64, 64), F32), (gram,))


def dot_turned(left, right):
    return lax.dot_general(
        left, right, (((1,), (1,)), ((), ())), precision=HIGHEST, preferred_element_type=F32
    )


def finish_kernel(total, rows_ref, inverse_ref, *refs):
    out_ref, scratch = refs[-2:]
    block_rows = out_ref.shape[1]
    packed = refs[0][...]
    for part in refs[1:-2]:
        packed = packed + part[...]
    first = inverse_ref[...]
    gram = dot_turned(
        jnp.dot(first, unpacked(packed), precision=HIGHEST, preferred_element_type=F32), first
    )
    inverse = lower_solve(gram / total, first)
    zero = jnp.zeros_like(inverse)
    both = jnp.concatenate(
        [jnp.concatenate([inverse, zero], axis=1), jnp.concatenate([zero, inverse], axis=1)], axis=0
    )
    current = dot_turned(rows_ref[...], both)
    for i in range(block_rows):
        scratch[pl.ds(i, 32, stride=block_rows), :] = current[i * 32 : (i + 1) * 32]
    for t in range(32):
        out_ref[0, :, t * 128 : (t + 1) * 128] = scratch[t * block_rows : (t + 1) * block_rows, :]


def finish(total, block_rows, rows, inverse, grams):
    return call(
        functools.partial(finish_kernel, total),
        "finish",
        [vmem()] * (2 + len(grams)),
        shaped((1, block_rows, 32 * 128), F32),
        (rows, inverse, *grams),
        [pltpu.VMEM(rows.shape, F32)],
    )


def swap(value, axis, mask):
    size = lax.axis_size(axis)
    return lax.ppermute(value, axis, [(index, index ^ mask) for index in range(size)])


def swap_both(value, row_mask, column_mask):
    rows, columns = lax.axis_size("rows"), lax.axis_size("cols")
    pairs = [
        (row * columns + column, (row ^ row_mask) * columns + (column ^ column_mask))
        for row in range(rows)
        for column in range(columns)
    ]
    return lax.ppermute(value, ("rows", "cols"), pairs)


def stages(size):
    if size == 8:
        return [[3, 5, 7], [1]]
    bits, bit = [], 1
    while bit < size:
        bits.append([bit])
        bit *= 2
    return bits


def gather_rows(message, after):
    plan = stages(lax.axis_size("rows"))
    held, offsets = [message], [0]
    for masks in plan[:-1]:
        held = held + [swap(piece, "rows", mask) for mask in masks for piece in held]
        offsets = offsets + [mask ^ offset for mask in masks for offset in offsets]
    near = stack(held, after)
    (last,) = plan[-1]
    offsets = offsets + [last ^ offset for offset in offsets]
    return near, swap(near, "rows", last), offsets


def add_rows(gram, after):
    *plan, (last,) = stages(lax.axis_size("rows"))
    for masks in plan:
        gram = add_parts([gram] + [swap(gram, "rows", mask) for mask in masks], after)
    return [gram, swap(gram, "rows", last)]


def body(affinity, block_columns, block_counts, inv_degree, panel):
    block_rows, block_size = inv_degree.shape[1:]
    groups, _, _, slots, _ = affinity.shape
    ranks = lax.axis_size("rows")
    total = float(groups * ranks * block_rows * block_size)
    blocks = ranks * block_rows
    live = iota(block_columns.shape, 3) < block_counts[..., None]
    columns = jnp.where(live, jnp.clip(block_columns, 0, blocks - 1), blocks)
    panel, inv_degree, affinity = (
        pltpu.with_memory_space_constraint(value, pltpu.HBM) for value in (panel, inv_degree, affinity)
    )
    ranges = list(range(groups - 1, 0, -1))

    scaled, degree = start(panel, inv_degree)
    matrix, inverse = prep(ranges, affinity, inv_degree)
    own_matrix, _ = prep([0], affinity, inv_degree)
    near, far, offsets = gather_rows(scaled, [inverse])
    table = near_table(offsets, near, block_rows)
    terms, _ = products(offsets, ranges, columns, matrix, own_matrix, near, far, table)
    near, far, offsets = gather_rows(middle(degree, inverse, terms), [])
    table = near_table(offsets, near, block_rows)
    terms, (notes,) = products(offsets, ranges, columns, matrix, own_matrix, near, far, table)
    devices = float(groups * ranks)
    rows, grams = collect(devices, total, degree, row_gram(near, far), notes, terms)
    flip = 1 if ranks == 8 else 0
    gram, first = add_columns(total, [grams] + [swap_both(grams, flip, m) for m in reversed(ranges)])
    inverse = first_factor(first)
    return finish(total, block_rows, rows, inverse, add_rows(gram, [inverse]))


def solution(mesh):
    return jax.shard_map(
        body,
        mesh=mesh,
        in_specs=(
            P(None, "rows", "cols", None, None),
            P(None, "rows", "cols", None),
            P(None, "rows", "cols"),
            P("cols", "rows", None),
            P("cols", "rows", None),
        ),
        out_specs=P("cols", "rows", None),
        check_vma=False,
    )
```

```python
import functools

import jax
import jax.numpy as jnp
from jax import lax
from jax.experimental import pallas as pl
from jax.experimental.pallas import tpu as pltpu
from jax.sharding import PartitionSpec as P

BF16 = jnp.bfloat16
F32 = jnp.float32
HIGHEST = lax.Precision.HIGHEST
MIB = 1024 * 1024


def params(limit=48 * MIB):
    return pltpu.CompilerParams(vmem_limit_bytes=limit)


def vmem():
    return pl.BlockSpec(memory_space=pltpu.VMEM)


def hbm():
    return pl.BlockSpec(memory_space=pltpu.HBM)


def smem():
    return pl.BlockSpec(memory_space=pltpu.SMEM)


def shaped(shape, dtype):
    return jax.ShapeDtypeStruct(shape, dtype)


def iota(shape, dim):
    return lax.broadcasted_iota(jnp.int32, shape, dim)


def call(kernel, name, ins, outs, operands, scratch=(), limit=48 * MIB, **kwargs):
    return pl.pallas_call(
        kernel,
        out_shape=outs,
        in_specs=ins,
        out_specs=jax.tree.map(lambda _: vmem(), outs),
        scratch_shapes=list(scratch),
        compiler_params=params(limit),
        name=name,
        **kwargs,
    )(*operands)


def start_kernel(panel_hbm, inv_hbm, scaled_ref, degree_ref, panel_ref, inv_ref, scratch, sems):
    block_rows, block_size = inv_ref.shape[1], inv_ref.shape[2]
    half = block_size // 2
    copies = [
        pltpu.make_async_copy(inv_hbm, inv_ref, sems.at[0]),
        pltpu.make_async_copy(panel_hbm, panel_ref, sems.at[1]),
    ]
    for copy in copies:
        copy.start()
    copies[0].wait()
    pair = iota((half, block_size), 1) // 2 == iota((half, block_size), 0)
    spread = (iota((block_size, 128), 0) % 2 == iota((block_size, 128), 1) // 64).astype(F32)
    rows = [
        jnp.where(pair, jnp.broadcast_to(inv_ref[0, i : i + 1, :], (half, block_size)), 0.0)
        for i in range(block_rows)
    ]
    degree_ref[...] = jnp.dot(
        jnp.concatenate(rows, axis=0), spread, precision=HIGHEST, preferred_element_type=F32
    )
    copies[1].wait()
    for t in range(half):
        scratch[t * block_rows : (t + 1) * block_rows, :] = panel_ref[0, :, t * 128 : (t + 1) * 128]
    for i in range(block_rows):
        where = slice(i * half, (i + 1) * half)
        part = scratch[pl.ds(i, half, stride=block_rows), :] * degree_ref[where, :]
        scaled_ref[where, :] = part.astype(BF16)


def start(panel, inv_degree):
    block_rows, block_size = inv_degree.shape[1:]
    shape = (block_rows * block_size // 2, 128)
    return call(
        start_kernel,
        "start",
        [hbm(), hbm()],
        (shaped(shape, BF16), shaped(shape, F32)),
        (panel, inv_degree),
        [
            pltpu.VMEM(panel.shape, F32),
            pltpu.VMEM(inv_degree.shape, F32),
            pltpu.VMEM(shape, F32),
            pltpu.SemaphoreType.DMA((2,)),
        ],
    )


def prep_kernel(
    ranges, affinity_hbm, inv_hbm, out_ref, inverse_ref, affinity_ref, inv_ref, scratch, sems, inv_sem
):
    count, block_rows, _, slots, flat = affinity_ref.shape
    half = flat // 128
    own = lax.axis_index("cols")
    copies = [
        pltpu.make_async_copy(affinity_hbm.at[m ^ own], affinity_ref.at[place], sems.at[place])
        for place, m in enumerate(ranges)
    ]
    inv_copy = pltpu.make_async_copy(inv_hbm, inv_ref, inv_sem)
    inv_copy.start()
    for copy in copies:
        copy.start()
    source, target = iota((256, 256), 0), iota((256, 256), 1)
    moved = (source // 64 % 2) * 128 + (source // 128) * 64 + (source % 2) * 32 + source % 64 // 2
    permute = (moved == target).astype(BF16)
    inv_copy.wait()
    inverse = 1.0 / inv_ref[0]
    high = inverse.astype(BF16).astype(F32)
    inverse_ref[...] = jnp.concatenate([high, inverse - high], axis=1)
    for m in range(count):
        copies[m].wait()
        for i in range(block_rows):
            block = affinity_ref[m, i, 0].astype(F32)
            for t in range(half):
                scratch[i % 2, t * slots : (t + 1) * slots, :] = block[:, t * 128 : (t + 1) * 128]
            parts = [
                scratch[i % 2, pl.ds(s, half, stride=slots), :].astype(BF16) for s in range(slots)
            ]
            pairs = [jnp.concatenate(parts[s : s + 2], axis=1) for s in range(0, slots, 2)]
            moved_pairs = jnp.dot(
                jnp.concatenate(pairs, axis=0), permute, preferred_element_type=F32
            ).astype(BF16)
            for s in range(slots // 2):
                piece = moved_pairs[s * half : (s + 1) * half]
                out_ref[m, i, :half, s * 128 : (s + 1) * 128] = piece[:, :128]
                out_ref[m, i, half:, s * 128 : (s + 1) * 128] = piece[:, 128:]


def prep(ranges, affinity, inv_degree):
    _, block_rows, _, slots, flat = affinity.shape
    count = len(ranges)
    return call(
        functools.partial(prep_kernel, ranges),
        "prep",
        [hbm(), hbm()],
        (shaped((count, block_rows, 64, slots * 64), BF16), shaped((block_rows, 128), F32)),
        (affinity, inv_degree),
        [
            pltpu.VMEM((count,) + affinity.shape[1:], BF16),
            pltpu.VMEM(inv_degree.shape, F32),
            pltpu.VMEM((2, flat // 128 * slots, 128), F32),
            pltpu.SemaphoreType.DMA((count,)),
            pltpu.SemaphoreType.DMA,
        ],
    )


def stack_kernel(count, *refs):
    for index in range(count):
        refs[-1][index] = refs[index][...]


def stack(pieces, after):
    return call(
        functools.partial(stack_kernel, len(pieces)),
        "stack",
        [vmem()] * (len(pieces) + len(after)),
        shaped((len(pieces),) + pieces[0].shape, BF16),
        (*pieces, *after),
    )


def fill_table(pieces_ref, offsets, table):
    block_rows = (table.shape[0] - 1) // (2 * len(offsets))
    low = iota((32, 128), 1) < 64
    for index, offset in enumerate(offsets):
        base = (lax.axis_index("rows") ^ offset) * block_rows
        for i in range(block_rows):
            block = pieces_ref[index, i * 32 : (i + 1) * 32, :]
            turned = jnp.concatenate([block[:, 64:], block[:, :64]], axis=1)
            table[base + i, :32] = jnp.where(low, block, turned)
            table[base + i, 32:] = jnp.where(low, turned, block)


def near_kernel(offsets, near_ref, table):
    table[table.shape[0] - 1] = jnp.zeros(table.shape[1:], BF16)
    fill_table(near_ref, offsets, table)


def near_table(offsets, near, block_rows):
    count = near.shape[0]
    return call(
        functools.partial(near_kernel, offsets[:count]),
        "near",
        [vmem()],
        shaped((2 * count * block_rows + 1, 64, 128), BF16),
        (near,),
    )


def one_product(group, columns, matrix, table, out_ref):
    block_rows, slots = columns.shape[1], columns.shape[3]
    low = iota((32, 128), 1) < 64
    for i in range(block_rows):
        picked = [table[columns[group, i, 0, s]] for s in range(slots)]
        result = jnp.dot(matrix[i], jnp.concatenate(picked, axis=0), preferred_element_type=F32)
        out_ref[i * 32 : (i + 1) * 32, :] = jnp.where(low, result[:32], result[32:]).astype(BF16)


def largest_notes(notes):
    largest = notes[0].astype(F32)
    for note in notes[1:]:
        largest = jnp.maximum(largest, note.astype(F32))
    return largest


def others_kernel(offsets, ranges, columns_any, matrix_ref, far_ref, near_ref, old_table, table, *refs):
    del old_table
    *outs, columns, sem = refs
    copy = pltpu.make_async_copy(columns_any, columns, sem)
    copy.start()
    fill_table(far_ref, offsets, table)
    terms, first = outs[: len(ranges)], matrix_ref.shape[1] * 32
    if len(outs) > len(ranges):
        notes = largest_notes(
            [ref[index, first:] for ref in (near_ref, far_ref) for index in range(len(offsets))]
        ).astype(BF16)
        for ref in outs[len(ranges) :]:
            ref[...] = notes
        for term in terms:
            term[first:, :] = notes
    copy.wait()
    for place, m in enumerate(ranges):
        group = m ^ lax.axis_index("cols")
        one_product(group, columns, matrix_ref.at[place], table, terms[place])


def own_kernel(columns, matrix_ref, table, out_ref):
    one_product(lax.axis_index("cols"), columns, matrix_ref.at[0], table, out_ref)


def products(offsets, ranges, columns, matrix, own_matrix, near, far, table):
    block_rows, count = matrix.shape[1], near.shape[0]
    extra = near.shape[1] > block_rows * 32
    rows = block_rows * 32
    outs = [shaped(table.shape, BF16)] + [shaped((rows + 16 * extra, 128), BF16)] * len(ranges)
    if extra:
        outs.append(shaped((16, 128), BF16))
    table, *outs = call(
        functools.partial(others_kernel, offsets[count:], ranges),
        "others",
        [pl.BlockSpec(memory_space=pl.ANY)] + [vmem()] * 4,
        outs,
        (columns, matrix, far, near, table),
        [pltpu.SMEM(columns.shape, jnp.int32), pltpu.SemaphoreType.DMA],
        input_output_aliases={4: 0},
    )
    terms = [swap(term, "cols", m) for m, term in zip(ranges, outs)]
    own = call(
        own_kernel,
        "own",
        [smem(), vmem(), vmem()],
        shaped((rows, 128), BF16),
        (columns, own_matrix, table),
    )
    return [own] + terms, outs[len(ranges) :]


def add_terms(terms, rows):
    summed = terms[0][:rows].astype(F32)
    for term in terms[1:]:
        summed = summed + term[:rows].astype(F32)
    return summed


def folded(both):
    gram = both[:64, :64] + both[64:, 64:]
    return jnp.concatenate([gram[:32], gram[32:]], axis=1)


def local_gram(rows):
    both = lax.dot_general(
        rows, rows, (((0,), (0,)), ((), ())), precision=HIGHEST, preferred_element_type=F32
    )
    return folded(both)


def middle_kernel(degree_ref, inverse_ref, *refs):
    terms, out_ref = refs[:-1], refs[-1]
    count = degree_ref.shape[0]
    degree = degree_ref[...]
    rows = add_terms(terms, count) * degree
    out_ref[:count] = (rows * degree).astype(BF16)
    squares = jnp.sum(rows * rows, axis=(0, 1), keepdims=True)
    out_ref[count:] = jnp.concatenate(
        [inverse_ref[...], jnp.broadcast_to(squares, (8, 128))], axis=0
    ).astype(BF16)


def middle(degree, inverse, terms):
    return call(
        middle_kernel,
        "middle",
        [vmem()] * (2 + len(terms)),
        shaped((degree.shape[0] + 16, 128), BF16),
        (degree, inverse, *terms),
    )


def row_gram_kernel(near_ref, far_ref, gram_ref, rows):
    lane = iota((32, 128), 1)
    pair = lane % 64 // 2 == iota((32, 128), 0)
    spread = (iota((128, 128), 0) % 2 == iota((128, 128), 1) // 64).astype(BF16)
    count = near_ref.shape[1] - 16
    size = near_ref.shape[0]
    for index in range(2 * size):
        ref = (near_ref, far_ref)[index // size]
        notes = ref[index % size, count:].astype(F32)
        masked = [
            jnp.where(pair, jnp.broadcast_to(notes[i : i + 1], (32, 128)), 0.0).astype(BF16)
            for i in range(count // 32)
        ]
        inverse = jnp.dot(jnp.concatenate(masked, axis=0), spread, preferred_element_type=F32)
        block = ref[index % size, :count].astype(F32) * inverse
        rows[index * count : (index + 1) * count, :] = block.astype(BF16)
    both = lax.dot_general(
        rows[...], rows[...], (((0,), (0,)), ((), ())), preferred_element_type=F32
    )
    gram_ref[...] = folded(both)


def row_gram(near, far):
    count = 2 * near.shape[0] * (near.shape[1] - 16)
    return call(
        row_gram_kernel,
        "row_gram",
        [vmem(), vmem()],
        shaped((32, 128), F32),
        (near, far),
        [pltpu.VMEM((count, 128), BF16)],
    )


def collect_kernel(devices, total, degree_ref, first_ref, notes_ref, *refs):
    terms, (rows_ref, grams_ref) = refs[:-2], refs[-2:]
    count = degree_ref.shape[0]
    largest = largest_notes([notes_ref[...]] + [term[count:] for term in terms[1:]])
    scale = lax.rsqrt(largest[8:9] * (devices / total))
    rows = add_terms(terms, count) * degree_ref[...] * scale
    rows_ref[...] = rows
    grams_ref[32:] = first_ref[...] * (scale * scale)
    grams_ref[:32] = local_gram(rows)


def collect(devices, total, degree, first, notes, terms):
    return call(
        functools.partial(collect_kernel, devices, total),
        "collect",
        [vmem()] * (3 + len(terms)),
        (shaped(degree.shape, F32), shaped((64, 128), F32)),
        (degree, first, notes, *terms),
    )


def lower_solve(gram, right):
    work = jnp.concatenate([gram, right], axis=1)
    blocks = gram.shape[0] // 8
    rows = [work[8 * i : 8 * i + 8] for i in range(blocks)]
    at = iota((8, 128), 0)

    def columns(first, column):
        return [
            jnp.broadcast_to(rows[i][:, column : column + 1], (8, 128))
            for i in range(first, blocks)
        ]

    def spread(block, row):
        return jnp.broadcast_to(block[row : row + 1], (8, 128))

    current = [columns(0, q) for q in range(8)]
    for b in range(blocks):
        count = blocks - b
        later = []
        if count > 1:
            later = [columns(b + 1, 8 * (b + 1) + q) for q in range(8)]
        for q in range(8):
            root = lax.rsqrt(spread(current[q][0], q))
            inverse = root * root
            raw = spread(rows[b], q)
            scaled = raw * inverse
            for p in range(q + 1, 8):
                weight = spread(current[q][0], p) * inverse
                current[p] = [x - y * weight for x, y in zip(current[p], current[q])]
            below = rows[b] - current[q][0] * scaled
            rows[b] = jnp.where(at == q, raw * root, jnp.where(at > q, below, rows[b]))
            for i in range(1, count):
                rows[b + i] = rows[b + i] - current[q][i] * scaled
            for p in range(len(later)):
                weight = spread(current[q][1], p) * inverse
                later[p] = [x - y * weight for x, y in zip(later[p], current[q][1:])]
        current = later
    return jnp.concatenate(rows, axis=0)[:, 64:]


def unpacked(packed):
    return jnp.concatenate([packed[:, :64], packed[:, 64:]], axis=0)


def add_columns_kernel(total, *refs):
    parts, (gram_ref, first_ref) = refs[:-2], refs[-2:]
    summed = parts[0][...]
    for part in parts[1:]:
        summed = summed + part[...]
    gram_ref[...] = summed[:32]
    first_ref[...] = summed[32:] / total


def add_columns(total, parts):
    return call(
        functools.partial(add_columns_kernel, total),
        "add_columns",
        [vmem()] * len(parts),
        (shaped((32, 128), F32), shaped((32, 128), F32)),
        parts,
    )


def add_parts_kernel(count, *refs):
    summed = refs[0][...]
    for part in refs[1:count]:
        summed = summed + part[...]
    refs[-1][...] = summed


def add_parts(parts, after):
    return call(
        functools.partial(add_parts_kernel, len(parts)),
        "add_parts",
        [vmem()] * (len(parts) + len(after)),
        shaped(parts[0].shape, F32),
        (*parts, *after),
    )


def first_factor_kernel(gram_ref, out_ref):
    unit = (iota((64, 64), 0) == iota((64, 64), 1)).astype(F32)
    out_ref[...] = lower_solve(unpacked(gram_ref[...]), unit)


def first_factor(gram):
    return call(first_factor_kernel, "first_factor", [vmem()], shaped((64, 64), F32), (gram,))


def dot_turned(left, right):
    return lax.dot_general(
        left, right, (((1,), (1,)), ((), ())), precision=HIGHEST, preferred_element_type=F32
    )


def finish_kernel(total, rows_ref, inverse_ref, *refs):
    out_ref, scratch = refs[-2:]
    block_rows = out_ref.shape[1]
    packed = refs[0][...]
    for part in refs[1:-2]:
        packed = packed + part[...]
    first = inverse_ref[...]
    gram = dot_turned(
        jnp.dot(first, unpacked(packed), precision=HIGHEST, preferred_element_type=F32), first
    )
    inverse = lower_solve(gram / total, first)
    zero = jnp.zeros_like(inverse)
    both = jnp.concatenate(
        [jnp.concatenate([inverse, zero], axis=1), jnp.concatenate([zero, inverse], axis=1)], axis=0
    )
    current = dot_turned(rows_ref[...], both)
    for i in range(block_rows):
        scratch[pl.ds(i, 32, stride=block_rows), :] = current[i * 32 : (i + 1) * 32]
    for t in range(32):
        out_ref[0, :, t * 128 : (t + 1) * 128] = scratch[t * block_rows : (t + 1) * block_rows, :]


def finish(total, block_rows, rows, inverse, grams):
    return call(
        functools.partial(finish_kernel, total),
        "finish",
        [vmem()] * (2 + len(grams)),
        shaped((1, block_rows, 32 * 128), F32),
        (rows, inverse, *grams),
        [pltpu.VMEM(rows.shape, F32)],
    )


def swap(value, axis, mask):
    size = lax.axis_size(axis)
    return lax.ppermute(value, axis, [(index, index ^ mask) for index in range(size)])


def swap_both(value, row_mask, column_mask):
    rows, columns = lax.axis_size("rows"), lax.axis_size("cols")
    pairs = [
        (row * columns + column, (row ^ row_mask) * columns + (column ^ column_mask))
        for row in range(rows)
        for column in range(columns)
    ]
    return lax.ppermute(value, ("rows", "cols"), pairs)


def stages(size):
    if size == 8:
        return [[7, 5, 3], [1]]
    bits, bit = [], 1
    while bit < size:
        bits.append([bit])
        bit *= 2
    return bits


def gather_rows(message, after):
    plan = stages(lax.axis_size("rows"))
    held, offsets = [message], [0]
    for masks in plan[:-1]:
        held = held + [swap(piece, "rows", mask) for mask in masks for piece in held]
        offsets = offsets + [mask ^ offset for mask in masks for offset in offsets]
    near = stack(held, after)
    (last,) = plan[-1]
    offsets = offsets + [last ^ offset for offset in offsets]
    return near, swap(near, "rows", last), offsets


def add_rows(gram, after):
    *plan, (last,) = stages(lax.axis_size("rows"))
    for masks in plan:
        gram = add_parts([gram] + [swap(gram, "rows", mask) for mask in masks], after)
    return [gram, swap(gram, "rows", last)]


def body(affinity, block_columns, block_counts, inv_degree, panel):
    block_rows, block_size = inv_degree.shape[1:]
    groups, _, _, slots, _ = affinity.shape
    ranks = lax.axis_size("rows")
    total = float(groups * ranks * block_rows * block_size)
    blocks = ranks * block_rows
    live = iota(block_columns.shape, 3) < block_counts[..., None]
    columns = jnp.where(live, jnp.clip(block_columns, 0, blocks - 1), blocks)
    panel, inv_degree, affinity = (
        pltpu.with_memory_space_constraint(value, pltpu.HBM) for value in (panel, inv_degree, affinity)
    )
    ranges = list(range(groups - 1, 0, -1))

    scaled, degree = start(panel, inv_degree)
    matrix, inverse = prep(ranges, affinity, inv_degree)
    own_matrix, _ = prep([0], affinity, inv_degree)
    near, far, offsets = gather_rows(scaled, [inverse])
    table = near_table(offsets, near, block_rows)
    terms, _ = products(offsets, ranges, columns, matrix, own_matrix, near, far, table)
    near, far, offsets = gather_rows(middle(degree, inverse, terms), [])
    table = near_table(offsets, near, block_rows)
    terms, (notes,) = products(offsets, ranges, columns, matrix, own_matrix, near, far, table)
    devices = float(groups * ranks)
    rows, grams = collect(devices, total, degree, row_gram(near, far), notes, terms)
    flip = 1 if ranks == 8 else 0
    gram, first = add_columns(total, [grams] + [swap_both(grams, flip, m) for m in ranges])
    inverse = first_factor(first)
    return finish(total, block_rows, rows, inverse, add_rows(gram, [inverse]))


def solution(mesh):
    return jax.shard_map(
        body,
        mesh=mesh,
        in_specs=(
            P(None, "rows", "cols", None, None),
            P(None, "rows", "cols", None),
            P(None, "rows", "cols"),
            P("cols", "rows", None),
            P("cols", "rows", None),
        ),
        out_specs=P("cols", "rows", None),
        check_vma=False,
    )
```

```python
import functools

import jax
import jax.numpy as jnp
from jax import lax
from jax.experimental import pallas as pl
from jax.experimental.pallas import tpu as pltpu
from jax.sharding import PartitionSpec as P

BF16 = jnp.bfloat16
F32 = jnp.float32
HIGHEST = lax.Precision.HIGHEST
MIB = 1024 * 1024


def params(limit=48 * MIB):
    return pltpu.CompilerParams(vmem_limit_bytes=limit)


def vmem():
    return pl.BlockSpec(memory_space=pltpu.VMEM)


def hbm():
    return pl.BlockSpec(memory_space=pltpu.HBM)


def smem():
    return pl.BlockSpec(memory_space=pltpu.SMEM)


def shaped(shape, dtype):
    return jax.ShapeDtypeStruct(shape, dtype)


def iota(shape, dim):
    return lax.broadcasted_iota(jnp.int32, shape, dim)


def call(kernel, name, ins, outs, operands, scratch=(), limit=48 * MIB, **kwargs):
    return pl.pallas_call(
        kernel,
        out_shape=outs,
        in_specs=ins,
        out_specs=jax.tree.map(lambda _: vmem(), outs),
        scratch_shapes=list(scratch),
        compiler_params=params(limit),
        name=name,
        **kwargs,
    )(*operands)


def start_kernel(panel_hbm, inv_hbm, scaled_ref, degree_ref, panel_ref, inv_ref, scratch, sems):
    block_rows, block_size = inv_ref.shape[1], inv_ref.shape[2]
    half = block_size // 2
    copies = [
        pltpu.make_async_copy(inv_hbm, inv_ref, sems.at[0]),
        pltpu.make_async_copy(panel_hbm, panel_ref, sems.at[1]),
    ]
    for copy in copies:
        copy.start()
    copies[0].wait()
    pair = iota((half, block_size), 1) // 2 == iota((half, block_size), 0)
    spread = (iota((block_size, 128), 0) % 2 == iota((block_size, 128), 1) // 64).astype(F32)
    rows = [
        jnp.where(pair, jnp.broadcast_to(inv_ref[0, i : i + 1, :], (half, block_size)), 0.0)
        for i in range(block_rows)
    ]
    degree_ref[...] = jnp.dot(
        jnp.concatenate(rows, axis=0), spread, precision=HIGHEST, preferred_element_type=F32
    )
    copies[1].wait()
    for t in range(half):
        scratch[t * block_rows : (t + 1) * block_rows, :] = panel_ref[0, :, t * 128 : (t + 1) * 128]
    for i in range(block_rows):
        where = slice(i * half, (i + 1) * half)
        part = scratch[pl.ds(i, half, stride=block_rows), :] * degree_ref[where, :]
        scaled_ref[where, :] = part.astype(BF16)


def start(panel, inv_degree):
    block_rows, block_size = inv_degree.shape[1:]
    shape = (block_rows * block_size // 2, 128)
    return call(
        start_kernel,
        "start",
        [hbm(), hbm()],
        (shaped(shape, BF16), shaped(shape, F32)),
        (panel, inv_degree),
        [
            pltpu.VMEM(panel.shape, F32),
            pltpu.VMEM(inv_degree.shape, F32),
            pltpu.VMEM(shape, F32),
            pltpu.SemaphoreType.DMA((2,)),
        ],
    )


def prep_kernel(
    ranges, affinity_hbm, inv_hbm, out_ref, inverse_ref, affinity_ref, inv_ref, scratch, sems, inv_sem
):
    count, block_rows, _, slots, flat = affinity_ref.shape
    half = flat // 128
    own = lax.axis_index("cols")
    copies = [
        pltpu.make_async_copy(affinity_hbm.at[m ^ own], affinity_ref.at[place], sems.at[place])
        for place, m in enumerate(ranges)
    ]
    inv_copy = pltpu.make_async_copy(inv_hbm, inv_ref, inv_sem)
    inv_copy.start()
    for copy in copies:
        copy.start()
    source, target = iota((256, 256), 0), iota((256, 256), 1)
    moved = (source // 64 % 2) * 128 + (source // 128) * 64 + (source % 2) * 32 + source % 64 // 2
    permute = (moved == target).astype(BF16)
    inv_copy.wait()
    inverse = 1.0 / inv_ref[0]
    high = inverse.astype(BF16).astype(F32)
    inverse_ref[...] = jnp.concatenate([high, inverse - high], axis=1)
    for m in range(count):
        copies[m].wait()
        for i in range(block_rows):
            block = affinity_ref[m, i, 0].astype(F32)
            for t in range(half):
                scratch[i % 2, t * slots : (t + 1) * slots, :] = block[:, t * 128 : (t + 1) * 128]
            parts = [
                scratch[i % 2, pl.ds(s, half, stride=slots), :].astype(BF16) for s in range(slots)
            ]
            pairs = [jnp.concatenate(parts[s : s + 2], axis=1) for s in range(0, slots, 2)]
            moved_pairs = jnp.dot(
                jnp.concatenate(pairs, axis=0), permute, preferred_element_type=F32
            ).astype(BF16)
            for s in range(slots // 2):
                piece = moved_pairs[s * half : (s + 1) * half]
                out_ref[m, i, :half, s * 128 : (s + 1) * 128] = piece[:, :128]
                out_ref[m, i, half:, s * 128 : (s + 1) * 128] = piece[:, 128:]


def prep(ranges, affinity, inv_degree):
    _, block_rows, _, slots, flat = affinity.shape
    count = len(ranges)
    return call(
        functools.partial(prep_kernel, ranges),
        "prep",
        [hbm(), hbm()],
        (shaped((count, block_rows, 64, slots * 64), BF16), shaped((block_rows, 128), F32)),
        (affinity, inv_degree),
        [
            pltpu.VMEM((count,) + affinity.shape[1:], BF16),
            pltpu.VMEM(inv_degree.shape, F32),
            pltpu.VMEM((2, flat // 128 * slots, 128), F32),
            pltpu.SemaphoreType.DMA((count,)),
            pltpu.SemaphoreType.DMA,
        ],
    )


def stack_kernel(count, *refs):
    for index in range(count):
        refs[-1][index] = refs[index][...]


def stack(pieces, after):
    return call(
        functools.partial(stack_kernel, len(pieces)),
        "stack",
        [vmem()] * (len(pieces) + len(after)),
        shaped((len(pieces),) + pieces[0].shape, BF16),
        (*pieces, *after),
    )


def fill_table(pieces_ref, offsets, table):
    block_rows = (table.shape[0] - 1) // (2 * len(offsets))
    low = iota((32, 128), 1) < 64
    for index, offset in enumerate(offsets):
        base = (lax.axis_index("rows") ^ offset) * block_rows
        for i in range(block_rows):
            block = pieces_ref[index, i * 32 : (i + 1) * 32, :]
            turned = jnp.concatenate([block[:, 64:], block[:, :64]], axis=1)
            table[base + i, :32] = jnp.where(low, block, turned)
            table[base + i, 32:] = jnp.where(low, turned, block)


def near_kernel(offsets, near_ref, table):
    table[table.shape[0] - 1] = jnp.zeros(table.shape[1:], BF16)
    fill_table(near_ref, offsets, table)


def near_table(offsets, near, block_rows):
    count = near.shape[0]
    return call(
        functools.partial(near_kernel, offsets[:count]),
        "near",
        [vmem()],
        shaped((2 * count * block_rows + 1, 64, 128), BF16),
        (near,),
    )


def one_product(group, columns, matrix, table, out_ref):
    block_rows, slots = matrix.shape[0], matrix.shape[2] // 64
    first = group * (block_rows * slots)
    low = iota((32, 128), 1) < 64
    for i in range(block_rows):
        picked = [table[columns[first + i * slots + s]] for s in range(slots)]
        result = jnp.dot(matrix[i], jnp.concatenate(picked, axis=0), preferred_element_type=F32)
        out_ref[i * 32 : (i + 1) * 32, :] = jnp.where(low, result[:32], result[32:]).astype(BF16)


def largest_notes(notes):
    largest = notes[0].astype(F32)
    for note in notes[1:]:
        largest = jnp.maximum(largest, note.astype(F32))
    return largest


def others_kernel(offsets, ranges, columns_any, matrix_ref, far_ref, near_ref, old_table, table, *refs):
    del old_table
    *outs, columns, sem = refs
    copy = pltpu.make_async_copy(columns_any, columns, sem)
    copy.start()
    fill_table(far_ref, offsets, table)
    terms, first = outs[: len(ranges)], matrix_ref.shape[1] * 32
    if len(outs) > len(ranges):
        notes = largest_notes(
            [ref[index, first:] for ref in (near_ref, far_ref) for index in range(len(offsets))]
        ).astype(BF16)
        for ref in outs[len(ranges) :]:
            ref[...] = notes
        for term in terms:
            term[first:, :] = notes
    copy.wait()
    for place, m in enumerate(ranges):
        group = m ^ lax.axis_index("cols")
        one_product(group, columns, matrix_ref.at[place], table, terms[place])


def own_kernel(columns, matrix_ref, table, out_ref):
    one_product(lax.axis_index("cols"), columns, matrix_ref.at[0], table, out_ref)


def products(offsets, ranges, columns, matrix, own_matrix, near, far, table):
    block_rows, count = matrix.shape[1], near.shape[0]
    extra = near.shape[1] > block_rows * 32
    rows = block_rows * 32
    outs = [shaped(table.shape, BF16)] + [shaped((rows + 16 * extra, 128), BF16)] * len(ranges)
    if extra:
        outs.append(shaped((16, 128), BF16))
    table, *outs = call(
        functools.partial(others_kernel, offsets[count:], ranges),
        "others",
        [pl.BlockSpec(memory_space=pl.ANY)] + [vmem()] * 4,
        outs,
        (columns, matrix, far, near, table),
        [pltpu.SMEM(columns.shape, jnp.int32), pltpu.SemaphoreType.DMA],
        input_output_aliases={4: 0},
    )
    terms = [swap(term, "cols", m) for m, term in zip(ranges, outs)]
    own = call(
        own_kernel,
        "own",
        [smem(), vmem(), vmem()],
        shaped((rows, 128), BF16),
        (columns, own_matrix, table),
    )
    return [own] + terms, outs[len(ranges) :]


def add_terms(terms, rows):
    summed = terms[0][:rows].astype(F32)
    for term in terms[1:]:
        summed = summed + term[:rows].astype(F32)
    return summed


def folded(both):
    gram = both[:64, :64] + both[64:, 64:]
    return jnp.concatenate([gram[:32], gram[32:]], axis=1)


def local_gram(rows):
    both = lax.dot_general(
        rows, rows, (((0,), (0,)), ((), ())), precision=HIGHEST, preferred_element_type=F32
    )
    return folded(both)


def middle_kernel(degree_ref, inverse_ref, *refs):
    terms, out_ref = refs[:-1], refs[-1]
    count = degree_ref.shape[0]
    degree = degree_ref[...]
    rows = add_terms(terms, count) * degree
    out_ref[:count] = (rows * degree).astype(BF16)
    squares = jnp.sum(rows * rows, axis=(0, 1), keepdims=True)
    out_ref[count:] = jnp.concatenate(
        [inverse_ref[...], jnp.broadcast_to(squares, (8, 128))], axis=0
    ).astype(BF16)


def middle(degree, inverse, terms):
    return call(
        middle_kernel,
        "middle",
        [vmem()] * (2 + len(terms)),
        shaped((degree.shape[0] + 16, 128), BF16),
        (degree, inverse, *terms),
    )


def row_gram_kernel(near_ref, far_ref, gram_ref, rows):
    lane = iota((32, 128), 1)
    pair = lane % 64 // 2 == iota((32, 128), 0)
    spread = (iota((128, 128), 0) % 2 == iota((128, 128), 1) // 64).astype(BF16)
    count = near_ref.shape[1] - 16
    size = near_ref.shape[0]
    for index in range(2 * size):
        ref = (near_ref, far_ref)[index // size]
        notes = ref[index % size, count:].astype(F32)
        masked = [
            jnp.where(pair, jnp.broadcast_to(notes[i : i + 1], (32, 128)), 0.0).astype(BF16)
            for i in range(count // 32)
        ]
        inverse = jnp.dot(jnp.concatenate(masked, axis=0), spread, preferred_element_type=F32)
        block = ref[index % size, :count].astype(F32) * inverse
        rows[index * count : (index + 1) * count, :] = block.astype(BF16)
    both = lax.dot_general(
        rows[...], rows[...], (((0,), (0,)), ((), ())), preferred_element_type=F32
    )
    gram_ref[...] = folded(both)


def row_gram(near, far):
    count = 2 * near.shape[0] * (near.shape[1] - 16)
    return call(
        row_gram_kernel,
        "row_gram",
        [vmem(), vmem()],
        shaped((32, 128), F32),
        (near, far),
        [pltpu.VMEM((count, 128), BF16)],
    )


def collect_kernel(devices, total, degree_ref, first_ref, notes_ref, *refs):
    terms, (rows_ref, grams_ref) = refs[:-2], refs[-2:]
    count = degree_ref.shape[0]
    largest = largest_notes([notes_ref[...]] + [term[count:] for term in terms[1:]])
    scale = lax.rsqrt(largest[8:9] * (devices / total))
    rows = add_terms(terms, count) * degree_ref[...] * scale
    rows_ref[...] = rows
    grams_ref[32:] = first_ref[...] * (scale * scale)
    grams_ref[:32] = local_gram(rows)


def collect(devices, total, degree, first, notes, terms):
    return call(
        functools.partial(collect_kernel, devices, total),
        "collect",
        [vmem()] * (3 + len(terms)),
        (shaped(degree.shape, F32), shaped((64, 128), F32)),
        (degree, first, notes, *terms),
    )


def lower_solve(gram, right):
    work = jnp.concatenate([gram, right], axis=1)
    blocks = gram.shape[0] // 8
    rows = [work[8 * i : 8 * i + 8] for i in range(blocks)]
    at = iota((8, 128), 0)

    def columns(first, column):
        return [
            jnp.broadcast_to(rows[i][:, column : column + 1], (8, 128))
            for i in range(first, blocks)
        ]

    def spread(block, row):
        return jnp.broadcast_to(block[row : row + 1], (8, 128))

    current = [columns(0, q) for q in range(8)]
    for b in range(blocks):
        count = blocks - b
        later = []
        if count > 1:
            later = [columns(b + 1, 8 * (b + 1) + q) for q in range(8)]
        for q in range(8):
            root = lax.rsqrt(spread(current[q][0], q))
            inverse = root * root
            raw = spread(rows[b], q)
            scaled = raw * inverse
            for p in range(q + 1, 8):
                weight = spread(current[q][0], p) * inverse
                current[p] = [x - y * weight for x, y in zip(current[p], current[q])]
            below = rows[b] - current[q][0] * scaled
            rows[b] = jnp.where(at == q, raw * root, jnp.where(at > q, below, rows[b]))
            for i in range(1, count):
                rows[b + i] = rows[b + i] - current[q][i] * scaled
            for p in range(len(later)):
                weight = spread(current[q][1], p) * inverse
                later[p] = [x - y * weight for x, y in zip(later[p], current[q][1:])]
        current = later
    return jnp.concatenate(rows, axis=0)[:, 64:]


def unpacked(packed):
    return jnp.concatenate([packed[:, :64], packed[:, 64:]], axis=0)


def add_columns_kernel(total, *refs):
    parts, (gram_ref, first_ref) = refs[:-2], refs[-2:]
    summed = parts[0][...]
    for part in parts[1:]:
        summed = summed + part[...]
    gram_ref[...] = summed[:32]
    first_ref[...] = summed[32:] / total


def add_columns(total, parts):
    return call(
        functools.partial(add_columns_kernel, total),
        "add_columns",
        [vmem()] * len(parts),
        (shaped((32, 128), F32), shaped((32, 128), F32)),
        parts,
    )


def add_parts_kernel(count, *refs):
    summed = refs[0][...]
    for part in refs[1:count]:
        summed = summed + part[...]
    refs[-1][...] = summed


def add_parts(parts, after):
    return call(
        functools.partial(add_parts_kernel, len(parts)),
        "add_parts",
        [vmem()] * (len(parts) + len(after)),
        shaped(parts[0].shape, F32),
        (*parts, *after),
    )


def first_factor_kernel(gram_ref, out_ref):
    unit = (iota((64, 64), 0) == iota((64, 64), 1)).astype(F32)
    out_ref[...] = lower_solve(unpacked(gram_ref[...]), unit)


def first_factor(gram):
    return call(first_factor_kernel, "first_factor", [vmem()], shaped((64, 64), F32), (gram,))


def dot_turned(left, right):
    return lax.dot_general(
        left, right, (((1,), (1,)), ((), ())), precision=HIGHEST, preferred_element_type=F32
    )


def finish_kernel(total, rows_ref, inverse_ref, *refs):
    out_ref, scratch = refs[-2:]
    block_rows = out_ref.shape[1]
    packed = refs[0][...]
    for part in refs[1:-2]:
        packed = packed + part[...]
    first = inverse_ref[...]
    gram = dot_turned(
        jnp.dot(first, unpacked(packed), precision=HIGHEST, preferred_element_type=F32), first
    )
    inverse = lower_solve(gram / total, first)
    zero = jnp.zeros_like(inverse)
    both = jnp.concatenate(
        [jnp.concatenate([inverse, zero], axis=1), jnp.concatenate([zero, inverse], axis=1)], axis=0
    )
    current = dot_turned(rows_ref[...], both)
    for i in range(block_rows):
        scratch[pl.ds(i, 32, stride=block_rows), :] = current[i * 32 : (i + 1) * 32]
    for t in range(32):
        out_ref[0, :, t * 128 : (t + 1) * 128] = scratch[t * block_rows : (t + 1) * block_rows, :]


def finish(total, block_rows, rows, inverse, grams):
    return call(
        functools.partial(finish_kernel, total),
        "finish",
        [vmem()] * (2 + len(grams)),
        shaped((1, block_rows, 32 * 128), F32),
        (rows, inverse, *grams),
        [pltpu.VMEM(rows.shape, F32)],
    )


def swap(value, axis, mask):
    size = lax.axis_size(axis)
    return lax.ppermute(value, axis, [(index, index ^ mask) for index in range(size)])


def swap_both(value, row_mask, column_mask):
    rows, columns = lax.axis_size("rows"), lax.axis_size("cols")
    pairs = [
        (row * columns + column, (row ^ row_mask) * columns + (column ^ column_mask))
        for row in range(rows)
        for column in range(columns)
    ]
    return lax.ppermute(value, ("rows", "cols"), pairs)


def stages(size):
    if size == 8:
        return [[7, 5, 3], [1]]
    bits, bit = [], 1
    while bit < size:
        bits.append([bit])
        bit *= 2
    return bits


def gather_rows(message, after):
    plan = stages(lax.axis_size("rows"))
    held, offsets = [message], [0]
    for masks in plan[:-1]:
        held = held + [swap(piece, "rows", mask) for mask in masks for piece in held]
        offsets = offsets + [mask ^ offset for mask in masks for offset in offsets]
    near = stack(held, after)
    (last,) = plan[-1]
    offsets = offsets + [last ^ offset for offset in offsets]
    return near, swap(near, "rows", last), offsets


def add_rows(gram, after):
    *plan, (last,) = stages(lax.axis_size("rows"))
    for masks in plan:
        gram = add_parts([gram] + [swap(gram, "rows", mask) for mask in masks], after)
    return [gram, swap(gram, "rows", last)]


def body(affinity, block_columns, block_counts, inv_degree, panel):
    block_rows, block_size = inv_degree.shape[1:]
    groups, _, _, slots, _ = affinity.shape
    ranks = lax.axis_size("rows")
    total = float(groups * ranks * block_rows * block_size)
    blocks = ranks * block_rows
    live = iota(block_columns.shape, 3) < block_counts[..., None]
    columns = jnp.where(live, jnp.clip(block_columns, 0, blocks - 1), blocks).reshape(-1)
    panel, inv_degree, affinity = (
        pltpu.with_memory_space_constraint(value, pltpu.HBM) for value in (panel, inv_degree, affinity)
    )
    ranges = list(range(groups - 1, 0, -1))

    scaled, degree = start(panel, inv_degree)
    matrix, inverse = prep(ranges, affinity, inv_degree)
    own_matrix, _ = prep([0], affinity, inv_degree)
    near, far, offsets = gather_rows(scaled, [inverse])
    table = near_table(offsets, near, block_rows)
    terms, _ = products(offsets, ranges, columns, matrix, own_matrix, near, far, table)
    near, far, offsets = gather_rows(middle(degree, inverse, terms), [])
    table = near_table(offsets, near, block_rows)
    terms, (notes,) = products(offsets, ranges, columns, matrix, own_matrix, near, far, table)
    devices = float(groups * ranks)
    rows, grams = collect(devices, total, degree, row_gram(near, far), notes, terms)
    flip = 1 if ranks == 8 else 0
    gram, first = add_columns(total, [grams] + [swap_both(grams, flip, m) for m in ranges])
    inverse = first_factor(first)
    return finish(total, block_rows, rows, inverse, add_rows(gram, [inverse]))


def solution(mesh):
    return jax.shard_map(
        body,
        mesh=mesh,
        in_specs=(
            P(None, "rows", "cols", None, None),
            P(None, "rows", "cols", None),
            P(None, "rows", "cols"),
            P("cols", "rows", None),
            P("cols", "rows", None),
        ),
        out_specs=P("cols", "rows", None),
        check_vma=False,
    )
```

```python
import functools

import jax
import jax.numpy as jnp
from jax import lax
from jax.experimental import pallas as pl
from jax.experimental.pallas import tpu as pltpu
from jax.sharding import PartitionSpec as P

BF16 = jnp.bfloat16
F32 = jnp.float32
HIGHEST = lax.Precision.HIGHEST
MIB = 1024 * 1024


def params(limit=48 * MIB):
    return pltpu.CompilerParams(vmem_limit_bytes=limit)


def vmem():
    return pl.BlockSpec(memory_space=pltpu.VMEM)


def hbm():
    return pl.BlockSpec(memory_space=pltpu.HBM)


def smem():
    return pl.BlockSpec(memory_space=pltpu.SMEM)


def shaped(shape, dtype):
    return jax.ShapeDtypeStruct(shape, dtype)


def iota(shape, dim):
    return lax.broadcasted_iota(jnp.int32, shape, dim)


def call(kernel, name, ins, outs, operands, scratch=(), limit=48 * MIB, **kwargs):
    return pl.pallas_call(
        kernel,
        out_shape=outs,
        in_specs=ins,
        out_specs=jax.tree.map(lambda _: vmem(), outs),
        scratch_shapes=list(scratch),
        compiler_params=params(limit),
        name=name,
        **kwargs,
    )(*operands)


def start_kernel(panel_hbm, inv_hbm, scaled_ref, degree_ref, panel_ref, inv_ref, scratch, sems):
    block_rows, block_size = inv_ref.shape[1], inv_ref.shape[2]
    half = block_size // 2
    copies = [
        pltpu.make_async_copy(inv_hbm, inv_ref, sems.at[0]),
        pltpu.make_async_copy(panel_hbm, panel_ref, sems.at[1]),
    ]
    for copy in copies:
        copy.start()
    copies[0].wait()
    pair = iota((half, block_size), 1) // 2 == iota((half, block_size), 0)
    spread = (iota((block_size, 128), 0) % 2 == iota((block_size, 128), 1) // 64).astype(F32)
    rows = [
        jnp.where(pair, jnp.broadcast_to(inv_ref[0, i : i + 1, :], (half, block_size)), 0.0)
        for i in range(block_rows)
    ]
    degree_ref[...] = jnp.dot(
        jnp.concatenate(rows, axis=0), spread, precision=HIGHEST, preferred_element_type=F32
    )
    copies[1].wait()
    for t in range(half):
        scratch[t * block_rows : (t + 1) * block_rows, :] = panel_ref[0, :, t * 128 : (t + 1) * 128]
    for i in range(block_rows):
        where = slice(i * half, (i + 1) * half)
        part = scratch[pl.ds(i, half, stride=block_rows), :] * degree_ref[where, :]
        scaled_ref[where, :] = part.astype(BF16)


def start(panel, inv_degree):
    block_rows, block_size = inv_degree.shape[1:]
    shape = (block_rows * block_size // 2, 128)
    return call(
        start_kernel,
        "start",
        [hbm(), hbm()],
        (shaped(shape, BF16), shaped(shape, F32)),
        (panel, inv_degree),
        [
            pltpu.VMEM(panel.shape, F32),
            pltpu.VMEM(inv_degree.shape, F32),
            pltpu.VMEM(shape, F32),
            pltpu.SemaphoreType.DMA((2,)),
        ],
    )


def prep_kernel(
    ranges, affinity_hbm, inv_hbm, out_ref, inverse_ref, affinity_ref, inv_ref, scratch, sems, inv_sem
):
    count, block_rows, _, slots, flat = affinity_ref.shape
    half = flat // 128
    own = lax.axis_index("cols")
    copies = [
        pltpu.make_async_copy(affinity_hbm.at[m ^ own], affinity_ref.at[place], sems.at[place])
        for place, m in enumerate(ranges)
    ]
    inv_copy = pltpu.make_async_copy(inv_hbm, inv_ref, inv_sem)
    inv_copy.start()
    for copy in copies:
        copy.start()
    source, target = iota((256, 256), 0), iota((256, 256), 1)
    moved = (source // 64 % 2) * 128 + (source // 128) * 64 + (source % 2) * 32 + source % 64 // 2
    permute = (moved == target).astype(BF16)
    inv_copy.wait()
    inverse = 1.0 / inv_ref[0]
    high = inverse.astype(BF16).astype(F32)
    inverse_ref[...] = jnp.concatenate([high, inverse - high], axis=1)
    for m in range(count):
        copies[m].wait()
        for i in range(block_rows):
            block = affinity_ref[m, i, 0].astype(F32)
            for t in range(half):
                scratch[i % 2, t * slots : (t + 1) * slots, :] = block[:, t * 128 : (t + 1) * 128]
            parts = [
                scratch[i % 2, pl.ds(s, half, stride=slots), :].astype(BF16) for s in range(slots)
            ]
            pairs = [jnp.concatenate(parts[s : s + 2], axis=1) for s in range(0, slots, 2)]
            moved_pairs = jnp.dot(
                jnp.concatenate(pairs, axis=0), permute, preferred_element_type=F32
            ).astype(BF16)
            for s in range(slots // 2):
                piece = moved_pairs[s * half : (s + 1) * half]
                out_ref[m, i, :half, s * 128 : (s + 1) * 128] = piece[:, :128]
                out_ref[m, i, half:, s * 128 : (s + 1) * 128] = piece[:, 128:]


def prep(ranges, affinity, inv_degree):
    _, block_rows, _, slots, flat = affinity.shape
    count = len(ranges)
    return call(
        functools.partial(prep_kernel, ranges),
        "prep",
        [hbm(), hbm()],
        (shaped((count, block_rows, 64, slots * 64), BF16), shaped((block_rows, 128), F32)),
        (affinity, inv_degree),
        [
            pltpu.VMEM((count,) + affinity.shape[1:], BF16),
            pltpu.VMEM(inv_degree.shape, F32),
            pltpu.VMEM((2, flat // 128 * slots, 128), F32),
            pltpu.SemaphoreType.DMA((count,)),
            pltpu.SemaphoreType.DMA,
        ],
    )


def stack_kernel(count, *refs):
    for index in range(count):
        refs[-1][index] = refs[index][...]


def stack(pieces, after):
    return call(
        functools.partial(stack_kernel, len(pieces)),
        "stack",
        [vmem()] * (len(pieces) + len(after)),
        shaped((len(pieces),) + pieces[0].shape, BF16),
        (*pieces, *after),
    )


def fill_table(stacks, offsets, table):
    block_rows = (table.shape[0] - 1) // (2 * len(offsets))
    low = iota((32, 128), 1) < 64
    pieces = [(ref, index) for ref in stacks for index in range(ref.shape[0])]
    for (ref, index), offset in zip(pieces, offsets):
        base = (lax.axis_index("rows") ^ offset) * block_rows
        for i in range(block_rows):
            block = ref[index, i * 32 : (i + 1) * 32, :]
            turned = jnp.concatenate([block[:, 64:], block[:, :64]], axis=1)
            table[base + i, :32] = jnp.where(low, block, turned)
            table[base + i, 32:] = jnp.where(low, turned, block)


def near_kernel(offsets, *refs):
    *near_refs, table = refs
    table[table.shape[0] - 1] = jnp.zeros(table.shape[1:], BF16)
    fill_table(near_refs, offsets, table)


def near_table(offsets, near, block_rows):
    count = len(offsets) // 2
    return call(
        functools.partial(near_kernel, offsets[:count]),
        "near",
        [vmem()] * len(near),
        shaped((2 * count * block_rows + 1, 64, 128), BF16),
        near,
    )


def one_product(group, columns, matrix, table, out_ref):
    block_rows, slots = matrix.shape[0], matrix.shape[2] // 64
    first = group * (block_rows * slots)
    low = iota((32, 128), 1) < 64
    for i in range(block_rows):
        picked = [table[columns[first + i * slots + s]] for s in range(slots)]
        result = jnp.dot(matrix[i], jnp.concatenate(picked, axis=0), preferred_element_type=F32)
        out_ref[i * 32 : (i + 1) * 32, :] = jnp.where(low, result[:32], result[32:]).astype(BF16)


def largest_notes(notes):
    largest = notes[0].astype(F32)
    for note in notes[1:]:
        largest = jnp.maximum(largest, note.astype(F32))
    return largest


def others_kernel(offsets, ranges, stacks, old_table, columns_any, matrix_ref, *refs):
    del old_table
    far_refs, near_refs = refs[:stacks], refs[stacks : 2 * stacks]
    table, *outs, columns, sem = refs[2 * stacks :]
    copy = pltpu.make_async_copy(columns_any, columns, sem)
    copy.start()
    fill_table(far_refs, offsets, table)
    terms, first = outs[: len(ranges)], matrix_ref.shape[1] * 32
    if len(outs) > len(ranges):
        notes = largest_notes(
            [ref[index, first:] for ref in near_refs + far_refs for index in range(ref.shape[0])]
        ).astype(BF16)
        for ref in outs[len(ranges) :]:
            ref[...] = notes
        for term in terms:
            term[first:, :] = notes
    copy.wait()
    for place, m in enumerate(ranges):
        group = m ^ lax.axis_index("cols")
        one_product(group, columns, matrix_ref.at[place], table, terms[place])


def own_kernel(columns, matrix_ref, table, out_ref):
    one_product(lax.axis_index("cols"), columns, matrix_ref.at[0], table, out_ref)


def products(offsets, ranges, columns, matrix, own_matrix, near, far, table):
    block_rows, count = matrix.shape[1], len(offsets) // 2
    extra = near[0].shape[1] > block_rows * 32
    rows = block_rows * 32
    outs = [shaped(table.shape, BF16)] + [shaped((rows + 16 * extra, 128), BF16)] * len(ranges)
    if extra:
        outs.append(shaped((16, 128), BF16))
    table, *outs = call(
        functools.partial(others_kernel, offsets[count:], ranges, len(near)),
        "others",
        [vmem(), pl.BlockSpec(memory_space=pl.ANY)] + [vmem()] * (1 + 2 * len(near)),
        outs,
        (table, columns, matrix, *far, *near),
        [pltpu.SMEM(columns.shape, jnp.int32), pltpu.SemaphoreType.DMA],
        input_output_aliases={0: 0},
    )
    terms = [swap(term, "cols", m) for m, term in zip(ranges, outs)]
    own = call(
        own_kernel,
        "own",
        [smem(), vmem(), vmem()],
        shaped((rows, 128), BF16),
        (columns, own_matrix, table),
    )
    return [own] + terms, outs[len(ranges) :]


def add_terms(terms, rows):
    summed = terms[0][:rows].astype(F32)
    for term in terms[1:]:
        summed = summed + term[:rows].astype(F32)
    return summed


def folded(both):
    gram = both[:64, :64] + both[64:, 64:]
    return jnp.concatenate([gram[:32], gram[32:]], axis=1)


def local_gram(rows):
    both = lax.dot_general(
        rows, rows, (((0,), (0,)), ((), ())), precision=HIGHEST, preferred_element_type=F32
    )
    return folded(both)


def middle_kernel(degree_ref, inverse_ref, *refs):
    terms, out_ref = refs[:-1], refs[-1]
    count = degree_ref.shape[0]
    degree = degree_ref[...]
    rows = add_terms(terms, count) * degree
    out_ref[:count] = (rows * degree).astype(BF16)
    squares = jnp.sum(rows * rows, axis=(0, 1), keepdims=True)
    out_ref[count:] = jnp.concatenate(
        [inverse_ref[...], jnp.broadcast_to(squares, (8, 128))], axis=0
    ).astype(BF16)


def middle(degree, inverse, terms):
    return call(
        middle_kernel,
        "middle",
        [vmem()] * (2 + len(terms)),
        shaped((degree.shape[0] + 16, 128), BF16),
        (degree, inverse, *terms),
    )


def row_gram_kernel(*refs):
    *stacks, gram_ref, rows = refs
    lane = iota((32, 128), 1)
    pair = lane % 64 // 2 == iota((32, 128), 0)
    spread = (iota((128, 128), 0) % 2 == iota((128, 128), 1) // 64).astype(BF16)
    count = stacks[0].shape[1] - 16
    pieces = [(ref, index) for ref in stacks for index in range(ref.shape[0])]
    for place, (ref, index) in enumerate(pieces):
        notes = ref[index, count:].astype(F32)
        masked = [
            jnp.where(pair, jnp.broadcast_to(notes[i : i + 1], (32, 128)), 0.0).astype(BF16)
            for i in range(count // 32)
        ]
        inverse = jnp.dot(jnp.concatenate(masked, axis=0), spread, preferred_element_type=F32)
        block = ref[index, :count].astype(F32) * inverse
        rows[place * count : (place + 1) * count, :] = block.astype(BF16)
    both = lax.dot_general(
        rows[...], rows[...], (((0,), (0,)), ((), ())), preferred_element_type=F32
    )
    gram_ref[...] = folded(both)


def row_gram(stacks):
    count = sum(stack.shape[0] for stack in stacks) * (stacks[0].shape[1] - 16)
    return call(
        row_gram_kernel,
        "row_gram",
        [vmem()] * len(stacks),
        shaped((32, 128), F32),
        stacks,
        [pltpu.VMEM((count, 128), BF16)],
    )


def collect_kernel(devices, total, degree_ref, first_ref, notes_ref, *refs):
    terms, (rows_ref, grams_ref) = refs[:-2], refs[-2:]
    count = degree_ref.shape[0]
    largest = largest_notes([notes_ref[...]] + [term[count:] for term in terms[1:]])
    scale = lax.rsqrt(largest[8:9] * (devices / total))
    rows = add_terms(terms, count) * degree_ref[...] * scale
    rows_ref[...] = rows
    grams_ref[32:] = first_ref[...] * (scale * scale)
    grams_ref[:32] = local_gram(rows)


def collect(devices, total, degree, first, notes, terms):
    return call(
        functools.partial(collect_kernel, devices, total),
        "collect",
        [vmem()] * (3 + len(terms)),
        (shaped(degree.shape, F32), shaped((64, 128), F32)),
        (degree, first, notes, *terms),
    )


def lower_solve(gram, right):
    work = jnp.concatenate([gram, right], axis=1)
    blocks = gram.shape[0] // 8
    rows = [work[8 * i : 8 * i + 8] for i in range(blocks)]
    at = iota((8, 128), 0)

    def columns(first, column):
        return [
            jnp.broadcast_to(rows[i][:, column : column + 1], (8, 128))
            for i in range(first, blocks)
        ]

    def spread(block, row):
        return jnp.broadcast_to(block[row : row + 1], (8, 128))

    current = [columns(0, q) for q in range(8)]
    for b in range(blocks):
        count = blocks - b
        later = []
        if count > 1:
            later = [columns(b + 1, 8 * (b + 1) + q) for q in range(8)]
        for q in range(8):
            root = lax.rsqrt(spread(current[q][0], q))
            inverse = root * root
            raw = spread(rows[b], q)
            scaled = raw * inverse
            for p in range(q + 1, 8):
                weight = spread(current[q][0], p) * inverse
                current[p] = [x - y * weight for x, y in zip(current[p], current[q])]
            below = rows[b] - current[q][0] * scaled
            rows[b] = jnp.where(at == q, raw * root, jnp.where(at > q, below, rows[b]))
            for i in range(1, count):
                rows[b + i] = rows[b + i] - current[q][i] * scaled
            for p in range(len(later)):
                weight = spread(current[q][1], p) * inverse
                later[p] = [x - y * weight for x, y in zip(later[p], current[q][1:])]
        current = later
    return jnp.concatenate(rows, axis=0)[:, 64:]


def unpacked(packed):
    return jnp.concatenate([packed[:, :64], packed[:, 64:]], axis=0)


def add_columns_kernel(total, *refs):
    parts, (gram_ref, first_ref) = refs[:-2], refs[-2:]
    summed = parts[0][...]
    for part in parts[1:]:
        summed = summed + part[...]
    gram_ref[...] = summed[:32]
    first_ref[...] = summed[32:] / total


def add_columns(total, parts):
    return call(
        functools.partial(add_columns_kernel, total),
        "add_columns",
        [vmem()] * len(parts),
        (shaped((32, 128), F32), shaped((32, 128), F32)),
        parts,
    )


def add_parts_kernel(count, *refs):
    summed = refs[0][...]
    for part in refs[1:count]:
        summed = summed + part[...]
    refs[-1][...] = summed


def add_parts(parts, after):
    return call(
        functools.partial(add_parts_kernel, len(parts)),
        "add_parts",
        [vmem()] * (len(parts) + len(after)),
        shaped(parts[0].shape, F32),
        (*parts, *after),
    )


def first_factor_kernel(gram_ref, out_ref):
    unit = (iota((64, 64), 0) == iota((64, 64), 1)).astype(F32)
    out_ref[...] = lower_solve(unpacked(gram_ref[...]), unit)


def first_factor(gram):
    return call(first_factor_kernel, "first_factor", [vmem()], shaped((64, 64), F32), (gram,))


def dot_turned(left, right):
    return lax.dot_general(
        left, right, (((1,), (1,)), ((), ())), precision=HIGHEST, preferred_element_type=F32
    )


def finish_kernel(total, rows_ref, inverse_ref, *refs):
    out_ref, scratch = refs[-2:]
    block_rows = out_ref.shape[1]
    packed = refs[0][...]
    for part in refs[1:-2]:
        packed = packed + part[...]
    first = inverse_ref[...]
    gram = dot_turned(
        jnp.dot(first, unpacked(packed), precision=HIGHEST, preferred_element_type=F32), first
    )
    inverse = lower_solve(gram / total, first)
    zero = jnp.zeros_like(inverse)
    both = jnp.concatenate(
        [jnp.concatenate([inverse, zero], axis=1), jnp.concatenate([zero, inverse], axis=1)], axis=0
    )
    current = dot_turned(rows_ref[...], both)
    for i in range(block_rows):
        scratch[pl.ds(i, 32, stride=block_rows), :] = current[i * 32 : (i + 1) * 32]
    for t in range(32):
        out_ref[0, :, t * 128 : (t + 1) * 128] = scratch[t * block_rows : (t + 1) * block_rows, :]


def finish(total, block_rows, rows, inverse, grams):
    return call(
        functools.partial(finish_kernel, total),
        "finish",
        [vmem()] * (2 + len(grams)),
        shaped((1, block_rows, 32 * 128), F32),
        (rows, inverse, *grams),
        [pltpu.VMEM(rows.shape, F32)],
    )


def swap(value, axis, mask):
    size = lax.axis_size(axis)
    return lax.ppermute(value, axis, [(index, index ^ mask) for index in range(size)])


def swap_both(value, row_mask, column_mask):
    rows, columns = lax.axis_size("rows"), lax.axis_size("cols")
    pairs = [
        (row * columns + column, (row ^ row_mask) * columns + (column ^ column_mask))
        for row in range(rows)
        for column in range(columns)
    ]
    return lax.ppermute(value, ("rows", "cols"), pairs)


def stages(size):
    if size == 8:
        return [[7, 5, 3], [1]]
    bits, bit = [], 1
    while bit < size:
        bits.append([bit])
        bit *= 2
    return bits


def gather_rows(message, after):
    plan = stages(lax.axis_size("rows"))
    held, offsets = [message], [0]
    for masks in plan[:-1]:
        held = held + [swap(piece, "rows", mask) for mask in masks for piece in held]
        offsets = offsets + [mask ^ offset for mask in masks for offset in offsets]
    split = len(held) // 2
    held, offsets = held[split:] + held[:split], offsets[split:] + offsets[:split]
    near = [stack(held[:split], []), stack(held[split:], after)]
    (last,) = plan[-1]
    offsets = offsets + [last ^ offset for offset in offsets]
    return near, [swap(pieces, "rows", last) for pieces in near], offsets


def add_rows(gram, after):
    *plan, (last,) = stages(lax.axis_size("rows"))
    for masks in plan:
        gram = add_parts([gram] + [swap(gram, "rows", mask) for mask in masks], after)
    return [gram, swap(gram, "rows", last)]


def body(affinity, block_columns, block_counts, inv_degree, panel):
    block_rows, block_size = inv_degree.shape[1:]
    groups, _, _, slots, _ = affinity.shape
    ranks = lax.axis_size("rows")
    total = float(groups * ranks * block_rows * block_size)
    blocks = ranks * block_rows
    live = iota(block_columns.shape, 3) < block_counts[..., None]
    columns = jnp.where(live, jnp.clip(block_columns, 0, blocks - 1), blocks).reshape(-1)
    panel, inv_degree, affinity = (
        pltpu.with_memory_space_constraint(value, pltpu.HBM) for value in (panel, inv_degree, affinity)
    )
    ranges = list(range(groups - 1, 0, -1))

    scaled, degree = start(panel, inv_degree)
    matrix, inverse = prep(ranges, affinity, inv_degree)
    own_matrix, _ = prep([0], affinity, inv_degree)
    near, far, offsets = gather_rows(scaled, [inverse])
    table = near_table(offsets, near, block_rows)
    terms, _ = products(offsets, ranges, columns, matrix, own_matrix, near, far, table)
    near, far, offsets = gather_rows(middle(degree, inverse, terms), [])
    table = near_table(offsets, near, block_rows)
    terms, (notes,) = products(offsets, ranges, columns, matrix, own_matrix, near, far, table)
    devices = float(groups * ranks)
    rows, grams = collect(devices, total, degree, row_gram(near + far), notes, terms)
    flip = 1 if ranks == 8 else 0
    gram, first = add_columns(total, [grams] + [swap_both(grams, flip, m) for m in ranges])
    inverse = first_factor(first)
    return finish(total, block_rows, rows, inverse, add_rows(gram, [inverse]))


def solution(mesh):
    return jax.shard_map(
        body,
        mesh=mesh,
        in_specs=(
            P(None, "rows", "cols", None, None),
            P(None, "rows", "cols", None),
            P(None, "rows", "cols"),
            P("cols", "rows", None),
            P("cols", "rows", None),
        ),
        out_specs=P("cols", "rows", None),
        check_vma=False,
    )
```

```python
import functools

import jax
import jax.numpy as jnp
from jax import lax
from jax.experimental import pallas as pl
from jax.experimental.pallas import tpu as pltpu
from jax.sharding import PartitionSpec as P

BF16 = jnp.bfloat16
F32 = jnp.float32
HIGHEST = lax.Precision.HIGHEST
MIB = 1024 * 1024


def params(limit=48 * MIB):
    return pltpu.CompilerParams(vmem_limit_bytes=limit)


def vmem():
    return pl.BlockSpec(memory_space=pltpu.VMEM)


def hbm():
    return pl.BlockSpec(memory_space=pltpu.HBM)


def shaped(shape, dtype):
    return jax.ShapeDtypeStruct(shape, dtype)


def iota(shape, dim):
    return lax.broadcasted_iota(jnp.int32, shape, dim)


def call(kernel, name, ins, outs, operands, scratch=(), limit=48 * MIB, **kwargs):
    return pl.pallas_call(
        kernel,
        out_shape=outs,
        in_specs=ins,
        out_specs=jax.tree.map(lambda _: vmem(), outs),
        scratch_shapes=list(scratch),
        compiler_params=params(limit),
        name=name,
        **kwargs,
    )(*operands)


def start_kernel(panel_hbm, inv_hbm, scaled_ref, degree_ref, panel_ref, inv_ref, scratch, sems):
    block_rows, block_size = inv_ref.shape[1], inv_ref.shape[2]
    half = block_size // 2
    copies = [
        pltpu.make_async_copy(inv_hbm, inv_ref, sems.at[0]),
        pltpu.make_async_copy(panel_hbm, panel_ref, sems.at[1]),
    ]
    for copy in copies:
        copy.start()
    copies[0].wait()
    pair = iota((half, block_size), 1) // 2 == iota((half, block_size), 0)
    spread = (iota((block_size, 128), 0) % 2 == iota((block_size, 128), 1) // 64).astype(F32)
    rows = [
        jnp.where(pair, jnp.broadcast_to(inv_ref[0, i : i + 1, :], (half, block_size)), 0.0)
        for i in range(block_rows)
    ]
    degree_ref[...] = jnp.dot(
        jnp.concatenate(rows, axis=0), spread, precision=HIGHEST, preferred_element_type=F32
    )
    copies[1].wait()
    for t in range(half):
        scratch[t * block_rows : (t + 1) * block_rows, :] = panel_ref[0, :, t * 128 : (t + 1) * 128]
    for i in range(block_rows):
        where = slice(i * half, (i + 1) * half)
        part = scratch[pl.ds(i, half, stride=block_rows), :] * degree_ref[where, :]
        scaled_ref[where, :] = part.astype(BF16)


def start(panel, inv_degree):
    block_rows, block_size = inv_degree.shape[1:]
    shape = (block_rows * block_size // 2, 128)
    return call(
        start_kernel,
        "start",
        [hbm(), hbm()],
        (shaped(shape, BF16), shaped(shape, F32)),
        (panel, inv_degree),
        [
            pltpu.VMEM(panel.shape, F32),
            pltpu.VMEM(inv_degree.shape, F32),
            pltpu.VMEM(shape, F32),
            pltpu.SemaphoreType.DMA((2,)),
        ],
    )


def prep_kernel(
    ranges, affinity_hbm, inv_hbm, out_ref, inverse_ref, affinity_ref, inv_ref, scratch, sems, inv_sem
):
    count, block_rows, _, slots, flat = affinity_ref.shape
    half = flat // 128
    own = lax.axis_index("cols")
    copies = [
        pltpu.make_async_copy(affinity_hbm.at[m ^ own], affinity_ref.at[place], sems.at[place])
        for place, m in enumerate(ranges)
    ]
    inv_copy = pltpu.make_async_copy(inv_hbm, inv_ref, inv_sem)
    inv_copy.start()
    for copy in copies:
        copy.start()
    source, target = iota((256, 256), 0), iota((256, 256), 1)
    moved = (source // 64 % 2) * 128 + (source // 128) * 64 + (source % 2) * 32 + source % 64 // 2
    permute = (moved == target).astype(BF16)
    inv_copy.wait()
    inverse = 1.0 / inv_ref[0]
    high = inverse.astype(BF16).astype(F32)
    inverse_ref[...] = jnp.concatenate([high, inverse - high], axis=1)
    for m in range(count):
        copies[m].wait()
        for i in range(block_rows):
            block = affinity_ref[m, i, 0].astype(F32)
            for t in range(half):
                scratch[i % 2, t * slots : (t + 1) * slots, :] = block[:, t * 128 : (t + 1) * 128]
            parts = [
                scratch[i % 2, pl.ds(s, half, stride=slots), :].astype(BF16) for s in range(slots)
            ]
            pairs = [jnp.concatenate(parts[s : s + 2], axis=1) for s in range(0, slots, 2)]
            moved_pairs = jnp.dot(
                jnp.concatenate(pairs, axis=0), permute, preferred_element_type=F32
            ).astype(BF16)
            for s in range(slots // 2):
                piece = moved_pairs[s * half : (s + 1) * half]
                out_ref[m, i, :half, s * 128 : (s + 1) * 128] = piece[:, :128]
                out_ref[m, i, half:, s * 128 : (s + 1) * 128] = piece[:, 128:]


def prep(ranges, affinity, inv_degree):
    _, block_rows, _, slots, flat = affinity.shape
    count = len(ranges)
    return call(
        functools.partial(prep_kernel, ranges),
        "prep",
        [hbm(), hbm()],
        (shaped((count, block_rows, 64, slots * 64), BF16), shaped((block_rows, 128), F32)),
        (affinity, inv_degree),
        [
            pltpu.VMEM((count,) + affinity.shape[1:], BF16),
            pltpu.VMEM(inv_degree.shape, F32),
            pltpu.VMEM((2, flat // 128 * slots, 128), F32),
            pltpu.SemaphoreType.DMA((count,)),
            pltpu.SemaphoreType.DMA,
        ],
    )


def stack_kernel(count, *refs):
    for index in range(count):
        refs[-1][index] = refs[index][...]


def stack(pieces, after):
    return call(
        functools.partial(stack_kernel, len(pieces)),
        "stack",
        [vmem()] * (len(pieces) + len(after)),
        shaped((len(pieces),) + pieces[0].shape, BF16),
        (*pieces, *after),
    )


def fill_table(stacks, offsets, table):
    block_rows = (table.shape[0] - 1) // (2 * len(offsets))
    low = iota((32, 128), 1) < 64
    pieces = [(ref, index) for ref in stacks for index in range(ref.shape[0])]
    for (ref, index), offset in zip(pieces, offsets):
        base = (lax.axis_index("rows") ^ offset) * block_rows
        for i in range(block_rows):
            block = ref[index, i * 32 : (i + 1) * 32, :]
            turned = jnp.concatenate([block[:, 64:], block[:, :64]], axis=1)
            table[base + i, :32] = jnp.where(low, block, turned)
            table[base + i, 32:] = jnp.where(low, turned, block)


def near_kernel(offsets, *refs):
    *near_refs, table = refs
    table[table.shape[0] - 1] = jnp.zeros(table.shape[1:], BF16)
    fill_table(near_refs, offsets, table)


def near_table(offsets, near, block_rows):
    count = len(offsets) // 2
    return call(
        functools.partial(near_kernel, offsets[:count]),
        "near",
        [vmem()] * len(near),
        shaped((2 * count * block_rows + 1, 64, 128), BF16),
        near,
    )


def one_product(group, columns, matrix, table, out_ref):
    block_rows, slots = matrix.shape[0], matrix.shape[2] // 64
    chosen = columns[group]
    low = iota((32, 128), 1) < 64
    for i in range(block_rows):
        picked = [table[chosen[i, s]] for s in range(slots)]
        result = jnp.dot(matrix[i], jnp.concatenate(picked, axis=0), preferred_element_type=F32)
        out_ref[i * 32 : (i + 1) * 32, :] = jnp.where(low, result[:32], result[32:]).astype(BF16)


def largest_notes(notes):
    largest = notes[0].astype(F32)
    for note in notes[1:]:
        largest = jnp.maximum(largest, note.astype(F32))
    return largest


def others_kernel(offsets, ranges, stacks, old_table, columns, matrix_ref, *refs):
    del old_table
    far_refs, near_refs = refs[:stacks], refs[stacks : 2 * stacks]
    table, *outs = refs[2 * stacks :]
    fill_table(far_refs, offsets, table)
    terms, first = outs[: len(ranges)], matrix_ref.shape[1] * 32
    if len(outs) > len(ranges):
        notes = largest_notes(
            [ref[index, first:] for ref in near_refs + far_refs for index in range(ref.shape[0])]
        ).astype(BF16)
        for ref in outs[len(ranges) :]:
            ref[...] = notes
        for term in terms:
            term[first:, :] = notes
    for place, m in enumerate(ranges):
        group = m ^ lax.axis_index("cols")
        one_product(group, columns, matrix_ref.at[place], table, terms[place])


def own_kernel(columns, matrix_ref, table, out_ref):
    one_product(lax.axis_index("cols"), columns, matrix_ref.at[0], table, out_ref)


def products(offsets, ranges, columns, matrix, own_matrix, near, far, table):
    block_rows, count = matrix.shape[1], len(offsets) // 2
    extra = near[0].shape[1] > block_rows * 32
    rows = block_rows * 32
    outs = [shaped(table.shape, BF16)] + [shaped((rows + 16 * extra, 128), BF16)] * len(ranges)
    if extra:
        outs.append(shaped((16, 128), BF16))
    table, *outs = call(
        functools.partial(others_kernel, offsets[count:], ranges, len(near)),
        "others",
        [vmem()] * (3 + 2 * len(near)),
        outs,
        (table, columns, matrix, *far, *near),
        input_output_aliases={0: 0},
    )
    terms = [swap(term, "cols", m) for m, term in zip(ranges, outs)]
    own = call(
        own_kernel,
        "own",
        [vmem()] * 3,
        shaped((rows, 128), BF16),
        (columns, own_matrix, table),
    )
    return [own] + terms, outs[len(ranges) :]


def add_terms(terms, rows):
    summed = terms[0][:rows].astype(F32)
    for term in terms[1:]:
        summed = summed + term[:rows].astype(F32)
    return summed


def folded(both):
    gram = both[:64, :64] + both[64:, 64:]
    return jnp.concatenate([gram[:32], gram[32:]], axis=1)


def local_gram(rows):
    both = lax.dot_general(
        rows, rows, (((0,), (0,)), ((), ())), precision=HIGHEST, preferred_element_type=F32
    )
    return folded(both)


def middle_kernel(degree_ref, inverse_ref, *refs):
    terms, out_ref = refs[:-1], refs[-1]
    count = degree_ref.shape[0]
    degree = degree_ref[...]
    rows = add_terms(terms, count) * degree
    out_ref[:count] = (rows * degree).astype(BF16)
    squares = jnp.sum(rows * rows, axis=(0, 1), keepdims=True)
    out_ref[count:] = jnp.concatenate(
        [inverse_ref[...], jnp.broadcast_to(squares, (8, 128))], axis=0
    ).astype(BF16)


def middle(degree, inverse, terms):
    return call(
        middle_kernel,
        "middle",
        [vmem()] * (2 + len(terms)),
        shaped((degree.shape[0] + 16, 128), BF16),
        (degree, inverse, *terms),
    )


def row_gram_kernel(*refs):
    *stacks, gram_ref, rows = refs
    lane = iota((32, 128), 1)
    pair = lane % 64 // 2 == iota((32, 128), 0)
    spread = (iota((128, 128), 0) % 2 == iota((128, 128), 1) // 64).astype(BF16)
    count = stacks[0].shape[1] - 16
    pieces = [(ref, index) for ref in stacks for index in range(ref.shape[0])]
    for place, (ref, index) in enumerate(pieces):
        notes = ref[index, count:].astype(F32)
        masked = [
            jnp.where(pair, jnp.broadcast_to(notes[i : i + 1], (32, 128)), 0.0).astype(BF16)
            for i in range(count // 32)
        ]
        inverse = jnp.dot(jnp.concatenate(masked, axis=0), spread, preferred_element_type=F32)
        block = ref[index, :count].astype(F32) * inverse
        rows[place * count : (place + 1) * count, :] = block.astype(BF16)
    both = lax.dot_general(
        rows[...], rows[...], (((0,), (0,)), ((), ())), preferred_element_type=F32
    )
    gram_ref[...] = folded(both)


def row_gram(stacks):
    count = sum(stack.shape[0] for stack in stacks) * (stacks[0].shape[1] - 16)
    return call(
        row_gram_kernel,
        "row_gram",
        [vmem()] * len(stacks),
        shaped((32, 128), F32),
        stacks,
        [pltpu.VMEM((count, 128), BF16)],
    )


def collect_kernel(devices, total, degree_ref, first_ref, notes_ref, *refs):
    terms, (rows_ref, grams_ref) = refs[:-2], refs[-2:]
    count = degree_ref.shape[0]
    largest = largest_notes([notes_ref[...]] + [term[count:] for term in terms[1:]])
    scale = lax.rsqrt(largest[8:9] * (devices / total))
    rows = add_terms(terms, count) * degree_ref[...] * scale
    rows_ref[...] = rows
    grams_ref[32:] = first_ref[...] * (scale * scale)
    grams_ref[:32] = local_gram(rows)


def collect(devices, total, degree, first, notes, terms):
    return call(
        functools.partial(collect_kernel, devices, total),
        "collect",
        [vmem()] * (3 + len(terms)),
        (shaped(degree.shape, F32), shaped((64, 128), F32)),
        (degree, first, notes, *terms),
    )


def lower_solve(gram, right):
    work = jnp.concatenate([gram, right], axis=1)
    blocks = gram.shape[0] // 8
    rows = [work[8 * i : 8 * i + 8] for i in range(blocks)]
    at = iota((8, 128), 0)

    def columns(first, column):
        return [
            jnp.broadcast_to(rows[i][:, column : column + 1], (8, 128))
            for i in range(first, blocks)
        ]

    def spread(block, row):
        return jnp.broadcast_to(block[row : row + 1], (8, 128))

    current = [columns(0, q) for q in range(8)]
    for b in range(blocks):
        count = blocks - b
        later = []
        if count > 1:
            later = [columns(b + 1, 8 * (b + 1) + q) for q in range(8)]
        for q in range(8):
            root = lax.rsqrt(spread(current[q][0], q))
            inverse = root * root
            raw = spread(rows[b], q)
            scaled = raw * inverse
            for p in range(q + 1, 8):
                weight = spread(current[q][0], p) * inverse
                current[p] = [x - y * weight for x, y in zip(current[p], current[q])]
            below = rows[b] - current[q][0] * scaled
            rows[b] = jnp.where(at == q, raw * root, jnp.where(at > q, below, rows[b]))
            for i in range(1, count):
                rows[b + i] = rows[b + i] - current[q][i] * scaled
            for p in range(len(later)):
                weight = spread(current[q][1], p) * inverse
                later[p] = [x - y * weight for x, y in zip(later[p], current[q][1:])]
        current = later
    return jnp.concatenate(rows, axis=0)[:, 64:]


def unpacked(packed):
    return jnp.concatenate([packed[:, :64], packed[:, 64:]], axis=0)


def add_columns_kernel(total, *refs):
    parts, (gram_ref, first_ref) = refs[:-2], refs[-2:]
    summed = parts[0][...]
    for part in parts[1:]:
        summed = summed + part[...]
    gram_ref[...] = summed[:32]
    first_ref[...] = summed[32:] / total


def add_columns(total, parts):
    return call(
        functools.partial(add_columns_kernel, total),
        "add_columns",
        [vmem()] * len(parts),
        (shaped((32, 128), F32), shaped((32, 128), F32)),
        parts,
    )


def add_parts_kernel(count, *refs):
    summed = refs[0][...]
    for part in refs[1:count]:
        summed = summed + part[...]
    refs[-1][...] = summed


def add_parts(parts, after):
    return call(
        functools.partial(add_parts_kernel, len(parts)),
        "add_parts",
        [vmem()] * (len(parts) + len(after)),
        shaped(parts[0].shape, F32),
        (*parts, *after),
    )


def first_factor_kernel(gram_ref, out_ref):
    unit = (iota((64, 64), 0) == iota((64, 64), 1)).astype(F32)
    out_ref[...] = lower_solve(unpacked(gram_ref[...]), unit)


def first_factor(gram):
    return call(first_factor_kernel, "first_factor", [vmem()], shaped((64, 64), F32), (gram,))


def dot_turned(left, right):
    return lax.dot_general(
        left, right, (((1,), (1,)), ((), ())), precision=HIGHEST, preferred_element_type=F32
    )


def finish_kernel(total, rows_ref, inverse_ref, *refs):
    out_ref, scratch = refs[-2:]
    block_rows = out_ref.shape[1]
    packed = refs[0][...]
    for part in refs[1:-2]:
        packed = packed + part[...]
    first = inverse_ref[...]
    gram = dot_turned(
        jnp.dot(first, unpacked(packed), precision=HIGHEST, preferred_element_type=F32), first
    )
    inverse = lower_solve(gram / total, first)
    zero = jnp.zeros_like(inverse)
    both = jnp.concatenate(
        [jnp.concatenate([inverse, zero], axis=1), jnp.concatenate([zero, inverse], axis=1)], axis=0
    )
    current = dot_turned(rows_ref[...], both)
    for i in range(block_rows):
        scratch[pl.ds(i, 32, stride=block_rows), :] = current[i * 32 : (i + 1) * 32]
    for t in range(32):
        out_ref[0, :, t * 128 : (t + 1) * 128] = scratch[t * block_rows : (t + 1) * block_rows, :]


def finish(total, block_rows, rows, inverse, grams):
    return call(
        functools.partial(finish_kernel, total),
        "finish",
        [vmem()] * (2 + len(grams)),
        shaped((1, block_rows, 32 * 128), F32),
        (rows, inverse, *grams),
        [pltpu.VMEM(rows.shape, F32)],
    )


def swap(value, axis, mask):
    size = lax.axis_size(axis)
    return lax.ppermute(value, axis, [(index, index ^ mask) for index in range(size)])


def swap_both(value, row_mask, column_mask):
    rows, columns = lax.axis_size("rows"), lax.axis_size("cols")
    pairs = [
        (row * columns + column, (row ^ row_mask) * columns + (column ^ column_mask))
        for row in range(rows)
        for column in range(columns)
    ]
    return lax.ppermute(value, ("rows", "cols"), pairs)


def stages(size):
    if size == 8:
        return [[7, 5, 3], [1]]
    bits, bit = [], 1
    while bit < size:
        bits.append([bit])
        bit *= 2
    return bits


def gather_rows(message, after):
    plan = stages(lax.axis_size("rows"))
    held, offsets = [message], [0]
    for masks in plan[:-1]:
        held = held + [swap(piece, "rows", mask) for mask in masks for piece in held]
        offsets = offsets + [mask ^ offset for mask in masks for offset in offsets]
    split = len(held) // 2
    held, offsets = held[split:] + held[:split], offsets[split:] + offsets[:split]
    near = [stack(held[:split], []), stack(held[split:], after)]
    (last,) = plan[-1]
    offsets = offsets + [last ^ offset for offset in offsets]
    return near, [swap(pieces, "rows", last) for pieces in near], offsets


def add_rows(gram, after):
    *plan, (last,) = stages(lax.axis_size("rows"))
    for masks in plan:
        gram = add_parts([gram] + [swap(gram, "rows", mask) for mask in masks], after)
    return [gram, swap(gram, "rows", last)]


def body(affinity, block_columns, block_counts, inv_degree, panel):
    block_rows, block_size = inv_degree.shape[1:]
    groups, _, _, slots, _ = affinity.shape
    ranks = lax.axis_size("rows")
    total = float(groups * ranks * block_rows * block_size)
    blocks = ranks * block_rows
    live = iota(block_columns.shape, 3) < block_counts[..., None]
    columns = jnp.where(live, jnp.clip(block_columns, 0, blocks - 1), blocks)[:, :, 0]
    panel, inv_degree, affinity = (
        pltpu.with_memory_space_constraint(value, pltpu.HBM) for value in (panel, inv_degree, affinity)
    )
    ranges = list(range(groups - 1, 0, -1))

    scaled, degree = start(panel, inv_degree)
    matrix, inverse = prep(ranges, affinity, inv_degree)
    own_matrix, _ = prep([0], affinity, inv_degree)
    near, far, offsets = gather_rows(scaled, [inverse])
    table = near_table(offsets, near, block_rows)
    terms, _ = products(offsets, ranges, columns, matrix, own_matrix, near, far, table)
    near, far, offsets = gather_rows(middle(degree, inverse, terms), [])
    table = near_table(offsets, near, block_rows)
    terms, (notes,) = products(offsets, ranges, columns, matrix, own_matrix, near, far, table)
    devices = float(groups * ranks)
    rows, grams = collect(devices, total, degree, row_gram(near + far), notes, terms)
    flip = 1 if ranks == 8 else 0
    gram, first = add_columns(total, [grams] + [swap_both(grams, flip, m) for m in ranges])
    inverse = first_factor(first)
    return finish(total, block_rows, rows, inverse, add_rows(gram, [inverse]))


def solution(mesh):
    return jax.shard_map(
        body,
        mesh=mesh,
        in_specs=(
            P(None, "rows", "cols", None, None),
            P(None, "rows", "cols", None),
            P(None, "rows", "cols"),
            P("cols", "rows", None),
            P("cols", "rows", None),
        ),
        out_specs=P("cols", "rows", None),
        check_vma=False,
    )
```

```python
import functools

import jax
import jax.numpy as jnp
from jax import lax
from jax.experimental import pallas as pl
from jax.experimental.pallas import tpu as pltpu
from jax.sharding import PartitionSpec as P

BF16 = jnp.bfloat16
F32 = jnp.float32
HIGHEST = lax.Precision.HIGHEST
MIB = 1024 * 1024


def params(limit=48 * MIB):
    return pltpu.CompilerParams(vmem_limit_bytes=limit)


def vmem():
    return pl.BlockSpec(memory_space=pltpu.VMEM)


def hbm():
    return pl.BlockSpec(memory_space=pltpu.HBM)


def shaped(shape, dtype):
    return jax.ShapeDtypeStruct(shape, dtype)


def iota(shape, dim):
    return lax.broadcasted_iota(jnp.int32, shape, dim)


def call(kernel, name, ins, outs, operands, scratch=(), limit=48 * MIB, **kwargs):
    return pl.pallas_call(
        kernel,
        out_shape=outs,
        in_specs=ins,
        out_specs=jax.tree.map(lambda _: vmem(), outs),
        scratch_shapes=list(scratch),
        compiler_params=params(limit),
        name=name,
        **kwargs,
    )(*operands)


def start_kernel(panel_hbm, inv_hbm, scaled_ref, degree_ref, panel_ref, inv_ref, scratch, sems):
    block_rows, block_size = inv_ref.shape[1], inv_ref.shape[2]
    half = block_size // 2
    copies = [
        pltpu.make_async_copy(inv_hbm, inv_ref, sems.at[0]),
        pltpu.make_async_copy(panel_hbm, panel_ref, sems.at[1]),
    ]
    for copy in copies:
        copy.start()
    copies[0].wait()
    pair = iota((half, block_size), 1) // 2 == iota((half, block_size), 0)
    spread = (iota((block_size, 128), 0) % 2 == iota((block_size, 128), 1) // 64).astype(F32)
    rows = [
        jnp.where(pair, jnp.broadcast_to(inv_ref[0, i : i + 1, :], (half, block_size)), 0.0)
        for i in range(block_rows)
    ]
    degree_ref[...] = jnp.dot(
        jnp.concatenate(rows, axis=0), spread, precision=HIGHEST, preferred_element_type=F32
    )
    copies[1].wait()
    for t in range(half):
        scratch[t * block_rows : (t + 1) * block_rows, :] = panel_ref[0, :, t * 128 : (t + 1) * 128]
    for i in range(block_rows):
        where = slice(i * half, (i + 1) * half)
        part = scratch[pl.ds(i, half, stride=block_rows), :] * degree_ref[where, :]
        scaled_ref[where, :] = part.astype(BF16)


def start(panel, inv_degree):
    block_rows, block_size = inv_degree.shape[1:]
    shape = (block_rows * block_size // 2, 128)
    return call(
        start_kernel,
        "start",
        [hbm(), hbm()],
        (shaped(shape, BF16), shaped(shape, F32)),
        (panel, inv_degree),
        [
            pltpu.VMEM(panel.shape, F32),
            pltpu.VMEM(inv_degree.shape, F32),
            pltpu.VMEM(shape, F32),
            pltpu.SemaphoreType.DMA((2,)),
        ],
    )


def prep_kernel(
    ranges, affinity_hbm, inv_hbm, out_ref, inverse_ref, affinity_ref, inv_ref, scratch, sems, inv_sem
):
    count, block_rows, _, slots, flat = affinity_ref.shape
    half = flat // 128
    own = lax.axis_index("cols")
    copies = [
        pltpu.make_async_copy(affinity_hbm.at[m ^ own], affinity_ref.at[place], sems.at[place])
        for place, m in enumerate(ranges)
    ]
    inv_copy = pltpu.make_async_copy(inv_hbm, inv_ref, inv_sem)
    inv_copy.start()
    for copy in copies:
        copy.start()
    source, target = iota((256, 256), 0), iota((256, 256), 1)
    moved = (source // 64 % 2) * 128 + (source // 128) * 64 + (source % 2) * 32 + source % 64 // 2
    permute = (moved == target).astype(BF16)
    inv_copy.wait()
    inverse = 1.0 / inv_ref[0]
    high = inverse.astype(BF16).astype(F32)
    inverse_ref[...] = jnp.concatenate([high, inverse - high], axis=1)
    for m in range(count):
        copies[m].wait()
        for i in range(block_rows):
            block = affinity_ref[m, i, 0].astype(F32)
            for t in range(half):
                scratch[i % 2, t * slots : (t + 1) * slots, :] = block[:, t * 128 : (t + 1) * 128]
            parts = [
                scratch[i % 2, pl.ds(s, half, stride=slots), :].astype(BF16) for s in range(slots)
            ]
            pairs = [jnp.concatenate(parts[s : s + 2], axis=1) for s in range(0, slots, 2)]
            moved_pairs = jnp.dot(
                jnp.concatenate(pairs, axis=0), permute, preferred_element_type=F32
            ).astype(BF16)
            for s in range(slots // 2):
                piece = moved_pairs[s * half : (s + 1) * half]
                out_ref[m, i, :half, s * 128 : (s + 1) * 128] = piece[:, :128]
                out_ref[m, i, half:, s * 128 : (s + 1) * 128] = piece[:, 128:]


def prep(ranges, affinity, inv_degree):
    _, block_rows, _, slots, flat = affinity.shape
    count = len(ranges)
    return call(
        functools.partial(prep_kernel, ranges),
        "prep",
        [hbm(), hbm()],
        (shaped((count, block_rows, 64, slots * 64), BF16), shaped((block_rows, 128), F32)),
        (affinity, inv_degree),
        [
            pltpu.VMEM((count,) + affinity.shape[1:], BF16),
            pltpu.VMEM(inv_degree.shape, F32),
            pltpu.VMEM((2, flat // 128 * slots, 128), F32),
            pltpu.SemaphoreType.DMA((count,)),
            pltpu.SemaphoreType.DMA,
        ],
    )


def stack_kernel(count, *refs):
    for index in range(count):
        refs[-1][index] = refs[index][...]


def stack(pieces, after):
    return call(
        functools.partial(stack_kernel, len(pieces)),
        "stack",
        [vmem()] * (len(pieces) + len(after)),
        shaped((len(pieces),) + pieces[0].shape, BF16),
        (*pieces, *after),
    )


def fill_table(stacks, offsets, table):
    block_rows = (table.shape[0] - 1) // (2 * len(offsets))
    low = iota((32, 128), 1) < 64
    pieces = [(ref, index) for ref in stacks for index in range(ref.shape[0])]
    for (ref, index), offset in zip(pieces, offsets):
        base = (lax.axis_index("rows") ^ offset) * block_rows
        for i in range(block_rows):
            block = ref[index, i * 32 : (i + 1) * 32, :]
            turned = jnp.concatenate([block[:, 64:], block[:, :64]], axis=1)
            table[base + i, :32] = jnp.where(low, block, turned)
            table[base + i, 32:] = jnp.where(low, turned, block)


def near_kernel(offsets, *refs):
    *near_refs, table = refs
    table[table.shape[0] - 1] = jnp.zeros(table.shape[1:], BF16)
    fill_table(near_refs, offsets, table)


def near_table(offsets, near, block_rows):
    count = len(offsets) // 2
    return call(
        functools.partial(near_kernel, offsets[:count]),
        "near",
        [vmem()] * len(near),
        shaped((2 * count * block_rows + 1, 64, 128), BF16),
        near,
    )


def one_product(group, columns, matrix, table, out_ref):
    block_rows, slots = matrix.shape[0], matrix.shape[2] // 64
    chosen = columns[group]
    low = iota((32, 128), 1) < 64
    for i in range(block_rows):
        picked = [table[chosen[i, s]] for s in range(slots)]
        result = jnp.dot(matrix[i], jnp.concatenate(picked, axis=0), preferred_element_type=F32)
        out_ref[i * 32 : (i + 1) * 32, :] = jnp.where(low, result[:32], result[32:]).astype(BF16)


def largest_notes(notes):
    largest = notes[0].astype(F32)
    for note in notes[1:]:
        largest = jnp.maximum(largest, note.astype(F32))
    return largest


def others_kernel(offsets, ranges, stacks, old_table, columns, matrix_ref, *refs):
    del old_table
    far_refs, near_refs = refs[:stacks], refs[stacks : 2 * stacks]
    table, *outs = refs[2 * stacks :]
    fill_table(far_refs, offsets, table)
    terms, first = outs[: len(ranges)], matrix_ref.shape[1] * 32
    if len(outs) > len(ranges):
        notes = largest_notes(
            [ref[index, first:] for ref in near_refs + far_refs for index in range(ref.shape[0])]
        ).astype(BF16)
        for ref in outs[len(ranges) :]:
            ref[...] = notes
        for term in terms:
            term[first:, :] = notes
    for place, m in enumerate(ranges):
        group = m ^ lax.axis_index("cols")
        one_product(group, columns, matrix_ref.at[place], table, terms[place])


def own_kernel(columns, matrix_ref, table, out_ref):
    one_product(lax.axis_index("cols"), columns, matrix_ref.at[0], table, out_ref)


def products(offsets, ranges, columns, matrix, own_matrix, near, far, table):
    block_rows, count = matrix.shape[1], len(offsets) // 2
    extra = near[0].shape[1] > block_rows * 32
    rows = block_rows * 32
    outs = [shaped(table.shape, BF16)] + [shaped((rows + 16 * extra, 128), BF16)] * len(ranges)
    if extra:
        outs.append(shaped((16, 128), BF16))
    table, *outs = call(
        functools.partial(others_kernel, offsets[count:], ranges, len(near)),
        "others",
        [vmem()] * (3 + 2 * len(near)),
        outs,
        (table, columns, matrix, *far, *near),
        input_output_aliases={0: 0},
    )
    terms = [swap(term, "cols", m) for m, term in zip(ranges, outs)]
    own = call(
        own_kernel,
        "own",
        [vmem()] * 3,
        shaped((rows, 128), BF16),
        (columns, own_matrix, table),
    )
    return [own] + terms, outs[len(ranges) :]


def add_terms(terms, rows):
    summed = terms[0][:rows].astype(F32)
    for term in terms[1:]:
        summed = summed + term[:rows].astype(F32)
    return summed


def folded(both):
    gram = both[:64, :64] + both[64:, 64:]
    return jnp.concatenate([gram[:32], gram[32:]], axis=1)


def local_gram(rows):
    both = lax.dot_general(
        rows, rows, (((0,), (0,)), ((), ())), precision=HIGHEST, preferred_element_type=F32
    )
    return folded(both)


def middle_kernel(degree_ref, inverse_ref, *refs):
    terms, out_ref = refs[:-1], refs[-1]
    count = degree_ref.shape[0]
    degree = degree_ref[...]
    rows = add_terms(terms, count) * degree
    out_ref[:count] = (rows * degree).astype(BF16)
    squares = jnp.sum(rows * rows, axis=(0, 1), keepdims=True)
    out_ref[count:] = jnp.concatenate(
        [inverse_ref[...], jnp.broadcast_to(squares, (8, 128))], axis=0
    ).astype(BF16)


def middle(degree, inverse, terms):
    return call(
        middle_kernel,
        "middle",
        [vmem()] * (2 + len(terms)),
        shaped((degree.shape[0] + 16, 128), BF16),
        (degree, inverse, *terms),
    )


def row_gram_kernel(*refs):
    *stacks, gram_ref, rows = refs
    lane = iota((32, 128), 1)
    pair = lane % 64 // 2 == iota((32, 128), 0)
    spread = (iota((128, 128), 0) % 2 == iota((128, 128), 1) // 64).astype(BF16)
    count = stacks[0].shape[1] - 16
    pieces = [(ref, index) for ref in stacks for index in range(ref.shape[0])]
    for place, (ref, index) in enumerate(pieces):
        notes = ref[index, count:].astype(F32)
        masked = [
            jnp.where(pair, jnp.broadcast_to(notes[i : i + 1], (32, 128)), 0.0).astype(BF16)
            for i in range(count // 32)
        ]
        inverse = jnp.dot(jnp.concatenate(masked, axis=0), spread, preferred_element_type=F32)
        block = ref[index, :count].astype(F32) * inverse
        rows[place * count : (place + 1) * count, :] = block.astype(BF16)
    both = lax.dot_general(
        rows[...], rows[...], (((0,), (0,)), ((), ())), preferred_element_type=F32
    )
    gram_ref[...] = folded(both)


def row_gram(stacks):
    count = sum(stack.shape[0] for stack in stacks) * (stacks[0].shape[1] - 16)
    return call(
        row_gram_kernel,
        "row_gram",
        [vmem()] * len(stacks),
        shaped((32, 128), F32),
        stacks,
        [pltpu.VMEM((count, 128), BF16)],
    )


def collect_kernel(devices, total, degree_ref, first_ref, notes_ref, *refs):
    terms, (rows_ref, grams_ref) = refs[:-2], refs[-2:]
    count = degree_ref.shape[0]
    largest = largest_notes([notes_ref[...]] + [term[count:] for term in terms[1:]])
    scale = lax.rsqrt(largest[8:9] * (devices / total))
    rows = add_terms(terms, count) * degree_ref[...] * scale
    rows_ref[...] = rows
    grams_ref[32:] = first_ref[...] * (scale * scale)
    grams_ref[:32] = local_gram(rows)


def collect(devices, total, degree, first, notes, terms):
    return call(
        functools.partial(collect_kernel, devices, total),
        "collect",
        [vmem()] * (3 + len(terms)),
        (shaped(degree.shape, F32), shaped((64, 128), F32)),
        (degree, first, notes, *terms),
    )


def lower_solve(gram, right):
    work = jnp.concatenate([gram, right], axis=1)
    blocks = gram.shape[0] // 8
    rows = [work[8 * i : 8 * i + 8] for i in range(blocks)]
    at = iota((8, 128), 0)

    def columns(first, column):
        return [
            jnp.broadcast_to(rows[i][:, column : column + 1], (8, 128))
            for i in range(first, blocks)
        ]

    def spread(block, row):
        return jnp.broadcast_to(block[row : row + 1], (8, 128))

    current = [columns(0, q) for q in range(8)]
    for b in range(blocks):
        count = blocks - b
        later = []
        if count > 1:
            later = [columns(b + 1, 8 * (b + 1) + q) for q in range(8)]
        for q in range(8):
            root = lax.rsqrt(spread(current[q][0], q))
            inverse = root * root
            raw = spread(rows[b], q)
            scaled = raw * inverse
            for p in range(q + 1, 8):
                weight = spread(current[q][0], p) * inverse
                current[p] = [x - y * weight for x, y in zip(current[p], current[q])]
            below = rows[b] - current[q][0] * scaled
            rows[b] = jnp.where(at == q, raw * root, jnp.where(at > q, below, rows[b]))
            for i in range(1, count):
                rows[b + i] = rows[b + i] - current[q][i] * scaled
            for p in range(len(later)):
                weight = spread(current[q][1], p) * inverse
                later[p] = [x - y * weight for x, y in zip(later[p], current[q][1:])]
        current = later
    return jnp.concatenate(rows, axis=0)[:, 64:]


def unpacked(packed):
    return jnp.concatenate([packed[:, :64], packed[:, 64:]], axis=0)


def add_columns_kernel(total, *refs):
    parts, (gram_ref, first_ref) = refs[:-2], refs[-2:]
    summed = parts[0][...]
    for part in parts[1:]:
        summed = summed + part[...]
    gram_ref[...] = summed[:32]
    first_ref[...] = summed[32:] / total


def add_columns(total, parts):
    return call(
        functools.partial(add_columns_kernel, total),
        "add_columns",
        [vmem()] * len(parts),
        (shaped((32, 128), F32), shaped((32, 128), F32)),
        parts,
    )


def add_parts_kernel(count, *refs):
    summed = refs[0][...]
    for part in refs[1:count]:
        summed = summed + part[...]
    refs[-1][...] = summed


def add_parts(parts, after):
    return call(
        functools.partial(add_parts_kernel, len(parts)),
        "add_parts",
        [vmem()] * (len(parts) + len(after)),
        shaped(parts[0].shape, F32),
        (*parts, *after),
    )


def first_factor_kernel(gram_ref, out_ref):
    unit = (iota((64, 64), 0) == iota((64, 64), 1)).astype(F32)
    out_ref[...] = lower_solve(unpacked(gram_ref[...]), unit)


def first_factor(gram):
    return call(first_factor_kernel, "first_factor", [vmem()], shaped((64, 64), F32), (gram,))


def dot_turned(left, right):
    return lax.dot_general(
        left, right, (((1,), (1,)), ((), ())), precision=HIGHEST, preferred_element_type=F32
    )


def finish_kernel(total, rows_ref, inverse_ref, *refs):
    out_ref, scratch = refs[-2:]
    block_rows = out_ref.shape[1]
    packed = refs[0][...]
    for part in refs[1:-2]:
        packed = packed + part[...]
    first = inverse_ref[...]
    gram = dot_turned(
        jnp.dot(first, unpacked(packed), precision=HIGHEST, preferred_element_type=F32), first
    )
    inverse = lower_solve(gram / total, first)
    zero = jnp.zeros_like(inverse)
    both = jnp.concatenate(
        [jnp.concatenate([inverse, zero], axis=1), jnp.concatenate([zero, inverse], axis=1)], axis=0
    )
    current = dot_turned(rows_ref[...], both)
    for i in range(block_rows):
        scratch[pl.ds(i, 32, stride=block_rows), :] = current[i * 32 : (i + 1) * 32]
    for t in range(32):
        out_ref[0, :, t * 128 : (t + 1) * 128] = scratch[t * block_rows : (t + 1) * block_rows, :]


def finish(total, block_rows, rows, inverse, grams):
    return call(
        functools.partial(finish_kernel, total),
        "finish",
        [vmem()] * (2 + len(grams)),
        shaped((1, block_rows, 32 * 128), F32),
        (rows, inverse, *grams),
        [pltpu.VMEM(rows.shape, F32)],
    )


def swap(value, axis, mask):
    size = lax.axis_size(axis)
    return lax.ppermute(value, axis, [(index, index ^ mask) for index in range(size)])


def swap_both(value, row_mask, column_mask):
    rows, columns = lax.axis_size("rows"), lax.axis_size("cols")
    pairs = [
        (row * columns + column, (row ^ row_mask) * columns + (column ^ column_mask))
        for row in range(rows)
        for column in range(columns)
    ]
    return lax.ppermute(value, ("rows", "cols"), pairs)


def stages(size):
    if size == 8:
        return [[7, 5, 3], [1]]
    bits, bit = [], 1
    while bit < size:
        bits.append([bit])
        bit *= 2
    return bits


def gather_rows(message, after):
    plan = stages(lax.axis_size("rows"))
    held, offsets = [message], [0]
    for masks in plan[:-1]:
        held = held + [swap(piece, "rows", mask) for mask in masks for piece in held]
        offsets = offsets + [mask ^ offset for mask in masks for offset in offsets]
    split = len(held) // 2
    held, offsets = held[split:] + held[:split], offsets[split:] + offsets[:split]
    near = [stack(held[:split], []), stack(held[split:], after)]
    (last,) = plan[-1]
    offsets = offsets + [last ^ offset for offset in offsets]
    return near, [swap(pieces, "rows", last) for pieces in near], offsets


def add_rows(gram, after):
    *plan, (last,) = stages(lax.axis_size("rows"))
    for masks in plan:
        gram = add_parts([gram] + [swap(gram, "rows", mask) for mask in masks], after)
    return [gram, swap(gram, "rows", last)]


def body(affinity, block_columns, block_counts, inv_degree, panel):
    block_rows, block_size = inv_degree.shape[1:]
    groups, _, _, slots, _ = affinity.shape
    ranks = lax.axis_size("rows")
    total = float(groups * ranks * block_rows * block_size)
    blocks = ranks * block_rows
    live = iota(block_columns.shape, 3) < block_counts[..., None]
    columns = jnp.where(live, jnp.clip(block_columns, 0, blocks - 1), blocks)[:, :, 0]
    panel, inv_degree, affinity = (
        pltpu.with_memory_space_constraint(value, pltpu.HBM) for value in (panel, inv_degree, affinity)
    )
    ranges = list(range(groups - 1, 0, -1))

    scaled, degree = start(panel, inv_degree)
    matrix, inverse = prep(ranges, affinity, inv_degree)
    own_matrix, _ = prep([0], affinity, inv_degree)
    near, far, offsets = gather_rows(scaled, [inverse])
    table = near_table(offsets, near, block_rows)
    terms, _ = products(offsets, ranges, columns, matrix, own_matrix, near, far, table)
    near, far, offsets = gather_rows(middle(degree, inverse, terms), [])
    table = near_table(offsets, near, block_rows)
    terms, (notes,) = products(offsets, ranges, columns, matrix, own_matrix, near, far, table)
    devices = float(groups * ranks)
    rows, grams = collect(devices, total, degree, row_gram(near + far), notes, terms)
    flip = 1 if ranks == 8 else 0
    order = [2, 3, 1] if groups == 4 else ranges
    gram, first = add_columns(total, [grams] + [swap_both(grams, flip, m) for m in order])
    inverse = first_factor(first)
    return finish(total, block_rows, rows, inverse, add_rows(gram, [inverse]))


def solution(mesh):
    return jax.shard_map(
        body,
        mesh=mesh,
        in_specs=(
            P(None, "rows", "cols", None, None),
            P(None, "rows", "cols", None),
            P(None, "rows", "cols"),
            P("cols", "rows", None),
            P("cols", "rows", None),
        ),
        out_specs=P("cols", "rows", None),
        check_vma=False,
    )
```

```python
import functools

import jax
import jax.numpy as jnp
from jax import lax
from jax.experimental import pallas as pl
from jax.experimental.pallas import tpu as pltpu
from jax.sharding import PartitionSpec as P

BF16 = jnp.bfloat16
F32 = jnp.float32
HIGHEST = lax.Precision.HIGHEST
MIB = 1024 * 1024


def params(limit=48 * MIB):
    return pltpu.CompilerParams(vmem_limit_bytes=limit)


def vmem():
    return pl.BlockSpec(memory_space=pltpu.VMEM)


def hbm():
    return pl.BlockSpec(memory_space=pltpu.HBM)


def shaped(shape, dtype):
    return jax.ShapeDtypeStruct(shape, dtype)


def iota(shape, dim):
    return lax.broadcasted_iota(jnp.int32, shape, dim)


def call(kernel, name, ins, outs, operands, scratch=(), limit=48 * MIB, **kwargs):
    return pl.pallas_call(
        kernel,
        out_shape=outs,
        in_specs=ins,
        out_specs=jax.tree.map(lambda _: vmem(), outs),
        scratch_shapes=list(scratch),
        compiler_params=params(limit),
        name=name,
        **kwargs,
    )(*operands)


def start_kernel(panel_hbm, inv_hbm, scaled_ref, panel_ref, inv_ref, scratch, sems):
    block_rows, half = inv_ref.shape[1], inv_ref.shape[2] // 2
    copies = [
        pltpu.make_async_copy(inv_hbm, inv_ref, sems.at[0]),
        pltpu.make_async_copy(panel_hbm, panel_ref, sems.at[1]),
    ]
    for copy in copies:
        copy.start()
    copies[0].wait()
    inv = inv_ref[0]
    low = iota((block_rows, 128), 1) < 64
    scales = []
    for t in range(half):
        even, odd = (
            jnp.broadcast_to(inv[:, a : a + 1], (block_rows, 128)) for a in (2 * t, 2 * t + 1)
        )
        scales.append(jnp.where(low, even, odd))
    copies[1].wait()
    for t in range(half):
        scratch[t * block_rows : (t + 1) * block_rows, :] = (
            panel_ref[0, :, t * 128 : (t + 1) * 128] * scales[t]
        )
    for i in range(block_rows):
        part = scratch[pl.ds(i, half, stride=block_rows), :]
        scaled_ref[i * half : (i + 1) * half, :] = part.astype(BF16)


def start(panel, inv_degree):
    block_rows, block_size = inv_degree.shape[1:]
    shape = (block_rows * block_size // 2, 128)
    return call(
        start_kernel,
        "start",
        [hbm(), hbm()],
        shaped(shape, BF16),
        (panel, inv_degree),
        [
            pltpu.VMEM(panel.shape, F32),
            pltpu.VMEM(inv_degree.shape, F32),
            pltpu.VMEM(shape, F32),
            pltpu.SemaphoreType.DMA((2,)),
        ],
    )


def prepare_scales(inv, degree_ref, inverse_ref):
    block_rows, block_size = inv.shape
    half = block_size // 2
    pair = iota((half, block_size), 1) // 2 == iota((half, block_size), 0)
    spread = (iota((block_size, 128), 0) % 2 == iota((block_size, 128), 1) // 64).astype(F32)
    rows = [
        jnp.where(pair, jnp.broadcast_to(inv[i : i + 1, :], (half, block_size)), 0.0)
        for i in range(block_rows)
    ]
    degree_ref[...] = jnp.dot(
        jnp.concatenate(rows, axis=0), spread, precision=HIGHEST, preferred_element_type=F32
    )
    inverse = 1.0 / inv
    high = inverse.astype(BF16).astype(F32)
    inverse_ref[...] = jnp.concatenate([high, inverse - high], axis=1)


def prep_kernel(ranges, affinity_hbm, *refs):
    *scale_refs, out_ref, affinity_ref, inv_ref, scratch, sems = refs
    count, block_rows, _, slots, flat = affinity_ref.shape
    half = flat // 128
    own = lax.axis_index("cols")
    copies = [
        pltpu.make_async_copy(affinity_hbm.at[m ^ own], affinity_ref.at[place], sems.at[place])
        for place, m in enumerate(ranges)
    ]
    if scale_refs:
        inv_copy = pltpu.make_async_copy(scale_refs[0], inv_ref, sems.at[count])
        inv_copy.start()
    for copy in copies:
        copy.start()
    source, target = iota((256, 256), 0), iota((256, 256), 1)
    moved = (source // 64 % 2) * 128 + (source // 128) * 64 + (source % 2) * 32 + source % 64 // 2
    permute = (moved == target).astype(BF16)
    if scale_refs:
        inv_copy.wait()
        prepare_scales(inv_ref[0], *scale_refs[1:])
    for m in range(count):
        copies[m].wait()
        for i in range(block_rows):
            block = affinity_ref[m, i, 0].astype(F32)
            for t in range(half):
                scratch[i % 2, t * slots : (t + 1) * slots, :] = block[:, t * 128 : (t + 1) * 128]
            parts = [
                scratch[i % 2, pl.ds(s, half, stride=slots), :].astype(BF16) for s in range(slots)
            ]
            pairs = [jnp.concatenate(parts[s : s + 2], axis=1) for s in range(0, slots, 2)]
            moved_pairs = jnp.dot(
                jnp.concatenate(pairs, axis=0), permute, preferred_element_type=F32
            ).astype(BF16)
            for s in range(slots // 2):
                piece = moved_pairs[s * half : (s + 1) * half]
                out_ref[m, i, :half, s * 128 : (s + 1) * 128] = piece[:, :128]
                out_ref[m, i, half:, s * 128 : (s + 1) * 128] = piece[:, 128:]


def prep(ranges, affinity, *scale_from):
    _, block_rows, _, slots, flat = affinity.shape
    count = len(ranges)
    outs = [shaped((count, block_rows, 64, slots * 64), BF16)]
    if scale_from:
        outs = [shaped((block_rows * 32, 128), F32), shaped((block_rows, 128), F32)] + outs
    return call(
        functools.partial(prep_kernel, ranges),
        "prep",
        [hbm()] * (1 + len(scale_from)),
        outs,
        (affinity, *scale_from),
        [
            pltpu.VMEM((count,) + affinity.shape[1:], BF16),
            pltpu.VMEM((1, block_rows, 64), F32),
            pltpu.VMEM((2, flat // 128 * slots, 128), F32),
            pltpu.SemaphoreType.DMA((count + 1,)),
        ],
    )


def stack_kernel(count, *refs):
    for index in range(count):
        refs[-1][index] = refs[index][...]


def stack(pieces, after):
    return call(
        functools.partial(stack_kernel, len(pieces)),
        "stack",
        [vmem()] * (len(pieces) + len(after)),
        shaped((len(pieces),) + pieces[0].shape, BF16),
        (*pieces, *after),
    )


def fill_table(stacks, offsets, table):
    block_rows = (table.shape[0] - 1) // (2 * len(offsets))
    low = iota((32, 128), 1) < 64
    pieces = [(ref, index) for ref in stacks for index in range(ref.shape[0])]
    for (ref, index), offset in zip(pieces, offsets):
        base = (lax.axis_index("rows") ^ offset) * block_rows
        for i in range(block_rows):
            block = ref[index, i * 32 : (i + 1) * 32, :]
            turned = jnp.concatenate([block[:, 64:], block[:, :64]], axis=1)
            table[base + i, :32] = jnp.where(low, block, turned)
            table[base + i, 32:] = jnp.where(low, turned, block)


def near_kernel(offsets, *refs):
    *near_refs, table = refs
    table[table.shape[0] - 1] = jnp.zeros(table.shape[1:], BF16)
    fill_table(near_refs, offsets, table)


def near_table(offsets, near, block_rows):
    count = len(offsets) // 2
    return call(
        functools.partial(near_kernel, offsets[:count]),
        "near",
        [vmem()] * len(near),
        shaped((2 * count * block_rows + 1, 64, 128), BF16),
        near,
    )


def one_product(group, columns, matrix, table, out_ref):
    block_rows, slots = matrix.shape[0], matrix.shape[2] // 64
    chosen = columns[group]
    low = iota((32, 128), 1) < 64
    for i in range(block_rows):
        picked = [table[chosen[i, s]] for s in range(slots)]
        result = jnp.dot(matrix[i], jnp.concatenate(picked, axis=0), preferred_element_type=F32)
        out_ref[i * 32 : (i + 1) * 32, :] = jnp.where(low, result[:32], result[32:]).astype(BF16)


def largest_notes(notes):
    largest = notes[0].astype(F32)
    for note in notes[1:]:
        largest = jnp.maximum(largest, note.astype(F32))
    return largest


def others_kernel(offsets, ranges, stacks, old_table, columns, matrix_ref, *refs):
    del old_table
    far_refs, near_refs = refs[:stacks], refs[stacks : 2 * stacks]
    table, *outs = refs[2 * stacks :]
    fill_table(far_refs, offsets, table)
    terms, first = outs[: len(ranges)], matrix_ref.shape[1] * 32
    if len(outs) > len(ranges):
        notes = largest_notes(
            [ref[index, first:] for ref in near_refs + far_refs for index in range(ref.shape[0])]
        ).astype(BF16)
        for ref in outs[len(ranges) :]:
            ref[...] = notes
        for term in terms:
            term[first:, :] = notes
    for place, m in enumerate(ranges):
        group = m ^ lax.axis_index("cols")
        one_product(group, columns, matrix_ref.at[place], table, terms[place])


def own_kernel(columns, matrix_ref, table, out_ref):
    one_product(lax.axis_index("cols"), columns, matrix_ref.at[0], table, out_ref)


def products(offsets, ranges, columns, matrix, own_matrix, near, far, table):
    block_rows, count = matrix.shape[1], len(offsets) // 2
    extra = near[0].shape[1] > block_rows * 32
    rows = block_rows * 32
    outs = [shaped(table.shape, BF16)] + [shaped((rows + 16 * extra, 128), BF16)] * len(ranges)
    if extra:
        outs.append(shaped((16, 128), BF16))
    table, *outs = call(
        functools.partial(others_kernel, offsets[count:], ranges, len(near)),
        "others",
        [vmem()] * (3 + 2 * len(near)),
        outs,
        (table, columns, matrix, *far, *near),
        input_output_aliases={0: 0},
    )
    terms = [swap(term, "cols", m) for m, term in zip(ranges, outs)]
    own = call(
        own_kernel,
        "own",
        [vmem()] * 3,
        shaped((rows, 128), BF16),
        (columns, own_matrix, table),
    )
    return [own] + terms, outs[len(ranges) :]


def add_terms(terms, rows):
    summed = terms[0][:rows].astype(F32)
    for term in terms[1:]:
        summed = summed + term[:rows].astype(F32)
    return summed


def folded(both):
    gram = both[:64, :64] + both[64:, 64:]
    return jnp.concatenate([gram[:32], gram[32:]], axis=1)


def local_gram(rows):
    both = lax.dot_general(
        rows, rows, (((0,), (0,)), ((), ())), precision=HIGHEST, preferred_element_type=F32
    )
    return folded(both)


def middle_kernel(degree_ref, inverse_ref, *refs):
    terms, out_ref = refs[:-1], refs[-1]
    count = degree_ref.shape[0]
    degree = degree_ref[...]
    rows = add_terms(terms, count) * degree
    out_ref[:count] = (rows * degree).astype(BF16)
    squares = jnp.sum(rows * rows, axis=(0, 1), keepdims=True)
    out_ref[count:] = jnp.concatenate(
        [inverse_ref[...], jnp.broadcast_to(squares, (8, 128))], axis=0
    ).astype(BF16)


def middle(degree, inverse, terms):
    return call(
        middle_kernel,
        "middle",
        [vmem()] * (2 + len(terms)),
        shaped((degree.shape[0] + 16, 128), BF16),
        (degree, inverse, *terms),
    )


def row_gram_kernel(*refs):
    *stacks, gram_ref, rows = refs
    lane = iota((32, 128), 1)
    pair = lane % 64 // 2 == iota((32, 128), 0)
    spread = (iota((128, 128), 0) % 2 == iota((128, 128), 1) // 64).astype(BF16)
    count = stacks[0].shape[1] - 16
    pieces = [(ref, index) for ref in stacks for index in range(ref.shape[0])]
    for place, (ref, index) in enumerate(pieces):
        notes = ref[index, count:].astype(F32)
        masked = [
            jnp.where(pair, jnp.broadcast_to(notes[i : i + 1], (32, 128)), 0.0).astype(BF16)
            for i in range(count // 32)
        ]
        inverse = jnp.dot(jnp.concatenate(masked, axis=0), spread, preferred_element_type=F32)
        block = ref[index, :count].astype(F32) * inverse
        rows[place * count : (place + 1) * count, :] = block.astype(BF16)
    both = lax.dot_general(
        rows[...], rows[...], (((0,), (0,)), ((), ())), preferred_element_type=F32
    )
    gram_ref[...] = folded(both)


def row_gram(stacks):
    count = sum(stack.shape[0] for stack in stacks) * (stacks[0].shape[1] - 16)
    return call(
        row_gram_kernel,
        "row_gram",
        [vmem()] * len(stacks),
        shaped((32, 128), F32),
        stacks,
        [pltpu.VMEM((count, 128), BF16)],
    )


def collect_kernel(devices, total, degree_ref, first_ref, notes_ref, *refs):
    terms, (rows_ref, grams_ref) = refs[:-2], refs[-2:]
    count = degree_ref.shape[0]
    largest = largest_notes([notes_ref[...]] + [term[count:] for term in terms[1:]])
    scale = lax.rsqrt(largest[8:9] * (devices / total))
    rows = add_terms(terms, count) * degree_ref[...] * scale
    rows_ref[...] = rows
    grams_ref[32:] = first_ref[...] * (scale * scale)
    grams_ref[:32] = local_gram(rows)


def collect(devices, total, degree, first, notes, terms):
    return call(
        functools.partial(collect_kernel, devices, total),
        "collect",
        [vmem()] * (3 + len(terms)),
        (shaped(degree.shape, F32), shaped((64, 128), F32)),
        (degree, first, notes, *terms),
    )


def lower_solve(gram, right):
    work = jnp.concatenate([gram, right], axis=1)
    blocks = gram.shape[0] // 8
    rows = [work[8 * i : 8 * i + 8] for i in range(blocks)]
    at = iota((8, 128), 0)

    def columns(first, column):
        return [
            jnp.broadcast_to(rows[i][:, column : column + 1], (8, 128))
            for i in range(first, blocks)
        ]

    def spread(block, row):
        return jnp.broadcast_to(block[row : row + 1], (8, 128))

    ahead = []
    for b in range(blocks):
        count = blocks - b
        current = ahead + [columns(b, 8 * b + q) for q in range(len(ahead), 8)]
        ahead = []
        if count > 1:
            ahead = [columns(b + 1, 8 * (b + 1) + q) for q in range(4)]
        for q in range(8):
            root = lax.rsqrt(spread(current[q][0], q))
            row = spread(rows[b], q) * root
            column = [x * root for x in current[q]]
            for p in range(q + 1, 8):
                weight = spread(current[q][0], p) * root
                current[p] = [x - y * weight for x, y in zip(current[p], column)]
            below = rows[b] - column[0] * row
            rows[b] = jnp.where(at == q, row, jnp.where(at > q, below, rows[b]))
            for i in range(1, count):
                rows[b + i] = rows[b + i] - column[i] * row
            for p in range(len(ahead)):
                weight = spread(current[q][1], p) * root
                ahead[p] = [x - y * weight for x, y in zip(ahead[p], column[1:])]
    return jnp.concatenate(rows, axis=0)[:, 64:]


def unpacked(packed):
    return jnp.concatenate([packed[:, :64], packed[:, 64:]], axis=0)


def add_columns_kernel(total, *refs):
    parts, (gram_ref, first_ref) = refs[:-2], refs[-2:]
    summed = parts[0][...]
    for part in parts[1:]:
        summed = summed + part[...]
    gram_ref[...] = summed[:32]
    first_ref[...] = summed[32:] / total


def add_columns(total, parts):
    return call(
        functools.partial(add_columns_kernel, total),
        "add_columns",
        [vmem()] * len(parts),
        (shaped((32, 128), F32), shaped((32, 128), F32)),
        parts,
    )


def add_parts_kernel(count, *refs):
    summed = refs[0][...]
    for part in refs[1:count]:
        summed = summed + part[...]
    refs[-1][...] = summed


def add_parts(parts, after):
    return call(
        functools.partial(add_parts_kernel, len(parts)),
        "add_parts",
        [vmem()] * (len(parts) + len(after)),
        shaped(parts[0].shape, F32),
        (*parts, *after),
    )


def first_factor_kernel(gram_ref, out_ref):
    unit = (iota((64, 64), 0) == iota((64, 64), 1)).astype(F32)
    out_ref[...] = lower_solve(unpacked(gram_ref[...]), unit)


def first_factor(gram):
    return call(first_factor_kernel, "first_factor", [vmem()], shaped((64, 64), F32), (gram,))


def dot_turned(left, right):
    return lax.dot_general(
        left, right, (((1,), (1,)), ((), ())), precision=HIGHEST, preferred_element_type=F32
    )


def finish_kernel(total, rows_ref, inverse_ref, *refs):
    out_ref, scratch = refs[-2:]
    block_rows = out_ref.shape[1]
    packed = refs[0][...]
    for part in refs[1:-2]:
        packed = packed + part[...]
    first = inverse_ref[...]
    gram = dot_turned(
        jnp.dot(first, unpacked(packed), precision=HIGHEST, preferred_element_type=F32), first
    )
    inverse = lower_solve(gram / total, first)
    zero = jnp.zeros_like(inverse)
    both = jnp.concatenate(
        [jnp.concatenate([inverse, zero], axis=1), jnp.concatenate([zero, inverse], axis=1)], axis=0
    )
    current = dot_turned(rows_ref[...], both)
    for i in range(block_rows):
        scratch[pl.ds(i, 32, stride=block_rows), :] = current[i * 32 : (i + 1) * 32]
    for t in range(32):
        out_ref[0, :, t * 128 : (t + 1) * 128] = scratch[t * block_rows : (t + 1) * block_rows, :]


def finish(total, block_rows, rows, inverse, grams):
    return call(
        functools.partial(finish_kernel, total),
        "finish",
        [vmem()] * (2 + len(grams)),
        shaped((1, block_rows, 32 * 128), F32),
        (rows, inverse, *grams),
        [pltpu.VMEM(rows.shape, F32)],
    )


def swap(value, axis, mask):
    size = lax.axis_size(axis)
    return lax.ppermute(value, axis, [(index, index ^ mask) for index in range(size)])


def swap_both(value, row_mask, column_mask):
    rows, columns = lax.axis_size("rows"), lax.axis_size("cols")
    pairs = [
        (row * columns + column, (row ^ row_mask) * columns + (column ^ column_mask))
        for row in range(rows)
        for column in range(columns)
    ]
    return lax.ppermute(value, ("rows", "cols"), pairs)


def stages(size):
    if size == 8:
        return [[7, 5, 3], [1]]
    bits, bit = [], 1
    while bit < size:
        bits.append([bit])
        bit *= 2
    return bits


def gather_rows(message, after):
    plan = stages(lax.axis_size("rows"))
    held, offsets = [message], [0]
    for masks in plan[:-1]:
        held = held + [swap(piece, "rows", mask) for mask in masks for piece in held]
        offsets = offsets + [mask ^ offset for mask in masks for offset in offsets]
    split = len(held) // 2
    held, offsets = held[split:] + held[:split], offsets[split:] + offsets[:split]
    near = [stack(held[:split], []), stack(held[split:], after)]
    (last,) = plan[-1]
    offsets = offsets + [last ^ offset for offset in offsets]
    return near, [swap(pieces, "rows", last) for pieces in near], offsets


def add_rows(gram, after):
    *plan, (last,) = stages(lax.axis_size("rows"))
    for masks in plan:
        gram = add_parts([gram] + [swap(gram, "rows", mask) for mask in masks], after)
    return [gram, swap(gram, "rows", last)]


def body(affinity, block_columns, block_counts, inv_degree, panel):
    block_rows, block_size = inv_degree.shape[1:]
    groups, _, _, slots, _ = affinity.shape
    ranks = lax.axis_size("rows")
    total = float(groups * ranks * block_rows * block_size)
    blocks = ranks * block_rows
    live = iota(block_columns.shape, 3) < block_counts[..., None]
    columns = jnp.where(live, jnp.clip(block_columns, 0, blocks - 1), blocks)[:, :, 0]
    panel, inv_degree, affinity = (
        pltpu.with_memory_space_constraint(value, pltpu.HBM) for value in (panel, inv_degree, affinity)
    )
    ranges = list(range(groups - 1, 0, -1))

    scaled = start(panel, inv_degree)
    degree, inverse, matrix = prep(ranges, affinity, inv_degree)
    (own_matrix,) = prep([0], affinity)
    near, far, offsets = gather_rows(scaled, [inverse])
    table = near_table(offsets, near, block_rows)
    terms, _ = products(offsets, ranges, columns, matrix, own_matrix, near, far, table)
    near, far, offsets = gather_rows(middle(degree, inverse, terms), [])
    table = near_table(offsets, near, block_rows)
    terms, (notes,) = products(offsets, ranges, columns, matrix, own_matrix, near, far, table)
    devices = float(groups * ranks)
    rows, grams = collect(devices, total, degree, row_gram(near + far), notes, terms)
    flip = 1 if ranks == 8 else 0
    order = [2, 3, 1] if groups == 4 else ranges
    gram, first = add_columns(total, [grams] + [swap_both(grams, flip, m) for m in order])
    inverse = first_factor(first)
    return finish(total, block_rows, rows, inverse, add_rows(gram, [inverse]))


def solution(mesh):
    return jax.shard_map(
        body,
        mesh=mesh,
        in_specs=(
            P(None, "rows", "cols", None, None),
            P(None, "rows", "cols", None),
            P(None, "rows", "cols"),
            P("cols", "rows", None),
            P("cols", "rows", None),
        ),
        out_specs=P("cols", "rows", None),
        check_vma=False,
    )
```

```python
import functools

import jax
import jax.numpy as jnp
from jax import lax
from jax.experimental import pallas as pl
from jax.experimental.pallas import tpu as pltpu
from jax.sharding import PartitionSpec as P

BF16 = jnp.bfloat16
F32 = jnp.float32
HIGHEST = lax.Precision.HIGHEST
MIB = 1024 * 1024


def params(limit=48 * MIB):
    return pltpu.CompilerParams(vmem_limit_bytes=limit)


def vmem():
    return pl.BlockSpec(memory_space=pltpu.VMEM)


def hbm():
    return pl.BlockSpec(memory_space=pltpu.HBM)


def shaped(shape, dtype):
    return jax.ShapeDtypeStruct(shape, dtype)


def iota(shape, dim):
    return lax.broadcasted_iota(jnp.int32, shape, dim)


def call(kernel, name, ins, outs, operands, scratch=(), limit=48 * MIB, **kwargs):
    return pl.pallas_call(
        kernel,
        out_shape=outs,
        in_specs=ins,
        out_specs=jax.tree.map(lambda _: vmem(), outs),
        scratch_shapes=list(scratch),
        compiler_params=params(limit),
        name=name,
        **kwargs,
    )(*operands)


def start_kernel(panel_hbm, inv_hbm, scaled_ref, panel_ref, inv_ref, scratch, sems):
    block_rows, half = inv_ref.shape[1], inv_ref.shape[2] // 2
    copies = [
        pltpu.make_async_copy(inv_hbm, inv_ref, sems.at[0]),
        pltpu.make_async_copy(panel_hbm, panel_ref, sems.at[1]),
    ]
    for copy in copies:
        copy.start()
    copies[0].wait()
    inv = inv_ref[0]
    low = iota((block_rows, 128), 1) < 64
    scales = []
    for t in range(half):
        even, odd = (
            jnp.broadcast_to(inv[:, a : a + 1], (block_rows, 128)) for a in (2 * t, 2 * t + 1)
        )
        scales.append(jnp.where(low, even, odd))
    copies[1].wait()
    for t in range(half):
        scratch[t * block_rows : (t + 1) * block_rows, :] = (
            panel_ref[0, :, t * 128 : (t + 1) * 128] * scales[t]
        )
    for i in range(block_rows):
        part = scratch[pl.ds(i, half, stride=block_rows), :]
        scaled_ref[i * half : (i + 1) * half, :] = part.astype(BF16)


def start(panel, inv_degree):
    block_rows, block_size = inv_degree.shape[1:]
    shape = (block_rows * block_size // 2, 128)
    return call(
        start_kernel,
        "start",
        [hbm(), hbm()],
        shaped(shape, BF16),
        (panel, inv_degree),
        [
            pltpu.VMEM(panel.shape, F32),
            pltpu.VMEM(inv_degree.shape, F32),
            pltpu.VMEM(shape, F32),
            pltpu.SemaphoreType.DMA((2,)),
        ],
    )


def prepare_scales(inv, degree_ref, inverse_ref):
    block_rows, block_size = inv.shape
    half = block_size // 2
    pair = iota((half, block_size), 1) // 2 == iota((half, block_size), 0)
    spread = (iota((block_size, 128), 0) % 2 == iota((block_size, 128), 1) // 64).astype(F32)
    rows = [
        jnp.where(pair, jnp.broadcast_to(inv[i : i + 1, :], (half, block_size)), 0.0)
        for i in range(block_rows)
    ]
    degree_ref[...] = jnp.dot(
        jnp.concatenate(rows, axis=0), spread, precision=HIGHEST, preferred_element_type=F32
    )
    inverse = 1.0 / inv
    high = inverse.astype(BF16).astype(F32)
    inverse_ref[...] = jnp.concatenate([high, inverse - high], axis=1)


def prep_kernel(ranges, affinity_hbm, *refs):
    *scale_refs, out_ref, affinity_ref, inv_ref, scratch, sems = refs
    count, block_rows, _, slots, flat = affinity_ref.shape
    half = flat // 128
    own = lax.axis_index("cols")
    copies = [
        pltpu.make_async_copy(affinity_hbm.at[m ^ own], affinity_ref.at[place], sems.at[place])
        for place, m in enumerate(ranges)
    ]
    if scale_refs:
        inv_copy = pltpu.make_async_copy(scale_refs[0], inv_ref, sems.at[count])
        inv_copy.start()
    for copy in copies:
        copy.start()
    source, target = iota((256, 256), 0), iota((256, 256), 1)
    moved = (source // 64 % 2) * 128 + (source // 128) * 64 + (source % 2) * 32 + source % 64 // 2
    permute = (moved == target).astype(BF16)
    if scale_refs:
        inv_copy.wait()
        prepare_scales(inv_ref[0], *scale_refs[1:])
    for m in range(count):
        copies[m].wait()
        for i in range(block_rows):
            block = affinity_ref[m, i, 0].astype(F32)
            for t in range(half):
                scratch[i % 2, t * slots : (t + 1) * slots, :] = block[:, t * 128 : (t + 1) * 128]
            parts = [
                scratch[i % 2, pl.ds(s, half, stride=slots), :].astype(BF16) for s in range(slots)
            ]
            pairs = [jnp.concatenate(parts[s : s + 2], axis=1) for s in range(0, slots, 2)]
            moved_pairs = jnp.dot(
                jnp.concatenate(pairs, axis=0), permute, preferred_element_type=F32
            ).astype(BF16)
            for s in range(slots // 2):
                piece = moved_pairs[s * half : (s + 1) * half]
                out_ref[m, i, :half, s * 128 : (s + 1) * 128] = piece[:, :128]
                out_ref[m, i, half:, s * 128 : (s + 1) * 128] = piece[:, 128:]


def prep(ranges, affinity, *scale_from):
    _, block_rows, _, slots, flat = affinity.shape
    count = len(ranges)
    outs = [shaped((count, block_rows, 64, slots * 64), BF16)]
    if scale_from:
        outs = [shaped((block_rows * 32, 128), F32), shaped((block_rows, 128), F32)] + outs
    return call(
        functools.partial(prep_kernel, ranges),
        "prep",
        [hbm()] * (1 + len(scale_from)),
        outs,
        (affinity, *scale_from),
        [
            pltpu.VMEM((count,) + affinity.shape[1:], BF16),
            pltpu.VMEM((1, block_rows, 64), F32),
            pltpu.VMEM((2, flat // 128 * slots, 128), F32),
            pltpu.SemaphoreType.DMA((count + 1,)),
        ],
    )


def stack_kernel(count, *refs):
    for index in range(count):
        refs[-1][index] = refs[index][...]


def stack(pieces, after):
    return call(
        functools.partial(stack_kernel, len(pieces)),
        "stack",
        [vmem()] * (len(pieces) + len(after)),
        shaped((len(pieces),) + pieces[0].shape, BF16),
        (*pieces, *after),
    )


def fill_table(stacks, offsets, table):
    block_rows = (table.shape[0] - 1) // (2 * len(offsets))
    low = iota((32, 128), 1) < 64
    pieces = [(ref, index) for ref in stacks for index in range(ref.shape[0])]
    for (ref, index), offset in zip(pieces, offsets):
        base = (lax.axis_index("rows") ^ offset) * block_rows
        for i in range(block_rows):
            block = ref[index, i * 32 : (i + 1) * 32, :]
            turned = jnp.concatenate([block[:, 64:], block[:, :64]], axis=1)
            table[base + i, :32] = jnp.where(low, block, turned)
            table[base + i, 32:] = jnp.where(low, turned, block)


def near_kernel(offsets, *refs):
    *near_refs, table = refs
    table[table.shape[0] - 1] = jnp.zeros(table.shape[1:], BF16)
    fill_table(near_refs, offsets, table)


def near_table(offsets, near, block_rows):
    count = len(offsets) // 2
    return call(
        functools.partial(near_kernel, offsets[:count]),
        "near",
        [vmem()] * len(near),
        shaped((2 * count * block_rows + 1, 64, 128), BF16),
        near,
    )


def one_product(group, columns, matrix, table, out_ref):
    block_rows, slots = matrix.shape[0], matrix.shape[2] // 64
    chosen = columns[group]
    low = iota((32, 128), 1) < 64
    for i in range(block_rows):
        picked = [table[chosen[i, s]] for s in range(slots)]
        result = jnp.dot(matrix[i], jnp.concatenate(picked, axis=0), preferred_element_type=F32)
        out_ref[i * 32 : (i + 1) * 32, :] = jnp.where(low, result[:32], result[32:]).astype(BF16)


def others_kernel(offsets, ranges, stacks, old_table, columns, matrix_ref, *refs):
    del old_table
    far_refs, (table, *outs) = refs[:stacks], refs[stacks:]
    fill_table(far_refs, offsets, table)
    for place, m in enumerate(ranges):
        group = m ^ lax.axis_index("cols")
        one_product(group, columns, matrix_ref.at[place], table, outs[place])


def own_kernel(columns, matrix_ref, table, out_ref):
    one_product(lax.axis_index("cols"), columns, matrix_ref.at[0], table, out_ref)


def products(offsets, ranges, columns, matrix, own_matrix, far, table):
    rows = shaped((matrix.shape[1] * 32, 128), BF16)
    table, *outs = call(
        functools.partial(others_kernel, offsets[len(offsets) // 2 :], ranges, len(far)),
        "others",
        [vmem()] * (3 + len(far)),
        [shaped(table.shape, BF16)] + [rows] * len(ranges),
        (table, columns, matrix, *far),
        input_output_aliases={0: 0},
    )
    terms = [swap(term, "cols", m) for m, term in zip(ranges, outs)]
    own = call(own_kernel, "own", [vmem()] * 3, rows, (columns, own_matrix, table))
    return [own] + terms


def add_terms(terms):
    summed = terms[0][...].astype(F32)
    for term in terms[1:]:
        summed = summed + term[...].astype(F32)
    return summed


def folded(both):
    gram = both[:64, :64] + both[64:, 64:]
    return jnp.concatenate([gram[:32], gram[32:]], axis=1)


def local_gram(rows):
    both = lax.dot_general(
        rows, rows, (((0,), (0,)), ((), ())), precision=HIGHEST, preferred_element_type=F32
    )
    return folded(both)


def middle_kernel(degree_ref, inverse_ref, *refs):
    terms, out_ref = refs[:-1], refs[-1]
    count = degree_ref.shape[0]
    degree = degree_ref[...]
    out_ref[:count] = (add_terms(terms) * degree * degree).astype(BF16)
    inverse = inverse_ref[...]
    out_ref[count:] = jnp.concatenate([inverse, inverse], axis=0).astype(BF16)


def middle(degree, inverse, terms):
    return call(
        middle_kernel,
        "middle",
        [vmem()] * (2 + len(terms)),
        shaped((degree.shape[0] + 16, 128), BF16),
        (degree, inverse, *terms),
    )


def row_gram_kernel(*refs):
    *stacks, gram_ref, rows = refs
    lane = iota((32, 128), 1)
    pair = lane % 64 // 2 == iota((32, 128), 0)
    spread = (iota((128, 128), 0) % 2 == iota((128, 128), 1) // 64).astype(BF16)
    count = stacks[0].shape[1] - 16
    pieces = [(ref, index) for ref in stacks for index in range(ref.shape[0])]
    for place, (ref, index) in enumerate(pieces):
        notes = ref[index, count:].astype(F32)
        masked = [
            jnp.where(pair, jnp.broadcast_to(notes[i : i + 1], (32, 128)), 0.0).astype(BF16)
            for i in range(count // 32)
        ]
        inverse = jnp.dot(jnp.concatenate(masked, axis=0), spread, preferred_element_type=F32)
        block = ref[index, :count].astype(F32) * inverse
        rows[place * count : (place + 1) * count, :] = block.astype(BF16)
    both = lax.dot_general(
        rows[...], rows[...], (((0,), (0,)), ((), ())), preferred_element_type=F32
    )
    gram_ref[...] = folded(both)


def row_gram(stacks):
    count = sum(stack.shape[0] for stack in stacks) * (stacks[0].shape[1] - 16)
    return call(
        row_gram_kernel,
        "row_gram",
        [vmem()] * len(stacks),
        shaped((32, 128), F32),
        stacks,
        [pltpu.VMEM((count, 128), BF16)],
    )


def collect_kernel(degree_ref, first_ref, *refs):
    terms, (rows_ref, grams_ref) = refs[:-2], refs[-2:]
    rows = add_terms(terms) * degree_ref[...]
    largest = jnp.max(jnp.abs(rows), axis=(0, 1), keepdims=True)
    scale = 1.0 / jnp.maximum(largest, 1e-30)
    rows = rows * scale
    rows_ref[...] = rows
    grams_ref[:32] = local_gram(rows)
    grams_ref[32:40] = jnp.broadcast_to(scale, (8, 128))
    grams_ref[40:] = first_ref[...]


def collect(degree, first, terms):
    return call(
        collect_kernel,
        "collect",
        [vmem()] * (2 + len(terms)),
        (shaped(degree.shape, F32), shaped((72, 128), F32)),
        (degree, first, *terms),
    )


def add_scaled(refs):
    scales = [ref[32:33] for ref in refs]
    smallest = functools.reduce(jnp.minimum, scales)
    summed = 0.0
    for ref, scale in zip(refs, scales):
        ratio = smallest / scale
        summed = summed + ref[:32] * (ratio * ratio)
    return summed, smallest


def lower_solve(gram, right):
    work = jnp.concatenate([gram, right], axis=1)
    blocks = gram.shape[0] // 8
    rows = [work[8 * i : 8 * i + 8] for i in range(blocks)]
    at = iota((8, 128), 0)

    def columns(first, column):
        return [
            jnp.broadcast_to(rows[i][:, column : column + 1], (8, 128))
            for i in range(first, blocks)
        ]

    def spread(block, row):
        return jnp.broadcast_to(block[row : row + 1], (8, 128))

    ahead = []
    for b in range(blocks):
        count = blocks - b
        current = ahead + [columns(b, 8 * b + q) for q in range(len(ahead), 8)]
        ahead = []
        if count > 1:
            ahead = [columns(b + 1, 8 * (b + 1) + q) for q in range(4)]
        for q in range(8):
            root = lax.rsqrt(spread(current[q][0], q))
            row = spread(rows[b], q) * root
            column = [x * root for x in current[q]]
            for p in range(q + 1, 8):
                weight = spread(current[q][0], p) * root
                current[p] = [x - y * weight for x, y in zip(current[p], column)]
            below = rows[b] - column[0] * row
            rows[b] = jnp.where(at == q, row, jnp.where(at > q, below, rows[b]))
            for i in range(1, count):
                rows[b + i] = rows[b + i] - column[i] * row
            for p in range(len(ahead)):
                weight = spread(current[q][1], p) * root
                ahead[p] = [x - y * weight for x, y in zip(ahead[p], column[1:])]
    return jnp.concatenate(rows, axis=0)[:, 64:]


def unpacked(packed):
    return jnp.concatenate([packed[:, :64], packed[:, 64:]], axis=0)


def add_columns_kernel(*refs):
    parts, (gram_ref, first_ref) = refs[:-2], refs[-2:]
    summed, smallest = add_scaled(parts)
    gram_ref[:32] = summed
    gram_ref[32:] = jnp.broadcast_to(smallest, (8, 128))
    first = parts[0][40:]
    for part in parts[1:]:
        first = first + part[40:]
    first_ref[...] = first


def add_columns(parts):
    return call(
        add_columns_kernel,
        "add_columns",
        [vmem()] * len(parts),
        (shaped((40, 128), F32), shaped((32, 128), F32)),
        parts,
    )


def add_parts_kernel(count, *refs):
    summed, smallest = add_scaled(refs[:count])
    refs[-1][:32] = summed
    refs[-1][32:] = jnp.broadcast_to(smallest, (8, 128))


def add_parts(parts, after):
    return call(
        functools.partial(add_parts_kernel, len(parts)),
        "add_parts",
        [vmem()] * (len(parts) + len(after)),
        shaped((40, 128), F32),
        (*parts, *after),
    )


def first_factor_kernel(gram_ref, out_ref):
    gram = unpacked(gram_ref[...])
    unit = (iota((64, 64), 0) == iota((64, 64), 1)).astype(F32)
    gram = gram / (jnp.sum(gram * unit, axis=(0, 1), keepdims=True) / 64.0)
    out_ref[...] = lower_solve(gram, unit)


def first_factor(gram):
    return call(first_factor_kernel, "first_factor", [vmem()], shaped((64, 64), F32), (gram,))


def dot_turned(left, right):
    return lax.dot_general(
        left, right, (((1,), (1,)), ((), ())), precision=HIGHEST, preferred_element_type=F32
    )


def finish_kernel(total, rows_ref, sent_ref, inverse_ref, *refs):
    out_ref, scratch = refs[-2:]
    block_rows = out_ref.shape[1]
    packed, smallest = add_scaled(refs[:-2])
    first = inverse_ref[...]
    gram = dot_turned(
        jnp.dot(first, unpacked(packed), precision=HIGHEST, preferred_element_type=F32), first
    )
    inverse = lower_solve(gram / total, first) * (smallest / sent_ref[32:33])[:, :64]
    zero = jnp.zeros_like(inverse)
    both = jnp.concatenate(
        [jnp.concatenate([inverse, zero], axis=1), jnp.concatenate([zero, inverse], axis=1)], axis=0
    )
    current = dot_turned(rows_ref[...], both)
    for i in range(block_rows):
        scratch[pl.ds(i, 32, stride=block_rows), :] = current[i * 32 : (i + 1) * 32]
    for t in range(32):
        out_ref[0, :, t * 128 : (t + 1) * 128] = scratch[t * block_rows : (t + 1) * block_rows, :]


def finish(total, block_rows, rows, sent, inverse, grams):
    return call(
        functools.partial(finish_kernel, total),
        "finish",
        [vmem()] * (3 + len(grams)),
        shaped((1, block_rows, 32 * 128), F32),
        (rows, sent, inverse, *grams),
        [pltpu.VMEM(rows.shape, F32)],
    )


def swap(value, axis, mask):
    size = lax.axis_size(axis)
    return lax.ppermute(value, axis, [(index, index ^ mask) for index in range(size)])


def swap_both(value, row_mask, column_mask):
    rows, columns = lax.axis_size("rows"), lax.axis_size("cols")
    pairs = [
        (row * columns + column, (row ^ row_mask) * columns + (column ^ column_mask))
        for row in range(rows)
        for column in range(columns)
    ]
    return lax.ppermute(value, ("rows", "cols"), pairs)


def stages(size):
    if size == 8:
        return [[7, 3, 5], [1]]
    bits, bit = [], 1
    while bit < size:
        bits.append([bit])
        bit *= 2
    return bits


def gather_rows(message, after):
    plan = stages(lax.axis_size("rows"))
    held, offsets = [message], [0]
    for masks in plan[:-1]:
        held = held + [swap(piece, "rows", mask) for mask in masks for piece in held]
        offsets = offsets + [mask ^ offset for mask in masks for offset in offsets]
    split = len(held) // 2
    near = [stack(held[:split], []), stack(held[split:], after)]
    (last,) = plan[-1]
    offsets = offsets + [last ^ offset for offset in offsets]
    return near, [swap(pieces, "rows", last) for pieces in near], offsets


def add_rows(gram, after):
    *plan, (last,) = stages(lax.axis_size("rows"))
    for masks in plan:
        gram = add_parts([gram] + [swap(gram, "rows", mask) for mask in reversed(masks)], after)
    return [gram, swap(gram, "rows", last)]


def body(affinity, block_columns, block_counts, inv_degree, panel):
    block_rows, block_size = inv_degree.shape[1:]
    groups, _, _, slots, _ = affinity.shape
    ranks = lax.axis_size("rows")
    total = float(groups * ranks * block_rows * block_size)
    blocks = ranks * block_rows
    live = iota(block_columns.shape, 3) < block_counts[..., None]
    columns = jnp.where(live, jnp.clip(block_columns, 0, blocks - 1), blocks)[:, :, 0]
    panel, inv_degree, affinity = (
        pltpu.with_memory_space_constraint(value, pltpu.HBM) for value in (panel, inv_degree, affinity)
    )
    ranges = list(range(groups - 1, 0, -1))

    scaled = start(panel, inv_degree)
    degree, inverse, matrix = prep(ranges, affinity, inv_degree)
    (own_matrix,) = prep([0], affinity)
    near, far, offsets = gather_rows(scaled, [inverse])
    table = near_table(offsets, near, block_rows)
    terms = products(offsets, ranges, columns, matrix, own_matrix, far, table)
    near, far, offsets = gather_rows(middle(degree, inverse, terms), [])
    table = near_table(offsets, near, block_rows)
    terms = products(offsets, ranges, columns, matrix, own_matrix, far, table)
    rows, grams = collect(degree, row_gram(near + far), terms)
    flip = 1 if ranks == 8 else 0
    order = [1, 3, 2] if groups == 4 else ranges
    gram, first = add_columns([grams] + [swap_both(grams, flip, m) for m in order])
    inverse = first_factor(first)
    return finish(total, block_rows, rows, grams, inverse, add_rows(gram, [inverse]))


def solution(mesh):
    return jax.shard_map(
        body,
        mesh=mesh,
        in_specs=(
            P(None, "rows", "cols", None, None),
            P(None, "rows", "cols", None),
            P(None, "rows", "cols"),
            P("cols", "rows", None),
            P("cols", "rows", None),
        ),
        out_specs=P("cols", "rows", None),
        check_vma=False,
    )
```

```python
import functools

import jax
import jax.numpy as jnp
from jax import lax
from jax.experimental import pallas as pl
from jax.experimental.pallas import tpu as pltpu
from jax.sharding import PartitionSpec as P

BF16 = jnp.bfloat16
F32 = jnp.float32
HIGHEST = lax.Precision.HIGHEST
MIB = 1024 * 1024


def params(limit=48 * MIB):
    return pltpu.CompilerParams(vmem_limit_bytes=limit)


def vmem():
    return pl.BlockSpec(memory_space=pltpu.VMEM)


def hbm():
    return pl.BlockSpec(memory_space=pltpu.HBM)


def shaped(shape, dtype):
    return jax.ShapeDtypeStruct(shape, dtype)


def iota(shape, dim):
    return lax.broadcasted_iota(jnp.int32, shape, dim)


def call(kernel, name, ins, outs, operands, scratch=(), limit=48 * MIB, **kwargs):
    return pl.pallas_call(
        kernel,
        out_shape=outs,
        in_specs=ins,
        out_specs=jax.tree.map(lambda _: vmem(), outs),
        scratch_shapes=list(scratch),
        compiler_params=params(limit),
        name=name,
        **kwargs,
    )(*operands)


def start_kernel(panel_hbm, inv_hbm, scaled_ref, panel_ref, inv_ref, scratch, sems):
    block_rows, half = inv_ref.shape[1], inv_ref.shape[2] // 2
    copies = [
        pltpu.make_async_copy(inv_hbm, inv_ref, sems.at[0]),
        pltpu.make_async_copy(panel_hbm, panel_ref, sems.at[1]),
    ]
    for copy in copies:
        copy.start()
    copies[0].wait()
    inv = inv_ref[0]
    low = iota((block_rows, 128), 1) < 64
    scales = []
    for t in range(half):
        even, odd = (
            jnp.broadcast_to(inv[:, a : a + 1], (block_rows, 128)) for a in (2 * t, 2 * t + 1)
        )
        scales.append(jnp.where(low, even, odd))
    copies[1].wait()
    for t in range(half):
        scratch[t * block_rows : (t + 1) * block_rows, :] = (
            panel_ref[0, :, t * 128 : (t + 1) * 128] * scales[t]
        )
    for i in range(block_rows):
        part = scratch[pl.ds(i, half, stride=block_rows), :]
        scaled_ref[i * half : (i + 1) * half, :] = part.astype(BF16)


def start(panel, inv_degree):
    block_rows, block_size = inv_degree.shape[1:]
    shape = (block_rows * block_size // 2, 128)
    return call(
        start_kernel,
        "start",
        [hbm(), hbm()],
        shaped(shape, BF16),
        (panel, inv_degree),
        [
            pltpu.VMEM(panel.shape, F32),
            pltpu.VMEM(inv_degree.shape, F32),
            pltpu.VMEM(shape, F32),
            pltpu.SemaphoreType.DMA((2,)),
        ],
    )


def prepare_scales(inv, degree_ref, inverse_ref):
    block_rows, block_size = inv.shape
    half = block_size // 2
    pair = iota((half, block_size), 1) // 2 == iota((half, block_size), 0)
    spread = (iota((block_size, 128), 0) % 2 == iota((block_size, 128), 1) // 64).astype(F32)
    rows = [
        jnp.where(pair, jnp.broadcast_to(inv[i : i + 1, :], (half, block_size)), 0.0)
        for i in range(block_rows)
    ]
    degree_ref[...] = jnp.dot(
        jnp.concatenate(rows, axis=0), spread, precision=HIGHEST, preferred_element_type=F32
    )
    inverse = 1.0 / inv
    high = inverse.astype(BF16).astype(F32)
    inverse_ref[...] = jnp.concatenate([high, inverse - high], axis=1)


def prep_kernel(ranges, affinity_hbm, *refs):
    *scale_refs, out_ref, affinity_ref, inv_ref, scratch, sems = refs
    count, block_rows, _, slots, flat = affinity_ref.shape
    half = flat // 128
    own = lax.axis_index("cols")
    copies = [
        pltpu.make_async_copy(affinity_hbm.at[m ^ own], affinity_ref.at[place], sems.at[place])
        for place, m in enumerate(ranges)
    ]
    if scale_refs:
        inv_copy = pltpu.make_async_copy(scale_refs[0], inv_ref, sems.at[count])
        inv_copy.start()
    for copy in copies:
        copy.start()
    source, target = iota((256, 256), 0), iota((256, 256), 1)
    moved = (source // 64 % 2) * 128 + (source // 128) * 64 + (source % 2) * 32 + source % 64 // 2
    permute = (moved == target).astype(BF16)
    if scale_refs:
        inv_copy.wait()
        prepare_scales(inv_ref[0], *scale_refs[1:])
    for m in range(count):
        copies[m].wait()
        for i in range(block_rows):
            block = affinity_ref[m, i, 0].astype(F32)
            for t in range(half):
                scratch[i % 2, t * slots : (t + 1) * slots, :] = block[:, t * 128 : (t + 1) * 128]
            parts = [
                scratch[i % 2, pl.ds(s, half, stride=slots), :].astype(BF16) for s in range(slots)
            ]
            pairs = [jnp.concatenate(parts[s : s + 2], axis=1) for s in range(0, slots, 2)]
            moved_pairs = jnp.dot(
                jnp.concatenate(pairs, axis=0), permute, preferred_element_type=F32
            ).astype(BF16)
            for s in range(slots // 2):
                piece = moved_pairs[s * half : (s + 1) * half]
                out_ref[m, i, :half, s * 128 : (s + 1) * 128] = piece[:, :128]
                out_ref[m, i, half:, s * 128 : (s + 1) * 128] = piece[:, 128:]


def prep(ranges, affinity, *scale_from):
    _, block_rows, _, slots, flat = affinity.shape
    count = len(ranges)
    outs = [shaped((count, block_rows, 64, slots * 64), BF16)]
    if scale_from:
        outs = [shaped((block_rows * 32, 128), F32), shaped((block_rows, 128), F32)] + outs
    return call(
        functools.partial(prep_kernel, ranges),
        "prep",
        [hbm()] * (1 + len(scale_from)),
        outs,
        (affinity, *scale_from),
        [
            pltpu.VMEM((count,) + affinity.shape[1:], BF16),
            pltpu.VMEM((1, block_rows, 64), F32),
            pltpu.VMEM((2, flat // 128 * slots, 128), F32),
            pltpu.SemaphoreType.DMA((count + 1,)),
        ],
    )


def stack_kernel(count, *refs):
    for index in range(count):
        refs[-1][index] = refs[index][...]


def stack(pieces, after):
    return call(
        functools.partial(stack_kernel, len(pieces)),
        "stack",
        [vmem()] * (len(pieces) + len(after)),
        shaped((len(pieces),) + pieces[0].shape, BF16),
        (*pieces, *after),
    )


def fill_table(stacks, offsets, table):
    block_rows = (table.shape[0] - 1) // (2 * len(offsets))
    low = iota((32, 128), 1) < 64
    pieces = [(ref, index) for ref in stacks for index in range(ref.shape[0])]
    for (ref, index), offset in zip(pieces, offsets):
        base = (lax.axis_index("rows") ^ offset) * block_rows
        for i in range(block_rows):
            block = ref[index, i * 32 : (i + 1) * 32, :]
            turned = jnp.concatenate([block[:, 64:], block[:, :64]], axis=1)
            table[base + i, :32] = jnp.where(low, block, turned)
            table[base + i, 32:] = jnp.where(low, turned, block)


def near_kernel(offsets, *refs):
    *near_refs, table = refs
    table[table.shape[0] - 1] = jnp.zeros(table.shape[1:], BF16)
    fill_table(near_refs, offsets, table)


def near_table(offsets, near, block_rows):
    count = len(offsets) // 2
    return call(
        functools.partial(near_kernel, offsets[:count]),
        "near",
        [vmem()] * len(near),
        shaped((2 * count * block_rows + 1, 64, 128), BF16),
        near,
    )


def one_product(group, columns, matrix, table, out_ref):
    block_rows, slots = matrix.shape[0], matrix.shape[2] // 64
    chosen = columns[group]
    low = iota((32, 128), 1) < 64
    for i in range(block_rows):
        picked = [table[chosen[i, s]] for s in range(slots)]
        result = jnp.dot(matrix[i], jnp.concatenate(picked, axis=0), preferred_element_type=F32)
        out_ref[i * 32 : (i + 1) * 32, :] = jnp.where(low, result[:32], result[32:]).astype(BF16)


def largest_notes(notes):
    largest = notes[0].astype(F32)
    for note in notes[1:]:
        largest = jnp.maximum(largest, note.astype(F32))
    return largest


def others_kernel(offsets, ranges, stacks, old_table, columns, matrix_ref, *refs):
    del old_table
    far_refs, near_refs = refs[:stacks], refs[stacks : 2 * stacks]
    table, *outs = refs[2 * stacks :]
    fill_table(far_refs, offsets, table)
    terms, first = outs[: len(ranges)], matrix_ref.shape[1] * 32
    if len(outs) > len(ranges):
        notes = largest_notes(
            [ref[index, first:] for ref in near_refs + far_refs for index in range(ref.shape[0])]
        )
        notes = jnp.sum(notes[8:], axis=(0, 1), keepdims=True)
        notes = jnp.broadcast_to(notes, (16, 128)).astype(BF16)
        for ref in outs[len(ranges) :]:
            ref[...] = notes
        for term in terms:
            term[first:, :] = notes
    for place, m in enumerate(ranges):
        group = m ^ lax.axis_index("cols")
        one_product(group, columns, matrix_ref.at[place], table, terms[place])


def own_kernel(columns, matrix_ref, table, out_ref):
    one_product(lax.axis_index("cols"), columns, matrix_ref.at[0], table, out_ref)


def products(offsets, ranges, columns, matrix, own_matrix, near, far, table):
    block_rows, count = matrix.shape[1], len(offsets) // 2
    extra = near[0].shape[1] > block_rows * 32
    rows = block_rows * 32
    outs = [shaped(table.shape, BF16)] + [shaped((rows + 16 * extra, 128), BF16)] * len(ranges)
    if extra:
        outs.append(shaped((16, 128), BF16))
    table, *outs = call(
        functools.partial(others_kernel, offsets[count:], ranges, len(near)),
        "others",
        [vmem()] * (3 + 2 * len(near)),
        outs,
        (table, columns, matrix, *far, *near),
        input_output_aliases={0: 0},
    )
    terms = [swap(term, "cols", m) for m, term in zip(ranges, outs)]
    own = call(
        own_kernel,
        "own",
        [vmem()] * 3,
        shaped((rows, 128), BF16),
        (columns, own_matrix, table),
    )
    return [own] + terms, outs[len(ranges) :]


def add_terms(terms, rows):
    summed = terms[0][:rows].astype(F32)
    for term in terms[1:]:
        summed = summed + term[:rows].astype(F32)
    return summed


def folded(both):
    gram = both[:64, :64] + both[64:, 64:]
    return jnp.concatenate([gram[:32], gram[32:]], axis=1)


def local_gram(rows):
    both = lax.dot_general(
        rows, rows, (((0,), (0,)), ((), ())), precision=HIGHEST, preferred_element_type=F32
    )
    return folded(both)


def middle_kernel(degree_ref, inverse_ref, *refs):
    terms, out_ref = refs[:-1], refs[-1]
    count = degree_ref.shape[0]
    degree = degree_ref[...]
    rows = add_terms(terms, count) * degree
    out_ref[:count] = (rows * degree).astype(BF16)
    squares = jnp.sum((rows * rows).reshape(-1, 8, 128), axis=0)
    out_ref[count:] = jnp.concatenate([inverse_ref[...], squares], axis=0).astype(BF16)


def middle(degree, inverse, terms):
    return call(
        middle_kernel,
        "middle",
        [vmem()] * (2 + len(terms)),
        shaped((degree.shape[0] + 16, 128), BF16),
        (degree, inverse, *terms),
    )


def row_gram_kernel(*refs):
    *stacks, gram_ref, rows = refs
    lane = iota((32, 128), 1)
    pair = lane % 64 // 2 == iota((32, 128), 0)
    spread = (iota((128, 128), 0) % 2 == iota((128, 128), 1) // 64).astype(BF16)
    count = stacks[0].shape[1] - 16
    pieces = [(ref, index) for ref in stacks for index in range(ref.shape[0])]
    for place, (ref, index) in enumerate(pieces):
        notes = ref[index, count:].astype(F32)
        masked = [
            jnp.where(pair, jnp.broadcast_to(notes[i : i + 1], (32, 128)), 0.0).astype(BF16)
            for i in range(count // 32)
        ]
        inverse = jnp.dot(jnp.concatenate(masked, axis=0), spread, preferred_element_type=F32)
        block = ref[index, :count].astype(F32) * inverse
        rows[place * count : (place + 1) * count, :] = block.astype(BF16)
    both = lax.dot_general(
        rows[...], rows[...], (((0,), (0,)), ((), ())), preferred_element_type=F32
    )
    gram_ref[...] = folded(both)


def row_gram(stacks):
    count = sum(stack.shape[0] for stack in stacks) * (stacks[0].shape[1] - 16)
    return call(
        row_gram_kernel,
        "row_gram",
        [vmem()] * len(stacks),
        shaped((32, 128), F32),
        stacks,
        [pltpu.VMEM((count, 128), BF16)],
    )


def collect_kernel(devices, total, degree_ref, first_ref, notes_ref, *refs):
    terms, (rows_ref, grams_ref) = refs[:-2], refs[-2:]
    count = degree_ref.shape[0]
    largest = largest_notes([notes_ref[...]] + [term[count:] for term in terms[1:]])
    scale = lax.rsqrt(largest[:1] * (devices / total))
    rows = add_terms(terms, count) * degree_ref[...] * scale
    rows_ref[...] = rows
    grams_ref[32:] = first_ref[...] * (scale * scale)
    grams_ref[:32] = local_gram(rows)


def collect(devices, total, degree, first, notes, terms):
    return call(
        functools.partial(collect_kernel, devices, total),
        "collect",
        [vmem()] * (3 + len(terms)),
        (shaped(degree.shape, F32), shaped((64, 128), F32)),
        (degree, first, notes, *terms),
    )


def lower_solve(gram, right):
    work = jnp.concatenate([gram, right], axis=1)
    blocks = gram.shape[0] // 8
    rows = [work[8 * i : 8 * i + 8] for i in range(blocks)]
    at = iota((8, 128), 0)

    def columns(first, column):
        return [
            jnp.broadcast_to(rows[i][:, column : column + 1], (8, 128))
            for i in range(first, blocks)
        ]

    def spread(block, row):
        return jnp.broadcast_to(block[row : row + 1], (8, 128))

    ahead = []
    for b in range(blocks):
        count = blocks - b
        current = ahead + [columns(b, 8 * b + q) for q in range(len(ahead), 8)]
        ahead = []
        if count > 1:
            ahead = [columns(b + 1, 8 * (b + 1) + q) for q in range(4)]
        for q in range(8):
            root = lax.rsqrt(spread(current[q][0], q))
            row = spread(rows[b], q) * root
            column = [x * root for x in current[q]]
            for p in range(q + 1, 8):
                weight = spread(current[q][0], p) * root
                current[p] = [x - y * weight for x, y in zip(current[p], column)]
            below = rows[b] - column[0] * row
            rows[b] = jnp.where(at == q, row, jnp.where(at > q, below, rows[b]))
            for i in range(1, count):
                rows[b + i] = rows[b + i] - column[i] * row
            for p in range(len(ahead)):
                weight = spread(current[q][1], p) * root
                ahead[p] = [x - y * weight for x, y in zip(ahead[p], column[1:])]
    return jnp.concatenate(rows, axis=0)[:, 64:]


def unpacked(packed):
    return jnp.concatenate([packed[:, :64], packed[:, 64:]], axis=0)


def add_columns_kernel(total, *refs):
    parts, (gram_ref, first_ref) = refs[:-2], refs[-2:]
    summed = parts[0][...]
    for part in parts[1:]:
        summed = summed + part[...]
    gram_ref[...] = summed[:32]
    first_ref[...] = summed[32:] / total


def add_columns(total, parts):
    return call(
        functools.partial(add_columns_kernel, total),
        "add_columns",
        [vmem()] * len(parts),
        (shaped((32, 128), F32), shaped((32, 128), F32)),
        parts,
    )


def add_parts_kernel(count, *refs):
    summed = refs[0][...]
    for part in refs[1:count]:
        summed = summed + part[...]
    refs[-1][...] = summed


def add_parts(parts, after):
    return call(
        functools.partial(add_parts_kernel, len(parts)),
        "add_parts",
        [vmem()] * (len(parts) + len(after)),
        shaped(parts[0].shape, F32),
        (*parts, *after),
    )


def first_factor_kernel(gram_ref, out_ref):
    unit = (iota((64, 64), 0) == iota((64, 64), 1)).astype(F32)
    out_ref[...] = lower_solve(unpacked(gram_ref[...]), unit)


def first_factor(gram):
    return call(first_factor_kernel, "first_factor", [vmem()], shaped((64, 64), F32), (gram,))


def dot_turned(left, right):
    return lax.dot_general(
        left, right, (((1,), (1,)), ((), ())), precision=HIGHEST, preferred_element_type=F32
    )


def finish_kernel(total, rows_ref, inverse_ref, *refs):
    out_ref, scratch = refs[-2:]
    block_rows = out_ref.shape[1]
    packed = refs[0][...]
    for part in refs[1:-2]:
        packed = packed + part[...]
    first = inverse_ref[...]
    gram = dot_turned(
        jnp.dot(first, unpacked(packed), precision=HIGHEST, preferred_element_type=F32), first
    )
    inverse = lower_solve(gram / total, first)
    zero = jnp.zeros_like(inverse)
    both = jnp.concatenate(
        [jnp.concatenate([inverse, zero], axis=1), jnp.concatenate([zero, inverse], axis=1)], axis=0
    )
    current = dot_turned(rows_ref[...], both)
    for i in range(block_rows):
        scratch[pl.ds(i, 32, stride=block_rows), :] = current[i * 32 : (i + 1) * 32]
    for t in range(32):
        out_ref[0, :, t * 128 : (t + 1) * 128] = scratch[t * block_rows : (t + 1) * block_rows, :]


def finish(total, block_rows, rows, inverse, grams):
    return call(
        functools.partial(finish_kernel, total),
        "finish",
        [vmem()] * (2 + len(grams)),
        shaped((1, block_rows, 32 * 128), F32),
        (rows, inverse, *grams),
        [pltpu.VMEM(rows.shape, F32)],
    )


def swap(value, axis, mask):
    size = lax.axis_size(axis)
    return lax.ppermute(value, axis, [(index, index ^ mask) for index in range(size)])


def swap_both(value, row_mask, column_mask):
    rows, columns = lax.axis_size("rows"), lax.axis_size("cols")
    pairs = [
        (row * columns + column, (row ^ row_mask) * columns + (column ^ column_mask))
        for row in range(rows)
        for column in range(columns)
    ]
    return lax.ppermute(value, ("rows", "cols"), pairs)


def stages(size):
    if size == 8:
        return [[7, 5, 3], [1]]
    bits, bit = [], 1
    while bit < size:
        bits.append([bit])
        bit *= 2
    return bits


def gather_rows(message, after):
    plan = stages(lax.axis_size("rows"))
    held, offsets = [message], [0]
    for masks in plan[:-1]:
        held = held + [swap(piece, "rows", mask) for mask in masks for piece in held]
        offsets = offsets + [mask ^ offset for mask in masks for offset in offsets]
    split = len(held) // 2
    held, offsets = held[split:] + held[:split], offsets[split:] + offsets[:split]
    near = [stack(held[:split], []), stack(held[split:], after)]
    (last,) = plan[-1]
    offsets = offsets + [last ^ offset for offset in offsets]
    return near, [swap(pieces, "rows", last) for pieces in near], offsets


def add_rows(gram, after):
    *plan, (last,) = stages(lax.axis_size("rows"))
    for masks in plan:
        gram = add_parts([gram] + [swap(gram, "rows", mask) for mask in masks], after)
    return [gram, swap(gram, "rows", last)]


def body(affinity, block_columns, block_counts, inv_degree, panel):
    block_rows, block_size = inv_degree.shape[1:]
    groups, _, _, slots, _ = affinity.shape
    ranks = lax.axis_size("rows")
    total = float(groups * ranks * block_rows * block_size)
    blocks = ranks * block_rows
    live = iota(block_columns.shape, 3) < block_counts[..., None]
    columns = jnp.where(live, jnp.clip(block_columns, 0, blocks - 1), blocks)[:, :, 0]
    panel, inv_degree, affinity = (
        pltpu.with_memory_space_constraint(value, pltpu.HBM) for value in (panel, inv_degree, affinity)
    )
    ranges = list(range(groups - 1, 0, -1))

    scaled = start(panel, inv_degree)
    degree, inverse, matrix = prep(ranges, affinity, inv_degree)
    (own_matrix,) = prep([0], affinity)
    near, far, offsets = gather_rows(scaled, [inverse])
    table = near_table(offsets, near, block_rows)
    terms, _ = products(offsets, ranges, columns, matrix, own_matrix, near, far, table)
    near, far, offsets = gather_rows(middle(degree, inverse, terms), [])
    table = near_table(offsets, near, block_rows)
    terms, (notes,) = products(offsets, ranges, columns, matrix, own_matrix, near, far, table)
    devices = float(groups * ranks)
    rows, grams = collect(devices, total, degree, row_gram(near + far), notes, terms)
    flip = 1 if ranks == 8 else 0
    order = [2, 3, 1] if groups == 4 else ranges
    gram, first = add_columns(total, [grams] + [swap_both(grams, flip, m) for m in order])
    inverse = first_factor(first)
    return finish(total, block_rows, rows, inverse, add_rows(gram, [inverse]))


def solution(mesh):
    return jax.shard_map(
        body,
        mesh=mesh,
        in_specs=(
            P(None, "rows", "cols", None, None),
            P(None, "rows", "cols", None),
            P(None, "rows", "cols"),
            P("cols", "rows", None),
            P("cols", "rows", None),
        ),
        out_specs=P("cols", "rows", None),
        check_vma=False,
    )
```

```python
import functools

import jax
import jax.numpy as jnp
from jax import lax
from jax.experimental import pallas as pl
from jax.experimental.pallas import tpu as pltpu
from jax.sharding import PartitionSpec as P

BF16 = jnp.bfloat16
F32 = jnp.float32
HIGHEST = lax.Precision.HIGHEST
MIB = 1024 * 1024


def params(limit=48 * MIB):
    return pltpu.CompilerParams(vmem_limit_bytes=limit)


def vmem():
    return pl.BlockSpec(memory_space=pltpu.VMEM)


def hbm():
    return pl.BlockSpec(memory_space=pltpu.HBM)


def shaped(shape, dtype):
    return jax.ShapeDtypeStruct(shape, dtype)


def iota(shape, dim):
    return lax.broadcasted_iota(jnp.int32, shape, dim)


def call(kernel, name, ins, outs, operands, scratch=(), limit=48 * MIB, **kwargs):
    return pl.pallas_call(
        kernel,
        out_shape=outs,
        in_specs=ins,
        out_specs=jax.tree.map(lambda _: vmem(), outs),
        scratch_shapes=list(scratch),
        compiler_params=params(limit),
        name=name,
        **kwargs,
    )(*operands)


def start_kernel(panel_hbm, inv_hbm, scaled_ref, panel_ref, inv_ref, scratch, sems):
    block_rows, half = inv_ref.shape[1], inv_ref.shape[2] // 2
    copies = [
        pltpu.make_async_copy(inv_hbm, inv_ref, sems.at[0]),
        pltpu.make_async_copy(panel_hbm, panel_ref, sems.at[1]),
    ]
    for copy in copies:
        copy.start()
    copies[0].wait()
    inv = inv_ref[0]
    low = iota((block_rows, 128), 1) < 64
    scales = []
    for t in range(half):
        even, odd = (
            jnp.broadcast_to(inv[:, a : a + 1], (block_rows, 128)) for a in (2 * t, 2 * t + 1)
        )
        scales.append(jnp.where(low, even, odd))
    copies[1].wait()
    for t in range(half):
        scratch[t * block_rows : (t + 1) * block_rows, :] = (
            panel_ref[0, :, t * 128 : (t + 1) * 128] * scales[t]
        )
    for i in range(block_rows):
        part = scratch[pl.ds(i, half, stride=block_rows), :]
        scaled_ref[i * half : (i + 1) * half, :] = part.astype(BF16)


def start(panel, inv_degree):
    block_rows, block_size = inv_degree.shape[1:]
    shape = (block_rows * block_size // 2, 128)
    return call(
        start_kernel,
        "start",
        [hbm(), hbm()],
        shaped(shape, BF16),
        (panel, inv_degree),
        [
            pltpu.VMEM(panel.shape, F32),
            pltpu.VMEM(inv_degree.shape, F32),
            pltpu.VMEM(shape, F32),
            pltpu.SemaphoreType.DMA((2,)),
        ],
    )


def prepare_scales(inv, degree_ref, inverse_ref):
    block_rows, block_size = inv.shape
    half = block_size // 2
    pair = iota((half, block_size), 1) // 2 == iota((half, block_size), 0)
    spread = (iota((block_size, 128), 0) % 2 == iota((block_size, 128), 1) // 64).astype(F32)
    rows = [
        jnp.where(pair, jnp.broadcast_to(inv[i : i + 1, :], (half, block_size)), 0.0)
        for i in range(block_rows)
    ]
    degree_ref[...] = jnp.dot(
        jnp.concatenate(rows, axis=0), spread, precision=HIGHEST, preferred_element_type=F32
    )
    inverse = 1.0 / inv
    high = inverse.astype(BF16).astype(F32)
    inverse_ref[...] = jnp.concatenate([high, inverse - high], axis=1)


def prep_kernel(ranges, affinity_hbm, *refs):
    *scale_refs, out_ref, affinity_ref, inv_ref, scratch, sems = refs
    count, block_rows, _, slots, flat = affinity_ref.shape
    half = flat // 128
    own = lax.axis_index("cols")
    copies = [
        pltpu.make_async_copy(affinity_hbm.at[m ^ own], affinity_ref.at[place], sems.at[place])
        for place, m in enumerate(ranges)
    ]
    if scale_refs:
        inv_copy = pltpu.make_async_copy(scale_refs[0], inv_ref, sems.at[count])
        inv_copy.start()
    for copy in copies:
        copy.start()
    source, target = iota((256, 256), 0), iota((256, 256), 1)
    moved = (source // 64 % 2) * 128 + (source // 128) * 64 + (source % 2) * 32 + source % 64 // 2
    permute = (moved == target).astype(BF16)
    if scale_refs:
        inv_copy.wait()
        prepare_scales(inv_ref[0], *scale_refs[1:])
    for m in range(count):
        copies[m].wait()
        for i in range(block_rows):
            block = affinity_ref[m, i, 0].astype(F32)
            for t in range(half):
                scratch[i % 2, t * slots : (t + 1) * slots, :] = block[:, t * 128 : (t + 1) * 128]
            parts = [
                scratch[i % 2, pl.ds(s, half, stride=slots), :].astype(BF16) for s in range(slots)
            ]
            pairs = [jnp.concatenate(parts[s : s + 2], axis=1) for s in range(0, slots, 2)]
            moved_pairs = jnp.dot(
                jnp.concatenate(pairs, axis=0), permute, preferred_element_type=F32
            ).astype(BF16)
            for s in range(slots // 2):
                piece = moved_pairs[s * half : (s + 1) * half]
                out_ref[m, i, :half, s * 128 : (s + 1) * 128] = piece[:, :128]
                out_ref[m, i, half:, s * 128 : (s + 1) * 128] = piece[:, 128:]


def prep(ranges, affinity, *scale_from):
    _, block_rows, _, slots, flat = affinity.shape
    count = len(ranges)
    outs = [shaped((count, block_rows, 64, slots * 64), BF16)]
    if scale_from:
        outs = [shaped((block_rows * 32, 128), F32), shaped((block_rows, 128), F32)] + outs
    return call(
        functools.partial(prep_kernel, ranges),
        "prep",
        [hbm()] * (1 + len(scale_from)),
        outs,
        (affinity, *scale_from),
        [
            pltpu.VMEM((count,) + affinity.shape[1:], BF16),
            pltpu.VMEM((1, block_rows, 64), F32),
            pltpu.VMEM((2, flat // 128 * slots, 128), F32),
            pltpu.SemaphoreType.DMA((count + 1,)),
        ],
    )


def stack_kernel(count, *refs):
    for index in range(count):
        refs[-1][index] = refs[index][...]


def stack(pieces, after):
    return call(
        functools.partial(stack_kernel, len(pieces)),
        "stack",
        [vmem()] * (len(pieces) + len(after)),
        shaped((len(pieces),) + pieces[0].shape, BF16),
        (*pieces, *after),
    )


def fill_table(stacks, offsets, table):
    block_rows = (table.shape[0] - 1) // (2 * len(offsets))
    low = iota((32, 128), 1) < 64
    pieces = [(ref, index) for ref in stacks for index in range(ref.shape[0])]
    for (ref, index), offset in zip(pieces, offsets):
        base = (lax.axis_index("rows") ^ offset) * block_rows
        for i in range(block_rows):
            block = ref[index, i * 32 : (i + 1) * 32, :]
            turned = jnp.concatenate([block[:, 64:], block[:, :64]], axis=1)
            table[base + i, :32] = jnp.where(low, block, turned)
            table[base + i, 32:] = jnp.where(low, turned, block)


def near_kernel(offsets, *refs):
    *near_refs, table = refs
    table[table.shape[0] - 1] = jnp.zeros(table.shape[1:], BF16)
    fill_table(near_refs, offsets, table)


def near_table(offsets, near, block_rows):
    count = len(offsets) // 2
    return call(
        functools.partial(near_kernel, offsets[:count]),
        "near",
        [vmem()] * len(near),
        shaped((2 * count * block_rows + 1, 64, 128), BF16),
        near,
    )


def one_product(group, columns, matrix, table, out_ref):
    block_rows, slots = matrix.shape[0], matrix.shape[2] // 64
    chosen = columns[group]
    low = iota((32, 128), 1) < 64
    for i in range(block_rows):
        picked = [table[chosen[i, s]] for s in range(slots)]
        result = jnp.dot(matrix[i], jnp.concatenate(picked, axis=0), preferred_element_type=F32)
        out_ref[i * 32 : (i + 1) * 32, :] = jnp.where(low, result[:32], result[32:]).astype(BF16)


def largest_notes(notes):
    largest = notes[0].astype(F32)
    for note in notes[1:]:
        largest = jnp.maximum(largest, note.astype(F32))
    return largest


def others_kernel(offsets, ranges, stacks, old_table, columns, matrix_ref, *refs):
    del old_table
    far_refs, near_refs = refs[:stacks], refs[stacks : 2 * stacks]
    table, *outs = refs[2 * stacks :]
    fill_table(far_refs, offsets, table)
    terms, first = outs[: len(ranges)], matrix_ref.shape[1] * 32
    if len(outs) > len(ranges):
        notes = largest_notes(
            [ref[index, first:] for ref in near_refs + far_refs for index in range(ref.shape[0])]
        )
        notes = jnp.sum(notes[8:], axis=(0, 1), keepdims=True)
        notes = jnp.broadcast_to(notes, (16, 128)).astype(BF16)
        for ref in outs[len(ranges) :]:
            ref[...] = notes
        for term in terms:
            term[first:, :] = notes
    for place, m in enumerate(ranges):
        group = m ^ lax.axis_index("cols")
        one_product(group, columns, matrix_ref.at[place], table, terms[place])


def own_kernel(columns, matrix_ref, table, out_ref):
    one_product(lax.axis_index("cols"), columns, matrix_ref.at[0], table, out_ref)


def products(offsets, ranges, columns, matrix, own_matrix, near, far, table):
    block_rows, count = matrix.shape[1], len(offsets) // 2
    extra = near[0].shape[1] > block_rows * 32
    rows = block_rows * 32
    outs = [shaped(table.shape, BF16)] + [shaped((rows + 16 * extra, 128), BF16)] * len(ranges)
    if extra:
        outs.append(shaped((16, 128), BF16))
    table, *outs = call(
        functools.partial(others_kernel, offsets[count:], ranges, len(near)),
        "others",
        [vmem()] * (3 + 2 * len(near)),
        outs,
        (table, columns, matrix, *far, *near),
        input_output_aliases={0: 0},
    )
    terms = [swap(term, "cols", m) for m, term in zip(ranges, outs)]
    own = call(
        own_kernel,
        "own",
        [vmem()] * 3,
        shaped((rows, 128), BF16),
        (columns, own_matrix, table),
    )
    return [own] + terms, outs[len(ranges) :]


def add_terms(terms, rows):
    summed = terms[0][:rows].astype(F32)
    for term in terms[1:]:
        summed = summed + term[:rows].astype(F32)
    return summed


def folded(both):
    gram = both[:64, :64] + both[64:, 64:]
    return jnp.concatenate([gram[:32], gram[32:]], axis=1)


def local_gram(rows):
    both = lax.dot_general(
        rows, rows, (((0,), (0,)), ((), ())), precision=HIGHEST, preferred_element_type=F32
    )
    return folded(both)


def middle_kernel(degree_ref, inverse_ref, *refs):
    terms, out_ref = refs[:-1], refs[-1]
    count = degree_ref.shape[0]
    degree = degree_ref[...]
    rows = add_terms(terms, count) * degree
    out_ref[:count] = (rows * degree).astype(BF16)
    squares = jnp.sum((rows * rows).reshape(-1, 8, 128), axis=0)
    out_ref[count:] = jnp.concatenate([inverse_ref[...], squares], axis=0).astype(BF16)


def middle(degree, inverse, terms):
    return call(
        middle_kernel,
        "middle",
        [vmem()] * (2 + len(terms)),
        shaped((degree.shape[0] + 16, 128), BF16),
        (degree, inverse, *terms),
    )


def row_gram_kernel(*refs):
    *stacks, gram_ref, rows = refs
    lane = iota((32, 128), 1)
    pair = lane % 64 // 2 == iota((32, 128), 0)
    spread = (iota((128, 128), 0) % 2 == iota((128, 128), 1) // 64).astype(BF16)
    count = stacks[0].shape[1] - 16
    pieces = [(ref, index) for ref in stacks for index in range(ref.shape[0])]
    for place, (ref, index) in enumerate(pieces):
        notes = ref[index, count:].astype(F32)
        masked = [
            jnp.where(pair, jnp.broadcast_to(notes[i : i + 1], (32, 128)), 0.0).astype(BF16)
            for i in range(count // 32)
        ]
        inverse = jnp.dot(jnp.concatenate(masked, axis=0), spread, preferred_element_type=F32)
        block = ref[index, :count].astype(F32) * inverse
        rows[place * count : (place + 1) * count, :] = block.astype(BF16)
    both = lax.dot_general(
        rows[...], rows[...], (((0,), (0,)), ((), ())), preferred_element_type=F32
    )
    gram_ref[...] = folded(both)


def row_gram(stacks):
    count = sum(stack.shape[0] for stack in stacks) * (stacks[0].shape[1] - 16)
    return call(
        row_gram_kernel,
        "row_gram",
        [vmem()] * len(stacks),
        shaped((32, 128), F32),
        stacks,
        [pltpu.VMEM((count, 128), BF16)],
    )


def collect_kernel(devices, total, degree_ref, first_ref, notes_ref, *refs):
    terms, (rows_ref, grams_ref) = refs[:-2], refs[-2:]
    count = degree_ref.shape[0]
    largest = largest_notes([notes_ref[...]] + [term[count:] for term in terms[1:]])
    scale = lax.rsqrt(largest[:1] * (devices / total))
    rows = add_terms(terms, count) * degree_ref[...] * scale
    rows_ref[...] = rows
    grams_ref[32:] = first_ref[...] * (scale * scale)
    grams_ref[:32] = local_gram(rows)


def collect(devices, total, degree, first, notes, terms):
    return call(
        functools.partial(collect_kernel, devices, total),
        "collect",
        [vmem()] * (3 + len(terms)),
        (shaped(degree.shape, F32), shaped((64, 128), F32)),
        (degree, first, notes, *terms),
    )


def lower_solve(gram, right):
    work = jnp.concatenate([gram, right], axis=1)
    blocks = gram.shape[0] // 8
    rows = [work[8 * i : 8 * i + 8] for i in range(blocks)]
    at = iota((8, 128), 0)

    def columns(first, column):
        return [
            jnp.broadcast_to(rows[i][:, column : column + 1], (8, 128))
            for i in range(first, blocks)
        ]

    def spread(block, row):
        return jnp.broadcast_to(block[row : row + 1], (8, 128))

    ahead = []
    for b in range(blocks):
        count = blocks - b
        current = ahead + [columns(b, 8 * b + q) for q in range(len(ahead), 8)]
        ahead = []
        if count > 1:
            ahead = [columns(b + 1, 8 * (b + 1) + q) for q in range(4)]
        for q in range(8):
            root = lax.rsqrt(spread(current[q][0], q))
            row = spread(rows[b], q) * root
            column = [x * root for x in current[q]]
            for p in range(q + 1, 8):
                weight = spread(current[q][0], p) * root
                current[p] = [x - y * weight for x, y in zip(current[p], column)]
            below = rows[b] - column[0] * row
            rows[b] = jnp.where(at == q, row, jnp.where(at > q, below, rows[b]))
            for i in range(1, count):
                rows[b + i] = rows[b + i] - column[i] * row
            for p in range(len(ahead)):
                weight = spread(current[q][1], p) * root
                ahead[p] = [x - y * weight for x, y in zip(ahead[p], column[1:])]
    return jnp.concatenate(rows, axis=0)[:, 64:]


def unpacked(packed):
    return jnp.concatenate([packed[:, :64], packed[:, 64:]], axis=0)


def add_columns_kernel(total, *refs):
    parts, (gram_ref, first_ref) = refs[:-2], refs[-2:]
    summed = parts[0][...]
    for part in parts[1:]:
        summed = summed + part[...]
    gram_ref[...] = summed[:32]
    first_ref[...] = summed[32:] / total


def add_columns(total, parts):
    return call(
        functools.partial(add_columns_kernel, total),
        "add_columns",
        [vmem()] * len(parts),
        (shaped((32, 128), F32), shaped((32, 128), F32)),
        parts,
    )


def add_parts_kernel(count, *refs):
    summed = refs[0][...]
    for part in refs[1:count]:
        summed = summed + part[...]
    refs[-1][...] = summed


def add_parts(parts, after):
    return call(
        functools.partial(add_parts_kernel, len(parts)),
        "add_parts",
        [vmem()] * (len(parts) + len(after)),
        shaped(parts[0].shape, F32),
        (*parts, *after),
    )


def first_factor_kernel(gram_ref, out_ref):
    unit = (iota((64, 64), 0) == iota((64, 64), 1)).astype(F32)
    out_ref[...] = lower_solve(unpacked(gram_ref[...]), unit)


def first_factor(gram):
    return call(first_factor_kernel, "first_factor", [vmem()], shaped((64, 64), F32), (gram,))


def dot_turned(left, right):
    return lax.dot_general(
        left, right, (((1,), (1,)), ((), ())), precision=HIGHEST, preferred_element_type=F32
    )


def finish_kernel(total, rows_ref, inverse_ref, *refs):
    out_ref, scratch = refs[-2:]
    block_rows = out_ref.shape[1]
    packed = refs[0][...]
    for part in refs[1:-2]:
        packed = packed + part[...]
    first = inverse_ref[...]
    gram = dot_turned(
        jnp.dot(first, unpacked(packed), precision=HIGHEST, preferred_element_type=F32), first
    )
    inverse = lower_solve(gram / total, first)
    zero = jnp.zeros_like(inverse)
    both = jnp.concatenate(
        [jnp.concatenate([inverse, zero], axis=1), jnp.concatenate([zero, inverse], axis=1)], axis=0
    )
    current = dot_turned(rows_ref[...], both)
    for i in range(block_rows):
        scratch[pl.ds(i, 32, stride=block_rows), :] = current[i * 32 : (i + 1) * 32]
    for t in range(32):
        out_ref[0, :, t * 128 : (t + 1) * 128] = scratch[t * block_rows : (t + 1) * block_rows, :]


def finish(total, block_rows, rows, inverse, grams):
    return call(
        functools.partial(finish_kernel, total),
        "finish",
        [vmem()] * (2 + len(grams)),
        shaped((1, block_rows, 32 * 128), F32),
        (rows, inverse, *grams),
        [pltpu.VMEM(rows.shape, F32)],
    )


def swap(value, axis, mask):
    size = lax.axis_size(axis)
    return lax.ppermute(value, axis, [(index, index ^ mask) for index in range(size)])


def swap_both(value, row_mask, column_mask):
    rows, columns = lax.axis_size("rows"), lax.axis_size("cols")
    pairs = [
        (row * columns + column, (row ^ row_mask) * columns + (column ^ column_mask))
        for row in range(rows)
        for column in range(columns)
    ]
    return lax.ppermute(value, ("rows", "cols"), pairs)


def stages(size):
    if size == 8:
        return [[7, 5, 3], [1]]
    bits, bit = [], 1
    while bit < size:
        bits.append([bit])
        bit *= 2
    return bits


def gather_rows(message, after):
    plan = stages(lax.axis_size("rows"))
    held, offsets = [message], [0]
    for masks in plan[:-1]:
        held = held + [swap(piece, "rows", mask) for mask in masks for piece in held]
        offsets = offsets + [mask ^ offset for mask in masks for offset in offsets]
    split = len(held) // 2
    if after:
        held, offsets = held[split:] + held[:split], offsets[split:] + offsets[:split]
        near = [stack(held[:split], []), stack(held[split:], after)]
    else:
        near = [piece[None] for piece in held]
    (last,) = plan[-1]
    offsets = offsets + [last ^ offset for offset in offsets]
    return near, [swap(pieces, "rows", last) for pieces in near], offsets


def add_rows(gram, after):
    *plan, (last,) = stages(lax.axis_size("rows"))
    for masks in plan:
        gram = add_parts([gram] + [swap(gram, "rows", mask) for mask in masks], after)
    return [gram, swap(gram, "rows", last)]


def body(affinity, block_columns, block_counts, inv_degree, panel):
    block_rows, block_size = inv_degree.shape[1:]
    groups, _, _, slots, _ = affinity.shape
    ranks = lax.axis_size("rows")
    total = float(groups * ranks * block_rows * block_size)
    blocks = ranks * block_rows
    live = iota(block_columns.shape, 3) < block_counts[..., None]
    columns = jnp.where(live, jnp.clip(block_columns, 0, blocks - 1), blocks)[:, :, 0]
    panel, inv_degree, affinity = (
        pltpu.with_memory_space_constraint(value, pltpu.HBM) for value in (panel, inv_degree, affinity)
    )
    ranges = list(range(groups - 1, 0, -1))

    scaled = start(panel, inv_degree)
    degree, inverse, matrix = prep(ranges, affinity, inv_degree)
    (own_matrix,) = prep([0], affinity)
    near, far, offsets = gather_rows(scaled, [inverse])
    table = near_table(offsets, near, block_rows)
    terms, _ = products(offsets, ranges, columns, matrix, own_matrix, near, far, table)
    near, far, offsets = gather_rows(middle(degree, inverse, terms), [])
    table = near_table(offsets, near, block_rows)
    terms, (notes,) = products(offsets, ranges, columns, matrix, own_matrix, near, far, table)
    devices = float(groups * ranks)
    rows, grams = collect(devices, total, degree, row_gram(near + far), notes, terms)
    flip = 1 if ranks == 8 else 0
    order = [2, 3, 1] if groups == 4 else ranges
    gram, first = add_columns(total, [grams] + [swap_both(grams, flip, m) for m in order])
    inverse = first_factor(first)
    return finish(total, block_rows, rows, inverse, add_rows(gram, [inverse]))


def solution(mesh):
    return jax.shard_map(
        body,
        mesh=mesh,
        in_specs=(
            P(None, "rows", "cols", None, None),
            P(None, "rows", "cols", None),
            P(None, "rows", "cols"),
            P("cols", "rows", None),
            P("cols", "rows", None),
        ),
        out_specs=P("cols", "rows", None),
        check_vma=False,
    )
```

```python
import functools

import jax
import jax.numpy as jnp
from jax import lax
from jax.experimental import pallas as pl
from jax.experimental.pallas import tpu as pltpu
from jax.sharding import PartitionSpec as P

BF16 = jnp.bfloat16
F32 = jnp.float32
HIGHEST = lax.Precision.HIGHEST
MIB = 1024 * 1024


def params(limit=48 * MIB):
    return pltpu.CompilerParams(vmem_limit_bytes=limit)


def vmem():
    return pl.BlockSpec(memory_space=pltpu.VMEM)


def hbm():
    return pl.BlockSpec(memory_space=pltpu.HBM)


def shaped(shape, dtype):
    return jax.ShapeDtypeStruct(shape, dtype)


def iota(shape, dim):
    return lax.broadcasted_iota(jnp.int32, shape, dim)


def call(kernel, name, ins, outs, operands, scratch=(), limit=48 * MIB, **kwargs):
    return pl.pallas_call(
        kernel,
        out_shape=outs,
        in_specs=ins,
        out_specs=jax.tree.map(lambda _: vmem(), outs),
        scratch_shapes=list(scratch),
        compiler_params=params(limit),
        name=name,
        **kwargs,
    )(*operands)


def start_kernel(panel_hbm, inv_hbm, scaled_ref, panel_ref, inv_ref, scratch, sems):
    block_rows, half = inv_ref.shape[1], inv_ref.shape[2] // 2
    copies = [
        pltpu.make_async_copy(inv_hbm, inv_ref, sems.at[0]),
        pltpu.make_async_copy(panel_hbm, panel_ref, sems.at[1]),
    ]
    for copy in copies:
        copy.start()
    copies[0].wait()
    inv = inv_ref[0]
    low = iota((block_rows, 128), 1) < 64
    scales = []
    for t in range(half):
        even, odd = (
            jnp.broadcast_to(inv[:, a : a + 1], (block_rows, 128)) for a in (2 * t, 2 * t + 1)
        )
        scales.append(jnp.where(low, even, odd))
    copies[1].wait()
    for t in range(half):
        scratch[t * block_rows : (t + 1) * block_rows, :] = (
            panel_ref[0, :, t * 128 : (t + 1) * 128] * scales[t]
        )
    for i in range(block_rows):
        part = scratch[pl.ds(i, half, stride=block_rows), :]
        scaled_ref[i * half : (i + 1) * half, :] = part.astype(BF16)


def start(panel, inv_degree):
    block_rows, block_size = inv_degree.shape[1:]
    shape = (block_rows * block_size // 2, 128)
    return call(
        start_kernel,
        "start",
        [hbm(), hbm()],
        shaped(shape, BF16),
        (panel, inv_degree),
        [
            pltpu.VMEM(panel.shape, F32),
            pltpu.VMEM(inv_degree.shape, F32),
            pltpu.VMEM(shape, F32),
            pltpu.SemaphoreType.DMA((2,)),
        ],
    )


def prepare_scales(inv, degree_ref, inverse_ref):
    block_rows, block_size = inv.shape
    half = block_size // 2
    pair = iota((half, block_size), 1) // 2 == iota((half, block_size), 0)
    spread = (iota((block_size, 128), 0) % 2 == iota((block_size, 128), 1) // 64).astype(F32)
    rows = [
        jnp.where(pair, jnp.broadcast_to(inv[i : i + 1, :], (half, block_size)), 0.0)
        for i in range(block_rows)
    ]
    degree_ref[...] = jnp.dot(
        jnp.concatenate(rows, axis=0), spread, precision=HIGHEST, preferred_element_type=F32
    )
    inverse = 1.0 / inv
    high = inverse.astype(BF16).astype(F32)
    inverse_ref[...] = jnp.concatenate([high, inverse - high], axis=1)


def prep_kernel(ranges, affinity_hbm, *refs):
    *scale_refs, out_ref, affinity_ref, inv_ref, scratch, sems = refs
    count, block_rows, _, slots, flat = affinity_ref.shape
    half = flat // 128
    own = lax.axis_index("cols")
    copies = [
        pltpu.make_async_copy(affinity_hbm.at[m ^ own], affinity_ref.at[place], sems.at[place])
        for place, m in enumerate(ranges)
    ]
    if scale_refs:
        inv_copy = pltpu.make_async_copy(scale_refs[0], inv_ref, sems.at[count])
        inv_copy.start()
    for copy in copies:
        copy.start()
    source, target = iota((256, 256), 0), iota((256, 256), 1)
    moved = (source // 64 % 2) * 128 + (source // 128) * 64 + (source % 2) * 32 + source % 64 // 2
    permute = (moved == target).astype(BF16)
    if scale_refs:
        inv_copy.wait()
        prepare_scales(inv_ref[0], *scale_refs[1:])
    for m in range(count):
        copies[m].wait()
        for i in range(block_rows):
            block = affinity_ref[m, i, 0].astype(F32)
            for t in range(half):
                scratch[i % 2, t * slots : (t + 1) * slots, :] = block[:, t * 128 : (t + 1) * 128]
            parts = [
                scratch[i % 2, pl.ds(s, half, stride=slots), :].astype(BF16) for s in range(slots)
            ]
            pairs = [jnp.concatenate(parts[s : s + 2], axis=1) for s in range(0, slots, 2)]
            moved_pairs = jnp.dot(
                jnp.concatenate(pairs, axis=0), permute, preferred_element_type=F32
            ).astype(BF16)
            for s in range(slots // 2):
                piece = moved_pairs[s * half : (s + 1) * half]
                out_ref[m, i, :half, s * 128 : (s + 1) * 128] = piece[:, :128]
                out_ref[m, i, half:, s * 128 : (s + 1) * 128] = piece[:, 128:]


def prep(ranges, affinity, *scale_from):
    _, block_rows, _, slots, flat = affinity.shape
    count = len(ranges)
    outs = [shaped((count, block_rows, 64, slots * 64), BF16)]
    if scale_from:
        outs = [shaped((block_rows * 32, 128), F32), shaped((block_rows, 128), F32)] + outs
    return call(
        functools.partial(prep_kernel, ranges),
        "prep",
        [hbm()] * (1 + len(scale_from)),
        outs,
        (affinity, *scale_from),
        [
            pltpu.VMEM((count,) + affinity.shape[1:], BF16),
            pltpu.VMEM((1, block_rows, 64), F32),
            pltpu.VMEM((2, flat // 128 * slots, 128), F32),
            pltpu.SemaphoreType.DMA((count + 1,)),
        ],
    )


def stack_kernel(count, *refs):
    for index in range(count):
        refs[-1][index] = refs[index][...]


def stack(pieces, after):
    return call(
        functools.partial(stack_kernel, len(pieces)),
        "stack",
        [vmem()] * (len(pieces) + len(after)),
        shaped((len(pieces),) + pieces[0].shape, BF16),
        (*pieces, *after),
    )


def fill_table(stacks, offsets, table):
    block_rows = (table.shape[0] - 1) // (2 * len(offsets))
    low = iota((32, 128), 1) < 64
    pieces = [(ref, index) for ref in stacks for index in range(ref.shape[0])]
    for (ref, index), offset in zip(pieces, offsets):
        base = (lax.axis_index("rows") ^ offset) * block_rows
        for i in range(block_rows):
            block = ref[index, i * 32 : (i + 1) * 32, :]
            turned = jnp.concatenate([block[:, 64:], block[:, :64]], axis=1)
            table[base + i, :32] = jnp.where(low, block, turned)
            table[base + i, 32:] = jnp.where(low, turned, block)


def near_kernel(offsets, *refs):
    *near_refs, table = refs
    table[table.shape[0] - 1] = jnp.zeros(table.shape[1:], BF16)
    fill_table(near_refs, offsets, table)


def near_table(offsets, near, block_rows):
    count = len(offsets) // 2
    return call(
        functools.partial(near_kernel, offsets[:count]),
        "near",
        [vmem()] * len(near),
        shaped((2 * count * block_rows + 1, 64, 128), BF16),
        near,
    )


def one_product(group, columns, matrix, table, out_ref):
    block_rows, slots = matrix.shape[0], matrix.shape[2] // 64
    chosen = columns[group]
    low = iota((32, 128), 1) < 64
    for i in range(block_rows):
        picked = [table[chosen[i, s]] for s in range(slots)]
        result = jnp.dot(matrix[i], jnp.concatenate(picked, axis=0), preferred_element_type=F32)
        out_ref[i * 32 : (i + 1) * 32, :] = jnp.where(low, result[:32], result[32:]).astype(BF16)


def largest_notes(notes):
    largest = notes[0].astype(F32)
    for note in notes[1:]:
        largest = jnp.maximum(largest, note.astype(F32))
    return largest


def others_kernel(offsets, ranges, stacks, old_table, columns, matrix_ref, *refs):
    del old_table
    far_refs, near_refs = refs[:stacks], refs[stacks : 2 * stacks]
    table, *outs = refs[2 * stacks :]
    fill_table(far_refs, offsets, table)
    terms, first = outs[: len(ranges)], matrix_ref.shape[1] * 32
    if len(outs) > len(ranges):
        notes = largest_notes(
            [ref[index, first:] for ref in near_refs + far_refs for index in range(ref.shape[0])]
        )
        notes = jnp.sum(notes[8:], axis=(0, 1), keepdims=True)
        notes = jnp.broadcast_to(notes, (16, 128)).astype(BF16)
        for ref in outs[len(ranges) :]:
            ref[...] = notes
        for term in terms:
            term[first:, :] = notes
    for place, m in enumerate(ranges):
        group = m ^ lax.axis_index("cols")
        one_product(group, columns, matrix_ref.at[place], table, terms[place])


def own_kernel(columns, matrix_ref, table, out_ref):
    one_product(lax.axis_index("cols"), columns, matrix_ref.at[0], table, out_ref)


def products(offsets, ranges, columns, matrix, own_matrix, near, far, table):
    block_rows, count = matrix.shape[1], len(offsets) // 2
    extra = near[0].shape[1] > block_rows * 32
    rows = block_rows * 32
    outs = [shaped(table.shape, BF16)] + [shaped((rows + 16 * extra, 128), BF16)] * len(ranges)
    if extra:
        outs.append(shaped((16, 128), BF16))
    table, *outs = call(
        functools.partial(others_kernel, offsets[count:], ranges, len(near)),
        "others",
        [vmem()] * (3 + 2 * len(near)),
        outs,
        (table, columns, matrix, *far, *near),
        input_output_aliases={0: 0},
    )
    terms = [swap(term, "cols", m) for m, term in zip(ranges, outs)]
    own = call(
        own_kernel,
        "own",
        [vmem()] * 3,
        shaped((rows, 128), BF16),
        (columns, own_matrix, table),
    )
    return [own] + terms, outs[len(ranges) :]


def add_terms(terms, rows):
    summed = terms[0][:rows].astype(F32)
    for term in terms[1:]:
        summed = summed + term[:rows].astype(F32)
    return summed


def folded(both):
    gram = both[:64, :64] + both[64:, 64:]
    return jnp.concatenate([gram[:32], gram[32:]], axis=1)


def local_gram(rows):
    both = lax.dot_general(
        rows, rows, (((0,), (0,)), ((), ())), precision=HIGHEST, preferred_element_type=F32
    )
    return folded(both)


def middle_kernel(degree_ref, inverse_ref, *refs):
    terms, out_ref = refs[:-1], refs[-1]
    count = degree_ref.shape[0]
    degree = degree_ref[...]
    rows = add_terms(terms, count) * degree
    out_ref[:count] = (rows * degree).astype(BF16)
    squares = jnp.sum((rows * rows).reshape(-1, 8, 128), axis=0)
    out_ref[count:] = jnp.concatenate([inverse_ref[...], squares], axis=0).astype(BF16)


def middle(degree, inverse, terms):
    return call(
        middle_kernel,
        "middle",
        [vmem()] * (2 + len(terms)),
        shaped((degree.shape[0] + 16, 128), BF16),
        (degree, inverse, *terms),
    )


def row_gram_kernel(*refs):
    *stacks, gram_ref, rows = refs
    lane = iota((32, 128), 1)
    pair = lane % 64 // 2 == iota((32, 128), 0)
    spread = (iota((128, 128), 0) % 2 == iota((128, 128), 1) // 64).astype(BF16)
    count = stacks[0].shape[1] - 16
    pieces = [(ref, index) for ref in stacks for index in range(ref.shape[0])]
    for place, (ref, index) in enumerate(pieces):
        notes = ref[index, count:].astype(F32)
        masked = [
            jnp.where(pair, jnp.broadcast_to(notes[i : i + 1], (32, 128)), 0.0).astype(BF16)
            for i in range(count // 32)
        ]
        inverse = jnp.dot(jnp.concatenate(masked, axis=0), spread, preferred_element_type=F32)
        block = ref[index, :count].astype(F32) * inverse
        rows[place * count : (place + 1) * count, :] = block.astype(BF16)
    both = lax.dot_general(
        rows[...], rows[...], (((0,), (0,)), ((), ())), preferred_element_type=F32
    )
    gram_ref[...] = folded(both)


def row_gram(stacks):
    count = sum(stack.shape[0] for stack in stacks) * (stacks[0].shape[1] - 16)
    return call(
        row_gram_kernel,
        "row_gram",
        [vmem()] * len(stacks),
        shaped((32, 128), F32),
        stacks,
        [pltpu.VMEM((count, 128), BF16)],
    )


def collect_kernel(devices, total, degree_ref, first_ref, notes_ref, *refs):
    terms, (rows_ref, grams_ref) = refs[:-2], refs[-2:]
    count = degree_ref.shape[0]
    largest = largest_notes([notes_ref[...]] + [term[count:] for term in terms[1:]])
    scale = lax.rsqrt(largest[:1] * (devices / total))
    rows = add_terms(terms, count) * degree_ref[...] * scale
    rows_ref[...] = rows
    grams_ref[32:] = first_ref[...] * (scale * scale)
    grams_ref[:32] = local_gram(rows)


def collect(devices, total, degree, first, notes, terms):
    return call(
        functools.partial(collect_kernel, devices, total),
        "collect",
        [vmem()] * (3 + len(terms)),
        (shaped(degree.shape, F32), shaped((64, 128), F32)),
        (degree, first, notes, *terms),
    )


def lower_solve(gram, right):
    work = jnp.concatenate([gram, right], axis=1)
    blocks = gram.shape[0] // 8
    rows = [work[8 * i : 8 * i + 8] for i in range(blocks)]
    at = iota((8, 128), 0)

    def columns(first, column):
        return [
            jnp.broadcast_to(rows[i][:, column : column + 1], (8, 128))
            for i in range(first, blocks)
        ]

    def spread(block, row):
        return jnp.broadcast_to(block[row : row + 1], (8, 128))

    ahead = []
    for b in range(blocks):
        count = blocks - b
        current = ahead + [columns(b, 8 * b + q) for q in range(len(ahead), 8)]
        ahead = []
        if count > 1:
            ahead = [columns(b + 1, 8 * (b + 1) + q) for q in range(4)]
        for q in range(8):
            root = lax.rsqrt(spread(current[q][0], q))
            row = spread(rows[b], q) * root
            column = [x * root for x in current[q]]
            for p in range(q + 1, 8):
                weight = spread(current[q][0], p) * root
                current[p] = [x - y * weight for x, y in zip(current[p], column)]
            below = rows[b] - column[0] * row
            rows[b] = jnp.where(at == q, row, jnp.where(at > q, below, rows[b]))
            for i in range(1, count):
                rows[b + i] = rows[b + i] - column[i] * row
            for p in range(len(ahead)):
                weight = spread(current[q][1], p) * root
                ahead[p] = [x - y * weight for x, y in zip(ahead[p], column[1:])]
    return jnp.concatenate(rows, axis=0)[:, 64:]


def unpacked(packed):
    return jnp.concatenate([packed[:, :64], packed[:, 64:]], axis=0)


def add_columns_kernel(total, *refs):
    parts, (gram_ref, first_ref) = refs[:-2], refs[-2:]
    summed = parts[0][...]
    for part in parts[1:]:
        summed = summed + part[...]
    gram_ref[...] = summed[:32]
    first_ref[...] = summed[32:] / total


def add_columns(total, parts):
    return call(
        functools.partial(add_columns_kernel, total),
        "add_columns",
        [vmem()] * len(parts),
        (shaped((32, 128), F32), shaped((32, 128), F32)),
        parts,
    )


def add_parts_kernel(count, *refs):
    summed = refs[0][...]
    for part in refs[1:count]:
        summed = summed + part[...]
    refs[-1][...] = summed


def add_parts(parts, after):
    return call(
        functools.partial(add_parts_kernel, len(parts)),
        "add_parts",
        [vmem()] * (len(parts) + len(after)),
        shaped(parts[0].shape, F32),
        (*parts, *after),
    )


def first_factor_kernel(gram_ref, out_ref):
    unit = (iota((64, 64), 0) == iota((64, 64), 1)).astype(F32)
    out_ref[...] = lower_solve(unpacked(gram_ref[...]), unit)


def first_factor(gram):
    return call(first_factor_kernel, "first_factor", [vmem()], shaped((64, 64), F32), (gram,))


def dot_turned(left, right):
    return lax.dot_general(
        left, right, (((1,), (1,)), ((), ())), precision=HIGHEST, preferred_element_type=F32
    )


def finish_kernel(total, rows_ref, inverse_ref, *refs):
    out_ref, scratch = refs[-2:]
    block_rows = out_ref.shape[1]
    packed = refs[0][...]
    for part in refs[1:-2]:
        packed = packed + part[...]
    first = inverse_ref[...]
    gram = dot_turned(
        jnp.dot(first, unpacked(packed), precision=HIGHEST, preferred_element_type=F32), first
    )
    inverse = lower_solve(gram / total, first)
    zero = jnp.zeros_like(inverse)
    both = jnp.concatenate(
        [jnp.concatenate([inverse, zero], axis=1), jnp.concatenate([zero, inverse], axis=1)], axis=0
    )
    current = dot_turned(rows_ref[...], both)
    for i in range(block_rows):
        scratch[pl.ds(i, 32, stride=block_rows), :] = current[i * 32 : (i + 1) * 32]
    for t in range(32):
        out_ref[0, :, t * 128 : (t + 1) * 128] = scratch[t * block_rows : (t + 1) * block_rows, :]


def finish(total, block_rows, rows, inverse, grams):
    return call(
        functools.partial(finish_kernel, total),
        "finish",
        [vmem()] * (2 + len(grams)),
        shaped((1, block_rows, 32 * 128), F32),
        (rows, inverse, *grams),
        [pltpu.VMEM(rows.shape, F32)],
    )


def swap(value, axis, mask):
    size = lax.axis_size(axis)
    return lax.ppermute(value, axis, [(index, index ^ mask) for index in range(size)])


def swap_both(value, row_mask, column_mask):
    rows, columns = lax.axis_size("rows"), lax.axis_size("cols")
    pairs = [
        (row * columns + column, (row ^ row_mask) * columns + (column ^ column_mask))
        for row in range(rows)
        for column in range(columns)
    ]
    return lax.ppermute(value, ("rows", "cols"), pairs)


def stages(size):
    if size == 8:
        return [[7, 5, 3], [1]]
    bits, bit = [], 1
    while bit < size:
        bits.append([bit])
        bit *= 2
    return bits


def gather_rows(message, after):
    plan = stages(lax.axis_size("rows"))
    held, offsets = [message], [0]
    for masks in plan[:-1]:
        held = held + [swap(piece, "rows", mask) for mask in masks for piece in held]
        offsets = offsets + [mask ^ offset for mask in masks for offset in offsets]
    near = [piece[None] for piece in held]
    if after:
        near[1] = stack([held[1]], after)
    (last,) = plan[-1]
    offsets = offsets + [last ^ offset for offset in offsets]
    return near, [swap(pieces, "rows", last) for pieces in near], offsets


def add_rows(gram, after):
    *plan, (last,) = stages(lax.axis_size("rows"))
    for masks in plan:
        gram = add_parts([gram] + [swap(gram, "rows", mask) for mask in masks], after)
    return [gram, swap(gram, "rows", last)]


def body(affinity, block_columns, block_counts, inv_degree, panel):
    block_rows, block_size = inv_degree.shape[1:]
    groups, _, _, slots, _ = affinity.shape
    ranks = lax.axis_size("rows")
    total = float(groups * ranks * block_rows * block_size)
    blocks = ranks * block_rows
    live = iota(block_columns.shape, 3) < block_counts[..., None]
    columns = jnp.where(live, jnp.clip(block_columns, 0, blocks - 1), blocks)[:, :, 0]
    panel, inv_degree, affinity = (
        pltpu.with_memory_space_constraint(value, pltpu.HBM) for value in (panel, inv_degree, affinity)
    )
    ranges = list(range(groups - 1, 0, -1))

    scaled = start(panel, inv_degree)
    degree, inverse, matrix = prep(ranges, affinity, inv_degree)
    (own_matrix,) = prep([0], affinity)
    near, far, offsets = gather_rows(scaled, [inverse])
    table = near_table(offsets, near, block_rows)
    terms, _ = products(offsets, ranges, columns, matrix, own_matrix, near, far, table)
    near, far, offsets = gather_rows(middle(degree, inverse, terms), [])
    table = near_table(offsets, near, block_rows)
    terms, (notes,) = products(offsets, ranges, columns, matrix, own_matrix, near, far, table)
    devices = float(groups * ranks)
    rows, grams = collect(devices, total, degree, row_gram(near + far), notes, terms)
    flip = 1 if ranks == 8 else 0
    order = [2, 3, 1] if groups == 4 else ranges
    gram, first = add_columns(total, [grams] + [swap_both(grams, flip, m) for m in order])
    inverse = first_factor(first)
    return finish(total, block_rows, rows, inverse, add_rows(gram, [inverse]))


def solution(mesh):
    return jax.shard_map(
        body,
        mesh=mesh,
        in_specs=(
            P(None, "rows", "cols", None, None),
            P(None, "rows", "cols", None),
            P(None, "rows", "cols"),
            P("cols", "rows", None),
            P("cols", "rows", None),
        ),
        out_specs=P("cols", "rows", None),
        check_vma=False,
    )
```

```python
import functools

import jax
import jax.numpy as jnp
from jax import lax
from jax.experimental import pallas as pl
from jax.experimental.pallas import tpu as pltpu
from jax.sharding import PartitionSpec as P

BF16 = jnp.bfloat16
F32 = jnp.float32
HIGHEST = lax.Precision.HIGHEST
MIB = 1024 * 1024


def params(limit=48 * MIB):
    return pltpu.CompilerParams(vmem_limit_bytes=limit)


def vmem():
    return pl.BlockSpec(memory_space=pltpu.VMEM)


def hbm():
    return pl.BlockSpec(memory_space=pltpu.HBM)


def shaped(shape, dtype):
    return jax.ShapeDtypeStruct(shape, dtype)


def iota(shape, dim):
    return lax.broadcasted_iota(jnp.int32, shape, dim)


def call(kernel, name, ins, outs, operands, scratch=(), limit=48 * MIB, **kwargs):
    return pl.pallas_call(
        kernel,
        out_shape=outs,
        in_specs=ins,
        out_specs=jax.tree.map(lambda _: vmem(), outs),
        scratch_shapes=list(scratch),
        compiler_params=params(limit),
        name=name,
        **kwargs,
    )(*operands)


def start_kernel(panel_hbm, inv_hbm, scaled_ref, panel_ref, inv_ref, scratch, sems):
    block_rows, half = inv_ref.shape[1], inv_ref.shape[2] // 2
    copies = [
        pltpu.make_async_copy(inv_hbm, inv_ref, sems.at[0]),
        pltpu.make_async_copy(panel_hbm, panel_ref, sems.at[1]),
    ]
    for copy in copies:
        copy.start()
    copies[0].wait()
    inv = inv_ref[0]
    low = iota((block_rows, 128), 1) < 64
    scales = []
    for t in range(half):
        even, odd = (
            jnp.broadcast_to(inv[:, a : a + 1], (block_rows, 128)) for a in (2 * t, 2 * t + 1)
        )
        scales.append(jnp.where(low, even, odd))
    copies[1].wait()
    for t in range(half):
        scratch[t * block_rows : (t + 1) * block_rows, :] = (
            panel_ref[0, :, t * 128 : (t + 1) * 128] * scales[t]
        )
    for i in range(block_rows):
        part = scratch[pl.ds(i, half, stride=block_rows), :]
        scaled_ref[i * half : (i + 1) * half, :] = part.astype(BF16)


def start(panel, inv_degree):
    block_rows, block_size = inv_degree.shape[1:]
    shape = (block_rows * block_size // 2, 128)
    return call(
        start_kernel,
        "start",
        [hbm(), hbm()],
        shaped(shape, BF16),
        (panel, inv_degree),
        [
            pltpu.VMEM(panel.shape, F32),
            pltpu.VMEM(inv_degree.shape, F32),
            pltpu.VMEM((shape[0] + block_rows, 128), F32),
            pltpu.SemaphoreType.DMA((2,)),
        ],
    )


def prepare_scales(inv, degree_ref, inverse_ref):
    block_rows, block_size = inv.shape
    half = block_size // 2
    pair = iota((half, block_size), 1) // 2 == iota((half, block_size), 0)
    spread = (iota((block_size, 128), 0) % 2 == iota((block_size, 128), 1) // 64).astype(F32)
    rows = [
        jnp.where(pair, jnp.broadcast_to(inv[i : i + 1, :], (half, block_size)), 0.0)
        for i in range(block_rows)
    ]
    degree_ref[...] = jnp.dot(
        jnp.concatenate(rows, axis=0), spread, precision=HIGHEST, preferred_element_type=F32
    )
    inverse = 1.0 / inv
    high = inverse.astype(BF16).astype(F32)
    inverse_ref[...] = jnp.concatenate([high, inverse - high], axis=1)


def prep_kernel(ranges, affinity_hbm, *refs):
    *scale_refs, out_ref, affinity_ref, inv_ref, scratch, sems = refs
    count, block_rows, _, slots, flat = affinity_ref.shape
    half = flat // 128
    own = lax.axis_index("cols")
    copies = [
        pltpu.make_async_copy(affinity_hbm.at[m ^ own], affinity_ref.at[place], sems.at[place])
        for place, m in enumerate(ranges)
    ]
    if scale_refs:
        inv_copy = pltpu.make_async_copy(scale_refs[0], inv_ref, sems.at[count])
        inv_copy.start()
    for copy in copies:
        copy.start()
    source, target = iota((256, 256), 0), iota((256, 256), 1)
    moved = (source // 64 % 2) * 128 + (source // 128) * 64 + (source % 2) * 32 + source % 64 // 2
    permute = (moved == target).astype(BF16)
    if scale_refs:
        inv_copy.wait()
        prepare_scales(inv_ref[0], *scale_refs[1:])
    for m in range(count):
        copies[m].wait()
        for i in range(block_rows):
            block = affinity_ref[m, i, 0].astype(F32)
            for t in range(half):
                scratch[i % 2, t * slots : (t + 1) * slots, :] = block[:, t * 128 : (t + 1) * 128]
            parts = [
                scratch[i % 2, pl.ds(s, half, stride=slots), :].astype(BF16) for s in range(slots)
            ]
            pairs = [jnp.concatenate(parts[s : s + 2], axis=1) for s in range(0, slots, 2)]
            moved_pairs = jnp.dot(
                jnp.concatenate(pairs, axis=0), permute, preferred_element_type=F32
            ).astype(BF16)
            for s in range(slots // 2):
                piece = moved_pairs[s * half : (s + 1) * half]
                out_ref[m, i, :half, s * 128 : (s + 1) * 128] = piece[:, :128]
                out_ref[m, i, half:, s * 128 : (s + 1) * 128] = piece[:, 128:]


def prep(ranges, affinity, *scale_from):
    _, block_rows, _, slots, flat = affinity.shape
    count = len(ranges)
    outs = [shaped((count, block_rows, 64, slots * 64), BF16)]
    if scale_from:
        outs = [shaped((block_rows * 32, 128), F32), shaped((block_rows, 128), F32)] + outs
    return call(
        functools.partial(prep_kernel, ranges),
        "prep",
        [hbm()] * (1 + len(scale_from)),
        outs,
        (affinity, *scale_from),
        [
            pltpu.VMEM((count,) + affinity.shape[1:], BF16),
            pltpu.VMEM((1, block_rows, 64), F32),
            pltpu.VMEM((2, (flat // 128 + 1) * slots, 128), F32),
            pltpu.SemaphoreType.DMA((count + 1,)),
        ],
    )


def stack_kernel(count, *refs):
    for index in range(count):
        refs[-1][index] = refs[index][...]


def stack(pieces, after):
    return call(
        functools.partial(stack_kernel, len(pieces)),
        "stack",
        [vmem()] * (len(pieces) + len(after)),
        shaped((len(pieces),) + pieces[0].shape, BF16),
        (*pieces, *after),
    )


def fill_table(stacks, offsets, table):
    block_rows = (table.shape[0] - 1) // (2 * len(offsets))
    low = iota((32, 128), 1) < 64
    pieces = [(ref, index) for ref in stacks for index in range(ref.shape[0])]
    for (ref, index), offset in zip(pieces, offsets):
        base = (lax.axis_index("rows") ^ offset) * block_rows
        for i in range(block_rows):
            block = ref[index, i * 32 : (i + 1) * 32, :]
            turned = jnp.concatenate([block[:, 64:], block[:, :64]], axis=1)
            table[base + i, :32] = jnp.where(low, block, turned)
            table[base + i, 32:] = jnp.where(low, turned, block)


def near_kernel(offsets, *refs):
    *near_refs, table = refs
    table[table.shape[0] - 1] = jnp.zeros(table.shape[1:], BF16)
    fill_table(near_refs, offsets, table)


def near_table(offsets, near, block_rows):
    count = len(offsets) // 2
    return call(
        functools.partial(near_kernel, offsets[:count]),
        "near",
        [vmem()] * len(near),
        shaped((2 * count * block_rows + 1, 64, 128), BF16),
        near,
    )


def one_product(group, columns, matrix, table, out_ref):
    block_rows, slots = matrix.shape[0], matrix.shape[2] // 64
    chosen = columns[group]
    low = iota((32, 128), 1) < 64
    for i in range(block_rows):
        picked = [table[chosen[i, s]] for s in range(slots)]
        result = jnp.dot(matrix[i], jnp.concatenate(picked, axis=0), preferred_element_type=F32)
        out_ref[i * 32 : (i + 1) * 32, :] = jnp.where(low, result[:32], result[32:]).astype(BF16)


def largest_notes(notes):
    largest = notes[0].astype(F32)
    for note in notes[1:]:
        largest = jnp.maximum(largest, note.astype(F32))
    return largest


def others_kernel(offsets, ranges, stacks, old_table, columns, matrix_ref, *refs):
    del old_table
    far_refs, near_refs = refs[:stacks], refs[stacks : 2 * stacks]
    table, *outs = refs[2 * stacks :]
    fill_table(far_refs, offsets, table)
    terms, first = outs[: len(ranges)], matrix_ref.shape[1] * 32
    if len(outs) > len(ranges):
        notes = largest_notes(
            [ref[index, first:] for ref in near_refs + far_refs for index in range(ref.shape[0])]
        )
        notes = jnp.sum(notes[8:], axis=(0, 1), keepdims=True)
        notes = jnp.broadcast_to(notes, (16, 128)).astype(BF16)
        for ref in outs[len(ranges) :]:
            ref[...] = notes
        for term in terms:
            term[first:, :] = notes
    for place, m in enumerate(ranges):
        group = m ^ lax.axis_index("cols")
        one_product(group, columns, matrix_ref.at[place], table, terms[place])


def own_kernel(columns, matrix_ref, table, out_ref):
    one_product(lax.axis_index("cols"), columns, matrix_ref.at[0], table, out_ref)


def products(offsets, ranges, columns, matrix, own_matrix, near, far, table):
    block_rows, count = matrix.shape[1], len(offsets) // 2
    extra = near[0].shape[1] > block_rows * 32
    rows = block_rows * 32
    outs = [shaped(table.shape, BF16)] + [shaped((rows + 16 * extra, 128), BF16)] * len(ranges)
    if extra:
        outs.append(shaped((16, 128), BF16))
    table, *outs = call(
        functools.partial(others_kernel, offsets[count:], ranges, len(near)),
        "others",
        [vmem()] * (3 + 2 * len(near)),
        outs,
        (table, columns, matrix, *far, *near),
        input_output_aliases={0: 0},
    )
    terms = [swap(term, "cols", m) for m, term in zip(ranges, outs)]
    own = call(
        own_kernel,
        "own",
        [vmem()] * 3,
        shaped((rows, 128), BF16),
        (columns, own_matrix, table),
    )
    return [own] + terms, outs[len(ranges) :]


def add_terms(terms, rows):
    summed = terms[0][:rows].astype(F32)
    for term in terms[1:]:
        summed = summed + term[:rows].astype(F32)
    return summed


def folded(both):
    gram = both[:64, :64] + both[64:, 64:]
    return jnp.concatenate([gram[:32], gram[32:]], axis=1)


def local_gram(rows):
    both = lax.dot_general(
        rows, rows, (((0,), (0,)), ((), ())), precision=HIGHEST, preferred_element_type=F32
    )
    return folded(both)


def middle_kernel(degree_ref, inverse_ref, *refs):
    terms, out_ref = refs[:-1], refs[-1]
    count = degree_ref.shape[0]
    degree = degree_ref[...]
    rows = add_terms(terms, count) * degree
    out_ref[:count] = (rows * degree).astype(BF16)
    squares = jnp.sum((rows * rows).reshape(-1, 8, 128), axis=0)
    out_ref[count:] = jnp.concatenate([inverse_ref[...], squares], axis=0).astype(BF16)


def middle(degree, inverse, terms):
    return call(
        middle_kernel,
        "middle",
        [vmem()] * (2 + len(terms)),
        shaped((degree.shape[0] + 16, 128), BF16),
        (degree, inverse, *terms),
    )


def row_gram_kernel(*refs):
    *stacks, gram_ref, rows = refs
    lane = iota((32, 128), 1)
    pair = lane % 64 // 2 == iota((32, 128), 0)
    spread = (iota((128, 128), 0) % 2 == iota((128, 128), 1) // 64).astype(BF16)
    count = stacks[0].shape[1] - 16
    pieces = [(ref, index) for ref in stacks for index in range(ref.shape[0])]
    for place, (ref, index) in enumerate(pieces):
        notes = ref[index, count:].astype(F32)
        masked = [
            jnp.where(pair, jnp.broadcast_to(notes[i : i + 1], (32, 128)), 0.0).astype(BF16)
            for i in range(count // 32)
        ]
        inverse = jnp.dot(jnp.concatenate(masked, axis=0), spread, preferred_element_type=F32)
        block = ref[index, :count].astype(F32) * inverse
        rows[place * count : (place + 1) * count, :] = block.astype(BF16)
    both = lax.dot_general(
        rows[...], rows[...], (((0,), (0,)), ((), ())), preferred_element_type=F32
    )
    gram_ref[...] = folded(both)


def row_gram(stacks):
    count = sum(stack.shape[0] for stack in stacks) * (stacks[0].shape[1] - 16)
    return call(
        row_gram_kernel,
        "row_gram",
        [vmem()] * len(stacks),
        shaped((32, 128), F32),
        stacks,
        [pltpu.VMEM((count, 128), BF16)],
    )


def collect_kernel(devices, total, degree_ref, first_ref, notes_ref, *refs):
    terms, (rows_ref, grams_ref) = refs[:-2], refs[-2:]
    count = degree_ref.shape[0]
    largest = largest_notes([notes_ref[...]] + [term[count:] for term in terms[1:]])
    scale = lax.rsqrt(largest[:1] * (devices / total))
    rows = add_terms(terms, count) * degree_ref[...] * scale
    rows_ref[...] = rows
    grams_ref[32:] = first_ref[...] * (scale * scale)
    grams_ref[:32] = local_gram(rows)


def collect(devices, total, degree, first, notes, terms):
    return call(
        functools.partial(collect_kernel, devices, total),
        "collect",
        [vmem()] * (3 + len(terms)),
        (shaped(degree.shape, F32), shaped((64, 128), F32)),
        (degree, first, notes, *terms),
    )


def lower_solve(gram, right):
    work = jnp.concatenate([gram, right], axis=1)
    blocks = gram.shape[0] // 8
    rows = [work[8 * i : 8 * i + 8] for i in range(blocks)]
    at = iota((8, 128), 0)

    def columns(first, column):
        return [
            jnp.broadcast_to(rows[i][:, column : column + 1], (8, 128))
            for i in range(first, blocks)
        ]

    def spread(block, row):
        return jnp.broadcast_to(block[row : row + 1], (8, 128))

    ahead = []
    for b in range(blocks):
        count = blocks - b
        current = ahead + [columns(b, 8 * b + q) for q in range(len(ahead), 8)]
        ahead = []
        if count > 1:
            ahead = [columns(b + 1, 8 * (b + 1) + q) for q in range(4)]
        for q in range(8):
            root = lax.rsqrt(spread(current[q][0], q))
            row = spread(rows[b], q) * root
            column = [x * root for x in current[q]]
            for p in range(q + 1, 8):
                weight = spread(current[q][0], p) * root
                current[p] = [x - y * weight for x, y in zip(current[p], column)]
            below = rows[b] - column[0] * row
            rows[b] = jnp.where(at == q, row, jnp.where(at > q, below, rows[b]))
            for i in range(1, count):
                rows[b + i] = rows[b + i] - column[i] * row
            for p in range(len(ahead)):
                weight = spread(current[q][1], p) * root
                ahead[p] = [x - y * weight for x, y in zip(ahead[p], column[1:])]
    return jnp.concatenate(rows, axis=0)[:, 64:]


def unpacked(packed):
    return jnp.concatenate([packed[:, :64], packed[:, 64:]], axis=0)


def add_columns_kernel(total, *refs):
    parts, (gram_ref, first_ref) = refs[:-2], refs[-2:]
    summed = parts[0][...]
    for part in parts[1:]:
        summed = summed + part[...]
    gram_ref[...] = summed[:32]
    first_ref[...] = summed[32:] / total


def add_columns(total, parts):
    return call(
        functools.partial(add_columns_kernel, total),
        "add_columns",
        [vmem()] * len(parts),
        (shaped((32, 128), F32), shaped((32, 128), F32)),
        parts,
    )


def add_parts_kernel(count, *refs):
    summed = refs[0][...]
    for part in refs[1:count]:
        summed = summed + part[...]
    refs[-1][...] = summed


def add_parts(parts, after):
    return call(
        functools.partial(add_parts_kernel, len(parts)),
        "add_parts",
        [vmem()] * (len(parts) + len(after)),
        shaped(parts[0].shape, F32),
        (*parts, *after),
    )


def first_factor_kernel(gram_ref, out_ref):
    unit = (iota((64, 64), 0) == iota((64, 64), 1)).astype(F32)
    out_ref[...] = lower_solve(unpacked(gram_ref[...]), unit)


def first_factor(gram):
    return call(first_factor_kernel, "first_factor", [vmem()], shaped((64, 64), F32), (gram,))


def dot_turned(left, right):
    return lax.dot_general(
        left, right, (((1,), (1,)), ((), ())), precision=HIGHEST, preferred_element_type=F32
    )


def finish_kernel(total, rows_ref, inverse_ref, *refs):
    out_ref, scratch = refs[-2:]
    block_rows = out_ref.shape[1]
    packed = refs[0][...]
    for part in refs[1:-2]:
        packed = packed + part[...]
    first = inverse_ref[...]
    gram = dot_turned(
        jnp.dot(first, unpacked(packed), precision=HIGHEST, preferred_element_type=F32), first
    )
    inverse = lower_solve(gram / total, first)
    zero = jnp.zeros_like(inverse)
    both = jnp.concatenate(
        [jnp.concatenate([inverse, zero], axis=1), jnp.concatenate([zero, inverse], axis=1)], axis=0
    )
    current = dot_turned(rows_ref[...], both)
    for i in range(block_rows):
        scratch[pl.ds(i, 32, stride=block_rows), :] = current[i * 32 : (i + 1) * 32]
    for t in range(32):
        out_ref[0, :, t * 128 : (t + 1) * 128] = scratch[t * block_rows : (t + 1) * block_rows, :]


def finish(total, block_rows, rows, inverse, grams):
    return call(
        functools.partial(finish_kernel, total),
        "finish",
        [vmem()] * (2 + len(grams)),
        shaped((1, block_rows, 32 * 128), F32),
        (rows, inverse, *grams),
        [pltpu.VMEM((rows.shape[0] + block_rows, 128), F32)],
    )


def swap(value, axis, mask):
    size = lax.axis_size(axis)
    return lax.ppermute(value, axis, [(index, index ^ mask) for index in range(size)])


def swap_both(value, row_mask, column_mask):
    rows, columns = lax.axis_size("rows"), lax.axis_size("cols")
    pairs = [
        (row * columns + column, (row ^ row_mask) * columns + (column ^ column_mask))
        for row in range(rows)
        for column in range(columns)
    ]
    return lax.ppermute(value, ("rows", "cols"), pairs)


def stages(size):
    if size == 8:
        return [[7, 5, 3], [1]]
    bits, bit = [], 1
    while bit < size:
        bits.append([bit])
        bit *= 2
    return bits


def gather_rows(message, after):
    plan = stages(lax.axis_size("rows"))
    held, offsets = [message], [0]
    for masks in plan[:-1]:
        held = held + [swap(piece, "rows", mask) for mask in masks for piece in held]
        offsets = offsets + [mask ^ offset for mask in masks for offset in offsets]
    near = [piece[None] for piece in held]
    if after:
        near[1] = stack([held[1]], after)
    (last,) = plan[-1]
    offsets = offsets + [last ^ offset for offset in offsets]
    return near, [swap(pieces, "rows", last) for pieces in near], offsets


def add_rows(gram, after):
    *plan, (last,) = stages(lax.axis_size("rows"))
    for masks in plan:
        gram = add_parts([gram] + [swap(gram, "rows", mask) for mask in masks], after)
    return [gram, swap(gram, "rows", last)]


def body(affinity, block_columns, block_counts, inv_degree, panel):
    block_rows, block_size = inv_degree.shape[1:]
    groups, _, _, slots, _ = affinity.shape
    ranks = lax.axis_size("rows")
    total = float(groups * ranks * block_rows * block_size)
    blocks = ranks * block_rows
    live = iota(block_columns.shape, 3) < block_counts[..., None]
    columns = jnp.where(live, jnp.clip(block_columns, 0, blocks - 1), blocks)[:, :, 0]
    panel, inv_degree, affinity = (
        pltpu.with_memory_space_constraint(value, pltpu.HBM) for value in (panel, inv_degree, affinity)
    )
    ranges = list(range(groups - 1, 0, -1))

    scaled = start(panel, inv_degree)
    degree, inverse, matrix = prep(ranges, affinity, inv_degree)
    (own_matrix,) = prep([0], affinity)
    near, far, offsets = gather_rows(scaled, [inverse])
    table = near_table(offsets, near, block_rows)
    terms, _ = products(offsets, ranges, columns, matrix, own_matrix, near, far, table)
    near, far, offsets = gather_rows(middle(degree, inverse, terms), [])
    table = near_table(offsets, near, block_rows)
    terms, (notes,) = products(offsets, ranges, columns, matrix, own_matrix, near, far, table)
    devices = float(groups * ranks)
    rows, grams = collect(devices, total, degree, row_gram(near + far), notes, terms)
    flip = 1 if ranks == 8 else 0
    order = [2, 3, 1] if groups == 4 else ranges
    gram, first = add_columns(total, [grams] + [swap_both(grams, flip, m) for m in order])
    inverse = first_factor(first)
    return finish(total, block_rows, rows, inverse, add_rows(gram, [inverse]))


def solution(mesh):
    return jax.shard_map(
        body,
        mesh=mesh,
        in_specs=(
            P(None, "rows", "cols", None, None),
            P(None, "rows", "cols", None),
            P(None, "rows", "cols"),
            P("cols", "rows", None),
            P("cols", "rows", None),
        ),
        out_specs=P("cols", "rows", None),
        check_vma=False,
    )
```

```python
import functools

import jax
import jax.numpy as jnp
from jax import lax
from jax.experimental import pallas as pl
from jax.experimental.pallas import tpu as pltpu
from jax.sharding import PartitionSpec as P

BF16 = jnp.bfloat16
F32 = jnp.float32
HIGHEST = lax.Precision.HIGHEST
MIB = 1024 * 1024


def params(limit=48 * MIB):
    return pltpu.CompilerParams(vmem_limit_bytes=limit)


def vmem():
    return pl.BlockSpec(memory_space=pltpu.VMEM)


def hbm():
    return pl.BlockSpec(memory_space=pltpu.HBM)


def shaped(shape, dtype):
    return jax.ShapeDtypeStruct(shape, dtype)


def iota(shape, dim):
    return lax.broadcasted_iota(jnp.int32, shape, dim)


def call(kernel, name, ins, outs, operands, scratch=(), limit=48 * MIB, **kwargs):
    return pl.pallas_call(
        kernel,
        out_shape=outs,
        in_specs=ins,
        out_specs=jax.tree.map(lambda _: vmem(), outs),
        scratch_shapes=list(scratch),
        compiler_params=params(limit),
        name=name,
        **kwargs,
    )(*operands)


def start_kernel(panel_hbm, inv_hbm, scaled_ref, panel_ref, inv_ref, scratch, sems):
    block_rows, half = inv_ref.shape[1], inv_ref.shape[2] // 2
    copies = [
        pltpu.make_async_copy(inv_hbm, inv_ref, sems.at[0]),
        pltpu.make_async_copy(panel_hbm, panel_ref, sems.at[1]),
    ]
    for copy in copies:
        copy.start()
    copies[0].wait()
    inv = inv_ref[0]
    low = iota((block_rows, 128), 1) < 64
    scales = []
    for t in range(half):
        even, odd = (
            jnp.broadcast_to(inv[:, a : a + 1], (block_rows, 128)) for a in (2 * t, 2 * t + 1)
        )
        scales.append(jnp.where(low, even, odd))
    copies[1].wait()
    for t in range(half):
        scratch[t * block_rows : (t + 1) * block_rows, :] = (
            panel_ref[0, :, t * 128 : (t + 1) * 128] * scales[t]
        )
    for i in range(block_rows):
        part = scratch[pl.ds(i, half, stride=block_rows), :]
        scaled_ref[i * half : (i + 1) * half, :] = part.astype(BF16)


def start(panel, inv_degree):
    block_rows, block_size = inv_degree.shape[1:]
    shape = (block_rows * block_size // 2, 128)
    return call(
        start_kernel,
        "start",
        [hbm(), hbm()],
        shaped(shape, BF16),
        (panel, inv_degree),
        [
            pltpu.VMEM(panel.shape, F32),
            pltpu.VMEM(inv_degree.shape, F32),
            pltpu.VMEM((shape[0] + block_rows, 128), F32),
            pltpu.SemaphoreType.DMA((2,)),
        ],
    )


def prepare_scales(inv, degree_ref, inverse_ref):
    block_rows, block_size = inv.shape
    half = block_size // 2
    pair = iota((half, block_size), 1) // 2 == iota((half, block_size), 0)
    spread = (iota((block_size, 128), 0) % 2 == iota((block_size, 128), 1) // 64).astype(F32)
    rows = [
        jnp.where(pair, jnp.broadcast_to(inv[i : i + 1, :], (half, block_size)), 0.0)
        for i in range(block_rows)
    ]
    degree_ref[...] = jnp.dot(
        jnp.concatenate(rows, axis=0), spread, precision=HIGHEST, preferred_element_type=F32
    )
    inverse = 1.0 / inv
    high = inverse.astype(BF16).astype(F32)
    inverse_ref[...] = jnp.concatenate([high, inverse - high], axis=1)


def prep_kernel(ranges, affinity_hbm, *refs):
    *scale_refs, out_ref, affinity_ref, inv_ref, scratch, sems = refs
    count, block_rows, _, slots, flat = affinity_ref.shape
    half = flat // 128
    own = lax.axis_index("cols")
    copies = [
        pltpu.make_async_copy(affinity_hbm.at[m ^ own], affinity_ref.at[place], sems.at[place])
        for place, m in enumerate(ranges)
    ]
    if scale_refs:
        inv_copy = pltpu.make_async_copy(scale_refs[0], inv_ref, sems.at[count])
        inv_copy.start()
    for copy in copies:
        copy.start()
    source, target = iota((256, 256), 0), iota((256, 256), 1)
    moved = (source // 64 % 2) * 128 + (source // 128) * 64 + (source % 2) * 32 + source % 64 // 2
    permute = (moved == target).astype(BF16)
    if scale_refs:
        inv_copy.wait()
        prepare_scales(inv_ref[0], *scale_refs[1:])
    for m in range(count):
        copies[m].wait()
        for i in range(block_rows):
            block = affinity_ref[m, i, 0].astype(F32)
            for t in range(half):
                scratch[i % 2, t * slots : (t + 1) * slots, :] = block[:, t * 128 : (t + 1) * 128]
            parts = [
                scratch[i % 2, pl.ds(s, half, stride=slots), :].astype(BF16) for s in range(slots)
            ]
            pairs = [jnp.concatenate(parts[s : s + 2], axis=1) for s in range(0, slots, 2)]
            moved_pairs = jnp.dot(
                jnp.concatenate(pairs, axis=0), permute, preferred_element_type=F32
            ).astype(BF16)
            for s in range(slots // 2):
                piece = moved_pairs[s * half : (s + 1) * half]
                out_ref[m, i, :half, s * 128 : (s + 1) * 128] = piece[:, :128]
                out_ref[m, i, half:, s * 128 : (s + 1) * 128] = piece[:, 128:]


def prep(ranges, affinity, *scale_from):
    _, block_rows, _, slots, flat = affinity.shape
    count = len(ranges)
    outs = [shaped((count, block_rows, 64, slots * 64), BF16)]
    if scale_from:
        outs = [shaped((block_rows * 32, 128), F32), shaped((block_rows, 128), F32)] + outs
    return call(
        functools.partial(prep_kernel, ranges),
        "prep",
        [hbm()] * (1 + len(scale_from)),
        outs,
        (affinity, *scale_from),
        [
            pltpu.VMEM((count,) + affinity.shape[1:], BF16),
            pltpu.VMEM((1, block_rows, 64), F32),
            pltpu.VMEM((2, (flat // 128 + 1) * slots, 128), F32),
            pltpu.SemaphoreType.DMA((count + 1,)),
        ],
    )


def stack_kernel(count, *refs):
    for index in range(count):
        refs[-1][index] = refs[index][...]


def stack(pieces, after):
    return call(
        functools.partial(stack_kernel, len(pieces)),
        "stack",
        [vmem()] * (len(pieces) + len(after)),
        shaped((len(pieces),) + pieces[0].shape, BF16),
        (*pieces, *after),
    )


def fill_table(stacks, offsets, table):
    block_rows = (table.shape[0] - 1) // lax.axis_size("rows")
    low = iota((32, 128), 1) < 64
    pieces = [(ref, index) for ref in stacks for index in range(ref.shape[0])]
    for (ref, index), offset in zip(pieces, offsets):
        base = (lax.axis_index("rows") ^ offset) * block_rows
        for i in range(block_rows):
            block = ref[index, i * 32 : (i + 1) * 32, :]
            turned = jnp.concatenate([block[:, 64:], block[:, :64]], axis=1)
            table[base + i, :32] = jnp.where(low, block, turned)
            table[base + i, 32:] = jnp.where(low, turned, block)


def near_kernel(offsets, *refs):
    *near_refs, table = refs
    table[table.shape[0] - 1] = jnp.zeros(table.shape[1:], BF16)
    fill_table(near_refs, offsets, table)


def near_table(offsets, near, block_rows):
    return call(
        functools.partial(near_kernel, offsets[: len(near)]),
        "near",
        [vmem()] * len(near),
        shaped((len(offsets) * block_rows + 1, 64, 128), BF16),
        near,
    )


def one_product(group, columns, matrix, table, out_ref):
    block_rows, slots = matrix.shape[0], matrix.shape[2] // 64
    chosen = columns[group]
    low = iota((32, 128), 1) < 64
    for i in range(block_rows):
        picked = [table[chosen[i, s]] for s in range(slots)]
        result = jnp.dot(matrix[i], jnp.concatenate(picked, axis=0), preferred_element_type=F32)
        out_ref[i * 32 : (i + 1) * 32, :] = jnp.where(low, result[:32], result[32:]).astype(BF16)


def largest_notes(notes):
    largest = notes[0].astype(F32)
    for note in notes[1:]:
        largest = jnp.maximum(largest, note.astype(F32))
    return largest


def others_kernel(offsets, ranges, filled, old_table, columns, matrix_ref, *refs):
    del old_table
    pieces, (table, *outs) = refs[: len(offsets)], refs[len(offsets) :]
    fill_table(pieces[filled:], offsets[filled:], table)
    terms, first = outs[: len(ranges)], matrix_ref.shape[1] * 32
    if len(outs) > len(ranges):
        notes = largest_notes(
            [ref[index, first:] for ref in pieces for index in range(ref.shape[0])]
        )
        notes = jnp.sum(notes[8:], axis=(0, 1), keepdims=True)
        notes = jnp.broadcast_to(notes, (16, 128)).astype(BF16)
        for ref in outs[len(ranges) :]:
            ref[...] = notes
        for term in terms:
            term[first:, :] = notes
    for place, m in enumerate(ranges):
        group = m ^ lax.axis_index("cols")
        one_product(group, columns, matrix_ref.at[place], table, terms[place])


def own_kernel(columns, matrix_ref, table, out_ref):
    one_product(lax.axis_index("cols"), columns, matrix_ref.at[0], table, out_ref)


def products(offsets, ranges, columns, matrix, own_matrix, pieces, filled, table):
    block_rows = matrix.shape[1]
    extra = pieces[0].shape[1] > block_rows * 32
    rows = block_rows * 32
    outs = [shaped(table.shape, BF16)] + [shaped((rows + 16 * extra, 128), BF16)] * len(ranges)
    if extra:
        outs.append(shaped((16, 128), BF16))
    table, *outs = call(
        functools.partial(others_kernel, offsets, ranges, filled),
        "others",
        [vmem()] * (3 + len(pieces)),
        outs,
        (table, columns, matrix, *pieces),
        input_output_aliases={0: 0},
    )
    terms = [swap(term, "cols", m) for m, term in zip(ranges, outs)]
    own = call(
        own_kernel,
        "own",
        [vmem()] * 3,
        shaped((rows, 128), BF16),
        (columns, own_matrix, table),
    )
    return [own] + terms, outs[len(ranges) :]


def add_terms(terms, rows):
    summed = terms[0][:rows].astype(F32)
    for term in terms[1:]:
        summed = summed + term[:rows].astype(F32)
    return summed


def folded(both):
    gram = both[:64, :64] + both[64:, 64:]
    return jnp.concatenate([gram[:32], gram[32:]], axis=1)


def local_gram(rows):
    both = lax.dot_general(
        rows, rows, (((0,), (0,)), ((), ())), precision=HIGHEST, preferred_element_type=F32
    )
    return folded(both)


def middle_kernel(degree_ref, inverse_ref, *refs):
    terms, out_ref = refs[:-1], refs[-1]
    count = degree_ref.shape[0]
    degree = degree_ref[...]
    rows = add_terms(terms, count) * degree
    out_ref[:count] = (rows * degree).astype(BF16)
    squares = jnp.sum((rows * rows).reshape(-1, 8, 128), axis=0)
    out_ref[count:] = jnp.concatenate([inverse_ref[...], squares], axis=0).astype(BF16)


def middle(degree, inverse, terms):
    return call(
        middle_kernel,
        "middle",
        [vmem()] * (2 + len(terms)),
        shaped((degree.shape[0] + 16, 128), BF16),
        (degree, inverse, *terms),
    )


def row_gram_kernel(*refs):
    *stacks, gram_ref, rows = refs
    lane = iota((32, 128), 1)
    pair = lane % 64 // 2 == iota((32, 128), 0)
    spread = (iota((128, 128), 0) % 2 == iota((128, 128), 1) // 64).astype(BF16)
    count = stacks[0].shape[1] - 16
    pieces = [(ref, index) for ref in stacks for index in range(ref.shape[0])]
    for place, (ref, index) in enumerate(pieces):
        notes = ref[index, count:].astype(F32)
        masked = [
            jnp.where(pair, jnp.broadcast_to(notes[i : i + 1], (32, 128)), 0.0).astype(BF16)
            for i in range(count // 32)
        ]
        inverse = jnp.dot(jnp.concatenate(masked, axis=0), spread, preferred_element_type=F32)
        block = ref[index, :count].astype(F32) * inverse
        rows[place * count : (place + 1) * count, :] = block.astype(BF16)
    both = lax.dot_general(
        rows[...], rows[...], (((0,), (0,)), ((), ())), preferred_element_type=F32
    )
    gram_ref[...] = folded(both)


def row_gram(stacks):
    count = sum(stack.shape[0] for stack in stacks) * (stacks[0].shape[1] - 16)
    return call(
        row_gram_kernel,
        "row_gram",
        [vmem()] * len(stacks),
        shaped((32, 128), F32),
        stacks,
        [pltpu.VMEM((count, 128), BF16)],
    )


def collect_kernel(devices, total, degree_ref, first_ref, notes_ref, *refs):
    terms, (rows_ref, grams_ref) = refs[:-2], refs[-2:]
    count = degree_ref.shape[0]
    largest = largest_notes([notes_ref[...]] + [term[count:] for term in terms[1:]])
    scale = lax.rsqrt(largest[:1] * (devices / total))
    rows = add_terms(terms, count) * degree_ref[...] * scale
    rows_ref[...] = rows
    grams_ref[32:] = first_ref[...] * (scale * scale)
    grams_ref[:32] = local_gram(rows)


def collect(devices, total, degree, first, notes, terms):
    return call(
        functools.partial(collect_kernel, devices, total),
        "collect",
        [vmem()] * (3 + len(terms)),
        (shaped(degree.shape, F32), shaped((64, 128), F32)),
        (degree, first, notes, *terms),
    )


def lower_solve(gram, right):
    work = jnp.concatenate([gram, right], axis=1)
    blocks = gram.shape[0] // 8
    rows = [work[8 * i : 8 * i + 8] for i in range(blocks)]
    at = iota((8, 128), 0)

    def columns(first, column):
        return [
            jnp.broadcast_to(rows[i][:, column : column + 1], (8, 128))
            for i in range(first, blocks)
        ]

    def spread(block, row):
        return jnp.broadcast_to(block[row : row + 1], (8, 128))

    ahead = []
    for b in range(blocks):
        count = blocks - b
        current = ahead + [columns(b, 8 * b + q) for q in range(len(ahead), 8)]
        ahead = []
        if count > 1:
            ahead = [columns(b + 1, 8 * (b + 1) + q) for q in range(4)]
        for q in range(8):
            root = lax.rsqrt(spread(current[q][0], q))
            row = spread(rows[b], q) * root
            column = [x * root for x in current[q]]
            for p in range(q + 1, 8):
                weight = spread(current[q][0], p) * root
                current[p] = [x - y * weight for x, y in zip(current[p], column)]
            below = rows[b] - column[0] * row
            rows[b] = jnp.where(at == q, row, jnp.where(at > q, below, rows[b]))
            for i in range(1, count):
                rows[b + i] = rows[b + i] - column[i] * row
            for p in range(len(ahead)):
                weight = spread(current[q][1], p) * root
                ahead[p] = [x - y * weight for x, y in zip(ahead[p], column[1:])]
    return jnp.concatenate(rows, axis=0)[:, 64:]


def unpacked(packed):
    return jnp.concatenate([packed[:, :64], packed[:, 64:]], axis=0)


def add_columns_kernel(total, *refs):
    parts, (gram_ref, first_ref) = refs[:-2], refs[-2:]
    summed = parts[0][...]
    for part in parts[1:]:
        summed = summed + part[...]
    gram_ref[...] = summed[:32]
    first_ref[...] = summed[32:] / total


def add_columns(total, parts):
    return call(
        functools.partial(add_columns_kernel, total),
        "add_columns",
        [vmem()] * len(parts),
        (shaped((32, 128), F32), shaped((32, 128), F32)),
        parts,
    )


def add_parts_kernel(count, *refs):
    summed = refs[0][...]
    for part in refs[1:count]:
        summed = summed + part[...]
    refs[-1][...] = summed


def add_parts(parts, after):
    return call(
        functools.partial(add_parts_kernel, len(parts)),
        "add_parts",
        [vmem()] * (len(parts) + len(after)),
        shaped(parts[0].shape, F32),
        (*parts, *after),
    )


def first_factor_kernel(gram_ref, out_ref):
    unit = (iota((64, 64), 0) == iota((64, 64), 1)).astype(F32)
    out_ref[...] = lower_solve(unpacked(gram_ref[...]), unit)


def first_factor(gram):
    return call(first_factor_kernel, "first_factor", [vmem()], shaped((64, 64), F32), (gram,))


def dot_turned(left, right):
    return lax.dot_general(
        left, right, (((1,), (1,)), ((), ())), precision=HIGHEST, preferred_element_type=F32
    )


def finish_kernel(total, rows_ref, inverse_ref, *refs):
    out_ref, scratch = refs[-2:]
    block_rows = out_ref.shape[1]
    packed = refs[0][...]
    for part in refs[1:-2]:
        packed = packed + part[...]
    first = inverse_ref[...]
    gram = dot_turned(
        jnp.dot(first, unpacked(packed), precision=HIGHEST, preferred_element_type=F32), first
    )
    inverse = lower_solve(gram / total, first)
    zero = jnp.zeros_like(inverse)
    both = jnp.concatenate(
        [jnp.concatenate([inverse, zero], axis=1), jnp.concatenate([zero, inverse], axis=1)], axis=0
    )
    current = dot_turned(rows_ref[...], both)
    for i in range(block_rows):
        scratch[pl.ds(i, 32, stride=block_rows), :] = current[i * 32 : (i + 1) * 32]
    for t in range(32):
        out_ref[0, :, t * 128 : (t + 1) * 128] = scratch[t * block_rows : (t + 1) * block_rows, :]


def finish(total, block_rows, rows, inverse, grams):
    return call(
        functools.partial(finish_kernel, total),
        "finish",
        [vmem()] * (2 + len(grams)),
        shaped((1, block_rows, 32 * 128), F32),
        (rows, inverse, *grams),
        [pltpu.VMEM((rows.shape[0] + block_rows, 128), F32)],
    )


def swap(value, axis, mask):
    size = lax.axis_size(axis)
    return lax.ppermute(value, axis, [(index, index ^ mask) for index in range(size)])


def swap_both(value, row_mask, column_mask):
    rows, columns = lax.axis_size("rows"), lax.axis_size("cols")
    pairs = [
        (row * columns + column, (row ^ row_mask) * columns + (column ^ column_mask))
        for row in range(rows)
        for column in range(columns)
    ]
    return lax.ppermute(value, ("rows", "cols"), pairs)


def stages(size):
    if size == 8:
        return [[7, 5, 3], [1]]
    bits, bit = [], 1
    while bit < size:
        bits.append([bit])
        bit *= 2
    return bits


def gather_rows(message, after):
    plan = stages(lax.axis_size("rows"))
    held, offsets = [message], [0]
    for masks in plan[:-1]:
        held = held + [swap(piece, "rows", mask) for mask in masks for piece in held]
        offsets = offsets + [mask ^ offset for mask in masks for offset in offsets]
    near = [piece[None] for piece in held]
    if after:
        near[1] = stack([held[1]], after)
    (last,) = plan[-1]
    offsets = offsets + [last ^ offset for offset in offsets]
    return near, [swap(pieces, "rows", last) for pieces in near], offsets


def add_rows(gram, after):
    *plan, (last,) = stages(lax.axis_size("rows"))
    for masks in plan:
        gram = add_parts([gram] + [swap(gram, "rows", mask) for mask in masks], after)
    return [gram, swap(gram, "rows", last)]


def body(affinity, block_columns, block_counts, inv_degree, panel):
    block_rows, block_size = inv_degree.shape[1:]
    groups, _, _, slots, _ = affinity.shape
    ranks = lax.axis_size("rows")
    total = float(groups * ranks * block_rows * block_size)
    blocks = ranks * block_rows
    live = iota(block_columns.shape, 3) < block_counts[..., None]
    columns = jnp.where(live, jnp.clip(block_columns, 0, blocks - 1), blocks)[:, :, 0]
    panel, inv_degree, affinity = (
        pltpu.with_memory_space_constraint(value, pltpu.HBM) for value in (panel, inv_degree, affinity)
    )
    ranges = list(range(groups - 1, 0, -1))

    scaled = start(panel, inv_degree)
    degree, inverse, matrix = prep(ranges, affinity, inv_degree)
    (own_matrix,) = prep([0], affinity)
    near, far, offsets = gather_rows(scaled, [inverse])
    pieces, filled = near + far, len(near) + len(far) // 2
    table = near_table(offsets, pieces[:filled], block_rows)
    terms, _ = products(offsets, ranges, columns, matrix, own_matrix, pieces, filled, table)
    near, far, offsets = gather_rows(middle(degree, inverse, terms), [])
    pieces, filled = near + far, len(near) + len(far) // 2
    table = near_table(offsets, pieces[:filled], block_rows)
    terms, (notes,) = products(offsets, ranges, columns, matrix, own_matrix, pieces, filled, table)
    devices = float(groups * ranks)
    rows, grams = collect(devices, total, degree, row_gram(near + far), notes, terms)
    flip = 1 if ranks == 8 else 0
    order = [2, 3, 1] if groups == 4 else ranges
    gram, first = add_columns(total, [grams] + [swap_both(grams, flip, m) for m in order])
    inverse = first_factor(first)
    return finish(total, block_rows, rows, inverse, add_rows(gram, [inverse]))


def solution(mesh):
    return jax.shard_map(
        body,
        mesh=mesh,
        in_specs=(
            P(None, "rows", "cols", None, None),
            P(None, "rows", "cols", None),
            P(None, "rows", "cols"),
            P("cols", "rows", None),
            P("cols", "rows", None),
        ),
        out_specs=P("cols", "rows", None),
        check_vma=False,
    )
```

```python
import functools

import jax
import jax.numpy as jnp
from jax import lax
from jax.experimental import pallas as pl
from jax.experimental.pallas import tpu as pltpu
from jax.sharding import PartitionSpec as P

BF16 = jnp.bfloat16
F32 = jnp.float32
HIGHEST = lax.Precision.HIGHEST
MIB = 1024 * 1024


def params(limit=48 * MIB):
    return pltpu.CompilerParams(vmem_limit_bytes=limit)


def vmem():
    return pl.BlockSpec(memory_space=pltpu.VMEM)


def hbm():
    return pl.BlockSpec(memory_space=pltpu.HBM)


def shaped(shape, dtype):
    return jax.ShapeDtypeStruct(shape, dtype)


def iota(shape, dim):
    return lax.broadcasted_iota(jnp.int32, shape, dim)


def call(kernel, name, ins, outs, operands, scratch=(), limit=48 * MIB, **kwargs):
    return pl.pallas_call(
        kernel,
        out_shape=outs,
        in_specs=ins,
        out_specs=jax.tree.map(lambda _: vmem(), outs),
        scratch_shapes=list(scratch),
        compiler_params=params(limit),
        name=name,
        **kwargs,
    )(*operands)


def start_kernel(panel_hbm, inv_hbm, scaled_ref, panel_ref, inv_ref, scratch, sems):
    block_rows, half = inv_ref.shape[1], inv_ref.shape[2] // 2
    copies = [
        pltpu.make_async_copy(inv_hbm, inv_ref, sems.at[0]),
        pltpu.make_async_copy(panel_hbm, panel_ref, sems.at[1]),
    ]
    for copy in copies:
        copy.start()
    copies[0].wait()
    inv = inv_ref[0]
    low = iota((block_rows, 128), 1) < 64
    scales = []
    for t in range(half):
        even, odd = (
            jnp.broadcast_to(inv[:, a : a + 1], (block_rows, 128)) for a in (2 * t, 2 * t + 1)
        )
        scales.append(jnp.where(low, even, odd))
    copies[1].wait()
    for t in range(half):
        scratch[t * block_rows : (t + 1) * block_rows, :] = (
            panel_ref[0, :, t * 128 : (t + 1) * 128] * scales[t]
        )
    for i in range(block_rows):
        part = scratch[pl.ds(i, half, stride=block_rows), :]
        scaled_ref[i * half : (i + 1) * half, :] = part.astype(BF16)


def start(panel, inv_degree):
    block_rows, block_size = inv_degree.shape[1:]
    shape = (block_rows * block_size // 2, 128)
    return call(
        start_kernel,
        "start",
        [hbm(), hbm()],
        shaped(shape, BF16),
        (panel, inv_degree),
        [
            pltpu.VMEM(panel.shape, F32),
            pltpu.VMEM(inv_degree.shape, F32),
            pltpu.VMEM((shape[0] + block_rows, 128), F32),
            pltpu.SemaphoreType.DMA((2,)),
        ],
    )


def prepare_scales(inv, degree_ref, inverse_ref):
    block_rows, block_size = inv.shape
    half = block_size // 2
    pair = iota((half, block_size), 1) // 2 == iota((half, block_size), 0)
    spread = (iota((block_size, 128), 0) % 2 == iota((block_size, 128), 1) // 64).astype(F32)
    rows = [
        jnp.where(pair, jnp.broadcast_to(inv[i : i + 1, :], (half, block_size)), 0.0)
        for i in range(block_rows)
    ]
    degree_ref[...] = jnp.dot(
        jnp.concatenate(rows, axis=0), spread, precision=HIGHEST, preferred_element_type=F32
    )
    inverse = 1.0 / inv
    high = inverse.astype(BF16).astype(F32)
    inverse_ref[...] = jnp.concatenate([high, inverse - high], axis=1)


def prep_kernel(ranges, affinity_hbm, *refs):
    *scale_refs, out_ref, affinity_ref, inv_ref, scratch, sems = refs
    count, block_rows, _, slots, flat = affinity_ref.shape
    half = flat // 128
    own = lax.axis_index("cols")
    copies = [
        pltpu.make_async_copy(affinity_hbm.at[m ^ own], affinity_ref.at[place], sems.at[place])
        for place, m in enumerate(ranges)
    ]
    if scale_refs:
        inv_copy = pltpu.make_async_copy(scale_refs[0], inv_ref, sems.at[count])
        inv_copy.start()
    for copy in copies:
        copy.start()
    source, target = iota((256, 256), 0), iota((256, 256), 1)
    moved = (source // 64 % 2) * 128 + (source // 128) * 64 + (source % 2) * 32 + source % 64 // 2
    permute = (moved == target).astype(BF16)
    if scale_refs:
        inv_copy.wait()
        prepare_scales(inv_ref[0], *scale_refs[1:])
    for m in range(count):
        copies[m].wait()
        for i in range(block_rows):
            block = affinity_ref[m, i, 0].astype(F32)
            for t in range(half):
                scratch[i % 2, t * slots : (t + 1) * slots, :] = block[:, t * 128 : (t + 1) * 128]
            parts = [
                scratch[i % 2, pl.ds(s, half, stride=slots), :].astype(BF16) for s in range(slots)
            ]
            pairs = [jnp.concatenate(parts[s : s + 2], axis=1) for s in range(0, slots, 2)]
            moved_pairs = jnp.dot(
                jnp.concatenate(pairs, axis=0), permute, preferred_element_type=F32
            ).astype(BF16)
            for s in range(slots // 2):
                piece = moved_pairs[s * half : (s + 1) * half]
                out_ref[m, i, :half, s * 128 : (s + 1) * 128] = piece[:, :128]
                out_ref[m, i, half:, s * 128 : (s + 1) * 128] = piece[:, 128:]


def prep(ranges, affinity, *scale_from):
    _, block_rows, _, slots, flat = affinity.shape
    count = len(ranges)
    outs = [shaped((count, block_rows, 64, slots * 64), BF16)]
    if scale_from:
        outs = [shaped((block_rows * 32, 128), F32), shaped((block_rows, 128), F32)] + outs
    return call(
        functools.partial(prep_kernel, ranges),
        "prep",
        [hbm()] * (1 + len(scale_from)),
        outs,
        (affinity, *scale_from),
        [
            pltpu.VMEM((count,) + affinity.shape[1:], BF16),
            pltpu.VMEM((1, block_rows, 64), F32),
            pltpu.VMEM((2, (flat // 128 + 1) * slots, 128), F32),
            pltpu.SemaphoreType.DMA((count + 1,)),
        ],
    )


def stack_kernel(count, *refs):
    for index in range(count):
        refs[-1][index] = refs[index][...]


def stack(pieces, after):
    return call(
        functools.partial(stack_kernel, len(pieces)),
        "stack",
        [vmem()] * (len(pieces) + len(after)),
        shaped((len(pieces),) + pieces[0].shape, BF16),
        (*pieces, *after),
    )


def fill_table(stacks, offsets, table):
    block_rows = (table.shape[0] - 1) // lax.axis_size("rows")
    low = iota((32, 128), 1) < 64
    pieces = [(ref, index) for ref in stacks for index in range(ref.shape[0])]
    for (ref, index), offset in zip(pieces, offsets):
        base = (lax.axis_index("rows") ^ offset) * block_rows
        for i in range(block_rows):
            block = ref[index, i * 32 : (i + 1) * 32, :]
            turned = jnp.concatenate([block[:, 64:], block[:, :64]], axis=1)
            table[base + i, :32] = jnp.where(low, block, turned)
            table[base + i, 32:] = jnp.where(low, turned, block)


def near_kernel(offsets, *refs):
    *near_refs, table = refs
    table[table.shape[0] - 1] = jnp.zeros(table.shape[1:], BF16)
    fill_table(near_refs, offsets, table)


def near_table(offsets, near, block_rows):
    return call(
        functools.partial(near_kernel, offsets[: len(near)]),
        "near",
        [vmem()] * len(near),
        shaped((len(offsets) * block_rows + 1, 64, 128), BF16),
        near,
    )


def one_product(group, columns, matrix, table, out_ref):
    block_rows, slots = matrix.shape[0], matrix.shape[2] // 64
    chosen = columns[group]
    low = iota((32, 128), 1) < 64
    for i in range(block_rows):
        picked = [table[chosen[i, s]] for s in range(slots)]
        result = jnp.dot(matrix[i], jnp.concatenate(picked, axis=0), preferred_element_type=F32)
        out_ref[i * 32 : (i + 1) * 32, :] = jnp.where(low, result[:32], result[32:]).astype(BF16)


def largest_notes(notes):
    largest = notes[0].astype(F32)
    for note in notes[1:]:
        largest = jnp.maximum(largest, note.astype(F32))
    return largest


def others_kernel(offsets, ranges, filled, old_table, columns, matrix_ref, *refs):
    del old_table
    pieces, (table, *outs) = refs[: len(offsets)], refs[len(offsets) :]
    fill_table(pieces[filled:], offsets[filled:], table)
    terms, first = outs[: len(ranges)], matrix_ref.shape[1] * 32
    if len(outs) > len(ranges):
        notes = largest_notes(
            [ref[index, first:] for ref in pieces for index in range(ref.shape[0])]
        )
        notes = jnp.sum(notes[8:], axis=(0, 1), keepdims=True)
        notes = jnp.broadcast_to(notes, (16, 128)).astype(BF16)
        for ref in outs[len(ranges) :]:
            ref[...] = notes
        for term in terms:
            term[first:, :] = notes
    for place, m in enumerate(ranges):
        group = m ^ lax.axis_index("cols")
        one_product(group, columns, matrix_ref.at[place], table, terms[place])


def own_kernel(columns, matrix_ref, table, out_ref):
    one_product(lax.axis_index("cols"), columns, matrix_ref.at[0], table, out_ref)


def products(offsets, ranges, columns, matrix, own_matrix, pieces, filled, table):
    block_rows = matrix.shape[1]
    extra = pieces[0].shape[1] > block_rows * 32
    rows = block_rows * 32
    outs = [shaped(table.shape, BF16)] + [shaped((rows + 16 * extra, 128), BF16)] * len(ranges)
    if extra:
        outs.append(shaped((16, 128), BF16))
    table, *outs = call(
        functools.partial(others_kernel, offsets, ranges, filled),
        "others",
        [vmem()] * (3 + len(pieces)),
        outs,
        (table, columns, matrix, *pieces),
        input_output_aliases={0: 0},
    )
    terms = [swap(term, "cols", m) for m, term in zip(ranges, outs)]
    own = call(
        own_kernel,
        "own",
        [vmem()] * 3,
        shaped((rows, 128), BF16),
        (columns, own_matrix, table),
    )
    return [own] + terms, outs[len(ranges) :]


def add_terms(terms, rows):
    summed = terms[0][:rows].astype(F32)
    for term in terms[1:]:
        summed = summed + term[:rows].astype(F32)
    return summed


def folded(both):
    gram = both[:64, :64] + both[64:, 64:]
    return jnp.concatenate([gram[:32], gram[32:]], axis=1)


def local_gram(rows):
    both = lax.dot_general(
        rows, rows, (((0,), (0,)), ((), ())), precision=HIGHEST, preferred_element_type=F32
    )
    return folded(both)


def middle_kernel(degree_ref, inverse_ref, *refs):
    terms, out_ref = refs[:-1], refs[-1]
    count = degree_ref.shape[0]
    degree = degree_ref[...]
    rows = add_terms(terms, count) * degree
    out_ref[:count] = (rows * degree).astype(BF16)
    squares = jnp.sum((rows * rows).reshape(-1, 8, 128), axis=0)
    out_ref[count:] = jnp.concatenate([inverse_ref[...], squares], axis=0).astype(BF16)


def middle(degree, inverse, terms):
    return call(
        middle_kernel,
        "middle",
        [vmem()] * (2 + len(terms)),
        shaped((degree.shape[0] + 16, 128), BF16),
        (degree, inverse, *terms),
    )


def row_gram_kernel(*refs):
    *stacks, gram_ref, rows = refs
    lane = iota((32, 128), 1)
    pair = lane % 64 // 2 == iota((32, 128), 0)
    spread = (iota((128, 128), 0) % 2 == iota((128, 128), 1) // 64).astype(BF16)
    count = stacks[0].shape[1] - 16
    pieces = [(ref, index) for ref in stacks for index in range(ref.shape[0])]
    for place, (ref, index) in enumerate(pieces):
        notes = ref[index, count:].astype(F32)
        masked = [
            jnp.where(pair, jnp.broadcast_to(notes[i : i + 1], (32, 128)), 0.0).astype(BF16)
            for i in range(count // 32)
        ]
        inverse = jnp.dot(jnp.concatenate(masked, axis=0), spread, preferred_element_type=F32)
        block = ref[index, :count].astype(F32) * inverse
        rows[place * count : (place + 1) * count, :] = block.astype(BF16)
    both = lax.dot_general(
        rows[...], rows[...], (((0,), (0,)), ((), ())), preferred_element_type=F32
    )
    gram_ref[...] = folded(both)


def row_gram(stacks):
    count = sum(stack.shape[0] for stack in stacks) * (stacks[0].shape[1] - 16)
    return call(
        row_gram_kernel,
        "row_gram",
        [vmem()] * len(stacks),
        shaped((32, 128), F32),
        stacks,
        [pltpu.VMEM((count, 128), BF16)],
    )


def collect_kernel(devices, total, degree_ref, first_ref, notes_ref, *refs):
    terms, (rows_ref, grams_ref) = refs[:-2], refs[-2:]
    count = degree_ref.shape[0]
    largest = largest_notes([notes_ref[...]] + [term[count:] for term in terms[1:]])
    scale = lax.rsqrt(largest[:1] * (devices / total))
    rows = add_terms(terms, count) * degree_ref[...] * scale
    rows_ref[...] = rows
    grams_ref[32:] = first_ref[...] * (scale * scale)
    grams_ref[:32] = local_gram(rows)


def collect(devices, total, degree, first, notes, terms):
    return call(
        functools.partial(collect_kernel, devices, total),
        "collect",
        [vmem()] * (3 + len(terms)),
        (shaped(degree.shape, F32), shaped((64, 128), F32)),
        (degree, first, notes, *terms),
    )


def lower_solve(gram, right):
    work = jnp.concatenate([gram, right], axis=1)
    blocks = gram.shape[0] // 8
    rows = [work[8 * i : 8 * i + 8] for i in range(blocks)]
    at = iota((8, 128), 0)

    def columns(first, column):
        return [
            jnp.broadcast_to(rows[i][:, column : column + 1], (8, 128))
            for i in range(first, blocks)
        ]

    def spread(block, row):
        return jnp.broadcast_to(block[row : row + 1], (8, 128))

    ahead = []
    for b in range(blocks):
        count = blocks - b
        current = ahead + [columns(b, 8 * b + q) for q in range(len(ahead), 8)]
        ahead = []
        if count > 1:
            ahead = [columns(b + 1, 8 * (b + 1) + q) for q in range(4)]
        for q in range(8):
            root = lax.rsqrt(spread(current[q][0], q))
            row = spread(rows[b], q) * root
            column = [x * root for x in current[q]]
            for p in range(q + 1, 8):
                weight = spread(current[q][0], p) * root
                current[p] = [x - y * weight for x, y in zip(current[p], column)]
            below = rows[b] - column[0] * row
            rows[b] = jnp.where(at == q, row, jnp.where(at > q, below, rows[b]))
            for i in range(1, count):
                rows[b + i] = rows[b + i] - column[i] * row
            for p in range(len(ahead)):
                weight = spread(current[q][1], p) * root
                ahead[p] = [x - y * weight for x, y in zip(ahead[p], column[1:])]
    return jnp.concatenate(rows, axis=0)[:, 64:]


def unpacked(packed):
    return jnp.concatenate([packed[:, :64], packed[:, 64:]], axis=0)


def add_columns_kernel(total, *refs):
    parts, (gram_ref, first_ref) = refs[:-2], refs[-2:]
    summed = parts[0][...]
    for part in parts[1:]:
        summed = summed + part[...]
    gram_ref[...] = summed[:32]
    first_ref[...] = summed[32:] / total


def add_columns(total, parts):
    return call(
        functools.partial(add_columns_kernel, total),
        "add_columns",
        [vmem()] * len(parts),
        (shaped((32, 128), F32), shaped((32, 128), F32)),
        parts,
    )


def add_parts_kernel(count, *refs):
    summed = refs[0][...]
    for part in refs[1:count]:
        summed = summed + part[...]
    refs[-1][...] = summed


def add_parts(parts, after):
    return call(
        functools.partial(add_parts_kernel, len(parts)),
        "add_parts",
        [vmem()] * (len(parts) + len(after)),
        shaped(parts[0].shape, F32),
        (*parts, *after),
    )


def first_factor_kernel(gram_ref, out_ref):
    unit = (iota((64, 64), 0) == iota((64, 64), 1)).astype(F32)
    out_ref[...] = lower_solve(unpacked(gram_ref[...]), unit)


def first_factor(gram):
    return call(first_factor_kernel, "first_factor", [vmem()], shaped((64, 64), F32), (gram,))


def dot_turned(left, right):
    return lax.dot_general(
        left, right, (((1,), (1,)), ((), ())), precision=HIGHEST, preferred_element_type=F32
    )


def finish_kernel(total, rows_ref, inverse_ref, *refs):
    out_hbm, out_ref, scratch, sems = refs[-4:]
    block_rows = out_ref.shape[1]
    packed = refs[0][...]
    for part in refs[1:-4]:
        packed = packed + part[...]
    first = inverse_ref[...]
    gram = dot_turned(
        jnp.dot(first, unpacked(packed), precision=HIGHEST, preferred_element_type=F32), first
    )
    inverse = lower_solve(gram / total, first)
    zero = jnp.zeros_like(inverse)
    both = jnp.concatenate(
        [jnp.concatenate([inverse, zero], axis=1), jnp.concatenate([zero, inverse], axis=1)], axis=0
    )
    copies = []
    for part in range(2):
        rows = [rows_ref[i * 32 + part * 16 : i * 32 + (part + 1) * 16, :] for i in range(block_rows)]
        current = dot_turned(jnp.concatenate(rows, axis=0), both)
        first = part * 16 * block_rows
        for i in range(block_rows):
            scratch[pl.ds(first + i, 16, stride=block_rows), :] = current[i * 16 : (i + 1) * 16]
        for t in range(part * 16, (part + 1) * 16):
            out_ref[0, :, t * 128 : (t + 1) * 128] = scratch[t * block_rows : (t + 1) * block_rows, :]
        lanes = pl.ds(part * 2048, 2048)
        copies.append(
            pltpu.make_async_copy(out_ref.at[:, :, lanes], out_hbm.at[:, :, lanes], sems.at[part])
        )
        copies[-1].start()
    for copy in copies:
        copy.wait()


def finish(total, block_rows, rows, inverse, grams):
    shape = (1, block_rows, 32 * 128)
    return pl.pallas_call(
        functools.partial(finish_kernel, total),
        out_shape=shaped(shape, F32),
        in_specs=[vmem()] * (2 + len(grams)),
        out_specs=hbm(),
        scratch_shapes=[
            pltpu.VMEM(shape, F32),
            pltpu.VMEM((rows.shape[0] + block_rows, 128), F32),
            pltpu.SemaphoreType.DMA((2,)),
        ],
        compiler_params=params(),
        name="finish",
    )(rows, inverse, *grams)


def swap(value, axis, mask):
    size = lax.axis_size(axis)
    return lax.ppermute(value, axis, [(index, index ^ mask) for index in range(size)])


def swap_both(value, row_mask, column_mask):
    rows, columns = lax.axis_size("rows"), lax.axis_size("cols")
    pairs = [
        (row * columns + column, (row ^ row_mask) * columns + (column ^ column_mask))
        for row in range(rows)
        for column in range(columns)
    ]
    return lax.ppermute(value, ("rows", "cols"), pairs)


def stages(size):
    if size == 8:
        return [[7, 5, 3], [1]]
    bits, bit = [], 1
    while bit < size:
        bits.append([bit])
        bit *= 2
    return bits


def gather_rows(message, after):
    plan = stages(lax.axis_size("rows"))
    held, offsets = [message], [0]
    for masks in plan[:-1]:
        held = held + [swap(piece, "rows", mask) for mask in masks for piece in held]
        offsets = offsets + [mask ^ offset for mask in masks for offset in offsets]
    near = [piece[None] for piece in held]
    if after:
        near[1] = stack([held[1]], after)
    (last,) = plan[-1]
    offsets = offsets + [last ^ offset for offset in offsets]
    return near, [swap(pieces, "rows", last) for pieces in near], offsets


def add_rows(gram, after):
    *plan, (last,) = stages(lax.axis_size("rows"))
    for masks in plan:
        gram = add_parts([gram] + [swap(gram, "rows", mask) for mask in masks], after)
    return [gram, swap(gram, "rows", last)]


def body(affinity, block_columns, block_counts, inv_degree, panel):
    block_rows, block_size = inv_degree.shape[1:]
    groups, _, _, slots, _ = affinity.shape
    ranks = lax.axis_size("rows")
    total = float(groups * ranks * block_rows * block_size)
    blocks = ranks * block_rows
    live = iota(block_columns.shape, 3) < block_counts[..., None]
    columns = jnp.where(live, jnp.clip(block_columns, 0, blocks - 1), blocks)[:, :, 0]
    panel, inv_degree, affinity = (
        pltpu.with_memory_space_constraint(value, pltpu.HBM) for value in (panel, inv_degree, affinity)
    )
    ranges = list(range(groups - 1, 0, -1))

    scaled = start(panel, inv_degree)
    degree, inverse, matrix = prep(ranges, affinity, inv_degree)
    (own_matrix,) = prep([0], affinity)
    near, far, offsets = gather_rows(scaled, [inverse])
    pieces, filled = near + far, len(near) + len(far) // 2
    table = near_table(offsets, pieces[:filled], block_rows)
    terms, _ = products(offsets, ranges, columns, matrix, own_matrix, pieces, filled, table)
    near, far, offsets = gather_rows(middle(degree, inverse, terms), [])
    pieces, filled = near + far, len(near) + len(far) // 2
    table = near_table(offsets, pieces[:filled], block_rows)
    terms, (notes,) = products(offsets, ranges, columns, matrix, own_matrix, pieces, filled, table)
    devices = float(groups * ranks)
    rows, grams = collect(devices, total, degree, row_gram(near + far), notes, terms)
    flip = 1 if ranks == 8 else 0
    order = [2, 3, 1] if groups == 4 else ranges
    gram, first = add_columns(total, [grams] + [swap_both(grams, flip, m) for m in order])
    inverse = first_factor(first)
    return finish(total, block_rows, rows, inverse, add_rows(gram, [inverse]))


def solution(mesh):
    return jax.shard_map(
        body,
        mesh=mesh,
        in_specs=(
            P(None, "rows", "cols", None, None),
            P(None, "rows", "cols", None),
            P(None, "rows", "cols"),
            P("cols", "rows", None),
            P("cols", "rows", None),
        ),
        out_specs=P("cols", "rows", None),
        check_vma=False,
    )
```

```python
import functools

import jax
import jax.numpy as jnp
from jax import lax
from jax.experimental import pallas as pl
from jax.experimental.pallas import tpu as pltpu
from jax.sharding import PartitionSpec as P

BF16 = jnp.bfloat16
F32 = jnp.float32
HIGHEST = lax.Precision.HIGHEST
MIB = 1024 * 1024


def params(limit=48 * MIB):
    return pltpu.CompilerParams(vmem_limit_bytes=limit)


def vmem():
    return pl.BlockSpec(memory_space=pltpu.VMEM)


def hbm():
    return pl.BlockSpec(memory_space=pltpu.HBM)


def shaped(shape, dtype):
    return jax.ShapeDtypeStruct(shape, dtype)


def iota(shape, dim):
    return lax.broadcasted_iota(jnp.int32, shape, dim)


def call(kernel, name, ins, outs, operands, scratch=(), limit=48 * MIB, **kwargs):
    return pl.pallas_call(
        kernel,
        out_shape=outs,
        in_specs=ins,
        out_specs=jax.tree.map(lambda _: vmem(), outs),
        scratch_shapes=list(scratch),
        compiler_params=params(limit),
        name=name,
        **kwargs,
    )(*operands)


def start_kernel(panel_hbm, inv_hbm, scaled_ref, panel_ref, inv_ref, scratch, sems):
    block_rows, half = inv_ref.shape[1], inv_ref.shape[2] // 2
    copies = [
        pltpu.make_async_copy(inv_hbm, inv_ref, sems.at[0]),
        pltpu.make_async_copy(panel_hbm, panel_ref, sems.at[1]),
    ]
    for copy in copies:
        copy.start()
    copies[0].wait()
    inv = inv_ref[0]
    low = iota((block_rows, 128), 1) < 64
    scales = []
    for t in range(half):
        even, odd = (
            jnp.broadcast_to(inv[:, a : a + 1], (block_rows, 128)) for a in (2 * t, 2 * t + 1)
        )
        scales.append(jnp.where(low, even, odd))
    copies[1].wait()
    for t in range(half):
        scratch[t * block_rows : (t + 1) * block_rows, :] = (
            panel_ref[0, :, t * 128 : (t + 1) * 128] * scales[t]
        )
    for i in range(block_rows):
        part = scratch[pl.ds(i, half, stride=block_rows), :]
        scaled_ref[i * half : (i + 1) * half, :] = part.astype(BF16)


def start(panel, inv_degree):
    block_rows, block_size = inv_degree.shape[1:]
    shape = (block_rows * block_size // 2, 128)
    return call(
        start_kernel,
        "start",
        [hbm(), hbm()],
        shaped(shape, BF16),
        (panel, inv_degree),
        [
            pltpu.VMEM(panel.shape, F32),
            pltpu.VMEM(inv_degree.shape, F32),
            pltpu.VMEM((shape[0] + block_rows, 128), F32),
            pltpu.SemaphoreType.DMA((2,)),
        ],
    )


def prepare_scales(inv, degree_ref, inverse_ref):
    block_rows, block_size = inv.shape
    half = block_size // 2
    pair = iota((half, block_size), 1) // 2 == iota((half, block_size), 0)
    spread = (iota((block_size, 128), 0) % 2 == iota((block_size, 128), 1) // 64).astype(F32)
    rows = [
        jnp.where(pair, jnp.broadcast_to(inv[i : i + 1, :], (half, block_size)), 0.0)
        for i in range(block_rows)
    ]
    degree_ref[...] = jnp.dot(
        jnp.concatenate(rows, axis=0), spread, precision=HIGHEST, preferred_element_type=F32
    )
    inverse = 1.0 / inv
    high = inverse.astype(BF16).astype(F32)
    inverse_ref[...] = jnp.concatenate([high, inverse - high], axis=1)


def prep_kernel(ranges, affinity_hbm, *refs):
    *scale_refs, out_ref, affinity_ref, inv_ref, scratch, sems = refs
    count, block_rows, _, slots, flat = affinity_ref.shape
    half = flat // 128
    own = lax.axis_index("cols")
    copies = [
        pltpu.make_async_copy(affinity_hbm.at[m ^ own], affinity_ref.at[place], sems.at[place])
        for place, m in enumerate(ranges)
    ]
    if scale_refs:
        inv_copy = pltpu.make_async_copy(scale_refs[0], inv_ref, sems.at[count])
        inv_copy.start()
    for copy in copies:
        copy.start()
    source, target = iota((256, 256), 0), iota((256, 256), 1)
    moved = (source // 64 % 2) * 128 + (source // 128) * 64 + (source % 2) * 32 + source % 64 // 2
    permute = (moved == target).astype(BF16)
    if scale_refs:
        inv_copy.wait()
        prepare_scales(inv_ref[0], *scale_refs[1:])
    for m in range(count):
        copies[m].wait()
        for i in range(block_rows):
            block = affinity_ref[m, i, 0].astype(F32)
            for t in range(half):
                scratch[i % 2, t * slots : (t + 1) * slots, :] = block[:, t * 128 : (t + 1) * 128]
            parts = [
                scratch[i % 2, pl.ds(s, half, stride=slots), :].astype(BF16) for s in range(slots)
            ]
            pairs = [jnp.concatenate(parts[s : s + 2], axis=1) for s in range(0, slots, 2)]
            moved_pairs = jnp.dot(
                jnp.concatenate(pairs, axis=0), permute, preferred_element_type=F32
            ).astype(BF16)
            for s in range(slots // 2):
                piece = moved_pairs[s * half : (s + 1) * half]
                out_ref[m, i, :half, s * 128 : (s + 1) * 128] = piece[:, :128]
                out_ref[m, i, half:, s * 128 : (s + 1) * 128] = piece[:, 128:]


def prep(ranges, affinity, *scale_from):
    _, block_rows, _, slots, flat = affinity.shape
    count = len(ranges)
    outs = [shaped((count, block_rows, 64, slots * 64), BF16)]
    if scale_from:
        outs = [shaped((block_rows * 32, 128), F32), shaped((block_rows, 128), F32)] + outs
    return call(
        functools.partial(prep_kernel, ranges),
        "prep",
        [hbm()] * (1 + len(scale_from)),
        outs,
        (affinity, *scale_from),
        [
            pltpu.VMEM((count,) + affinity.shape[1:], BF16),
            pltpu.VMEM((1, block_rows, 64), F32),
            pltpu.VMEM((2, (flat // 128 + 1) * slots, 128), F32),
            pltpu.SemaphoreType.DMA((count + 1,)),
        ],
    )


def stack_kernel(count, *refs):
    for index in range(count):
        refs[-1][index] = refs[index][...]


def stack(pieces, after):
    return call(
        functools.partial(stack_kernel, len(pieces)),
        "stack",
        [vmem()] * (len(pieces) + len(after)),
        shaped((len(pieces),) + pieces[0].shape, BF16),
        (*pieces, *after),
    )


def fill_table(stacks, offsets, table):
    block_rows = (table.shape[0] - 1) // lax.axis_size("rows")
    low = iota((32, 128), 1) < 64
    pieces = [(ref, index) for ref in stacks for index in range(ref.shape[0])]
    for (ref, index), offset in zip(pieces, offsets):
        base = (lax.axis_index("rows") ^ offset) * block_rows
        for i in range(block_rows):
            block = ref[index, i * 32 : (i + 1) * 32, :]
            turned = jnp.concatenate([block[:, 64:], block[:, :64]], axis=1)
            table[base + i, :32] = jnp.where(low, block, turned)
            table[base + i, 32:] = jnp.where(low, turned, block)


def near_kernel(offsets, *refs):
    *near_refs, table = refs
    table[table.shape[0] - 1] = jnp.zeros(table.shape[1:], BF16)
    fill_table(near_refs, offsets, table)


def near_table(offsets, near, block_rows):
    return call(
        functools.partial(near_kernel, offsets[: len(near)]),
        "near",
        [vmem()] * len(near),
        shaped((len(offsets) * block_rows + 1, 64, 128), BF16),
        near,
    )


def one_product(group, columns, matrix, table, out_ref):
    block_rows, slots = matrix.shape[0], matrix.shape[2] // 64
    chosen = columns[group]
    low = iota((32, 128), 1) < 64
    for i in range(block_rows):
        picked = [table[chosen[i, s]] for s in range(slots)]
        result = jnp.dot(matrix[i], jnp.concatenate(picked, axis=0), preferred_element_type=F32)
        out_ref[i * 32 : (i + 1) * 32, :] = jnp.where(low, result[:32], result[32:]).astype(BF16)


def largest_notes(notes):
    largest = notes[0].astype(F32)
    for note in notes[1:]:
        largest = jnp.maximum(largest, note.astype(F32))
    return largest


def others_kernel(offsets, ranges, filled, old_table, columns, matrix_ref, *refs):
    del old_table
    pieces, (table, *outs) = refs[: len(offsets)], refs[len(offsets) :]
    fill_table(pieces[filled:], offsets[filled:], table)
    terms, first = outs[: len(ranges)], matrix_ref.shape[1] * 32
    if len(outs) > len(ranges):
        notes = largest_notes(
            [ref[index, first:] for ref in pieces for index in range(ref.shape[0])]
        )
        notes = jnp.sum(notes[8:], axis=(0, 1), keepdims=True)
        notes = jnp.broadcast_to(notes, (16, 128)).astype(BF16)
        for ref in outs[len(ranges) :]:
            ref[...] = notes
        for term in terms:
            term[first:, :] = notes
    for place, m in enumerate(ranges):
        group = m ^ lax.axis_index("cols")
        one_product(group, columns, matrix_ref.at[place], table, terms[place])


def own_kernel(columns, matrix_ref, table, out_ref):
    one_product(lax.axis_index("cols"), columns, matrix_ref.at[0], table, out_ref)


def products(offsets, ranges, columns, matrix, own_matrix, pieces, filled, table):
    block_rows = matrix.shape[1]
    extra = pieces[0].shape[1] > block_rows * 32
    rows = block_rows * 32
    outs = [shaped(table.shape, BF16)] + [shaped((rows + 16 * extra, 128), BF16)] * len(ranges)
    if extra:
        outs.append(shaped((16, 128), BF16))
    table, *outs = call(
        functools.partial(others_kernel, offsets, ranges, filled),
        "others",
        [vmem()] * (3 + len(pieces)),
        outs,
        (table, columns, matrix, *pieces),
        input_output_aliases={0: 0},
    )
    terms = [swap(term, "cols", m) for m, term in zip(ranges, outs)]
    own = call(
        own_kernel,
        "own",
        [vmem()] * 3,
        shaped((rows, 128), BF16),
        (columns, own_matrix, table),
    )
    return [own] + terms, outs[len(ranges) :]


def add_terms(terms, rows):
    summed = terms[0][:rows].astype(F32)
    for term in terms[1:]:
        summed = summed + term[:rows].astype(F32)
    return summed


def folded(both):
    gram = both[:64, :64] + both[64:, 64:]
    return jnp.concatenate([gram[:32], gram[32:]], axis=1)


def local_gram(rows):
    both = lax.dot_general(
        rows, rows, (((0,), (0,)), ((), ())), precision=HIGHEST, preferred_element_type=F32
    )
    return folded(both)


def middle_kernel(degree_ref, inverse_ref, *refs):
    terms, out_ref = refs[:-1], refs[-1]
    count = degree_ref.shape[0]
    degree = degree_ref[...]
    rows = add_terms(terms, count) * degree
    out_ref[:count] = (rows * degree).astype(BF16)
    squares = jnp.sum((rows * rows).reshape(-1, 8, 128), axis=0)
    out_ref[count:] = jnp.concatenate([inverse_ref[...], squares], axis=0).astype(BF16)


def middle(degree, inverse, terms):
    return call(
        middle_kernel,
        "middle",
        [vmem()] * (2 + len(terms)),
        shaped((degree.shape[0] + 16, 128), BF16),
        (degree, inverse, *terms),
    )


def row_gram_kernel(*refs):
    *stacks, gram_ref, rows = refs
    lane = iota((32, 128), 1)
    pair = lane % 64 // 2 == iota((32, 128), 0)
    spread = (iota((128, 128), 0) % 2 == iota((128, 128), 1) // 64).astype(BF16)
    count = stacks[0].shape[1] - 16
    pieces = [(ref, index) for ref in stacks for index in range(ref.shape[0])]
    for place, (ref, index) in enumerate(pieces):
        notes = ref[index, count:].astype(F32)
        masked = [
            jnp.where(pair, jnp.broadcast_to(notes[i : i + 1], (32, 128)), 0.0).astype(BF16)
            for i in range(count // 32)
        ]
        inverse = jnp.dot(jnp.concatenate(masked, axis=0), spread, preferred_element_type=F32)
        block = ref[index, :count].astype(F32) * inverse
        rows[place * count : (place + 1) * count, :] = block.astype(BF16)
    both = lax.dot_general(
        rows[...], rows[...], (((0,), (0,)), ((), ())), preferred_element_type=F32
    )
    gram_ref[...] = folded(both)


def row_gram(stacks):
    count = sum(stack.shape[0] for stack in stacks) * (stacks[0].shape[1] - 16)
    return call(
        row_gram_kernel,
        "row_gram",
        [vmem()] * len(stacks),
        shaped((32, 128), F32),
        stacks,
        [pltpu.VMEM((count, 128), BF16)],
    )


def collect_kernel(devices, total, degree_ref, first_ref, notes_ref, *refs):
    terms, (rows_ref, grams_ref) = refs[:-2], refs[-2:]
    count = degree_ref.shape[0]
    largest = largest_notes([notes_ref[...]] + [term[count:] for term in terms[1:]])
    scale = lax.rsqrt(largest[:1] * (devices / total))
    rows = add_terms(terms, count) * degree_ref[...] * scale
    rows_ref[...] = rows
    grams_ref[32:] = first_ref[...] * (scale * scale)
    grams_ref[:32] = local_gram(rows)


def collect(devices, total, degree, first, notes, terms):
    return call(
        functools.partial(collect_kernel, devices, total),
        "collect",
        [vmem()] * (3 + len(terms)),
        (shaped(degree.shape, F32), shaped((64, 128), F32)),
        (degree, first, notes, *terms),
    )


def lower_solve(gram, right):
    work = jnp.concatenate([gram, right], axis=1)
    blocks = gram.shape[0] // 8
    rows = [work[8 * i : 8 * i + 8] for i in range(blocks)]
    at = iota((8, 128), 0)

    def columns(first, column):
        return [
            jnp.broadcast_to(rows[i][:, column : column + 1], (8, 128))
            for i in range(first, blocks)
        ]

    def spread(block, row):
        return jnp.broadcast_to(block[row : row + 1], (8, 128))

    ahead = []
    for b in range(blocks):
        count = blocks - b
        current = ahead + [columns(b, 8 * b + q) for q in range(len(ahead), 8)]
        ahead = []
        if count > 1:
            ahead = [columns(b + 1, 8 * (b + 1) + q) for q in range(4)]
        for q in range(8):
            root = lax.rsqrt(spread(current[q][0], q))
            row = spread(rows[b], q) * root
            column = [x * root for x in current[q]]
            for p in range(q + 1, 8):
                weight = spread(current[q][0], p) * root
                current[p] = [x - y * weight for x, y in zip(current[p], column)]
            below = rows[b] - column[0] * row
            rows[b] = jnp.where(at == q, row, jnp.where(at > q, below, rows[b]))
            for i in range(1, count):
                rows[b + i] = rows[b + i] - column[i] * row
            for p in range(len(ahead)):
                weight = spread(current[q][1], p) * root
                ahead[p] = [x - y * weight for x, y in zip(ahead[p], column[1:])]
    return jnp.concatenate(rows, axis=0)[:, 64:]


def unpacked(packed):
    return jnp.concatenate([packed[:, :64], packed[:, 64:]], axis=0)


def add_columns_kernel(total, *refs):
    parts, (gram_ref, first_ref) = refs[:-2], refs[-2:]
    summed = parts[0][...]
    for part in parts[1:]:
        summed = summed + part[...]
    gram_ref[...] = summed[:32]
    first_ref[...] = summed[32:] / total


def add_columns(total, parts):
    return call(
        functools.partial(add_columns_kernel, total),
        "add_columns",
        [vmem()] * len(parts),
        (shaped((32, 128), F32), shaped((32, 128), F32)),
        parts,
    )


def add_parts_kernel(count, *refs):
    summed = refs[0][...]
    for part in refs[1:count]:
        summed = summed + part[...]
    refs[-1][...] = summed


def add_parts(parts, after):
    return call(
        functools.partial(add_parts_kernel, len(parts)),
        "add_parts",
        [vmem()] * (len(parts) + len(after)),
        shaped(parts[0].shape, F32),
        (*parts, *after),
    )


def first_factor_kernel(gram_ref, out_ref):
    unit = (iota((64, 64), 0) == iota((64, 64), 1)).astype(F32)
    out_ref[...] = lower_solve(unpacked(gram_ref[...]), unit)


def first_factor(gram):
    return call(first_factor_kernel, "first_factor", [vmem()], shaped((64, 64), F32), (gram,))


def dot_turned(left, right):
    return lax.dot_general(
        left, right, (((1,), (1,)), ((), ())), precision=HIGHEST, preferred_element_type=F32
    )


def halves(value):
    high = value.astype(BF16)
    return high, (value - high.astype(F32)).astype(BF16)


def finish_kernel(total, rows_ref, inverse_ref, *refs):
    out_ref, scratch = refs[-2:]
    block_rows = out_ref.shape[1]
    packed = refs[0][...]
    for part in refs[1:-2]:
        packed = packed + part[...]
    first = inverse_ref[...]
    gram = dot_turned(
        jnp.dot(first, unpacked(packed), precision=HIGHEST, preferred_element_type=F32), first
    )
    inverse = lower_solve(gram / total, first)
    zero = jnp.zeros_like(inverse)
    both = jnp.concatenate(
        [jnp.concatenate([inverse, zero], axis=1), jnp.concatenate([zero, inverse], axis=1)], axis=0
    )
    high, low = halves(rows_ref[...])
    both_high, both_low = halves(both)
    current = lax.dot_general(
        jnp.concatenate([high, low, high], axis=1),
        jnp.concatenate([both_high, both_high, both_low], axis=1),
        (((1,), (1,)), ((), ())),
        preferred_element_type=F32,
    )
    for i in range(block_rows):
        scratch[pl.ds(i, 32, stride=block_rows), :] = current[i * 32 : (i + 1) * 32]
    for t in range(32):
        out_ref[0, :, t * 128 : (t + 1) * 128] = scratch[t * block_rows : (t + 1) * block_rows, :]


def finish(total, block_rows, rows, inverse, grams):
    return call(
        functools.partial(finish_kernel, total),
        "finish",
        [vmem()] * (2 + len(grams)),
        shaped((1, block_rows, 32 * 128), F32),
        (rows, inverse, *grams),
        [pltpu.VMEM((rows.shape[0] + block_rows, 128), F32)],
    )


def swap(value, axis, mask):
    size = lax.axis_size(axis)
    return lax.ppermute(value, axis, [(index, index ^ mask) for index in range(size)])


def swap_both(value, row_mask, column_mask):
    rows, columns = lax.axis_size("rows"), lax.axis_size("cols")
    pairs = [
        (row * columns + column, (row ^ row_mask) * columns + (column ^ column_mask))
        for row in range(rows)
        for column in range(columns)
    ]
    return lax.ppermute(value, ("rows", "cols"), pairs)


def stages(size):
    if size == 8:
        return [[7, 5, 3], [1]]
    bits, bit = [], 1
    while bit < size:
        bits.append([bit])
        bit *= 2
    return bits


def gather_rows(message, after):
    plan = stages(lax.axis_size("rows"))
    held, offsets = [message], [0]
    for masks in plan[:-1]:
        held = held + [swap(piece, "rows", mask) for mask in masks for piece in held]
        offsets = offsets + [mask ^ offset for mask in masks for offset in offsets]
    near = [piece[None] for piece in held]
    if after:
        near[1] = stack([held[1]], after)
    (last,) = plan[-1]
    offsets = offsets + [last ^ offset for offset in offsets]
    return near, [swap(pieces, "rows", last) for pieces in near], offsets


def add_rows(gram, after):
    *plan, (last,) = stages(lax.axis_size("rows"))
    for masks in plan:
        gram = add_parts([gram] + [swap(gram, "rows", mask) for mask in masks], after)
    return [gram, swap(gram, "rows", last)]


def body(affinity, block_columns, block_counts, inv_degree, panel):
    block_rows, block_size = inv_degree.shape[1:]
    groups, _, _, slots, _ = affinity.shape
    ranks = lax.axis_size("rows")
    total = float(groups * ranks * block_rows * block_size)
    blocks = ranks * block_rows
    live = iota(block_columns.shape, 3) < block_counts[..., None]
    columns = jnp.where(live, jnp.clip(block_columns, 0, blocks - 1), blocks)[:, :, 0]
    panel, inv_degree, affinity = (
        pltpu.with_memory_space_constraint(value, pltpu.HBM) for value in (panel, inv_degree, affinity)
    )
    ranges = list(range(groups - 1, 0, -1))

    scaled = start(panel, inv_degree)
    degree, inverse, matrix = prep(ranges, affinity, inv_degree)
    (own_matrix,) = prep([0], affinity)
    near, far, offsets = gather_rows(scaled, [inverse])
    pieces, filled = near + far, len(near) + len(far) // 2
    table = near_table(offsets, pieces[:filled], block_rows)
    terms, _ = products(offsets, ranges, columns, matrix, own_matrix, pieces, filled, table)
    near, far, offsets = gather_rows(middle(degree, inverse, terms), [])
    pieces, filled = near + far, len(near) + len(far) // 2
    table = near_table(offsets, pieces[:filled], block_rows)
    terms, (notes,) = products(offsets, ranges, columns, matrix, own_matrix, pieces, filled, table)
    devices = float(groups * ranks)
    rows, grams = collect(devices, total, degree, row_gram(near + far), notes, terms)
    flip = 1 if ranks == 8 else 0
    order = [2, 3, 1] if groups == 4 else ranges
    gram, first = add_columns(total, [grams] + [swap_both(grams, flip, m) for m in order])
    inverse = first_factor(first)
    return finish(total, block_rows, rows, inverse, add_rows(gram, [inverse]))


def solution(mesh):
    return jax.shard_map(
        body,
        mesh=mesh,
        in_specs=(
            P(None, "rows", "cols", None, None),
            P(None, "rows", "cols", None),
            P(None, "rows", "cols"),
            P("cols", "rows", None),
            P("cols", "rows", None),
        ),
        out_specs=P("cols", "rows", None),
        check_vma=False,
    )
```
